32 devices in a mesh: dp: 2 (over x), seq: 4 (over z), mp: 4 (over y, core).
Axes of the slice: x: 2, y: 2, z: 4, core: 2. Of those that a mesh axis runs over, the one named last changes fastest.
Arguments:
- inputs: bfloat16 [8, 1024, 1536], P('dp', 'seq', 'mp'), may hold values from -6 to 6
- gain_mix: bfloat16 [1536], P('mp'), may hold values from 0.25 to 1.75
- w_in: bfloat16 [1536, 3, 1536], P(None, None, 'mp'), may hold values from -0.15625 to 0.15625
- kernel: bfloat16 [3, 1536], P(None, 'mp'), may hold values from -3.5 to 3.5
- w_out: bfloat16 [1536, 1536], P('mp'), may hold values from -0.15625 to 0.15625
- gain_ff: bfloat16 [1536], P('mp'), may hold values from 0.25 to 1.75
- w_gate: bfloat16 [1536, 6912], P(None, 'mp'), may hold values from -0.15625 to 0.15625
- w_up: bfloat16 [1536, 6912], P(None, 'mp'), may hold values from -0.15625 to 0.15625
- w_down: bfloat16 [6912, 1536], P('mp'), may hold values from -0.109375 to 0.109375
- cotangent: bfloat16 [8, 1024, 1536], P('dp', 'seq', 'mp'), may hold values from -6 to 6
Outputs:
- block_out: bfloat16 [8, 1024, 1536], P('dp', 'seq', 'mp')
- grad_input: bfloat16 [8, 1024, 1536], P('dp', 'seq', 'mp')
- grad_gain_mix: float32 [1536], P('mp')
- grad_w_in: float32 [1536, 3, 1536], P(('dp', 'seq'), None, 'mp')
- grad_kernel: float32 [3, 1536], P(None, 'mp')
- grad_w_out: float32 [1536, 1536], P('mp', ('dp', 'seq'))
- grad_gain_ff: float32 [1536], P('mp')
- grad_w_gate: float32 [1536, 6912], P(('dp', 'seq'), 'mp')
- grad_w_up: float32 [1536, 6912], P(('dp', 'seq'), 'mp')
- grad_w_down: float32 [6912, 1536], P('mp', ('dp', 'seq'))
The draws below stay inside these ranges and needn't reach their ends.
All inputs are finite; a program needn't handle non-finite values.
Results may differ from the reference program's by a relative error of at most 0.011.
Values may be sent and summed in bfloat16 or wider, within the bound.
A program may use at most 192 MiB of HBM per device.

```python
import jax
import jax.numpy as jnp
from jax import lax

D = 1536
FF = 6912
KERNEL = 3
SEQS = 8
LENGTH = 1024


def level_of(own_key, extent, shards, low, top_value):
    def one(axis_at, shards_of):
        draws = jax.random.uniform(jax.random.fold_in(jax.random.fold_in(own_key, 6), axis_at), (shards_of,), jnp.float32, low / len(shards), top_value / len(shards))
        return jnp.repeat(jnp.exp(draws), extent[axis_at] // shards_of).reshape((-1,) + (1,) * (len(extent) - axis_at - 1))

    gain = one(*shards[0])
    for cut in shards[1:]:
        gain = gain * one(*cut)
    return gain


def centred(stream_key, shape, deviation, limit, shards=(), kind=jnp.bfloat16):
    loudness = level_of(stream_key, shape, shards, -0.22, 0.18) if shards else 1.0
    values = jax.random.normal(stream_key, shape, jnp.float32) * deviation * loudness
    return jnp.minimum(jnp.maximum(values, -limit), limit).astype(kind)


def setup_inputs(seed: int = 0) -> dict:
    seeds = jax.random.split(jax.random.key(seed), 11)
    inputs = centred(seeds[0], (SEQS, LENGTH, D), 1.0, 6.0, ((0, 2), (1, 4), (2, 4)))
    gain_mix = jnp.clip(1.0 + 0.15 * jax.random.normal(seeds[1], (D,), jnp.float32), 0.25, 1.75).astype(jnp.bfloat16)
    w_in = centred(seeds[2], (D, 3, D), D ** -0.5, 0.15625, ((2, 4),))
    kernel = centred(seeds[3], (KERNEL, D), KERNEL ** -0.5, 3.5, ((1, 4),))
    w_out = centred(seeds[4], (D, D), D ** -0.5, 0.15625, ((0, 4),))
    gain_ff = jnp.clip(1.0 + 0.15 * jax.random.normal(seeds[5], (D,), jnp.float32), 0.25, 1.75).astype(jnp.bfloat16)
    w_gate = centred(seeds[6], (D, FF), D ** -0.5, 0.15625, ((1, 4),))
    w_up = centred(seeds[7], (D, FF), D ** -0.5, 0.15625, ((1, 4),))
    w_down = centred(seeds[8], (FF, D), (FF // 2) ** -0.5, 0.109375, ((0, 4),))
    cotangent = centred(seeds[9], (SEQS, LENGTH, D), 1.0, 6.0, ((0, 2), (1, 4), (2, 4)))
    return {"inputs": inputs, "gain_mix": gain_mix, "w_in": w_in, "kernel": kernel, "w_out": w_out, "gain_ff": gain_ff, "w_gate": w_gate, "w_up": w_up, "w_down": w_down, "cotangent": cotangent}


@jax.custom_vjp
def low(v):
    return lax.optimization_barrier(v.astype(jnp.bfloat16)).astype(jnp.float32)

@jax.custom_vjp
def low_back(v):
    return v

def low_keep(v):
    return (low(v), None)

def low_pass(kept, grad):
    return (grad,)

def back_keep(v):
    return (v, None)

def back_low(kept, grad):
    return (low(grad),)
low.defvjp(low_keep, low_pass)
low_back.defvjp(back_keep, back_low)
EPS = 1e-05

def scaled(values, gain_vec):
    scale = lax.rsqrt(lax.optimization_barrier(jnp.mean(values * values, axis=-1, keepdims=True)) + EPS)
    return values * scale * gain_vec

def matmul(left, right):
    return jnp.dot(left, right, precision=lax.Precision.HIGHEST)

def forward(inputs, gain_mix, w_in, kernel, w_out, gain_ff, w_gate, w_up, w_down):
    normed_in = low(scaled(inputs, gain_mix))
    proj = low_back(jnp.einsum('td,dkc->tkc', normed_in, w_in, precision=lax.Precision.HIGHEST))
    b_times_x = low(proj[:, 0] * proj[:, 2])
    padded = jnp.concatenate([jnp.zeros((2, b_times_x.shape[1]), jnp.float32), b_times_x], 0)
    conv = low_back(kernel[0] * padded[:-2] + kernel[1] * padded[1:-1] + kernel[2] * padded[2:])
    mixed = low(proj[:, 1] * conv)
    hidden_one = inputs + low_back(matmul(mixed, w_out))
    normed_ff = low(scaled(hidden_one, gain_ff))
    gate = low_back(matmul(normed_ff, w_gate))
    up_proj = low_back(matmul(normed_ff, w_up))
    hidden = low(jax.nn.silu(gate) * up_proj)
    return hidden_one + low_back(matmul(hidden, w_down))

def reference(inputs, gain_mix, w_in, kernel, w_out, gain_ff, w_gate, w_up, w_down, cotangent):
    weights = (gain_mix.astype(jnp.float32), w_in.astype(jnp.float32), kernel.astype(jnp.float32), w_out.astype(jnp.float32), gain_ff.astype(jnp.float32), w_gate.astype(jnp.float32), w_up.astype(jnp.float32), w_down.astype(jnp.float32))
    zeros = tuple((jnp.zeros(weight.shape, jnp.float32) for weight in weights))

    def one_sequence(totals, pair):
        seq_in, seq_grad = pair
        result, pull = jax.vjp(forward, seq_in.astype(jnp.float32), *weights)
        grads = pull(seq_grad.astype(jnp.float32))
        totals = tuple((total + grad for total, grad in zip(totals, grads[1:])))
        return (totals, (result.astype(jnp.bfloat16), grads[0].astype(jnp.bfloat16)))
    totals, (block_out, grad_input) = lax.scan(one_sequence, zeros, (inputs, cotangent))
    return (block_out, grad_input, totals[0], totals[1], totals[2], totals[3], totals[4], totals[5], totals[6], totals[7])
```

```python
import jax
import jax.numpy as jnp
from jax import lax
from jax.sharding import PartitionSpec as P

EPS = 1e-05


def shifted(array, axis, by):
    count = lax.axis_size(axis)
    pairs = [(i, i + by) for i in range(count) if 0 <= i + by < count]
    return lax.ppermute(array, axis, pairs)


def contract_rows(left, right):
    return lax.dot_general(
        left, right, (((0,), (0,)), ((), ())), preferred_element_type=jnp.float32
    )


def contract_cols(left, right):
    return lax.dot_general(
        left, right, (((1,), (1,)), ((), ())), preferred_element_type=jnp.float32
    )


def on_device(inputs, gain_mix, w_in, kernel, w_out, gain_ff, w_gate, w_up, w_down, cotangent):
    groups, seq_rows, local_width = inputs.shape
    full_width = local_width * lax.axis_size("mp")
    tokens = groups * seq_rows
    x_float = inputs.reshape(tokens, local_width).astype(jnp.float32)
    gain_one = gain_mix.astype(jnp.float32)
    gain_two = gain_ff.astype(jnp.float32)
    taps = kernel.astype(jnp.float32)

    def row_total(values):
        return lax.psum(jnp.sum(values, axis=-1, keepdims=True), "mp")

    def all_features(values):
        return lax.all_gather(values, "mp", axis=1, tiled=True)

    def share_sums(values):
        return lax.psum_scatter(
            values.astype(jnp.bfloat16), "mp", scatter_dimension=1, tiled=True
        ).astype(jnp.float32)

    def scattered(values, dim):
        return lax.psum_scatter(
            values.astype(jnp.bfloat16), ("dp", "seq"), scatter_dimension=dim, tiled=True
        ).astype(jnp.float32)

    def norm_scale(values):
        return lax.rsqrt(row_total(values * values) / full_width + EPS)

    def norm_back(values, scale, gain_vec, upstream):
        inner = row_total(gain_vec * upstream * values)
        grad_values = scale * gain_vec * upstream - values * scale**3 * inner / full_width
        return (grad_values, jnp.sum(upstream * values * scale, axis=0))

    scale_one = norm_scale(x_float)
    normed_in = all_features((x_float * scale_one * gain_one).astype(jnp.bfloat16))
    proj = jnp.einsum("td,dkc->tkc", normed_in, w_in, preferred_element_type=jnp.float32)
    b_gate = proj[:, 0]
    c_gate = proj[:, 1]
    values_v = proj[:, 2]
    b_times_x = (b_gate * values_v).astype(jnp.bfloat16).reshape(groups, seq_rows, local_width)
    before = shifted(b_times_x[:, seq_rows - 2 :], "seq", 1)
    padded = jnp.concatenate([before, b_times_x], 1).astype(jnp.float32)
    conv = taps[0] * padded[:, :-2] + taps[1] * padded[:, 1:-1] + taps[2] * padded[:, 2:]
    conv = conv.reshape(tokens, local_width)
    mixed = (c_gate * conv).astype(jnp.bfloat16)
    hidden_one = x_float + share_sums(jnp.dot(mixed, w_out, preferred_element_type=jnp.float32))
    scale_two = norm_scale(hidden_one)
    normed_ff = all_features((hidden_one * scale_two * gain_two).astype(jnp.bfloat16))
    gate = jnp.dot(normed_ff, w_gate, preferred_element_type=jnp.float32)
    up_proj = jnp.dot(normed_ff, w_up, preferred_element_type=jnp.float32)
    sigma = jax.nn.sigmoid(gate)
    active = gate * sigma
    hidden = (active * up_proj).astype(jnp.bfloat16)
    ffn_out = share_sums(jnp.dot(hidden, w_down, preferred_element_type=jnp.float32))
    block_out = (hidden_one + ffn_out).astype(jnp.bfloat16).reshape(groups, seq_rows, local_width)
    grad_flat = cotangent.reshape(tokens, local_width)
    grad_full = all_features(grad_flat)
    grad_down = contract_rows(hidden, grad_full)
    grad_hidden = contract_cols(grad_full, w_down)
    grad_gate_act = (grad_hidden * up_proj * sigma * (1.0 + gate * (1.0 - sigma))).astype(
        jnp.bfloat16
    )
    grad_up_act = (grad_hidden * active).astype(jnp.bfloat16)
    grad_gate = contract_rows(normed_ff, grad_gate_act)
    grad_up = contract_rows(normed_ff, grad_up_act)
    grad_normed_ff = share_sums(
        contract_cols(grad_gate_act, w_gate) + contract_cols(grad_up_act, w_up)
    )
    grad_norm_two, grad_gain_two = norm_back(hidden_one, scale_two, gain_two, grad_normed_ff)
    grad_hidden_one = grad_flat.astype(jnp.float32) + grad_norm_two
    grad_out_full = all_features(grad_hidden_one.astype(jnp.bfloat16))
    grad_out = contract_rows(mixed, grad_out_full)
    grad_mixed = contract_cols(grad_out_full, w_out)
    grad_c = grad_mixed * conv
    grad_conv = (grad_mixed * c_gate).astype(jnp.bfloat16).reshape(groups, seq_rows, local_width)
    after = shifted(grad_conv[:, :2], "seq", -1)
    extended = jnp.concatenate([grad_conv, after], 1).astype(jnp.float32)
    grad_bx = taps[2] * extended[:, :-2] + taps[1] * extended[:, 1:-1] + taps[0] * extended[:, 2:]
    grad_bx = grad_bx.reshape(tokens, local_width)
    conv_grad_float = extended[:, :-2]
    grad_taps = jnp.stack(
        [
            jnp.sum(conv_grad_float * padded[:, :-2], axis=(0, 1)),
            jnp.sum(conv_grad_float * padded[:, 1:-1], axis=(0, 1)),
            jnp.sum(conv_grad_float * padded[:, 2:], axis=(0, 1)),
        ]
    )
    grad_proj = jnp.stack([grad_bx * values_v, grad_c, grad_bx * b_gate], 1).astype(jnp.bfloat16)
    grad_in = jnp.einsum("td,tkc->dkc", normed_in, grad_proj, preferred_element_type=jnp.float32)
    grad_normed_in = share_sums(
        jnp.einsum("tkc,dkc->td", grad_proj, w_in, preferred_element_type=jnp.float32)
    )
    grad_norm_one, grad_gain_one = norm_back(x_float, scale_one, gain_one, grad_normed_in)
    grad_input = (
        (grad_hidden_one + grad_norm_one)
        .astype(jnp.bfloat16)
        .reshape(groups, seq_rows, local_width)
    )
    small_sums = lax.psum((grad_gain_one, grad_taps, grad_gain_two), ("dp", "seq"))
    by_row = (
        scattered(grad_in, 0),
        scattered(grad_gate, 0),
        scattered(grad_up, 0),
    )
    by_col = (
        scattered(grad_out, 1),
        scattered(grad_down, 1),
    )
    return (
        block_out,
        grad_input,
        small_sums[0],
        by_row[0],
        small_sums[1],
        by_col[0],
        small_sums[2],
        by_row[1],
        by_row[2],
        by_col[1],
    )


def solution(mesh):
    placed = (
        P("dp", "seq", "mp"),
        P("mp"),
        P(None, None, "mp"),
        P(None, "mp"),
        P("mp", None),
        P("mp"),
        P(None, "mp"),
        P(None, "mp"),
        P("mp", None),
        P("dp", "seq", "mp"),
    )
    return jax.shard_map(
        on_device,
        mesh=mesh,
        in_specs=placed,
        out_specs=(
            P("dp", "seq", "mp"),
            P("dp", "seq", "mp"),
            P("mp"),
            P(("dp", "seq"), None, "mp"),
            P(None, "mp"),
            P("mp", ("dp", "seq")),
            P("mp"),
            P(("dp", "seq"), "mp"),
            P(("dp", "seq"), "mp"),
            P("mp", ("dp", "seq")),
        ),
        check_vma=False,
    )
```

```python
import functools

import jax
import jax.numpy as jnp
from jax import lax
from jax.experimental import pallas as pl
from jax.experimental.pallas import tpu as pltpu
from jax.sharding import PartitionSpec as P

EPS = 1e-05
MESH = pl.DeviceIdType.MESH
BF = jnp.bfloat16
F32 = jnp.float32
ROWS = 32
ANY = pl.BlockSpec(memory_space=pl.ANY)
VMEM = pl.BlockSpec(memory_space=pltpu.VMEM)


def nn(left, right):
    return lax.dot_general(left, right, (((1,), (0,)), ((), ())), preferred_element_type=F32)


def nt(left, right):
    return lax.dot_general(left, right, (((1,), (1,)), ((), ())), preferred_element_type=F32)


def backward_kernel(
    dims,
    hidden_h, gate_h, up_h, a1_h, a2_h, x_h, h1_h, cot_h, bcv_h, before_v,
    wd_h, wg_h, wu_h, wo_h, wi_h, gains_v, taps_v,
    gdown_h, ggate_h, gup_h, gout_h, gin_h, gx_h, small_v,
    lt, r, w0, wg, wu, wo, cotc, h1c, xc, xo, bcv, bxp, dbuf, dcp, dhoc, dh1s, r1s,
    xs, xr, s_buf, zs, zr, ob,
    ck, cs, cr, ys, yr, da2f, ck2, cs2, cr2, ys2, yr2, qk2,
    ins, inr, iys, iyr, gxb, halo_s, halo_r,
    xs_sem, xr_sem, zs_sem, zr_sem, ob_sem, c_sem, y_sem, f_sem, c2_sem, y2_sem,
    i_sem, iy_sem, halo_sem, w_sem, l_sem, gx_sem,
):
    tokens, chunk, width, ff, local, nseq = dims
    chunks = tokens // chunk
    block = width // (2 * nseq)
    per = block // ROWS
    units = 4 * per
    depth = nseq + 1
    p = lax.axis_index("dp")
    z = lax.axis_index("seq")
    me = lax.axis_index("mp")
    y, c = me // 2, me % 2
    x_dev = {"dp": 1 - p}
    up_dev = {"seq": z + 1}
    dn_dev = {"seq": z - 1}
    y_dev = {"mp": (1 - y) * 2 + c}
    c_dev = {"mp": y * 2 + 1 - c}
    last = nseq - 1

    def remote(src, dst, sems, where, at=None):
        s_sem, r_sem = (sems.at[0], sems.at[1]) if at is None else (sems.at[0, at], sems.at[1, at])
        return pltpu.make_async_remote_copy(
            src_ref=src, dst_ref=dst, send_sem=s_sem, recv_sem=r_sem,
            device_id=where, device_id_type=MESH,
        )

    def load(src, dst, sem):
        return pltpu.make_async_copy(src, dst, sem)

    first_loads = [
        load(cot_h, r.at[2, :, pl.ds(0, width)], w_sem.at[0]),
        load(hidden_h, r.at[0], w_sem.at[1]),
    ]
    gate_load = load(gate_h, r.at[1], w_sem.at[2])
    up_load = load(up_h, r.at[2], w_sem.at[3])
    wd_load = load(wd_h, w0, w_sem.at[4])
    wg_load = load(wg_h, wg, w_sem.at[5])
    wu_load = load(wu_h, wu, w_sem.at[6])
    wo_load = load(wo_h, wo, w_sem.at[7])
    wi_loads = [
        load(wi_h.at[k], w0.at[pl.ds(0, width), pl.ds(k * local, local)], w_sem.at[8 + k])
        for k in range(3)
    ]
    for one in first_loads:
        one.start()
    gate_load.start()
    wd_load.start()
    wg_load.start()
    wu_load.start()
    wo_load.start()

    barrier = pltpu.get_barrier_semaphore()
    for dev in (x_dev, y_dev, c_dev):
        pl.semaphore_signal(barrier, inc=1, device_id=dev, device_id_type=MESH)

    @pl.when(z < last)
    def _():
        pl.semaphore_signal(barrier, inc=1, device_id=up_dev, device_id_type=MESH)

    @pl.when(z > 0)
    def _():
        pl.semaphore_signal(barrier, inc=1, device_id=dn_dev, device_id_type=MESH)

    peers = 3 + jnp.where(z < last, 1, 0) + jnp.where(z > 0, 1, 0)
    pl.semaphore_wait(barrier, peers)

    small_v[...] = jnp.zeros_like(small_v)

    def transpose_into(index, src, at):
        for q in range(4):
            lt[index, pl.ds(q * local, local), pl.ds(at, chunk)] = src(q).T

    for one in first_loads:
        one.wait()

    def cot_t(i, _):
        at = pl.multiple_of(i * chunk, chunk)
        transpose_into(0, lambda q: r[2, pl.ds(at, chunk), pl.ds(q * local, local)], at)
        return 0

    lax.fori_loop(0, chunks, cot_t, 0)
    up_load.start()

    def x_copy(u):
        return pltpu.make_async_remote_copy(
            src_ref=xs.at[lax.rem(u, 2)], dst_ref=xr.at[lax.rem(u, 4)],
            send_sem=xs_sem.at[lax.rem(u, 2)], recv_sem=xr_sem.at[lax.rem(u, 4)],
            device_id=x_dev, device_id_type=MESH,
        )

    def zs_at(u, step):
        first = sum(last - one for one in range(step))
        return first + lax.rem(u, last - step)

    def z_copy(u, way, step):
        return pltpu.make_async_remote_copy(
            src_ref=zs.at[way, zs_at(u, step)], dst_ref=zr.at[way, step, lax.rem(u, 3)],
            send_sem=zs_sem.at[way, step, lax.rem(u, 3)], recv_sem=zr_sem.at[way, step, lax.rem(u, 3)],
            device_id=dn_dev if way else up_dev, device_id_type=MESH,
        )

    def sends(way, step):
        return z >= last - step if way else jnp.logical_and(z <= step, z < last)

    def receives(way, step):
        if way:
            return jnp.logical_and(z < last, z >= last - 1 - step)
        return jnp.logical_and(z > 0, z <= step + 1)

    def can_send(way, step):
        if way:
            return jnp.logical_and(z > 0, z >= last - step)
        return jnp.logical_and(z < last, z <= step)

    def z_step(u, step):
        sl, slot = lax.rem(u, 6), lax.rem(u, 3)
        for way in (0, 1):
            quarter = z - last + step if way else last - step + z
            if step > 0:
                @pl.when(jnp.logical_and(receives(way, step - 1), can_send(way, step)))
                def _(way=way, quarter=quarter):
                    z_copy(u, way, step - 1).wait_recv()
                    value = s_buf[sl, pl.ds(quarter * ROWS, ROWS), :].astype(F32) + zr[
                        way, step - 1, slot
                    ].astype(F32)
                    zs[way, zs_at(u, step)] = value.astype(BF)

                fresh = jnp.logical_and(can_send(way, step), jnp.logical_not(receives(way, step - 1)))
            else:
                fresh = can_send(way, step)

            @pl.when(fresh)
            def _(way=way, quarter=quarter):
                zs[way, zs_at(u, step)] = s_buf[sl, pl.ds(quarter * ROWS, ROWS), :]

            @pl.when(can_send(way, step))
            def _(way=way):
                z_copy(u, way, step).start()

    def compute(u, kind):
        k = lax.rem(u, per)
        at = k * ROWS

        def rows_of(index, half):
            return [
                lt[index, pl.ds(pl.multiple_of((half * nseq + s) * block + at, ROWS), ROWS), :]
                for s in range(nseq)
            ]

        m = ROWS * nseq
        if kind == 3:
            left = jnp.concatenate(rows_of(0, 1 - p) + rows_of(0, p), 0)
            out = nn(left, r[0, :, pl.ds(0, local)])
            xs[lax.rem(u, 2), :, pl.ds(0, local)] = out[:m].astype(BF)
            s_buf[lax.rem(u, 6), :, pl.ds(0, local)] = out[m:].astype(BF)
            left = jnp.concatenate(rows_of(1, 1 - p) + rows_of(1, p), 0)
            out = nn(left, r[0, :, pl.ds(local, 3 * local)])
            xs[lax.rem(u, 2), :, pl.ds(local, 3 * local)] = out[:m].astype(BF)
            s_buf[lax.rem(u, 6), :, pl.ds(local, 3 * local)] = out[m:].astype(BF)
        else:
            if kind == 0:
                li, ri = 0, 0
            else:
                li, ri = 1, u // per
            left = jnp.concatenate(rows_of(li, 1 - p) + rows_of(li, p), 0)
            cut = (ff // 2 + 127) // 128 * 128
            for lo, n in ((0, cut), (cut, ff - cut)):
                out = nn(left, r[ri, :, pl.ds(lo, n)])
                xs[lax.rem(u, 2), :, pl.ds(lo, n)] = out[:m].astype(BF)
                s_buf[lax.rem(u, 6), :, pl.ds(lo, n)] = out[m:].astype(BF)

    def out_do(u, what):
        slot = lax.rem(u, 2)
        rows = pl.ds(pl.multiple_of(lax.rem(u, per) * ROWS, ROWS), ROWS)
        for g, target in enumerate((gdown_h, ggate_h, gup_h)):
            @pl.when(u // per == g)
            def _(target=target):
                getattr(load(ob.at[slot], target.at[rows, :], ob_sem.at[slot]), what)()

        @pl.when(u // per == 3)
        def _():
            out = load(ob.at[slot, :, pl.ds(0, local)], gout_h.at[rows, :], ob_sem.at[slot])
            getattr(out, what)()
            for k in range(3):
                part = ob.at[slot, :, pl.ds((k + 1) * local, local)]
                one = load(part, gin_h.at[k, rows, :], ob_sem.at[slot + 2 + 2 * k])
                getattr(one, what)()

    def finish(u):
        sl, slot = lax.rem(u, 6), lax.rem(u, 3)

        @pl.when(u >= 2)
        def _():
            out_do(u - 2, "wait")

        ob[lax.rem(u, 2)] = s_buf[sl, pl.ds(z * ROWS, ROWS), :].astype(F32)
        for way in (0, 1):
            @pl.when(receives(way, last - 1))
            def _(way=way):
                z_copy(u, way, last - 1).wait_recv()
                ob[lax.rem(u, 2)] += zr[way, last - 1, slot].astype(F32)

        for way in (0, 1):
            for step in range(last):
                @pl.when(can_send(way, step))
                def _(way=way, step=step):
                    z_copy(u, way, step).wait_send()

        out_do(u, "start")

    def tick(t, kind=None, guard=True):
        def within(u, f):
            if guard:
                @pl.when(jnp.logical_and(u >= 0, u < units))
                def _():
                    f()
            else:
                f()

        within(t - depth, lambda: finish(t - depth))
        for step in range(last - 1, 0, -1):
            within(t - 2 - step, lambda step=step: z_step(t - 2 - step, step))

        def x_in():
            u = t - 2
            x_copy(u).wait()
            sl = lax.rem(u, 6)
            s_buf[sl] = (s_buf[sl].astype(F32) + xr[lax.rem(u, 4)].astype(F32)).astype(BF)
            z_step(u, 0)

        within(t - 2, x_in)
        if kind is not None:
            compute(t, kind)
            x_copy(t).start()

    def rows_at(i):
        return pl.ds(pl.multiple_of(i * chunk, chunk), chunk)

    def cot_load(i, slot, sem):
        return load(cot_h.at[rows_at(i), :], cotc.at[slot], l_sem.at[sem, slot])

    def h1_load(i):
        return load(h1_h.at[rows_at(i), :], h1c, l_sem.at[1, 0])

    def bcv_load(i):
        return load(bcv_h.at[:, rows_at(i), :], bcv, l_sem.at[2, 0])

    def x_load(i):
        return load(x_h.at[rows_at(i), :], xc, l_sem.at[3, 0])

    def hidden_back(i):
        slot = lax.rem(i, 2)
        cot_load(i, slot, 0).wait()

        @pl.when(i + 1 < chunks)
        def _():
            cot_load(i + 1, 1 - slot, 0).start()

        cut = (ff // 2 + 127) // 128 * 128
        for lo, n in ((0, cut), (cut, ff - cut)):
            cols = pl.ds(lo, n)
            dbuf[:, pl.ds(0, n)] = nt(cotc[slot], w0[pl.ds(lo, n), :])

            def by_rows(b, _, cols=cols, n=n):
                some = pl.ds(pl.multiple_of(i * chunk + b * 16, 16), 16)
                dhid = dbuf[pl.ds(pl.multiple_of(b * 16, 16), 16), pl.ds(0, n)]
                gate = r[1, some, cols].astype(F32)
                up = r[2, some, cols].astype(F32)
                sig = jax.nn.sigmoid(gate)
                r[1, some, cols] = (dhid * up * sig * (1.0 + gate * (1.0 - sig))).astype(BF)
                r[2, some, cols] = (dhid * gate * sig).astype(BF)
                return 0

            lax.fori_loop(0, chunk // 16, by_rows, 0)

    def split_store(pair, value, keep, send):
        for side in (0, 1):
            part = value[:, side * local : (side + 1) * local]

            @pl.when(c == side)
            def _(part=part):
                keep[pair] = part

            @pl.when(c != side)
            def _(part=part):
                send[pair] = part.astype(BF)

    def stage_a(i):
        slot = lax.rem(i, 2)
        rows = rows_at(i)
        for pair in (0, 1):
            cols = pl.ds(pair * 2 * local, 2 * local)
            value = nn(r[1, rows, :], wg[:, cols]) + nn(r[2, rows, :], wu[:, cols])
            split_store(pair, value, ck, cs)
        remote(cs, cr.at[slot], c_sem, c_dev, slot).start()
        cot_load(i, slot, 0).start()

    def stage_b(i):
        slot = lax.rem(i, 2)
        remote(cs, cr.at[slot], c_sem, c_dev, slot).wait()
        ys[...] = (ck[...] + cr[slot].astype(F32)).astype(BF)
        remote(ys, yr.at[slot], y_sem, y_dev, slot).start()

    def stage_c(i):
        slot = lax.rem(i, 2)
        remote(ys, yr.at[slot], y_sem, y_dev, slot).wait()
        da2f[slot, :, c] = (ys[...].astype(F32) + yr[slot].astype(F32)).astype(BF)
        remote(da2f.at[slot, :, c], da2f.at[slot, :, c], f_sem, c_dev, slot).start()
        h1_load(i).start()
        bcv_load(i).start()

    def stage_d(i):
        slot = lax.rem(i, 2)
        remote(da2f.at[slot, :, c], da2f.at[slot, :, c], f_sem, c_dev, slot).wait()
        cot_load(i, slot, 0).wait()
        h1_load(i).wait()
        bcv_load(i).wait()
        x_load(i).start()
        at = pl.multiple_of(i * chunk, chunk)
        own = pl.ds(pl.multiple_of(me * local, 128), local)

        def by_rows(b, _):
            some = pl.ds(pl.multiple_of(b * 16, 16), 16)
            ssq = jnp.zeros((16, local), F32)
            inner = jnp.zeros((16, local), F32)
            for q in range(4):
                cols = pl.ds(q * local, local)
                h1 = h1c[some, cols].astype(F32)
                ssq += h1 * h1
                inner += da2f[slot, q // 2, q % 2, some, :].astype(F32) * gains_v[1:2, cols] * h1
            r2 = lax.rsqrt(jnp.sum(ssq, -1, keepdims=True) / width + EPS)
            scale = r2 * r2 * r2 * jnp.sum(inner, -1, keepdims=True) / width

            def grad(cols, da2):
                h1 = h1c[some, cols].astype(F32)
                return cotc[slot, some, cols].astype(F32) + r2 * (da2 * gains_v[1:2, cols]) - h1 * scale

            for q in range(4):
                cols = pl.ds(q * local, local)
                dhoc[some, cols] = grad(cols, da2f[slot, q // 2, q % 2, some, :].astype(F32)).astype(BF)
            da2 = da2f[slot, y, c, some, :].astype(F32)
            dh1s[i, some, :] = grad(own, da2)
            terms = da2 * h1c[some, own].astype(F32) * r2
            small_v[pl.ds(8, 8), :] += terms[:8] + terms[8:]
            return 0

        lax.fori_loop(0, chunk // 16, by_rows, 0)
        for q in range(4):
            cols = pl.ds(q * local, local)
            lt[0, cols, pl.ds(at, chunk)] = dhoc[:, cols].T
        dmixed = nt(dhoc[...], wo[...])
        b_gate, c_gate, value = bcv[0], bcv[1], bcv[2]
        bxp[pl.ds(0, 8), :] = before_v[i]
        bxp[pl.ds(8, chunk), :] = (b_gate.astype(F32) * value.astype(F32)).astype(BF).astype(F32)
        shifts = [bxp[pl.ds(6 + k, chunk), :] for k in range(3)]
        conv = sum(taps_v[k : k + 1, :] * shifts[k] for k in range(3))
        r[0, pl.ds(at, chunk), pl.ds(0, local)] = (c_gate.astype(F32) * conv).astype(BF)
        r[0, pl.ds(at, chunk), pl.ds(2 * local, local)] = (dmixed * conv).astype(BF)
        dconv = (dmixed * c_gate.astype(F32)).astype(BF).astype(F32)
        dcp[slot, pl.ds(0, chunk), :] = dconv
        halo_s[i] = dconv[:8]
        for k in range(3):
            small_v[1 + k : 2 + k, :] += jnp.sum(dconv * shifts[k], 0, keepdims=True)

        @pl.when(z > 0)
        def _():
            halo_copy(i).start()

    def halo_copy(i):
        return remote(halo_s.at[i], halo_r.at[i], halo_sem, dn_dev, i)

    def stage_e(i):
        slot = lax.rem(i, 2)
        x_load(i).wait()

        @pl.when(z > 0)
        def _():
            halo_copy(i).wait_send()

        @pl.when(z < last)
        def _():
            halo_copy(i).wait_recv()
            dcp[slot, pl.ds(chunk, 8), :] = halo_r[i]

        @pl.when(z == last)
        def _():
            dcp[slot, pl.ds(chunk, 8), :] = jnp.zeros((8, local), F32)

        dbx = sum(taps_v[2 - k : 3 - k, :] * dcp[slot, pl.ds(k, chunk), :] for k in range(3))
        rows = rows_at(i)
        r[0, rows, pl.ds(local, local)] = (dbx * bcv[2].astype(F32)).astype(BF)
        r[0, rows, pl.ds(3 * local, local)] = (dbx * bcv[0].astype(F32)).astype(BF)
        inner = jnp.zeros((chunk, 1), F32)
        ssq = jnp.zeros((chunk, 1), F32)
        for pair in (0, 1):
            cols = pl.ds(pair * 2 * local, 2 * local)
            value = nt(r[0, rows, pl.ds(local, 3 * local)], w0[cols, pl.ds(0, 3 * local)])
            x = xc[:, cols].astype(F32)
            inner += jnp.sum(value * x * gains_v[0:1, cols], -1, keepdims=True)
            ssq += jnp.sum(x * x, -1, keepdims=True)
            split_store(pair, value, ck2, cs2)
        xo[...] = xc[:, pl.ds(pl.multiple_of(me * local, 128), local)]
        ins[...] = jnp.broadcast_to(inner, ins.shape)
        r1s[slot] = jnp.broadcast_to(lax.rsqrt(ssq / width + EPS), r1s.shape[1:])
        remote(cs2, cr2.at[slot], c2_sem, c_dev, slot).start()
        remote(ins, inr.at[slot], i_sem, c_dev, slot).start()

    def stage_f(i):
        slot = lax.rem(i, 2)
        remote(cs2, cr2.at[slot], c2_sem, c_dev, slot).wait()
        remote(ins, inr.at[slot], i_sem, c_dev, slot).wait()
        ys2[...] = (ck2[1 - y] + cr2[slot, 1 - y].astype(F32)).astype(BF)
        qk2[...] = ck2[y] + cr2[slot, y].astype(F32)
        iys[...] = ins[...] + inr[slot]
        remote(ys2, yr2.at[slot], y2_sem, y_dev, slot).start()
        remote(iys, iyr.at[slot], iy_sem, y_dev, slot).start()

    def gx_copy(i):
        return load(gxb, gx_h.at[rows_at(i), :], gx_sem)

    def stage_g(i):
        slot = lax.rem(i, 2)
        remote(ys2, yr2.at[slot], y2_sem, y_dev, slot).wait()
        remote(iys, iyr.at[slot], iy_sem, y_dev, slot).wait()
        da1 = qk2[...] + yr2[slot].astype(F32)
        inner = (iys[:, :1] + iyr[slot, :, :1])
        r1 = r1s[slot, :, :1]
        own = pl.ds(pl.multiple_of(me * local, 128), local)
        x = xo[...].astype(F32)
        gain = gains_v[0:1, own]
        small_v[0:1, :] += jnp.sum(da1 * x * r1, 0, keepdims=True)

        @pl.when(i > 0)
        def _():
            gx_copy(i - 1).wait()

        gxb[...] = (dh1s[i] + r1 * gain * da1 - x * (r1 * r1 * r1 * inner / width)).astype(BF)
        gx_copy(i).start()

    def valid(i, f):
        @pl.when(jnp.logical_and(i >= 0, i < chunks))
        def _():
            f(i)

    def part_one(i, _):
        tick(i, 0)

        @pl.when(i == 0)
        def _():
            cot_load(0, 0, 0).start()
            gate_load.wait()
            up_load.wait()
            wd_load.wait()

        hidden_back(i)
        return 0

    lax.fori_loop(0, chunks, part_one, 0)
    for one in wi_loads:
        one.start()
    wg_load.wait()
    wu_load.wait()
    wo_load.wait()
    for one in wi_loads:
        one.wait()

    def a_transposed(src_h, i):
        one = load(src_h.at[rows_at(i), :], dhoc, l_sem.at[4, 0])
        one.start()
        one.wait()
        at = pl.multiple_of(i * chunk, chunk)
        transpose_into(1, lambda q: dhoc[:, pl.ds(q * local, local)], at)

    def part_two(j, kind):
        t = chunks + 2 * j
        tick(t, kind)
        valid(j - 3, stage_g)
        valid(j - 2, stage_e)
        valid(j - 1, stage_c)
        valid(j, stage_a)
        tick(t + 1, kind)
        valid(j, stage_b)
        valid(j - 1, stage_d)
        valid(j - 2, stage_f)

    def a2_body(i, _):
        a_transposed(a2_h, i)
        return 0

    lax.fori_loop(0, chunks, a2_body, 0)
    part_two(0, 0)

    def loop_rest(j, _):
        part_two(j, 1)
        return 0

    lax.fori_loop(1, 1 + (2 * per) // 2, loop_rest, 0)

    def a1_body(i, _):
        a_transposed(a1_h, i)
        return 0

    lax.fori_loop(0, chunks, a1_body, 0)
    gx_copy(chunks - 1).wait()

    def part_three(k, _):
        tick(3 * per + k, 3)
        return 0

    lax.fori_loop(0, per, part_three, 0)

    def part_four(k, _):
        tick(units + k)
        return 0

    lax.fori_loop(0, depth, part_four, 0)
    out_do(units - 2, "wait")
    out_do(units - 1, "wait")


def backward(dims, hidden, gate, up, a1, a2, x_full, h1, cot, bcv, before, wd, wg, wu, wo, wi, gains, taps):
    tokens, chunk, width, ff, local, nseq = dims
    block = width // (2 * nseq)
    chunks = tokens // chunk
    last = nseq - 1
    m = ROWS * nseq
    DMA = pltpu.SemaphoreType.DMA
    shape = jax.ShapeDtypeStruct
    scratch = [
        pltpu.VMEM((2, width, tokens), BF),
        pltpu.VMEM((3, tokens, ff), BF),
        pltpu.VMEM((ff, width), BF),
        pltpu.VMEM((ff, width), BF),
        pltpu.VMEM((ff, width), BF),
        pltpu.VMEM((local, width), BF),
        pltpu.VMEM((2, chunk, width), BF),
        pltpu.VMEM((chunk, width), BF),
        pltpu.VMEM((chunk, width), BF),
        pltpu.VMEM((chunk, local), BF),
        pltpu.VMEM((3, chunk, local), BF),
        pltpu.VMEM((8 + chunk, local), F32),
        pltpu.VMEM((chunk, (ff // 2 + 127) // 128 * 128), F32),
        pltpu.VMEM((2, 8 + chunk, local), F32),
        pltpu.VMEM((chunk, width), BF),
        pltpu.VMEM((chunks, chunk, local), F32),
        pltpu.VMEM((2, chunk, 128), F32),
        pltpu.VMEM((2, m, ff), BF),
        pltpu.VMEM((4, m, ff), BF),
        pltpu.VMEM((6, m, ff), BF),
        pltpu.VMEM((2, last * (last + 1) // 2, ROWS, ff), BF),
        pltpu.VMEM((2, last, 3, ROWS, ff), BF),
        pltpu.VMEM((2, ROWS, ff), F32),
        pltpu.VMEM((2, chunk, local), F32),
        pltpu.VMEM((2, chunk, local), BF),
        pltpu.VMEM((2, 2, chunk, local), BF),
        pltpu.VMEM((2, chunk, local), BF),
        pltpu.VMEM((2, 2, chunk, local), BF),
        pltpu.VMEM((2, 2, 2, chunk, local), BF),
        pltpu.VMEM((2, chunk, local), F32),
        pltpu.VMEM((2, chunk, local), BF),
        pltpu.VMEM((2, 2, chunk, local), BF),
        pltpu.VMEM((chunk, local), BF),
        pltpu.VMEM((2, chunk, local), BF),
        pltpu.VMEM((chunk, local), F32),
        pltpu.VMEM((chunk, 128), F32),
        pltpu.VMEM((2, chunk, 128), F32),
        pltpu.VMEM((chunk, 128), F32),
        pltpu.VMEM((2, chunk, 128), F32),
        pltpu.VMEM((chunk, local), BF),
        pltpu.VMEM((chunks, 8, local), F32),
        pltpu.VMEM((chunks, 8, local), F32),
        DMA((2,)), DMA((4,)), DMA((2, last, 3)), DMA((2, last, 3)), DMA((8,)),
        DMA((2, 2)), DMA((2, 2)), DMA((2, 2)), DMA((2, 2)), DMA((2, 2)),
        DMA((2, 2)), DMA((2, 2)), DMA((2, chunks)), DMA((12,)), DMA((5, 2)), DMA(()),
    ]
    return pl.pallas_call(
        functools.partial(backward_kernel, dims),
        out_shape=(
            shape((block, ff), F32), shape((block, ff), F32), shape((block, ff), F32),
            shape((block, local), F32), shape((3, block, local), F32),
            shape((tokens, local), BF), shape((16, local), F32),
        ),
        in_specs=[ANY] * 9 + [VMEM] + [ANY] * 5 + [VMEM] * 2,
        out_specs=(ANY,) * 6 + (VMEM,),
        scratch_shapes=scratch,
        compiler_params=pltpu.CompilerParams(
            collective_id=0, has_side_effects=True, vmem_limit_bytes=63 * 2**20
        ),
    )(hidden, gate, up, a1, a2, x_full, h1, cot, bcv, before, wd, wg, wu, wo, wi, gains, taps)


def shifted(array, axis, by):
    count = lax.axis_size(axis)
    pairs = [(i, i + by) for i in range(count) if 0 <= i + by < count]
    return lax.ppermute(array, axis, pairs)


def fused_device(inputs, gain_mix, w_in, kernel, w_out, gain_ff, w_gate, w_up, w_down, cotangent):
    groups, seq_rows, local = inputs.shape
    width = local * lax.axis_size("mp")
    ff = w_down.shape[0]
    tokens = groups * seq_rows
    nseq = lax.axis_size("seq")
    dims = (tokens, seq_rows, width, ff, local, nseq)
    x_own = inputs.reshape(tokens, local)
    taps = kernel.astype(F32)
    wi = w_in.transpose(1, 0, 2)
    wg, wu = w_gate.T, w_up.T

    def all_features(values):
        return lax.all_gather(values, "mp", axis=1, tiled=True)

    def share_sums(values):
        return lax.psum_scatter(values.astype(BF), "mp", scatter_dimension=1, tiled=True)

    gains = all_features(jnp.stack([gain_mix, gain_ff])).astype(F32)
    x_full = all_features(x_own)
    cot = all_features(cotangent.reshape(tokens, local))

    def normed(values, gain):
        values = values.astype(F32)
        scale = lax.rsqrt(jnp.mean(values * values, -1, keepdims=True) + EPS)
        return (values * scale * gain).astype(BF)

    a1 = normed(x_full, gains[0])
    proj = [jnp.dot(a1, wi[k], preferred_element_type=F32) for k in range(3)]
    bcv = jnp.stack(proj).astype(BF)
    bx = (bcv[0].astype(F32) * bcv[2].astype(F32)).astype(BF).reshape(groups, seq_rows, local)
    before = shifted(bx[:, seq_rows - 8 :], "seq", 1)
    padded = jnp.concatenate([before[:, 6:], bx], 1).astype(F32)
    conv = taps[0] * padded[:, :-2] + taps[1] * padded[:, 1:-1] + taps[2] * padded[:, 2:]
    mixed = (bcv[1].astype(F32) * conv.reshape(tokens, local)).astype(BF)
    h1_own = x_own.astype(F32) + share_sums(jnp.dot(mixed, w_out, preferred_element_type=F32)).astype(F32)
    h1 = all_features(h1_own.astype(BF))
    a2 = normed(h1, gains[1])
    gate = lax.dot_general(a2, wg, (((1,), (1,)), ((), ())), preferred_element_type=F32)
    up = lax.dot_general(a2, wu, (((1,), (1,)), ((), ())), preferred_element_type=F32)
    hidden = (gate * jax.nn.sigmoid(gate) * up).astype(BF)
    ffn = share_sums(jnp.dot(hidden, w_down, preferred_element_type=F32))
    block_out = (h1_own + ffn.astype(F32)).astype(BF)
    gdown, ggate, gup, gout, gin, gx, small = backward(
        dims, hidden, gate.astype(BF), up.astype(BF), a1, a2, x_full, h1, cot, bcv,
        before.astype(F32), w_down, wg, wu, w_out, wi, gains, taps,
    )
    small = small.at[4].set(small[8:].sum(0))[:8]
    small = lax.psum(small, ("dp", "seq"))
    whole = (groups, seq_rows, local)
    return (
        block_out.reshape(whole), gx.reshape(whole), small[0], gin.transpose(1, 0, 2), small[1:4],
        gout.T, small[4], ggate, gup, gdown.T,
    )


def contract_rows(left, right):
    return lax.dot_general(
        left, right, (((0,), (0,)), ((), ())), preferred_element_type=jnp.float32
    )


def contract_cols(left, right):
    return lax.dot_general(
        left, right, (((1,), (1,)), ((), ())), preferred_element_type=jnp.float32
    )


def plain_device(inputs, gain_mix, w_in, kernel, w_out, gain_ff, w_gate, w_up, w_down, cotangent):
    groups, seq_rows, local_width = inputs.shape
    full_width = local_width * lax.axis_size("mp")
    tokens = groups * seq_rows
    x_float = inputs.reshape(tokens, local_width).astype(jnp.float32)
    gain_one = gain_mix.astype(jnp.float32)
    gain_two = gain_ff.astype(jnp.float32)
    taps = kernel.astype(jnp.float32)

    def row_total(values):
        return lax.psum(jnp.sum(values, axis=-1, keepdims=True), "mp")

    def all_features(values):
        return lax.all_gather(values, "mp", axis=1, tiled=True)

    def share_sums(values):
        return lax.psum_scatter(
            values.astype(jnp.bfloat16), "mp", scatter_dimension=1, tiled=True
        ).astype(jnp.float32)

    def scattered(values, dim):
        return lax.psum_scatter(
            values.astype(jnp.bfloat16), ("dp", "seq"), scatter_dimension=dim, tiled=True
        ).astype(jnp.float32)

    def norm_scale(values):
        return lax.rsqrt(row_total(values * values) / full_width + EPS)

    def norm_back(values, scale, gain_vec, upstream):
        inner = row_total(gain_vec * upstream * values)
        grad_values = scale * gain_vec * upstream - values * scale**3 * inner / full_width
        return (grad_values, jnp.sum(upstream * values * scale, axis=0))

    scale_one = norm_scale(x_float)
    normed_in = all_features((x_float * scale_one * gain_one).astype(jnp.bfloat16))
    proj = jnp.einsum("td,dkc->tkc", normed_in, w_in, preferred_element_type=jnp.float32)
    b_gate = proj[:, 0]
    c_gate = proj[:, 1]
    values_v = proj[:, 2]
    b_times_x = (b_gate * values_v).astype(jnp.bfloat16).reshape(groups, seq_rows, local_width)
    before = shifted(b_times_x[:, seq_rows - 2 :], "seq", 1)
    padded = jnp.concatenate([before, b_times_x], 1).astype(jnp.float32)
    conv = taps[0] * padded[:, :-2] + taps[1] * padded[:, 1:-1] + taps[2] * padded[:, 2:]
    conv = conv.reshape(tokens, local_width)
    mixed = (c_gate * conv).astype(jnp.bfloat16)
    hidden_one = x_float + share_sums(jnp.dot(mixed, w_out, preferred_element_type=jnp.float32))
    scale_two = norm_scale(hidden_one)
    normed_ff = all_features((hidden_one * scale_two * gain_two).astype(jnp.bfloat16))
    gate = jnp.dot(normed_ff, w_gate, preferred_element_type=jnp.float32)
    up_proj = jnp.dot(normed_ff, w_up, preferred_element_type=jnp.float32)
    sigma = jax.nn.sigmoid(gate)
    active = gate * sigma
    hidden = (active * up_proj).astype(jnp.bfloat16)
    ffn_out = share_sums(jnp.dot(hidden, w_down, preferred_element_type=jnp.float32))
    block_out = (hidden_one + ffn_out).astype(jnp.bfloat16).reshape(groups, seq_rows, local_width)
    grad_flat = cotangent.reshape(tokens, local_width)
    grad_full = all_features(grad_flat)
    grad_down = contract_rows(hidden, grad_full)
    grad_hidden = contract_cols(grad_full, w_down)
    grad_gate_act = (grad_hidden * up_proj * sigma * (1.0 + gate * (1.0 - sigma))).astype(
        jnp.bfloat16
    )
    grad_up_act = (grad_hidden * active).astype(jnp.bfloat16)
    grad_gate = contract_rows(normed_ff, grad_gate_act)
    grad_up = contract_rows(normed_ff, grad_up_act)
    grad_normed_ff = share_sums(
        contract_cols(grad_gate_act, w_gate) + contract_cols(grad_up_act, w_up)
    )
    grad_norm_two, grad_gain_two = norm_back(hidden_one, scale_two, gain_two, grad_normed_ff)
    grad_hidden_one = grad_flat.astype(jnp.float32) + grad_norm_two
    grad_out_full = all_features(grad_hidden_one.astype(jnp.bfloat16))
    grad_out = contract_rows(mixed, grad_out_full)
    grad_mixed = contract_cols(grad_out_full, w_out)
    grad_c = grad_mixed * conv
    grad_conv = (grad_mixed * c_gate).astype(jnp.bfloat16).reshape(groups, seq_rows, local_width)
    after = shifted(grad_conv[:, :2], "seq", -1)
    extended = jnp.concatenate([grad_conv, after], 1).astype(jnp.float32)
    grad_bx = taps[2] * extended[:, :-2] + taps[1] * extended[:, 1:-1] + taps[0] * extended[:, 2:]
    grad_bx = grad_bx.reshape(tokens, local_width)
    conv_grad_float = extended[:, :-2]
    grad_taps = jnp.stack(
        [
            jnp.sum(conv_grad_float * padded[:, :-2], axis=(0, 1)),
            jnp.sum(conv_grad_float * padded[:, 1:-1], axis=(0, 1)),
            jnp.sum(conv_grad_float * padded[:, 2:], axis=(0, 1)),
        ]
    )
    grad_proj = jnp.stack([grad_bx * values_v, grad_c, grad_bx * b_gate], 1).astype(jnp.bfloat16)
    grad_in = jnp.einsum("td,tkc->dkc", normed_in, grad_proj, preferred_element_type=jnp.float32)
    grad_normed_in = share_sums(
        jnp.einsum("tkc,dkc->td", grad_proj, w_in, preferred_element_type=jnp.float32)
    )
    grad_norm_one, grad_gain_one = norm_back(x_float, scale_one, gain_one, grad_normed_in)
    grad_input = (
        (grad_hidden_one + grad_norm_one)
        .astype(jnp.bfloat16)
        .reshape(groups, seq_rows, local_width)
    )
    small_sums = lax.psum((grad_gain_one, grad_taps, grad_gain_two), ("dp", "seq"))
    by_row = (
        scattered(grad_in, 0),
        scattered(grad_gate, 0),
        scattered(grad_up, 0),
    )
    by_col = (
        scattered(grad_out, 1),
        scattered(grad_down, 1),
    )
    return (
        block_out,
        grad_input,
        small_sums[0],
        by_row[0],
        small_sums[1],
        by_col[0],
        small_sums[2],
        by_row[1],
        by_row[2],
        by_col[1],
    )


def solution(mesh):
    placed = (
        P("dp", "seq", "mp"),
        P("mp"),
        P(None, None, "mp"),
        P(None, "mp"),
        P("mp", None),
        P("mp"),
        P(None, "mp"),
        P(None, "mp"),
        P("mp", None),
        P("dp", "seq", "mp"),
    )
    sizes = mesh.shape
    fused = sizes["dp"] == 2 and sizes["seq"] == 4 and sizes["mp"] == 4
    return jax.shard_map(
        fused_device if fused else plain_device,
        mesh=mesh,
        in_specs=placed,
        out_specs=(
            P("dp", "seq", "mp"),
            P("dp", "seq", "mp"),
            P("mp"),
            P(("dp", "seq"), None, "mp"),
            P(None, "mp"),
            P("mp", ("dp", "seq")),
            P("mp"),
            P(("dp", "seq"), "mp"),
            P(("dp", "seq"), "mp"),
            P("mp", ("dp", "seq")),
        ),
        check_vma=False,
    )
```

```python
import functools

import jax
import jax.numpy as jnp
from jax import lax
from jax.experimental import pallas as pl
from jax.experimental.pallas import tpu as pltpu
from jax.sharding import PartitionSpec as P

EPS = 1e-05
MESH = pl.DeviceIdType.MESH
BF = jnp.bfloat16
F32 = jnp.float32
ROWS = 32
ANY = pl.BlockSpec(memory_space=pl.ANY)
VMEM = pl.BlockSpec(memory_space=pltpu.VMEM)


def nn(left, right):
    return lax.dot_general(left, right, (((1,), (0,)), ((), ())), preferred_element_type=F32)


def nt(left, right):
    return lax.dot_general(left, right, (((1,), (1,)), ((), ())), preferred_element_type=F32)


def block_kernel(
    dims,
    x_in, cot_in, own_v, wd_h, wg_h, wu_h, wo_h, wi_h,
    gdown_h, ggate_h, gup_h, gout_h, gin_h, gx_h, out_h, small_v,
    x_h, cot_h, h1_h, bcv_h,
    lt, r, w0, wg, wu, wo, cotc, xc, xo, bcv, bxp, dbuf, dcp, dhoc, dh1s, r1s, gv,
    xs, xr, s_buf, zs, zr, ob,
    kf, cs, cr, ys, yr4, da2f, cs2, ys2, yr2,
    ins, inr, iys, iyr, gxb, halo_s, halo_r, before_s, before_r, small_r,
    xs_sem, xr_sem, zs_sem, zr_sem, ob_sem, c_sem, y_sem, f_sem, c2_sem, y2_sem,
    i_sem, iy_sem, halo_sem, before_sem, gather_sem, own_sem, w_sem, l_sem, bcv_sem, h1_sem, gx_sem,
    small_sem,
):
    tokens, chunk, width, ff, local, nseq = dims
    chunks = tokens // chunk
    block = width // (2 * nseq)
    per = block // ROWS
    units = 4 * per
    depth = nseq + 1
    p = lax.axis_index("dp")
    z = lax.axis_index("seq")
    me = lax.axis_index("mp")
    y, c = me // 2, me % 2
    x_dev = {"dp": 1 - p}
    up_dev = {"seq": z + 1}
    dn_dev = {"seq": z - 1}
    y_dev = {"mp": (1 - y) * 2 + c}
    c_dev = {"mp": y * 2 + 1 - c}
    last = nseq - 1
    ck, ck2, qk2 = kf.at[pl.ds(0, 2)], kf.at[pl.ds(2, 2)], kf.at[4]
    third = ff // 3 // 128 * 128
    cuts = ((0, third), (third, third), (2 * third, ff - 2 * third))

    def remote(src, dst, sems, where, at=None):
        s_sem, r_sem = (sems.at[0], sems.at[1]) if at is None else (sems.at[0, at], sems.at[1, at])
        return pltpu.make_async_remote_copy(
            src_ref=src, dst_ref=dst, send_sem=s_sem, recv_sem=r_sem,
            device_id=where, device_id_type=MESH,
        )

    def load(src, dst, sem):
        return pltpu.make_async_copy(src, dst, sem)

    def wi_load(k):
        return load(wi_h.at[k], w0.at[pl.ds(0, width), pl.ds(k * local, local)], w_sem.at[k])

    wd_load = load(wd_h, w0, w_sem.at[3])
    wg_load = load(wg_h, wg, w_sem.at[4])
    wu_load = load(wu_h, wu, w_sem.at[5])
    wo_load = load(wo_h, wo, w_sem.at[6])
    for k in range(3):
        wi_load(k).start()
    wo_load.start()
    gv[me] = own_v[...]

    barrier = pltpu.get_barrier_semaphore()
    for dev in (x_dev, y_dev, c_dev):
        pl.semaphore_signal(barrier, inc=1, device_id=dev, device_id_type=MESH)

    @pl.when(z < last)
    def _():
        pl.semaphore_signal(barrier, inc=1, device_id=up_dev, device_id_type=MESH)

    @pl.when(z > 0)
    def _():
        pl.semaphore_signal(barrier, inc=1, device_id=dn_dev, device_id_type=MESH)

    peers = 3 + jnp.where(z < last, 1, 0) + jnp.where(z > 0, 1, 0)
    pl.semaphore_wait(barrier, peers)

    small_v[...] = jnp.zeros_like(small_v)

    def rows_at(i):
        return pl.ds(pl.multiple_of(i * chunk, chunk), chunk)

    def gather(which, i, leg):
        if which == 2:
            src = mine = own_v
            dst = gv
            at = (2, 0)
        else:
            src, dst = (x_in, x_h) if which == 0 else (cot_in, cot_h)
            mine = src.at[rows_at(i), :]
            at = (which, i)
        slot = (lambda q: dst.at[q]) if which == 2 else (lambda q: dst.at[q, rows_at(i), :])
        sems = [gather_sem.at[leg, way, at[0], at[1]] for way in (0, 1)]
        if leg == 0:
            pair, where = (mine, slot(me)), y_dev
        elif leg == 1:
            pair, where = (mine, slot(me)), c_dev
        else:
            from_y = (1 - y) * 2 + c
            pair, where = (slot(from_y), slot(from_y)), c_dev
        return pltpu.make_async_remote_copy(
            src_ref=pair[0], dst_ref=pair[1], send_sem=sems[0], recv_sem=sems[1],
            device_id=where, device_id_type=MESH,
        )

    def gather_start(which, i):
        gather(which, i, 0).start()
        gather(which, i, 1).start()

    def gather_pass(which, i):
        gather(which, i, 0).wait_recv()
        gather(which, i, 2).start()

    def gather_end(which, i):
        gather(which, i, 0).wait_send()
        gather(which, i, 1).wait()
        gather(which, i, 2).wait()

    own_copies = [
        load(x_in, x_h.at[me], own_sem.at[0]),
        load(cot_in, cot_h.at[me], own_sem.at[1]),
    ]
    for i in range(chunks):
        gather_start(0, i)
        if i == 0:
            gather_start(2, 0)
    for one in own_copies:
        one.start()
    wg_load.start()
    wu_load.start()

    def x_copy(u):
        return pltpu.make_async_remote_copy(
            src_ref=xs.at[lax.rem(u, 2)], dst_ref=xr.at[lax.rem(u, 4)],
            send_sem=xs_sem.at[lax.rem(u, 2)], recv_sem=xr_sem.at[lax.rem(u, 4)],
            device_id=x_dev, device_id_type=MESH,
        )

    def zs_at(u, step):
        first = sum(last - one for one in range(step))
        return first + lax.rem(u, last - step)

    def z_copy(u, way, step):
        return pltpu.make_async_remote_copy(
            src_ref=zs.at[way, zs_at(u, step)], dst_ref=zr.at[way, step, lax.rem(u, 3)],
            send_sem=zs_sem.at[way, step, lax.rem(u, 3)], recv_sem=zr_sem.at[way, step, lax.rem(u, 3)],
            device_id=dn_dev if way else up_dev, device_id_type=MESH,
        )

    def sends(way, step):
        return z >= last - step if way else jnp.logical_and(z <= step, z < last)

    def receives(way, step):
        if way:
            return jnp.logical_and(z < last, z >= last - 1 - step)
        return jnp.logical_and(z > 0, z <= step + 1)

    def can_send(way, step):
        if way:
            return jnp.logical_and(z > 0, z >= last - step)
        return jnp.logical_and(z < last, z <= step)

    def z_step(u, step):
        sl, slot = lax.rem(u, 6), lax.rem(u, 3)
        for way in (0, 1):
            quarter = z - last + step if way else last - step + z
            if step > 0:
                @pl.when(jnp.logical_and(receives(way, step - 1), can_send(way, step)))
                def _(way=way, quarter=quarter):
                    z_copy(u, way, step - 1).wait_recv()
                    value = s_buf[sl, pl.ds(quarter * ROWS, ROWS), :].astype(F32) + zr[
                        way, step - 1, slot
                    ].astype(F32)
                    zs[way, zs_at(u, step)] = value.astype(BF)

                fresh = jnp.logical_and(can_send(way, step), jnp.logical_not(receives(way, step - 1)))
            else:
                fresh = can_send(way, step)

            @pl.when(fresh)
            def _(way=way, quarter=quarter):
                zs[way, zs_at(u, step)] = s_buf[sl, pl.ds(quarter * ROWS, ROWS), :]

            @pl.when(can_send(way, step))
            def _(way=way):
                z_copy(u, way, step).start()

    def compute(u, kind):
        k = lax.rem(u, per)
        at = k * ROWS

        def rows_of(index, half):
            return [
                lt[index, pl.ds(pl.multiple_of((half * nseq + s) * block + at, ROWS), ROWS), :]
                for s in range(nseq)
            ]

        m = ROWS * nseq
        if kind == 3:
            left = jnp.concatenate(rows_of(0, 1 - p) + rows_of(0, p), 0)
            out = nn(left, r[0, :, pl.ds(0, local)])
            xs[lax.rem(u, 2), :, pl.ds(0, local)] = out[:m].astype(BF)
            s_buf[lax.rem(u, 6), :, pl.ds(0, local)] = out[m:].astype(BF)
            left = jnp.concatenate(rows_of(1, 1 - p) + rows_of(1, p), 0)
            out = nn(left, r[0, :, pl.ds(local, 3 * local)])
            xs[lax.rem(u, 2), :, pl.ds(local, 3 * local)] = out[:m].astype(BF)
            s_buf[lax.rem(u, 6), :, pl.ds(local, 3 * local)] = out[m:].astype(BF)
        else:
            if kind == 0:
                li, ri = 0, 0
            else:
                li, ri = 1, u // per
            left = jnp.concatenate(rows_of(li, 1 - p) + rows_of(li, p), 0)
            for lo, n in cuts:
                out = nn(left, r[ri, :, pl.ds(lo, n)])
                xs[lax.rem(u, 2), :, pl.ds(lo, n)] = out[:m].astype(BF)
                s_buf[lax.rem(u, 6), :, pl.ds(lo, n)] = out[m:].astype(BF)

    def out_do(u, what):
        slot = lax.rem(u, 2)
        rows = pl.ds(pl.multiple_of(lax.rem(u, per) * ROWS, ROWS), ROWS)
        for g, target in enumerate((gdown_h, ggate_h, gup_h)):
            @pl.when(u // per == g)
            def _(target=target):
                getattr(load(ob.at[slot], target.at[rows, :], ob_sem.at[slot]), what)()

        @pl.when(u // per == 3)
        def _():
            out = load(ob.at[slot, :, pl.ds(0, local)], gout_h.at[rows, :], ob_sem.at[slot])
            getattr(out, what)()
            for k in range(3):
                part = ob.at[slot, :, pl.ds((k + 1) * local, local)]
                one = load(part, gin_h.at[k, rows, :], ob_sem.at[slot + 2 + 2 * k])
                getattr(one, what)()

    def finish(u):
        sl, slot = lax.rem(u, 6), lax.rem(u, 3)

        @pl.when(u >= 2)
        def _():
            out_do(u - 2, "wait")

        for way in (0, 1):
            @pl.when(receives(way, last - 1))
            def _(way=way):
                z_copy(u, way, last - 1).wait_recv()

        def end(ways):
            total = s_buf[sl, pl.ds(z * ROWS, ROWS), :].astype(F32)
            for way in ways:
                total += zr[way, last - 1, slot].astype(F32)
            ob[lax.rem(u, 2)] = total.astype(BF)

        pl.when(z == 0)(lambda: end((1,)))
        pl.when(z == last)(lambda: end((0,)))
        pl.when(jnp.logical_and(z > 0, z < last))(lambda: end((0, 1)))

        for way in (0, 1):
            for step in range(last):
                @pl.when(can_send(way, step))
                def _(way=way, step=step):
                    z_copy(u, way, step).wait_send()

        out_do(u, "start")

    def tick(t, kind=None, guard=True):
        def within(u, f):
            if guard:
                @pl.when(jnp.logical_and(u >= 0, u < units))
                def _():
                    f()
            else:
                f()

        within(t - depth, lambda: finish(t - depth))
        for step in range(last - 1, 0, -1):
            within(t - 2 - step, lambda step=step: z_step(t - 2 - step, step))

        def x_in():
            u = t - 2
            x_copy(u).wait()
            sl = lax.rem(u, 6)
            s_buf[sl] = (s_buf[sl].astype(F32) + xr[lax.rem(u, 4)].astype(F32)).astype(BF)
            z_step(u, 0)

        within(t - 2, x_in)
        if kind is not None:
            compute(t, kind)
            x_copy(t).start()

    def in_slices(src, to, slot):
        return [load(src(q), to(q), l_sem.at[slot, q]) for q in range(4)]

    def cot_load(i, slot):
        return in_slices(
            lambda q: cot_h.at[q, rows_at(i), :],
            lambda q: cotc.at[slot, :, pl.ds(q * local, local)],
            slot,
        )

    def start(copies):
        for one in copies:
            one.start()

    def wait(copies):
        for one in copies:
            one.wait()

    def h1_load(i):
        return load(h1_h.at[:, rows_at(i), :], xc, l_sem.at[2, 0])

    def bcv_load(i):
        return load(bcv_h.at[:, rows_at(i), :], bcv, l_sem.at[2, 1])

    def x_load(i):
        return load(x_h.at[:, rows_at(i), :], xc, l_sem.at[2, 2])

    def gain(row, q):
        return gv[q, row : row + 1, :]

    def by_sixteen(f):
        def body(b, _):
            f(pl.ds(pl.multiple_of(b * 16, 16), 16))
            return 0

        lax.fori_loop(0, chunk // 16, body, 0)

    def normed_to(src, row, after=None):
        def f(some):
            ssq = jnp.zeros((16, local), F32)
            for q in range(4):
                values = src(q, some).astype(F32)
                ssq += values * values
            scale = lax.rsqrt(jnp.sum(ssq, -1, keepdims=True) / width + EPS)
            for q in range(4):
                dhoc[some, pl.ds(q * local, local)] = (src(q, some).astype(F32) * scale * gain(row, q)).astype(BF)

        by_sixteen(f)

    def transposed_to(index, i):
        at = pl.multiple_of(i * chunk, chunk)
        for q in range(4):
            cols = pl.ds(q * local, local)
            lt[index, cols, pl.ds(at, chunk)] = dhoc[:, cols].T

    def before_copy(i):
        return remote(before_s.at[i], before_r.at[i], before_sem, up_dev, i)

    def bcv_store(i):
        return load(bcv, bcv_h.at[:, rows_at(i), :], bcv_sem)

    def h1_store(i, slot, pair, core):
        return load(da2f.at[slot, pair, core], h1_h.at[2 * pair + core, rows_at(i), :], h1_sem.at[pair, core])

    def project(i):
        gather_end(0, i)
        x_load(i).start()
        x_load(i).wait()
        normed_to(lambda q, some: xc[q, some, :], 0)
        value = nn(dhoc[...], w0[pl.ds(0, width), pl.ds(0, 3 * local)])

        @pl.when(i > 0)
        def _():
            bcv_store(i - 1).wait()

        for k in range(3):
            bcv[k] = value[:, k * local : (k + 1) * local].astype(BF)
        dcp[pl.ds(0, chunk), :] = value[:, local : 2 * local]
        bx = (value[:, :local] * value[:, 2 * local :]).astype(BF)
        bcv[3] = bx
        bxp[pl.ds(8, chunk), :] = bx.astype(F32)
        before_s[i] = bxp[pl.ds(chunk, 8), :]

        @pl.when(z < last)
        def _():
            before_copy(i).start()

        bcv_store(i).start()

    def conv_of():
        shifts = [bxp[pl.ds(6 + k, chunk), :] for k in range(3)]
        return sum(own_v[2 + k : 3 + k, :] * shifts[k] for k in range(3)), shifts

    def mix(i):
        slot = lax.rem(i, 2)

        @pl.when(z < last)
        def _():
            before_copy(i).wait_send()

        @pl.when(z > 0)
        def _():
            before_copy(i).wait_recv()

        @pl.when(z == 0)
        def _():
            before_r[i] = jnp.zeros((8, local), F32)

        bxp[pl.ds(0, 8), :] = before_r[i]
        mixed = (dcp[pl.ds(0, chunk), :] * conv_of()[0]).astype(BF)
        for pair in (0, 1):
            split_store(pair, nn(mixed, wo[:, pl.ds(pair * 2 * local, 2 * local)]), ck, cs)
        remote(cs, cr.at[slot], c_sem, c_dev, slot).start()

    def share(i):
        slot = lax.rem(i, 2)
        remote(cs, cr.at[slot], c_sem, c_dev, slot).wait()
        for pair in (0, 1):
            total = ck[pair] + cr[slot, pair].astype(F32)
            kf[2 + 2 * slot + pair] = total + xc[2 * pair + c].astype(F32)
            ys[slot, pair] = total.astype(BF)
        remote(ys.at[slot], yr4.at[i], y_sem, y_dev, i).start()

    def residual(i):
        slot = lax.rem(i, 2)
        remote(ys.at[slot], yr4.at[i], y_sem, y_dev, i).wait()

        @pl.when(i >= 1)
        def _():
            for pair in (0, 1):
                for core in (0, 1):
                    h1_store(i - 1, 1 - slot, pair, core).wait()

        for pair in (0, 1):
            h1 = kf[2 + 2 * slot + pair] + yr4[i, pair].astype(F32)
            da2f[slot, pair, c] = h1.astype(BF)

            @pl.when(y == pair)
            def _(h1=h1):
                dh1s[i] = h1
        remote(da2f.at[slot, :, c], da2f.at[slot, :, c], f_sem, c_dev, slot).start()

    def feed(i):
        slot = lax.rem(i, 2)
        remote(da2f.at[slot, :, c], da2f.at[slot, :, c], f_sem, c_dev, slot).wait()
        for pair in (0, 1):
            for core in (0, 1):
                h1_store(i, slot, pair, core).start()
        normed_to(lambda q, some: da2f[slot, q // 2, q % 2, some, :], 1)
        transposed_to(1, i)
        for lo, n in cuts:
            dbuf[0, :, pl.ds(0, n)] = nt(dhoc[...], wg[pl.ds(lo, n), :])
            dbuf[1, :, pl.ds(0, n)] = nt(dhoc[...], wu[pl.ds(lo, n), :])

            def by_rows(b, _, lo=lo, n=n):
                cols = pl.ds(lo, n)
                here = pl.ds(pl.multiple_of(b * 16, 16), 16)
                some = pl.ds(pl.multiple_of(i * chunk + b * 16, 16), 16)
                gate = dbuf[0, here, pl.ds(0, n)]
                up = dbuf[1, here, pl.ds(0, n)]
                r[0, some, cols] = (gate * jax.nn.sigmoid(gate) * up).astype(BF)
                r[1, some, cols] = gate.astype(BF)
                r[2, some, cols] = up.astype(BF)
                return 0

            lax.fori_loop(0, chunk // 16, by_rows, 0)

    def hidden_back(i):
        slot = lax.rem(i, 2)
        wait(cot_load(i, slot))

        @pl.when(i + 1 < chunks)
        def _():
            start(cot_load(i + 1, 1 - slot))

        for lo, n in cuts:
            cols = pl.ds(lo, n)
            dbuf[0, :, pl.ds(0, n)] = nt(cotc[slot], w0[pl.ds(lo, n), :])

            def by_rows(b, _, cols=cols, n=n):
                some = pl.ds(pl.multiple_of(i * chunk + b * 16, 16), 16)
                dhid = dbuf[0, pl.ds(pl.multiple_of(b * 16, 16), 16), pl.ds(0, n)]
                gate = r[1, some, cols].astype(F32)
                up = r[2, some, cols].astype(F32)
                sig = jax.nn.sigmoid(gate)
                r[1, some, cols] = (dhid * up * sig * (1.0 + gate * (1.0 - sig))).astype(BF)
                r[2, some, cols] = (dhid * gate * sig).astype(BF)
                return 0

            lax.fori_loop(0, chunk // 16, by_rows, 0)

    def split_store(pair, value, keep, send):
        for side in (0, 1):
            part = value[:, side * local : (side + 1) * local]

            @pl.when(c == side)
            def _(part=part):
                keep[pair] = part

            @pl.when(c != side)
            def _(part=part):
                send[pair] = part.astype(BF)

    def stage_a(i):
        slot = lax.rem(i, 2)
        rows = rows_at(i)
        for pair in (0, 1):
            cols = pl.ds(pair * 2 * local, 2 * local)
            value = nn(r[1, rows, :], wg[:, cols]) + nn(r[2, rows, :], wu[:, cols])
            split_store(pair, value, ck, cs)
        remote(cs, cr.at[slot], c_sem, c_dev, slot).start()
        start(cot_load(i, slot))

    def stage_b(i):
        slot = lax.rem(i, 2)
        remote(cs, cr.at[slot], c_sem, c_dev, slot).wait()
        ys[slot] = (ck[...] + cr[slot].astype(F32)).astype(BF)
        remote(ys.at[slot], yr4.at[slot], y_sem, y_dev, slot).start()

    def stage_c(i):
        slot = lax.rem(i, 2)
        remote(ys.at[slot], yr4.at[slot], y_sem, y_dev, slot).wait()
        da2f[slot, :, c] = (ys[slot].astype(F32) + yr4[slot].astype(F32)).astype(BF)
        remote(da2f.at[slot, :, c], da2f.at[slot, :, c], f_sem, c_dev, slot).start()
        h1_load(i).start()
        bcv_load(i).start()

    def stage_d(i):
        slot = lax.rem(i, 2)
        remote(da2f.at[slot, :, c], da2f.at[slot, :, c], f_sem, c_dev, slot).wait()
        wait(cot_load(i, slot))
        h1_load(i).wait()
        bcv_load(i).wait()
        at = pl.multiple_of(i * chunk, chunk)
        own = pl.ds(pl.multiple_of(me * local, 128), local)

        def by_rows(b, _):
            some = pl.ds(pl.multiple_of(b * 16, 16), 16)
            ssq = jnp.zeros((16, local), F32)
            inner = jnp.zeros((16, local), F32)
            for q in range(4):
                cols = pl.ds(q * local, local)
                h1 = xc[q, some, :].astype(F32)
                ssq += h1 * h1
                inner += da2f[slot, q // 2, q % 2, some, :].astype(F32) * gain(1, q) * h1
            r2 = lax.rsqrt(jnp.sum(ssq, -1, keepdims=True) / width + EPS)
            scale = r2 * r2 * r2 * jnp.sum(inner, -1, keepdims=True) / width

            def grad(q, cols, da2):
                h1 = xc[q, some, :].astype(F32)
                return cotc[slot, some, cols].astype(F32) + r2 * (da2 * gain(1, q)) - h1 * scale

            for q in range(4):
                cols = pl.ds(q * local, local)
                dhoc[some, cols] = grad(q, cols, da2f[slot, q // 2, q % 2, some, :].astype(F32)).astype(BF)
            da2 = da2f[slot, y, c, some, :].astype(F32)
            dh1s[i, some, :] = grad(me, own, da2)
            terms = da2 * xc[me, some, :].astype(F32) * r2
            small_v[pl.ds(8, 8), :] += terms[:8] + terms[8:]
            return 0

        lax.fori_loop(0, chunk // 16, by_rows, 0)
        x_load(i).start()
        transposed_to(0, i)
        dmixed = nt(dhoc[...], wo[...])
        c_gate = bcv[1]
        bxp[pl.ds(0, 8), :] = before_r[i]
        bxp[pl.ds(8, chunk), :] = bcv[3].astype(F32)
        conv, shifts = conv_of()
        r[0, pl.ds(at, chunk), pl.ds(0, local)] = (c_gate.astype(F32) * conv).astype(BF)
        r[0, pl.ds(at, chunk), pl.ds(2 * local, local)] = (dmixed * conv).astype(BF)
        dconv = (dmixed * c_gate.astype(F32)).astype(BF).astype(F32)
        dcp[pl.ds(0, chunk), :] = dconv
        halo_s[i] = dconv[:8]
        for k in range(3):
            small_v[1 + k : 2 + k, :] += jnp.sum(dconv * shifts[k], 0, keepdims=True)

        @pl.when(z > 0)
        def _():
            halo_copy(i).start()

    def halo_copy(i):
        return remote(halo_s.at[i], halo_r.at[i], halo_sem, dn_dev, i)

    def stage_e(i):
        slot = lax.rem(i, 2)
        x_load(i).wait()

        @pl.when(z > 0)
        def _():
            halo_copy(i).wait_send()

        @pl.when(z < last)
        def _():
            halo_copy(i).wait_recv()
            dcp[pl.ds(chunk, 8), :] = halo_r[i]

        @pl.when(z == last)
        def _():
            dcp[pl.ds(chunk, 8), :] = jnp.zeros((8, local), F32)

        dbx = sum(own_v[4 - k : 5 - k, :] * dcp[pl.ds(k, chunk), :] for k in range(3))
        rows = rows_at(i)
        r[0, rows, pl.ds(local, local)] = (dbx * bcv[2].astype(F32)).astype(BF)
        r[0, rows, pl.ds(3 * local, local)] = (dbx * bcv[0].astype(F32)).astype(BF)
        inner = jnp.zeros((chunk, 1), F32)
        ssq = jnp.zeros((chunk, 1), F32)
        for pair in (0, 1):
            cols = pl.ds(pair * 2 * local, 2 * local)
            value = nt(r[0, rows, pl.ds(local, 3 * local)], w0[cols, pl.ds(0, 3 * local)])
            for side in (0, 1):
                q = 2 * pair + side
                x = xc[q].astype(F32)
                part = value[:, side * local : (side + 1) * local]
                inner += jnp.sum(part * x * gain(0, q), -1, keepdims=True)
                ssq += jnp.sum(x * x, -1, keepdims=True)
            split_store(pair, value, ck2, cs2)
        xo[...] = xc[me]
        ins[...] = jnp.broadcast_to(inner, ins.shape)
        r1s[slot] = jnp.broadcast_to(lax.rsqrt(ssq / width + EPS), r1s.shape[1:])
        remote(cs2, yr4.at[2 + slot], c2_sem, c_dev, slot).start()
        remote(ins, inr.at[slot], i_sem, c_dev, slot).start()

    def stage_f(i):
        slot = lax.rem(i, 2)
        remote(cs2, yr4.at[2 + slot], c2_sem, c_dev, slot).wait()
        remote(ins, inr.at[slot], i_sem, c_dev, slot).wait()
        ys2[...] = (ck2[1 - y] + yr4[2 + slot, 1 - y].astype(F32)).astype(BF)
        qk2[...] = ck2[y] + yr4[2 + slot, y].astype(F32)
        iys[...] = ins[...] + inr[slot]
        remote(ys2, yr2.at[slot], y2_sem, y_dev, slot).start()
        remote(iys, iyr.at[slot], iy_sem, y_dev, slot).start()

    def gx_copy(i):
        return load(gxb, gx_h.at[rows_at(i), :], gx_sem)

    def stage_g(i):
        slot = lax.rem(i, 2)
        remote(ys2, yr2.at[slot], y2_sem, y_dev, slot).wait()
        remote(iys, iyr.at[slot], iy_sem, y_dev, slot).wait()
        da1 = qk2[...] + yr2[slot].astype(F32)
        inner = (iys[:, :1] + iyr[slot, :, :1])
        r1 = r1s[slot, :, :1]
        x = xo[...].astype(F32)
        scaled = gain(0, me)
        small_v[0:1, :] += jnp.sum(da1 * x * r1, 0, keepdims=True)

        @pl.when(i > 0)
        def _():
            gx_copy(i - 1).wait()

        gxb[...] = (dh1s[i] + r1 * scaled * da1 - x * (r1 * r1 * r1 * inner / width)).astype(BF)
        gx_copy(i).start()

    def out_start(i):
        rows = rows_at(i)
        for pair in (0, 1):
            cols = pl.ds(pair * 2 * local, 2 * local)
            split_store(pair, nn(r[0, rows, :], w0[:, cols]), ck2, cs2)
        remote(cs2, yr4.at[2 + lax.rem(i, 2)], c2_sem, c_dev, lax.rem(i, 2)).start()

    def out_share(i):
        slot = lax.rem(i, 2)
        remote(cs2, yr4.at[2 + slot], c2_sem, c_dev, slot).wait()
        ys2[...] = (ck2[1 - y] + yr4[2 + slot, 1 - y].astype(F32)).astype(BF)
        qk2[...] = ck2[y] + yr4[2 + slot, y].astype(F32)
        remote(ys2, yr2.at[slot], y2_sem, y_dev, slot).start()

    def out_copy(i):
        return load(gxb, out_h.at[rows_at(i), :], gx_sem)

    def out_end(i):
        slot = lax.rem(i, 2)
        remote(ys2, yr2.at[slot], y2_sem, y_dev, slot).wait()

        @pl.when(i > 0)
        def _():
            out_copy(i - 1).wait()

        gxb[...] = (dh1s[i] + (qk2[...] + yr2[slot].astype(F32))).astype(BF)
        out_copy(i).start()

    def valid(i, f):
        @pl.when(jnp.logical_and(i >= 0, i < chunks))
        def _():
            f(i)

    gather_pass(0, 0)
    gather_pass(2, 0)
    for k in range(3):
        wi_load(k).wait()
    wo_load.wait()
    gather_end(2, 0)
    for one in own_copies:
        one.wait()

    def forward(j, _):
        @pl.when(j < chunks)
        def _():
            project(j)

            @pl.when(j + 1 < chunks)
            def _():
                gather_pass(0, j + 1)

            mix(j)

        @pl.when(j == chunks - 1)
        def _():
            wd_load.start()

        @pl.when(j >= 2)
        def _():
            residual(j - 2)

        @pl.when(j < chunks)
        def _():
            share(j)

        @pl.when(j == chunks - 1)
        def _():
            for i in range(chunks):
                gather_start(1, i)

        @pl.when(j == 2)
        def _():
            wg_load.wait()
            wu_load.wait()

        @pl.when(j >= 2)
        def _():
            feed(j - 2)

        return 0

    lax.fori_loop(0, chunks + 2, forward, 0)
    bcv_store(chunks - 1).wait()
    for pair in (0, 1):
        for core in (0, 1):
            h1_store(chunks - 1, (chunks - 1) % 2, pair, core).wait()

    def cot_pass(i, _):
        gather_pass(1, i)
        return 0

    lax.fori_loop(0, chunks, cot_pass, 0)

    def cot_turn(i, _):
        gather_end(1, i)
        slot = lax.rem(i, 2)
        start(cot_load(i, slot))
        wait(cot_load(i, slot))
        at = pl.multiple_of(i * chunk, chunk)
        for q in range(4):
            cols = pl.ds(q * local, local)
            lt[0, cols, pl.ds(at, chunk)] = cotc[slot, :, cols].T
        return 0

    lax.fori_loop(0, chunks, cot_turn, 0)
    start(cot_load(0, 0))

    def part_one(i, _):
        tick(i, 0)

        @pl.when(i == 0)
        def _():
            wd_load.wait()

        valid(i - 2, out_end)
        valid(i - 1, out_share)
        out_start(i)
        hidden_back(i)
        return 0

    lax.fori_loop(0, chunks, part_one, 0)
    for k in range(3):
        wi_load(k).start()

    def part_two(j, kind):
        t = chunks + 2 * j
        tick(t, kind)

        @pl.when(j == 0)
        def _():
            out_end(chunks - 2)
            out_share(chunks - 1)

        valid(j - 3, stage_g)
        valid(j - 2, stage_e)
        valid(j - 1, stage_c)
        valid(j, stage_a)
        tick(t + 1, kind)

        @pl.when(j == 0)
        def _():
            out_end(chunks - 1)
            out_copy(chunks - 1).wait()

        valid(j, stage_b)
        valid(j - 1, stage_d)
        valid(j - 2, stage_f)

    part_two(0, 0)
    for k in range(3):
        wi_load(k).wait()

    def loop_rest(j, _):
        part_two(j, 1)
        return 0

    lax.fori_loop(1, 1 + (2 * per) // 2, loop_rest, 0)

    def a1_turn(i, _):
        x_load(i).start()
        x_load(i).wait()
        normed_to(lambda q, some: xc[q, some, :], 0)
        transposed_to(1, i)
        return 0

    lax.fori_loop(0, chunks, a1_turn, 0)
    gx_copy(chunks - 1).wait()
    small_v[4:5, :] = jnp.sum(small_v[8:16, :], 0, keepdims=True)

    def small_x():
        return pltpu.make_async_remote_copy(
            src_ref=small_v.at[pl.ds(0, 8)], dst_ref=small_r.at[0], send_sem=small_sem.at[0, 0],
            recv_sem=small_sem.at[0, 1], device_id=x_dev, device_id_type=MESH,
        )

    def small_z(way):
        return pltpu.make_async_remote_copy(
            src_ref=small_r.at[1 + way], dst_ref=small_r.at[3 + way], send_sem=small_sem.at[1 + way, 0],
            recv_sem=small_sem.at[1 + way, 1], device_id=dn_dev if way else up_dev, device_id_type=MESH,
        )

    small_x().start()

    def small_step(k):
        @pl.when(k == 0)
        def _():
            small_x().wait()
            total = small_v[pl.ds(0, 8), :] + small_r[0]
            small_v[pl.ds(0, 8), :] = total
            small_r[1] = total
            small_r[2] = total

        for way in (0, 1):
            turn = last - z if way else z

            @pl.when(jnp.logical_and(turn < last, k == turn))
            def _(way=way, turn=turn):
                @pl.when(turn > 0)
                def _():
                    small_z(way).wait_recv()
                    small_r[1 + way] = small_v[pl.ds(0, 8), :] + small_r[3 + way]

                small_z(way).start()

    def small_end():
        for way in (0, 1):
            turn = last - z if way else z

            @pl.when(turn < last)
            def _(way=way):
                small_z(way).wait_send()

            @pl.when(turn == last)
            def _(way=way):
                small_z(way).wait_recv()

            @pl.when(turn > 0)
            def _(way=way):
                small_v[pl.ds(0, 8), :] += small_r[3 + way]

    def part_three(k, _):
        tick(3 * per + k, 3)
        small_step(k)
        return 0

    lax.fori_loop(0, per, part_three, 0)

    def part_four(k, _):
        tick(units + k)
        return 0

    lax.fori_loop(0, depth, part_four, 0)
    small_end()
    out_do(units - 2, "wait")
    out_do(units - 1, "wait")


def block(dims, x_own, cot_own, own, wd, wg, wu, wo, wi):
    tokens, chunk, width, ff, local, nseq = dims
    rows = width // (2 * nseq)
    chunks = tokens // chunk
    last = nseq - 1
    m = ROWS * nseq
    DMA = pltpu.SemaphoreType.DMA
    shape = jax.ShapeDtypeStruct
    third = ff // 3 // 128 * 128
    scratch = [
        pltpu.VMEM((2, width, tokens), BF),
        pltpu.VMEM((3, tokens, ff), BF),
        pltpu.VMEM((ff, width), BF),
        pltpu.VMEM((ff, width), BF),
        pltpu.VMEM((ff, width), BF),
        pltpu.VMEM((local, width), BF),
        pltpu.VMEM((2, chunk, width), BF),
        pltpu.VMEM((4, chunk, local), BF),
        pltpu.VMEM((chunk, local), BF),
        pltpu.VMEM((4, chunk, local), BF),
        pltpu.VMEM((8 + chunk, local), F32),
        pltpu.VMEM((2, chunk, ff - 2 * third), F32),
        pltpu.VMEM((8 + chunk, local), F32),
        pltpu.VMEM((chunk, width), BF),
        pltpu.VMEM((chunks, chunk, local), F32),
        pltpu.VMEM((2, chunk, 128), F32),
        pltpu.VMEM((4, 8, local), F32),
        pltpu.VMEM((2, m, ff), BF),
        pltpu.VMEM((4, m, ff), BF),
        pltpu.VMEM((6, m, ff), BF),
        pltpu.VMEM((2, last * (last + 1) // 2, ROWS, ff), BF),
        pltpu.VMEM((2, last, 3, ROWS, ff), BF),
        pltpu.VMEM((2, ROWS, ff), BF),
        pltpu.VMEM((6, chunk, local), F32),
        pltpu.VMEM((2, chunk, local), BF),
        pltpu.VMEM((2, 2, chunk, local), BF),
        pltpu.VMEM((2, 2, chunk, local), BF),
        pltpu.VMEM((4, 2, chunk, local), BF),
        pltpu.VMEM((2, 2, 2, chunk, local), BF),
        pltpu.VMEM((2, chunk, local), BF),
        pltpu.VMEM((chunk, local), BF),
        pltpu.VMEM((2, chunk, local), BF),
        pltpu.VMEM((chunk, 128), F32),
        pltpu.VMEM((2, chunk, 128), F32),
        pltpu.VMEM((chunk, 128), F32),
        pltpu.VMEM((2, chunk, 128), F32),
        pltpu.VMEM((chunk, local), BF),
        pltpu.VMEM((chunks, 8, local), F32),
        pltpu.VMEM((chunks, 8, local), F32),
        pltpu.VMEM((chunks, 8, local), F32),
        pltpu.VMEM((chunks, 8, local), F32),
        pltpu.VMEM((5, 8, local), F32),
        DMA((2,)), DMA((4,)), DMA((2, last, 3)), DMA((2, last, 3)), DMA((8,)),
        DMA((2, 2)), DMA((2, chunks)), DMA((2, 2)), DMA((2, 2)), DMA((2, 2)),
        DMA((2, 2)), DMA((2, 2)), DMA((2, chunks)), DMA((2, chunks)), DMA((3, 2, 3, chunks)),
        DMA((2,)), DMA((7,)), DMA((3, 4)), DMA(()), DMA((2, 2)), DMA(()), DMA((3, 2)),
    ]
    return pl.pallas_call(
        functools.partial(block_kernel, dims),
        out_shape=(
            shape((rows, ff), BF), shape((rows, ff), BF), shape((rows, ff), BF),
            shape((rows, local), BF), shape((3, rows, local), BF),
            shape((tokens, local), BF), shape((tokens, local), BF), shape((16, local), F32),
            shape((4, tokens, local), BF), shape((4, tokens, local), BF),
            shape((4, tokens, local), BF), shape((4, tokens, local), BF),
        ),
        in_specs=[ANY, ANY, VMEM] + [ANY] * 5,
        out_specs=(ANY,) * 7 + (VMEM,) + (ANY,) * 4,
        scratch_shapes=scratch,
        compiler_params=pltpu.CompilerParams(
            collective_id=0, has_side_effects=True, vmem_limit_bytes=63 * 2**20
        ),
    )(x_own, cot_own, own, wd, wg, wu, wo, wi)


def shifted(array, axis, by):
    count = lax.axis_size(axis)
    pairs = [(i, i + by) for i in range(count) if 0 <= i + by < count]
    return lax.ppermute(array, axis, pairs)


def fused_device(inputs, gain_mix, w_in, kernel, w_out, gain_ff, w_gate, w_up, w_down, cotangent):
    groups, seq_rows, local = inputs.shape
    width = local * lax.axis_size("mp")
    ff = w_down.shape[0]
    tokens = groups * seq_rows
    dims = (tokens, seq_rows, width, ff, local, lax.axis_size("seq"))
    own = jnp.concatenate(
        [gain_mix[None], gain_ff[None], kernel, jnp.zeros((3, local), BF)], 0
    ).astype(F32)
    gdown, ggate, gup, gout, gin, gx, out, small = block(
        dims, inputs.reshape(tokens, local), cotangent.reshape(tokens, local), own,
        w_down, w_gate.T, w_up.T, w_out, w_in.transpose(1, 0, 2),
    )[:8]
    whole = (groups, seq_rows, local)
    return (
        out.reshape(whole), gx.reshape(whole), small[0], gin.transpose(1, 0, 2).astype(F32), small[1:4],
        gout.T.astype(F32), small[4], ggate.astype(F32), gup.astype(F32), gdown.T.astype(F32),
    )


def contract_rows(left, right):
    return lax.dot_general(
        left, right, (((0,), (0,)), ((), ())), preferred_element_type=jnp.float32
    )


def contract_cols(left, right):
    return lax.dot_general(
        left, right, (((1,), (1,)), ((), ())), preferred_element_type=jnp.float32
    )


def plain_device(inputs, gain_mix, w_in, kernel, w_out, gain_ff, w_gate, w_up, w_down, cotangent):
    groups, seq_rows, local_width = inputs.shape
    full_width = local_width * lax.axis_size("mp")
    tokens = groups * seq_rows
    x_float = inputs.reshape(tokens, local_width).astype(jnp.float32)
    gain_one = gain_mix.astype(jnp.float32)
    gain_two = gain_ff.astype(jnp.float32)
    taps = kernel.astype(jnp.float32)

    def row_total(values):
        return lax.psum(jnp.sum(values, axis=-1, keepdims=True), "mp")

    def all_features(values):
        return lax.all_gather(values, "mp", axis=1, tiled=True)

    def share_sums(values):
        return lax.psum_scatter(
            values.astype(jnp.bfloat16), "mp", scatter_dimension=1, tiled=True
        ).astype(jnp.float32)

    def scattered(values, dim):
        return lax.psum_scatter(
            values.astype(jnp.bfloat16), ("dp", "seq"), scatter_dimension=dim, tiled=True
        ).astype(jnp.float32)

    def norm_scale(values):
        return lax.rsqrt(row_total(values * values) / full_width + EPS)

    def norm_back(values, scale, gain_vec, upstream):
        inner = row_total(gain_vec * upstream * values)
        grad_values = scale * gain_vec * upstream - values * scale**3 * inner / full_width
        return (grad_values, jnp.sum(upstream * values * scale, axis=0))

    scale_one = norm_scale(x_float)
    normed_in = all_features((x_float * scale_one * gain_one).astype(jnp.bfloat16))
    proj = jnp.einsum("td,dkc->tkc", normed_in, w_in, preferred_element_type=jnp.float32)
    b_gate = proj[:, 0]
    c_gate = proj[:, 1]
    values_v = proj[:, 2]
    b_times_x = (b_gate * values_v).astype(jnp.bfloat16).reshape(groups, seq_rows, local_width)
    before = shifted(b_times_x[:, seq_rows - 2 :], "seq", 1)
    padded = jnp.concatenate([before, b_times_x], 1).astype(jnp.float32)
    conv = taps[0] * padded[:, :-2] + taps[1] * padded[:, 1:-1] + taps[2] * padded[:, 2:]
    conv = conv.reshape(tokens, local_width)
    mixed = (c_gate * conv).astype(jnp.bfloat16)
    hidden_one = x_float + share_sums(jnp.dot(mixed, w_out, preferred_element_type=jnp.float32))
    scale_two = norm_scale(hidden_one)
    normed_ff = all_features((hidden_one * scale_two * gain_two).astype(jnp.bfloat16))
    gate = jnp.dot(normed_ff, w_gate, preferred_element_type=jnp.float32)
    up_proj = jnp.dot(normed_ff, w_up, preferred_element_type=jnp.float32)
    sigma = jax.nn.sigmoid(gate)
    active = gate * sigma
    hidden = (active * up_proj).astype(jnp.bfloat16)
    ffn_out = share_sums(jnp.dot(hidden, w_down, preferred_element_type=jnp.float32))
    block_out = (hidden_one + ffn_out).astype(jnp.bfloat16).reshape(groups, seq_rows, local_width)
    grad_flat = cotangent.reshape(tokens, local_width)
    grad_full = all_features(grad_flat)
    grad_down = contract_rows(hidden, grad_full)
    grad_hidden = contract_cols(grad_full, w_down)
    grad_gate_act = (grad_hidden * up_proj * sigma * (1.0 + gate * (1.0 - sigma))).astype(
        jnp.bfloat16
    )
    grad_up_act = (grad_hidden * active).astype(jnp.bfloat16)
    grad_gate = contract_rows(normed_ff, grad_gate_act)
    grad_up = contract_rows(normed_ff, grad_up_act)
    grad_normed_ff = share_sums(
        contract_cols(grad_gate_act, w_gate) + contract_cols(grad_up_act, w_up)
    )
    grad_norm_two, grad_gain_two = norm_back(hidden_one, scale_two, gain_two, grad_normed_ff)
    grad_hidden_one = grad_flat.astype(jnp.float32) + grad_norm_two
    grad_out_full = all_features(grad_hidden_one.astype(jnp.bfloat16))
    grad_out = contract_rows(mixed, grad_out_full)
    grad_mixed = contract_cols(grad_out_full, w_out)
    grad_c = grad_mixed * conv
    grad_conv = (grad_mixed * c_gate).astype(jnp.bfloat16).reshape(groups, seq_rows, local_width)
    after = shifted(grad_conv[:, :2], "seq", -1)
    extended = jnp.concatenate([grad_conv, after], 1).astype(jnp.float32)
    grad_bx = taps[2] * extended[:, :-2] + taps[1] * extended[:, 1:-1] + taps[0] * extended[:, 2:]
    grad_bx = grad_bx.reshape(tokens, local_width)
    conv_grad_float = extended[:, :-2]
    grad_taps = jnp.stack(
        [
            jnp.sum(conv_grad_float * padded[:, :-2], axis=(0, 1)),
            jnp.sum(conv_grad_float * padded[:, 1:-1], axis=(0, 1)),
            jnp.sum(conv_grad_float * padded[:, 2:], axis=(0, 1)),
        ]
    )
    grad_proj = jnp.stack([grad_bx * values_v, grad_c, grad_bx * b_gate], 1).astype(jnp.bfloat16)
    grad_in = jnp.einsum("td,tkc->dkc", normed_in, grad_proj, preferred_element_type=jnp.float32)
    grad_normed_in = share_sums(
        jnp.einsum("tkc,dkc->td", grad_proj, w_in, preferred_element_type=jnp.float32)
    )
    grad_norm_one, grad_gain_one = norm_back(x_float, scale_one, gain_one, grad_normed_in)
    grad_input = (
        (grad_hidden_one + grad_norm_one)
        .astype(jnp.bfloat16)
        .reshape(groups, seq_rows, local_width)
    )
    small_sums = lax.psum((grad_gain_one, grad_taps, grad_gain_two), ("dp", "seq"))
    by_row = (
        scattered(grad_in, 0),
        scattered(grad_gate, 0),
        scattered(grad_up, 0),
    )
    by_col = (
        scattered(grad_out, 1),
        scattered(grad_down, 1),
    )
    return (
        block_out,
        grad_input,
        small_sums[0],
        by_row[0],
        small_sums[1],
        by_col[0],
        small_sums[2],
        by_row[1],
        by_row[2],
        by_col[1],
    )


def solution(mesh):
    placed = (
        P("dp", "seq", "mp"),
        P("mp"),
        P(None, None, "mp"),
        P(None, "mp"),
        P("mp", None),
        P("mp"),
        P(None, "mp"),
        P(None, "mp"),
        P("mp", None),
        P("dp", "seq", "mp"),
    )
    sizes = mesh.shape
    fused = sizes["dp"] == 2 and sizes["seq"] == 4 and sizes["mp"] == 4
    return jax.shard_map(
        fused_device if fused else plain_device,
        mesh=mesh,
        in_specs=placed,
        out_specs=(
            P("dp", "seq", "mp"),
            P("dp", "seq", "mp"),
            P("mp"),
            P(("dp", "seq"), None, "mp"),
            P(None, "mp"),
            P("mp", ("dp", "seq")),
            P("mp"),
            P(("dp", "seq"), "mp"),
            P(("dp", "seq"), "mp"),
            P("mp", ("dp", "seq")),
        ),
        check_vma=False,
    )
```

```python
import functools

import jax
import jax.numpy as jnp
from jax import lax
from jax.experimental import pallas as pl
from jax.experimental.pallas import tpu as pltpu
from jax.sharding import PartitionSpec as P

EPS = 1e-05
MESH = pl.DeviceIdType.MESH
BF = jnp.bfloat16
F32 = jnp.float32
ROWS = 32
SECOND = 3
LAG = 3
WAIT = 3
PLACES = {
    "out_start": (2, (1, 4, 7, 8)),
    "out_share": (2, (2, 5, 8, 10)),
    "out_end": (1, (4, 7, 9, 12)),
    "a": (2, (3, 8, 10, 14)),
    "b": (2, (4, 9, 12, 15)),
    "c": (1, (8, 11, 14, 18)),
    "d": (2, (9, 13, 17, 19)),
    "e": (2, (12, 15, 18, 20)),
    "f": (2, (14, 16, 19, 21)),
    "g": (2, (15, 18, 20, 22)),
    "a1": (2, (15, 16, 17, 19)),
}
HIDDEN = (1, {2: 3, 3: 4, 4: 5, 5: 7, 6: 12})
ANY = pl.BlockSpec(memory_space=pl.ANY)
VMEM = pl.BlockSpec(memory_space=pltpu.VMEM)


def nn(left, right):
    return lax.dot_general(left, right, (((1,), (0,)), ((), ())), preferred_element_type=F32)


def nt(left, right):
    return lax.dot_general(left, right, (((1,), (1,)), ((), ())), preferred_element_type=F32)


def block_kernel(
    dims,
    x_in, cot_in, own_v, wd_h, wg_h, wu_h, wo_h, wi_h,
    gdown_h, ggate_h, gup_h, gout_h, gin_h, gx_h, out_h, small_v,
    x_h, cot_h, h1_h, bcv_h,
    lt, r, w0, wg, wu, wo, cotc, xc, xo, bcv, bxp, dbuf, dcp, dhoc, dh1s, r1s, gv,
    xs, xr, s_buf, zs, zr, ob, vs, vr, vk,
    kf, cs, cr, ys, yr4, da2f, cs2, ys2, yr2,
    ins, inr, iys, iyr, gxb, halo_s, halo_r, before_s, before_r, small_r,
    xs_sem, xr_sem, zs_sem, zr_sem, ob_sem, c_sem, y_sem, f_sem, c2_sem, y2_sem,
    i_sem, iy_sem, halo_sem, before_sem, gather_sem, w_sem, l_sem, bcv_sem, h1_sem, gx_sem,
    small_sem, v_sem,
):
    tokens, chunk, width, ff, local, nseq = dims
    chunks = tokens // chunk
    block = width // (2 * nseq)
    per = block // ROWS
    beat = per + 1
    ticks = 4 * beat
    p = lax.axis_index("dp")
    z = lax.axis_index("seq")
    me = lax.axis_index("mp")
    y, c = me // 2, me % 2
    x_dev = {"dp": 1 - p}
    up_dev = {"seq": z + 1}
    dn_dev = {"seq": z - 1}
    y_dev = {"mp": (1 - y) * 2 + c}
    c_dev = {"mp": y * 2 + 1 - c}
    last = nseq - 1
    ck, ck2, qk2 = kf.at[pl.ds(0, 2)], kf.at[pl.ds(2, 2)], kf.at[4]
    third = ff // 3 // 128 * 128
    cuts = ((0, third), (third, third), (2 * third, ff - 2 * third))

    def remote(src, dst, sems, where, at=None):
        s_sem, r_sem = (sems.at[0], sems.at[1]) if at is None else (sems.at[0, at], sems.at[1, at])
        return pltpu.make_async_remote_copy(
            src_ref=src, dst_ref=dst, send_sem=s_sem, recv_sem=r_sem,
            device_id=where, device_id_type=MESH,
        )

    def load(src, dst, sem):
        return pltpu.make_async_copy(src, dst, sem)

    def wi_load(k):
        return load(wi_h.at[k], w0.at[pl.ds(0, width), pl.ds(k * local, local)], w_sem.at[k])

    wd_load = load(wd_h, w0, w_sem.at[3])
    wg_load = load(wg_h, wg, w_sem.at[4])
    wu_load = load(wu_h, wu, w_sem.at[5])
    wo_load = load(wo_h, wo, w_sem.at[6])
    for k in range(3):
        wi_load(k).start()
    wo_load.start()
    gv[me] = own_v[...]

    barrier = pltpu.get_barrier_semaphore()
    for dev in (x_dev, y_dev, c_dev):
        pl.semaphore_signal(barrier, inc=1, device_id=dev, device_id_type=MESH)

    @pl.when(z < last)
    def _():
        pl.semaphore_signal(barrier, inc=1, device_id=up_dev, device_id_type=MESH)

    @pl.when(z > 0)
    def _():
        pl.semaphore_signal(barrier, inc=1, device_id=dn_dev, device_id_type=MESH)

    peers = 3 + jnp.where(z < last, 1, 0) + jnp.where(z > 0, 1, 0)
    pl.semaphore_wait(barrier, peers)

    small_v[...] = jnp.zeros_like(small_v)

    def rows_at(i):
        return pl.ds(pl.multiple_of(i * chunk, chunk), chunk)

    def gather(which, i, leg):
        if which == 2:
            src = mine = own_v
            dst = gv
            at = (2, 0)
        else:
            src, dst = (x_in, x_h) if which == 0 else (cot_in, cot_h)
            mine = src.at[rows_at(i), :]
            at = (which, i)
        slot = (lambda q: dst.at[q]) if which == 2 else (lambda q: dst.at[q, rows_at(i), :])
        sems = [gather_sem.at[leg, way, at[0], at[1]] for way in (0, 1)]
        if leg == 0:
            pair, where = (mine, slot(me)), y_dev
        elif leg == 1:
            pair, where = (mine, slot(me)), c_dev
        else:
            from_y = (1 - y) * 2 + c
            pair, where = (slot(from_y), slot(from_y)), c_dev
        return pltpu.make_async_remote_copy(
            src_ref=pair[0], dst_ref=pair[1], send_sem=sems[0], recv_sem=sems[1],
            device_id=where, device_id_type=MESH,
        )

    def gather_start(which, i):
        gather(which, i, 0).start()
        gather(which, i, 1).start()

    def gather_pass(which, i):
        gather(which, i, 0).wait_recv()
        gather(which, i, 2).start()

    def gather_end(which, i):
        gather(which, i, 0).wait_send()
        gather(which, i, 1).wait()
        gather(which, i, 2).wait()

    for i in range(chunks):
        gather_start(0, i)
        if i == 0:
            gather_start(2, 0)
    wg_load.start()
    wu_load.start()

    def on_size(t, f):
        pl.when(t // beat < 3)(lambda: f(pl.ds(0, ff)))
        pl.when(t // beat == 3)(lambda: f(pl.ds(0, 4 * local)))

    def place(t):
        return lax.rem(t, beat)

    def is_first(t):
        return place(t) == 0

    def is_second(t):
        return place(t) == SECOND

    def is_plain(t):
        return jnp.logical_and(place(t) != 0, place(t) != SECOND)

    def row_block(t):
        plain = place(t) - jnp.where(place(t) > SECOND, 2, 1)
        return jnp.where(is_plain(t), plain, per - 1)

    def x_number(t):
        return t // beat * (per - 1) + row_block(t)

    def x_do(t, what):
        n = x_number(t)

        def f(cols):
            copy = pltpu.make_async_remote_copy(
                src_ref=xs.at[lax.rem(n, 3), :, cols], dst_ref=xr.at[lax.rem(n, 5), :, cols],
                send_sem=xs_sem.at[lax.rem(n, 3)], recv_sem=xr_sem.at[lax.rem(n, 5)],
                device_id=x_dev, device_id_type=MESH,
            )
            getattr(copy, what)()

        on_size(t, f)

    def v_do(t, what):
        def f(cols):
            copy = pltpu.make_async_remote_copy(
                src_ref=vs.at[:, cols], dst_ref=vr.at[:, cols], send_sem=v_sem.at[0], recv_sem=v_sem.at[1],
                device_id=x_dev, device_id_type=MESH,
            )
            getattr(copy, what)()

        on_size(t, f)

    def zs_at(t, step):
        return 2 * step + lax.rem(t, 2)

    def zr_at(t, step):
        count = 3 if 0 < step < last - 1 else 4
        return 3 * step + min(step, 1) + lax.rem(t, count)

    def z_do(t, way, step, what):
        def f(cols):
            copy = pltpu.make_async_remote_copy(
                src_ref=zs.at[way, zs_at(t, step), :, cols], dst_ref=zr.at[way, zr_at(t, step), :, cols],
                send_sem=zs_sem.at[way, zs_at(t, step)], recv_sem=zr_sem.at[way, zr_at(t, step)],
                device_id=dn_dev if way else up_dev, device_id_type=MESH,
            )
            getattr(copy, what)()

        on_size(t, f)

    def receives(way, step):
        if way:
            return jnp.logical_and(z < last, z >= last - 1 - step)
        return jnp.logical_and(z > 0, z <= step + 1)

    def can_send(way, step):
        if way:
            return jnp.logical_and(z > 0, z >= last - step)
        return jnp.logical_and(z < last, z <= step)

    def z_arrived(t, step):
        for way in (0, 1):
            @pl.when(receives(way, step))
            def _(way=way):
                z_do(t, way, step, "wait_recv")

            @pl.when(can_send(way, step))
            def _(way=way):
                z_do(t, way, step, "wait_send")

    def z_step(t, step):
        sl = lax.rem(t, LAG + 4)
        if step > 0:
            z_arrived(t, step - 1)
        for way in (0, 1):
            quarter = z - last + step if way else last - step + z
            fresh = can_send(way, step)
            if step > 0:
                @pl.when(jnp.logical_and(receives(way, step - 1), can_send(way, step)))
                def _(way=way, quarter=quarter):
                    value = s_buf[sl, pl.ds(quarter * ROWS, ROWS), :].astype(F32) + zr[
                        way, zr_at(t, step - 1)
                    ].astype(F32)
                    zs[way, zs_at(t, step)] = value.astype(BF)

                fresh = jnp.logical_and(fresh, jnp.logical_not(receives(way, step - 1)))

            @pl.when(fresh)
            def _(way=way, quarter=quarter):
                zs[way, zs_at(t, step)] = s_buf[sl, pl.ds(quarter * ROWS, ROWS), :]

        for way in (0, 1):
            @pl.when(can_send(way, step))
            def _(way=way):
                z_do(t, way, step, "start")

    def compute(t, kind):
        sl = lax.rem(t, LAG + 4)
        at = row_block(t) * ROWS
        m = ROWS * nseq

        def rows_of(index, half):
            rows = [pl.ds(pl.multiple_of((half * nseq + s) * block + at, ROWS), ROWS) for s in range(nseq)]
            if kind == 3 and index == 1:
                return [wg[some, pl.ds(0, tokens)] for some in rows]
            return [lt[index, some, :] for some in rows]

        if kind == 3:
            parts = [(0, 0, 0, local)] + [(1, 0, k * local, local) for k in (1, 2, 3)]
        elif kind == 0:
            parts = [(0, 0, lo, n) for lo, n in cuts]
        else:
            parts = [(1, t // beat, lo, n) for lo, n in cuts]

        @pl.when(is_plain(t))
        def _():
            slot = lax.rem(x_number(t), 3)
            left = [jnp.concatenate(rows_of(i, 1 - p) + rows_of(i, p), 0) for i in sorted({q[0] for q in parts})]
            for i, ri, lo, n in parts:
                cols = pl.ds(lo, n)
                out = nn(left[i if len(left) == 2 else 0], r[ri, :, cols])
                xs[slot, :, cols] = out[:m].astype(BF)
                s_buf[sl, :, cols] = out[m:].astype(BF)
            x_do(t, "start")

        @pl.when(jnp.logical_not(is_plain(t)))
        def _():
            half = jnp.where(is_first(t), p, 1 - p)
            left = [jnp.concatenate(rows_of(i, half), 0) for i in sorted({q[0] for q in parts})]
            for i, ri, lo, n in parts:
                cols = pl.ds(lo, n)
                s_buf[sl, :, cols] = nn(left[i if len(left) == 2 else 0], r[ri, :, cols]).astype(BF)

    def out_do(src, t, sems, what):
        rows = pl.ds(pl.multiple_of(row_block(t) * ROWS, ROWS), ROWS)
        for g, target in enumerate((gdown_h, ggate_h, gup_h)):
            @pl.when(t // beat == g)
            def _(target=target):
                getattr(load(src, target.at[rows, :], ob_sem.at[sems, 0]), what)()

        @pl.when(t // beat == 3)
        def _():
            getattr(load(src.at[:, pl.ds(0, local)], gout_h.at[rows, :], ob_sem.at[sems, 0]), what)()
            for k in range(3):
                part = src.at[:, pl.ds((k + 1) * local, local)]
                getattr(load(part, gin_h.at[k, rows, :], ob_sem.at[sems, 1 + k]), what)()

    def plain_out(t, what):
        slot = lax.rem(x_number(t), 2)
        out_do(ob.at[slot], t, slot, what)

    def finish(t):
        sl = lax.rem(t, LAG + 4)
        z_arrived(t, last - 1)

        def total(then):
            def end(ways):
                value = s_buf[sl, pl.ds(z * ROWS, ROWS), :].astype(F32)
                for way in ways:
                    value += zr[way, zr_at(t, last - 1)].astype(F32)
                then(value)

            pl.when(z == 0)(lambda: end((1,)))
            pl.when(z == last)(lambda: end((0,)))
            pl.when(jnp.logical_and(z > 0, z < last))(lambda: end((0, 1)))

        @pl.when(is_plain(t))
        def _():
            n = x_number(t)
            before = t - jnp.where(place(t) == per, 2, 3)

            @pl.when(n >= 2)
            def _():
                plain_out(before, "wait")

            def put(value):
                ob[lax.rem(n, 2)] = value.astype(BF)

            total(put)
            plain_out(t, "start")

        @pl.when(is_first(t))
        def _():
            def put(value):
                vk[...] = value

            total(put)

        @pl.when(is_second(t))
        def _():
            def put(value):
                vs[...] = value.astype(BF)

            total(put)
            v_do(t, "start")

    def v_end(t):
        @pl.when(is_second(t))
        def _():
            v_do(t, "wait")

            @pl.when(t >= beat)
            def _():
                out_do(ob.at[2], t - beat, 2, "wait")

            ob[2] = (vk[...] + vr[...].astype(F32)).astype(BF)
            out_do(ob.at[2], t, 2, "start")

    def within(t, f):
        @pl.when(jnp.logical_and(t >= 0, t < ticks))
        def _():
            f(t)

    def tick_a(t, full=False):
        within(t - LAG - 4 - WAIT, v_end)
        within(t - LAG - 4, finish)

        def x_in(u):
            @pl.when(is_plain(u))
            def _():
                x_do(u, "wait")
                sl = lax.rem(u, LAG + 4)
                arrived = xr[lax.rem(x_number(u), 5)].astype(F32)
                s_buf[sl] = (s_buf[sl].astype(F32) + arrived).astype(BF)

            z_step(u, 0)

        within(t - LAG, x_in)
        if full:
            pl.when(t // beat == 0)(lambda: compute(t, 0))
            pl.when(jnp.logical_and(t // beat > 0, t // beat < 3))(lambda: compute(t, 1))
            pl.when(t // beat == 3)(lambda: compute(t, 3))

    def tick_b(t):
        within(t - LAG - 1, lambda u: z_step(u, 1))

    def tick_c(t):
        within(t - LAG - 2, lambda u: z_step(u, 2))

    def in_slices(own, others, to, slot):
        copies = [load(own, to(me), l_sem.at[slot, 0])]
        for step in range(1, 4):
            q = lax.rem(me + step, 4)
            copies.append(load(others(q), to(q), l_sem.at[slot, step]))
        return copies

    def cot_load(i):
        return in_slices(
            cot_in.at[rows_at(i), :],
            lambda q: cot_h.at[q, rows_at(i), :],
            lambda q: cotc.at[:, pl.ds(pl.multiple_of(q * local, 128), local)],
            0,
        )

    def x_load(i):
        return in_slices(x_in.at[rows_at(i), :], lambda q: x_h.at[q, rows_at(i), :], lambda q: xc.at[q], 1)

    def start(copies):
        for one in copies:
            one.start()

    def wait(copies):
        for one in copies:
            one.wait()

    def h1_load(i):
        return load(h1_h.at[:, rows_at(i), :], xc, l_sem.at[2, 0])

    def bcv_load(i):
        return load(bcv_h.at[:, rows_at(i), :], bcv, l_sem.at[2, 1])

    def gain(row, q):
        return gv[q, row : row + 1, :]

    def by_sixteen(f):
        def body(b, _):
            f(pl.ds(pl.multiple_of(b * 16, 16), 16))
            return 0

        lax.fori_loop(0, chunk // 16, body, 0)

    def normed_to(src, row, after=None):
        def f(some):
            ssq = jnp.zeros((16, local), F32)
            for q in range(4):
                values = src(q, some).astype(F32)
                ssq += values * values
            scale = lax.rsqrt(jnp.sum(ssq, -1, keepdims=True) / width + EPS)
            for q in range(4):
                dhoc[some, pl.ds(q * local, local)] = (src(q, some).astype(F32) * scale * gain(row, q)).astype(BF)

        by_sixteen(f)

    def transposed_to(index, i):
        at = pl.multiple_of(i * chunk, chunk)
        for q in range(4):
            cols = pl.ds(q * local, local)
            lt[index, cols, pl.ds(at, chunk)] = dhoc[:, cols].T

    def before_copy(i):
        return remote(before_s.at[i], before_r.at[i], before_sem, up_dev, i)

    def bcv_store(i):
        return load(bcv, bcv_h.at[:, rows_at(i), :], bcv_sem)

    def h1_store(i, slot, pair, core):
        return load(da2f.at[slot, pair, core], h1_h.at[2 * pair + core, rows_at(i), :], h1_sem.at[pair, core])

    def project(i):
        gather_end(0, i)
        start(x_load(i))
        wait(x_load(i))
        normed_to(lambda q, some: xc[q, some, :], 0)
        value = nn(dhoc[...], w0[pl.ds(0, width), pl.ds(0, 3 * local)])

        @pl.when(i > 0)
        def _():
            bcv_store(i - 1).wait()

        for k in range(3):
            bcv[k] = value[:, k * local : (k + 1) * local].astype(BF)
        dcp[pl.ds(0, chunk), :] = value[:, local : 2 * local]
        bx = (value[:, :local] * value[:, 2 * local :]).astype(BF)
        bcv[3] = bx
        bxp[pl.ds(8, chunk), :] = bx.astype(F32)
        before_s[i] = bxp[pl.ds(chunk, 8), :]

        @pl.when(z < last)
        def _():
            before_copy(i).start()

        bcv_store(i).start()

    def conv_of():
        shifts = [bxp[pl.ds(6 + k, chunk), :] for k in range(3)]
        return sum(own_v[2 + k : 3 + k, :] * shifts[k] for k in range(3)), shifts

    def mix(i):
        slot = lax.rem(i, 2)

        @pl.when(z < last)
        def _():
            before_copy(i).wait_send()

        @pl.when(z > 0)
        def _():
            before_copy(i).wait_recv()

        @pl.when(z == 0)
        def _():
            before_r[i] = jnp.zeros((8, local), F32)

        bxp[pl.ds(0, 8), :] = before_r[i]
        mixed = (dcp[pl.ds(0, chunk), :] * conv_of()[0]).astype(BF)
        for pair in (0, 1):
            split_store(pair, nn(mixed, wo[:, pl.ds(pair * 2 * local, 2 * local)]), ck, cs)
        remote(cs, cr.at[slot], c_sem, c_dev, slot).start()

    def share(i):
        slot = lax.rem(i, 2)
        remote(cs, cr.at[slot], c_sem, c_dev, slot).wait()
        for pair in (0, 1):
            total = ck[pair] + cr[slot, pair].astype(F32)
            kf[2 + 2 * slot + pair] = total + xc[2 * pair + c].astype(F32)
            ys[slot, pair] = total.astype(BF)
        remote(ys.at[slot], yr4.at[i], y_sem, y_dev, i).start()

    def residual(i):
        slot = lax.rem(i, 2)
        remote(ys.at[slot], yr4.at[i], y_sem, y_dev, i).wait()

        @pl.when(i >= 1)
        def _():
            for pair in (0, 1):
                for core in (0, 1):
                    h1_store(i - 1, 1 - slot, pair, core).wait()

        for pair in (0, 1):
            h1 = kf[2 + 2 * slot + pair] + yr4[i, pair].astype(F32)
            da2f[slot, pair, c] = h1.astype(BF)

            @pl.when(y == pair)
            def _(h1=h1):
                dh1s[i] = h1
        remote(da2f.at[slot, :, c], da2f.at[slot, :, c], f_sem, c_dev, slot).start()

    def cot_turn(i):
        gather_end(1, i)
        start(cot_load(i))
        wait(cot_load(i))
        at = pl.multiple_of(i * chunk, chunk)
        for q in range(4):
            cols = pl.ds(q * local, local)
            lt[0, cols, pl.ds(at, chunk)] = cotc[:, cols].T

    def feed(i):
        slot = lax.rem(i, 2)
        remote(da2f.at[slot, :, c], da2f.at[slot, :, c], f_sem, c_dev, slot).wait()
        for pair in (0, 1):
            for core in (0, 1):
                h1_store(i, slot, pair, core).start()
        normed_to(lambda q, some: da2f[slot, q // 2, q % 2, some, :], 1)
        transposed_to(1, i)
        rows = rows_at(i)
        for lo, n in cuts:
            dbuf[:, pl.ds(0, n)] = nt(dhoc[...], wg[pl.ds(lo, n), :])
            r[2, rows, pl.ds(lo, n)] = nt(dhoc[...], wu[pl.ds(lo, n), :]).astype(BF)

            def by_rows(b, _, lo=lo, n=n):
                cols = pl.ds(lo, n)
                here = pl.ds(pl.multiple_of(b * 16, 16), 16)
                some = pl.ds(pl.multiple_of(i * chunk + b * 16, 16), 16)
                gate = dbuf[here, pl.ds(0, n)]
                up = r[2, some, cols].astype(F32)
                r[0, some, cols] = (gate * jax.nn.sigmoid(gate) * up).astype(BF)
                r[1, some, cols] = gate.astype(BF)
                return 0

            lax.fori_loop(0, chunk // 16, by_rows, 0)

    def hidden_back(piece):
        i = piece // 3

        @pl.when(lax.rem(piece, 3) == 0)
        def _():
            wait(cot_load(i))

        for k, cut in enumerate(cuts):
            pl.when(lax.rem(piece, 3) == k)(functools.partial(hidden_cut, i, *cut))

        @pl.when(jnp.logical_and(lax.rem(piece, 3) == 2, i + 1 < chunks))
        def _():
            start(cot_load(i + 1))

    def hidden_cut(i, lo, n):
        if True:
            cols = pl.ds(lo, n)
            dbuf[:, pl.ds(0, n)] = nt(cotc[...], w0[pl.ds(lo, n), :])

            def by_rows(b, _, cols=cols, n=n):
                some = pl.ds(pl.multiple_of(i * chunk + b * 16, 16), 16)
                dhid = dbuf[pl.ds(pl.multiple_of(b * 16, 16), 16), pl.ds(0, n)]
                gate = r[1, some, cols].astype(F32)
                up = r[2, some, cols].astype(F32)
                sig = jax.nn.sigmoid(gate)
                r[1, some, cols] = (dhid * up * sig * (1.0 + gate * (1.0 - sig))).astype(BF)
                r[2, some, cols] = (dhid * gate * sig).astype(BF)
                return 0

            lax.fori_loop(0, chunk // 16, by_rows, 0)

    def split_store(pair, value, keep, send):
        for side in (0, 1):
            part = value[:, side * local : (side + 1) * local]

            @pl.when(c == side)
            def _(part=part):
                keep[pair] = part

            @pl.when(c != side)
            def _(part=part):
                send[pair] = part.astype(BF)

    def stage_a(i):
        slot = lax.rem(i, 2)
        rows = rows_at(i)
        for pair in (0, 1):
            cols = pl.ds(pair * 2 * local, 2 * local)
            value = nn(r[1, rows, :], wg[:, cols]) + nn(r[2, rows, :], wu[:, cols])
            split_store(pair, value, ck, cs)
        remote(cs, cr.at[slot], c_sem, c_dev, slot).start()

        @pl.when(i == chunks - 1)
        def _():
            start(x_whole())

    def x_whole():
        copies = [load(x_in, wu.at[pl.ds(0, tokens), pl.ds(pl.multiple_of(me * local, 128), local)], l_sem.at[3, 0])]
        for step in range(1, 4):
            q = lax.rem(me + step, 4)
            cols = pl.ds(pl.multiple_of(q * local, 128), local)
            copies.append(load(x_h.at[q], wu.at[pl.ds(0, tokens), cols], l_sem.at[3, step]))
        return copies

    def stage_a1(i):
        @pl.when(i == 0)
        def _():
            wait(x_whole())

        at = pl.multiple_of(i * chunk, chunk)
        normed_to(lambda q, some: wu[pl.ds(at + some.start, 16), pl.ds(q * local, local)], 0)
        for q in range(4):
            cols = pl.ds(q * local, local)
            wg[cols, pl.ds(at, chunk)] = dhoc[:, cols].T

    def stage_loads(i):
        start(cot_load(i))
        h1_load(i).start()
        bcv_load(i).start()

    def stage_b(i):
        slot = lax.rem(i, 2)
        remote(cs, cr.at[slot], c_sem, c_dev, slot).wait()
        ys[slot] = (ck[...] + cr[slot].astype(F32)).astype(BF)
        remote(ys.at[slot], yr4.at[slot], y_sem, y_dev, slot).start()

    def stage_c(i):
        slot = lax.rem(i, 2)
        remote(ys.at[slot], yr4.at[slot], y_sem, y_dev, slot).wait()
        da2f[slot, :, c] = (ys[slot].astype(F32) + yr4[slot].astype(F32)).astype(BF)
        remote(da2f.at[slot, :, c], da2f.at[slot, :, c], f_sem, c_dev, slot).start()

    def stage_d(i):
        slot = lax.rem(i, 2)
        remote(da2f.at[slot, :, c], da2f.at[slot, :, c], f_sem, c_dev, slot).wait()
        wait(cot_load(i))
        h1_load(i).wait()
        bcv_load(i).wait()
        at = pl.multiple_of(i * chunk, chunk)
        own = pl.ds(pl.multiple_of(me * local, 128), local)

        def by_rows(b, _):
            some = pl.ds(pl.multiple_of(b * 16, 16), 16)
            ssq = jnp.zeros((16, local), F32)
            inner = jnp.zeros((16, local), F32)
            for q in range(4):
                cols = pl.ds(q * local, local)
                h1 = xc[q, some, :].astype(F32)
                ssq += h1 * h1
                inner += da2f[slot, q // 2, q % 2, some, :].astype(F32) * gain(1, q) * h1
            r2 = lax.rsqrt(jnp.sum(ssq, -1, keepdims=True) / width + EPS)
            scale = r2 * r2 * r2 * jnp.sum(inner, -1, keepdims=True) / width

            def grad(q, cols, da2):
                h1 = xc[q, some, :].astype(F32)
                return cotc[some, cols].astype(F32) + r2 * (da2 * gain(1, q)) - h1 * scale

            for q in range(4):
                cols = pl.ds(q * local, local)
                dhoc[some, cols] = grad(q, cols, da2f[slot, q // 2, q % 2, some, :].astype(F32)).astype(BF)
            da2 = da2f[slot, y, c, some, :].astype(F32)
            dh1s[i, some, :] = grad(me, own, da2)
            terms = da2 * xc[me, some, :].astype(F32) * r2
            small_v[pl.ds(8, 8), :] += terms[:8] + terms[8:]
            return 0

        lax.fori_loop(0, chunk // 16, by_rows, 0)
        start(x_load(i))
        transposed_to(0, i)
        dmixed = nt(dhoc[...], wo[...])
        c_gate = bcv[1]
        bxp[pl.ds(0, 8), :] = before_r[i]
        bxp[pl.ds(8, chunk), :] = bcv[3].astype(F32)
        conv, shifts = conv_of()
        r[0, pl.ds(at, chunk), pl.ds(0, local)] = (c_gate.astype(F32) * conv).astype(BF)
        r[0, pl.ds(at, chunk), pl.ds(2 * local, local)] = (dmixed * conv).astype(BF)
        dconv = (dmixed * c_gate.astype(F32)).astype(BF).astype(F32)
        dcp[pl.ds(0, chunk), :] = dconv
        halo_s[i] = dconv[:8]
        for k in range(3):
            small_v[1 + k : 2 + k, :] += jnp.sum(dconv * shifts[k], 0, keepdims=True)

        @pl.when(z > 0)
        def _():
            halo_copy(i).start()

    def halo_copy(i):
        return remote(halo_s.at[i], halo_r.at[i], halo_sem, dn_dev, i)

    def stage_e(i):
        slot = lax.rem(i, 2)

        @pl.when(i == 0)
        def _():
            for k in range(3):
                wi_load(k).wait()
            out_copy(chunks - 1).wait()

        wait(x_load(i))

        @pl.when(z > 0)
        def _():
            halo_copy(i).wait_send()

        @pl.when(z < last)
        def _():
            halo_copy(i).wait_recv()
            dcp[pl.ds(chunk, 8), :] = halo_r[i]

        @pl.when(z == last)
        def _():
            dcp[pl.ds(chunk, 8), :] = jnp.zeros((8, local), F32)

        dbx = sum(own_v[4 - k : 5 - k, :] * dcp[pl.ds(k, chunk), :] for k in range(3))
        rows = rows_at(i)
        r[0, rows, pl.ds(local, local)] = (dbx * bcv[2].astype(F32)).astype(BF)
        r[0, rows, pl.ds(3 * local, local)] = (dbx * bcv[0].astype(F32)).astype(BF)
        inner = jnp.zeros((chunk, 1), F32)
        ssq = jnp.zeros((chunk, 1), F32)
        for pair in (0, 1):
            cols = pl.ds(pair * 2 * local, 2 * local)
            value = nt(r[0, rows, pl.ds(local, 3 * local)], w0[cols, pl.ds(0, 3 * local)])
            for side in (0, 1):
                q = 2 * pair + side
                x = xc[q].astype(F32)
                part = value[:, side * local : (side + 1) * local]
                inner += jnp.sum(part * x * gain(0, q), -1, keepdims=True)
                ssq += jnp.sum(x * x, -1, keepdims=True)
            split_store(pair, value, ck2, cs2)
        xo[...] = xc[me]
        ins[...] = jnp.broadcast_to(inner, (chunk, 128)).T[:8]
        r1s[...] = jnp.broadcast_to(lax.rsqrt(ssq / width + EPS), r1s.shape)
        remote(cs2, yr4.at[2 + slot], c2_sem, c_dev, slot).start()
        remote(ins, inr.at[slot], i_sem, c_dev, slot).start()

        @pl.when(i + 1 < chunks)
        def _():
            stage_loads(i + 1)

    def stage_f(i):
        slot = lax.rem(i, 2)
        remote(cs2, yr4.at[2 + slot], c2_sem, c_dev, slot).wait()
        remote(ins, inr.at[slot], i_sem, c_dev, slot).wait()
        ys2[...] = (ck2[1 - y] + yr4[2 + slot, 1 - y].astype(F32)).astype(BF)
        qk2[...] = ck2[y] + yr4[2 + slot, y].astype(F32)
        iys[...] = ins[...] + inr[slot]
        remote(ys2, yr2.at[slot], y2_sem, y_dev, slot).start()
        remote(iys, iyr.at[slot], iy_sem, y_dev, slot).start()

    def gx_copy(i):
        return load(gxb, gx_h.at[rows_at(i), :], gx_sem)

    def stage_g(i):
        slot = lax.rem(i, 2)
        remote(ys2, yr2.at[slot], y2_sem, y_dev, slot).wait()
        remote(iys, iyr.at[slot], iy_sem, y_dev, slot).wait()
        da1 = qk2[...] + yr2[slot].astype(F32)
        inner = jnp.broadcast_to(iys[:1] + iyr[slot, :1], (128, chunk)).T[:, :1]
        r1 = r1s[:, :1]
        x = xo[...].astype(F32)
        scaled = gain(0, me)
        small_v[0:1, :] += jnp.sum(da1 * x * r1, 0, keepdims=True)

        @pl.when(i > 0)
        def _():
            gx_copy(i - 1).wait()

        gxb[...] = (dh1s[i] + r1 * scaled * da1 - x * (r1 * r1 * r1 * inner / width)).astype(BF)
        gx_copy(i).start()

    def out_start(i):
        rows = rows_at(i)
        for pair in (0, 1):
            cols = pl.ds(pair * 2 * local, 2 * local)
            split_store(pair, nn(r[0, rows, :], w0[:, cols]), ck2, cs2)
        remote(cs2, yr4.at[2 + lax.rem(i, 2)], c2_sem, c_dev, lax.rem(i, 2)).start()

        @pl.when(i == chunks - 1)
        def _():
            for k in range(3):
                wi_load(k).start()

    def out_share(i):
        slot = lax.rem(i, 2)
        remote(cs2, yr4.at[2 + slot], c2_sem, c_dev, slot).wait()
        ys2[...] = (ck2[1 - y] + yr4[2 + slot, 1 - y].astype(F32)).astype(BF)
        qk2[...] = ck2[y] + yr4[2 + slot, y].astype(F32)
        remote(ys2, yr2.at[slot], y2_sem, y_dev, slot).start()

    def out_copy(i):
        return load(gxb, out_h.at[rows_at(i), :], gx_sem)

    def out_end(i):
        slot = lax.rem(i, 2)
        remote(ys2, yr2.at[slot], y2_sem, y_dev, slot).wait()

        @pl.when(i > 0)
        def _():
            out_copy(i - 1).wait()

        gxb[...] = (dh1s[i] + (qk2[...] + yr2[slot].astype(F32))).astype(BF)
        out_copy(i).start()

    def valid(i, f):
        @pl.when(jnp.logical_and(i >= 0, i < chunks))
        def _():
            f(i)

    gather_pass(0, 0)
    gather_pass(2, 0)
    for k in range(3):
        wi_load(k).wait()
    wo_load.wait()
    gather_end(2, 0)

    def forward(j, _):
        @pl.when(j < chunks)
        def _():
            project(j)

            @pl.when(j + 1 < chunks)
            def _():
                gather_pass(0, j + 1)

            mix(j)

        @pl.when(j == chunks - 1)
        def _():
            wd_load.start()

        @pl.when(j >= 2)
        def _():
            residual(j - 2)

        @pl.when(j < chunks)
        def _():
            share(j)

        @pl.when(j < chunks - 2)
        def _():
            gather_start(1, j)

        @pl.when(j == chunks - 1)
        def _():
            gather_start(1, chunks - 2)
            gather_start(1, chunks - 1)

        @pl.when(j == 2)
        def _():
            wg_load.wait()
            wu_load.wait()

        @pl.when(j >= 2)
        def _():
            gather_pass(1, j - 2)
            feed(j - 2)

        @pl.when(j >= 3)
        def _():
            cot_turn(j - 3)

        return 0

    lax.fori_loop(0, chunks + 2, forward, 0)
    bcv_store(chunks - 1).wait()
    for pair in (0, 1):
        for core in (0, 1):
            h1_store(chunks - 1, (chunks - 1) % 2, pair, core).wait()

    cot_turn(chunks - 1)
    start(cot_load(0))

    def small_x():
        return pltpu.make_async_remote_copy(
            src_ref=small_v.at[pl.ds(0, 8)], dst_ref=small_r.at[0], send_sem=small_sem.at[0, 0],
            recv_sem=small_sem.at[0, 1], device_id=x_dev, device_id_type=MESH,
        )

    def small_z(way):
        return pltpu.make_async_remote_copy(
            src_ref=small_r.at[1 + way], dst_ref=small_r.at[3 + way], send_sem=small_sem.at[1 + way, 0],
            recv_sem=small_sem.at[1 + way, 1], device_id=dn_dev if way else up_dev, device_id_type=MESH,
        )

    def small_step(k):
        @pl.when(k == 0)
        def _():
            small_x().wait()
            total = small_v[pl.ds(0, 8), :] + small_r[0]
            small_v[pl.ds(0, 8), :] = total
            small_r[1] = total
            small_r[2] = total

        for way in (0, 1):
            turn = last - z if way else z

            @pl.when(jnp.logical_and(turn < last, k == turn))
            def _(way=way, turn=turn):
                @pl.when(turn > 0)
                def _():
                    small_z(way).wait_recv()
                    small_r[1 + way] = small_v[pl.ds(0, 8), :] + small_r[3 + way]

                small_z(way).start()

    def small_end():
        for way in (0, 1):
            turn = last - z if way else z

            @pl.when(turn < last)
            def _(way=way):
                small_z(way).wait_send()

            @pl.when(turn == last)
            def _(way=way):
                small_z(way).wait_recv()

            @pl.when(turn > 0)
            def _(way=way):
                small_v[pl.ds(0, 8), :] += small_r[3 + way]

    def stage_last(i):
        stage_g(i)

        @pl.when(i == chunks - 1)
        def _():
            small_v[4:5, :] = jnp.sum(small_v[8:16, :], 0, keepdims=True)
            small_x().start()

    order = (
        ("g", stage_last), ("out_end", out_end), ("out_share", out_share), ("b", stage_b), ("f", stage_f),
        ("c", stage_c), ("e", stage_e), ("d", stage_d), ("out_start", out_start), ("a", stage_a),
        ("hidden", None), ("a1", stage_a1),
    )

    def stages(t, third):
        for name, f in order:
            if name == "hidden":
                if HIDDEN[0] != third:
                    continue
                done = 0
                low = high = 0
                for at, upto in HIDDEN[1].items():
                    low = jnp.where(t == at, done, low)
                    high = jnp.where(t == at, upto, high)
                    done = upto

                def piece(k, _):
                    hidden_back(k)
                    return 0

                lax.fori_loop(low, high, piece, 0)
            elif PLACES[name][0] == third:
                where = PLACES[name][1]
                i = sum(jnp.where(t >= at, 1, 0) for at in where[1:])
                now = functools.reduce(jnp.logical_or, [t == at for at in where])
                pl.when(now)(functools.partial(f, i))

    def each_tick(t, _):
        tick_a(t, True)

        @pl.when(t == 0)
        def _():
            wd_load.wait()

        @pl.when(t == beat)
        def _():
            stage_loads(0)

        stages(t, 0)
        tick_b(t)
        stages(t, 1)
        tick_c(t)
        stages(t, 2)

        @pl.when(t > PLACES["g"][1][-1])
        def _():
            small_step(t - PLACES["g"][1][-1] - 1)

        return 0

    lax.fori_loop(0, ticks, each_tick, 0)
    gx_copy(chunks - 1).wait()

    def part_four(k, _):
        tick_a(ticks + k)
        tick_b(ticks + k)
        tick_c(ticks + k)
        return 0

    lax.fori_loop(0, LAG + 4, part_four, 0)
    small_end()
    plain_out(ticks - 2, "wait")
    plain_out(ticks - 1, "wait")
    out_do(ob.at[2], 3 * beat + SECOND, 2, "wait")


def block(dims, x_own, cot_own, own, wd, wg, wu, wo, wi):
    tokens, chunk, width, ff, local, nseq = dims
    rows = width // (2 * nseq)
    chunks = tokens // chunk
    last = nseq - 1
    m = ROWS * nseq
    DMA = pltpu.SemaphoreType.DMA
    shape = jax.ShapeDtypeStruct
    third = ff // 3 // 128 * 128
    scratch = [
        pltpu.VMEM((2, width, tokens), BF),
        pltpu.VMEM((3, tokens, ff), BF),
        pltpu.VMEM((ff, width), BF),
        pltpu.VMEM((ff, width), BF),
        pltpu.VMEM((ff, width), BF),
        pltpu.VMEM((local, width), BF),
        pltpu.VMEM((chunk, width), BF),
        pltpu.VMEM((4, chunk, local), BF),
        pltpu.VMEM((chunk, local), BF),
        pltpu.VMEM((4, chunk, local), BF),
        pltpu.VMEM((8 + chunk, local), F32),
        pltpu.VMEM((chunk, ff - 2 * third), F32),
        pltpu.VMEM((8 + chunk, local), F32),
        pltpu.VMEM((chunk, width), BF),
        pltpu.VMEM((chunks, chunk, local), F32),
        pltpu.VMEM((chunk, 128), F32),
        pltpu.VMEM((4, 8, local), F32),
        pltpu.VMEM((3, m, ff), BF),
        pltpu.VMEM((5, m, ff), BF),
        pltpu.VMEM((LAG + 4, m, ff), BF),
        pltpu.VMEM((2, 2 * last, ROWS, ff), BF),
        pltpu.VMEM((2, 3 * last + 2, ROWS, ff), BF),
        pltpu.VMEM((3, ROWS, ff), BF),
        pltpu.VMEM((ROWS, ff), BF),
        pltpu.VMEM((ROWS, ff), BF),
        pltpu.VMEM((ROWS, ff), F32),
        pltpu.VMEM((6, chunk, local), F32),
        pltpu.VMEM((2, chunk, local), BF),
        pltpu.VMEM((2, 2, chunk, local), BF),
        pltpu.VMEM((2, 2, chunk, local), BF),
        pltpu.VMEM((4, 2, chunk, local), BF),
        pltpu.VMEM((2, 2, 2, chunk, local), BF),
        pltpu.VMEM((2, chunk, local), BF),
        pltpu.VMEM((chunk, local), BF),
        pltpu.VMEM((2, chunk, local), BF),
        pltpu.VMEM((8, chunk), F32),
        pltpu.VMEM((2, 8, chunk), F32),
        pltpu.VMEM((8, chunk), F32),
        pltpu.VMEM((2, 8, chunk), F32),
        pltpu.VMEM((chunk, local), BF),
        pltpu.VMEM((chunks, 8, local), F32),
        pltpu.VMEM((chunks, 8, local), F32),
        pltpu.VMEM((chunks, 8, local), F32),
        pltpu.VMEM((chunks, 8, local), F32),
        pltpu.VMEM((5, 8, local), F32),
        DMA((3,)), DMA((5,)), DMA((2, 2 * last)), DMA((2, 3 * last + 2)), DMA((3, 4)),
        DMA((2, 2)), DMA((2, chunks)), DMA((2, 2)), DMA((2, 2)), DMA((2, 2)),
        DMA((2, 2)), DMA((2, 2)), DMA((2, chunks)), DMA((2, chunks)), DMA((3, 2, 3, chunks)),
        DMA((7,)), DMA((4, 4)), DMA(()), DMA((2, 2)), DMA(()), DMA((3, 2)), DMA((2,)),
    ]
    return pl.pallas_call(
        functools.partial(block_kernel, dims),
        out_shape=(
            shape((rows, ff), BF), shape((rows, ff), BF), shape((rows, ff), BF),
            shape((rows, local), BF), shape((3, rows, local), BF),
            shape((tokens, local), BF), shape((tokens, local), BF), shape((16, local), F32),
            shape((4, tokens, local), BF), shape((4, tokens, local), BF),
            shape((4, tokens, local), BF), shape((4, tokens, local), BF),
        ),
        in_specs=[ANY, ANY, VMEM] + [ANY] * 5,
        out_specs=(ANY,) * 7 + (VMEM,) + (ANY,) * 4,
        scratch_shapes=scratch,
        compiler_params=pltpu.CompilerParams(
            collective_id=0, has_side_effects=True, vmem_limit_bytes=63 * 2**20
        ),
    )(x_own, cot_own, own, wd, wg, wu, wo, wi)


def shifted(array, axis, by):
    count = lax.axis_size(axis)
    pairs = [(i, i + by) for i in range(count) if 0 <= i + by < count]
    return lax.ppermute(array, axis, pairs)


def fused_device(inputs, gain_mix, w_in, kernel, w_out, gain_ff, w_gate, w_up, w_down, cotangent):
    groups, seq_rows, local = inputs.shape
    width = local * lax.axis_size("mp")
    ff = w_down.shape[0]
    tokens = groups * seq_rows
    dims = (tokens, seq_rows, width, ff, local, lax.axis_size("seq"))
    own = jnp.concatenate(
        [gain_mix[None], gain_ff[None], kernel, jnp.zeros((3, local), BF)], 0
    ).astype(F32)
    gdown, ggate, gup, gout, gin, gx, out, small = block(
        dims, inputs.reshape(tokens, local), cotangent.reshape(tokens, local), own,
        w_down, w_gate.T, w_up.T, w_out, w_in.transpose(1, 0, 2),
    )[:8]
    whole = (groups, seq_rows, local)
    return (
        out.reshape(whole), gx.reshape(whole), small[0], gin.transpose(1, 0, 2).astype(F32), small[1:4],
        gout.T.astype(F32), small[4], ggate.astype(F32), gup.astype(F32), gdown.T.astype(F32),
    )


def contract_rows(left, right):
    return lax.dot_general(
        left, right, (((0,), (0,)), ((), ())), preferred_element_type=jnp.float32
    )


def contract_cols(left, right):
    return lax.dot_general(
        left, right, (((1,), (1,)), ((), ())), preferred_element_type=jnp.float32
    )


def plain_device(inputs, gain_mix, w_in, kernel, w_out, gain_ff, w_gate, w_up, w_down, cotangent):
    groups, seq_rows, local_width = inputs.shape
    full_width = local_width * lax.axis_size("mp")
    tokens = groups * seq_rows
    x_float = inputs.reshape(tokens, local_width).astype(jnp.float32)
    gain_one = gain_mix.astype(jnp.float32)
    gain_two = gain_ff.astype(jnp.float32)
    taps = kernel.astype(jnp.float32)

    def row_total(values):
        return lax.psum(jnp.sum(values, axis=-1, keepdims=True), "mp")

    def all_features(values):
        return lax.all_gather(values, "mp", axis=1, tiled=True)

    def share_sums(values):
        return lax.psum_scatter(
            values.astype(jnp.bfloat16), "mp", scatter_dimension=1, tiled=True
        ).astype(jnp.float32)

    def scattered(values, dim):
        return lax.psum_scatter(
            values.astype(jnp.bfloat16), ("dp", "seq"), scatter_dimension=dim, tiled=True
        ).astype(jnp.float32)

    def norm_scale(values):
        return lax.rsqrt(row_total(values * values) / full_width + EPS)

    def norm_back(values, scale, gain_vec, upstream):
        inner = row_total(gain_vec * upstream * values)
        grad_values = scale * gain_vec * upstream - values * scale**3 * inner / full_width
        return (grad_values, jnp.sum(upstream * values * scale, axis=0))

    scale_one = norm_scale(x_float)
    normed_in = all_features((x_float * scale_one * gain_one).astype(jnp.bfloat16))
    proj = jnp.einsum("td,dkc->tkc", normed_in, w_in, preferred_element_type=jnp.float32)
    b_gate = proj[:, 0]
    c_gate = proj[:, 1]
    values_v = proj[:, 2]
    b_times_x = (b_gate * values_v).astype(jnp.bfloat16).reshape(groups, seq_rows, local_width)
    before = shifted(b_times_x[:, seq_rows - 2 :], "seq", 1)
    padded = jnp.concatenate([before, b_times_x], 1).astype(jnp.float32)
    conv = taps[0] * padded[:, :-2] + taps[1] * padded[:, 1:-1] + taps[2] * padded[:, 2:]
    conv = conv.reshape(tokens, local_width)
    mixed = (c_gate * conv).astype(jnp.bfloat16)
    hidden_one = x_float + share_sums(jnp.dot(mixed, w_out, preferred_element_type=jnp.float32))
    scale_two = norm_scale(hidden_one)
    normed_ff = all_features((hidden_one * scale_two * gain_two).astype(jnp.bfloat16))
    gate = jnp.dot(normed_ff, w_gate, preferred_element_type=jnp.float32)
    up_proj = jnp.dot(normed_ff, w_up, preferred_element_type=jnp.float32)
    sigma = jax.nn.sigmoid(gate)
    active = gate * sigma
    hidden = (active * up_proj).astype(jnp.bfloat16)
    ffn_out = share_sums(jnp.dot(hidden, w_down, preferred_element_type=jnp.float32))
    block_out = (hidden_one + ffn_out).astype(jnp.bfloat16).reshape(groups, seq_rows, local_width)
    grad_flat = cotangent.reshape(tokens, local_width)
    grad_full = all_features(grad_flat)
    grad_down = contract_rows(hidden, grad_full)
    grad_hidden = contract_cols(grad_full, w_down)
    grad_gate_act = (grad_hidden * up_proj * sigma * (1.0 + gate * (1.0 - sigma))).astype(
        jnp.bfloat16
    )
    grad_up_act = (grad_hidden * active).astype(jnp.bfloat16)
    grad_gate = contract_rows(normed_ff, grad_gate_act)
    grad_up = contract_rows(normed_ff, grad_up_act)
    grad_normed_ff = share_sums(
        contract_cols(grad_gate_act, w_gate) + contract_cols(grad_up_act, w_up)
    )
    grad_norm_two, grad_gain_two = norm_back(hidden_one, scale_two, gain_two, grad_normed_ff)
    grad_hidden_one = grad_flat.astype(jnp.float32) + grad_norm_two
    grad_out_full = all_features(grad_hidden_one.astype(jnp.bfloat16))
    grad_out = contract_rows(mixed, grad_out_full)
    grad_mixed = contract_cols(grad_out_full, w_out)
    grad_c = grad_mixed * conv
    grad_conv = (grad_mixed * c_gate).astype(jnp.bfloat16).reshape(groups, seq_rows, local_width)
    after = shifted(grad_conv[:, :2], "seq", -1)
    extended = jnp.concatenate([grad_conv, after], 1).astype(jnp.float32)
    grad_bx = taps[2] * extended[:, :-2] + taps[1] * extended[:, 1:-1] + taps[0] * extended[:, 2:]
    grad_bx = grad_bx.reshape(tokens, local_width)
    conv_grad_float = extended[:, :-2]
    grad_taps = jnp.stack(
        [
            jnp.sum(conv_grad_float * padded[:, :-2], axis=(0, 1)),
            jnp.sum(conv_grad_float * padded[:, 1:-1], axis=(0, 1)),
            jnp.sum(conv_grad_float * padded[:, 2:], axis=(0, 1)),
        ]
    )
    grad_proj = jnp.stack([grad_bx * values_v, grad_c, grad_bx * b_gate], 1).astype(jnp.bfloat16)
    grad_in = jnp.einsum("td,tkc->dkc", normed_in, grad_proj, preferred_element_type=jnp.float32)
    grad_normed_in = share_sums(
        jnp.einsum("tkc,dkc->td", grad_proj, w_in, preferred_element_type=jnp.float32)
    )
    grad_norm_one, grad_gain_one = norm_back(x_float, scale_one, gain_one, grad_normed_in)
    grad_input = (
        (grad_hidden_one + grad_norm_one)
        .astype(jnp.bfloat16)
        .reshape(groups, seq_rows, local_width)
    )
    small_sums = lax.psum((grad_gain_one, grad_taps, grad_gain_two), ("dp", "seq"))
    by_row = (
        scattered(grad_in, 0),
        scattered(grad_gate, 0),
        scattered(grad_up, 0),
    )
    by_col = (
        scattered(grad_out, 1),
        scattered(grad_down, 1),
    )
    return (
        block_out,
        grad_input,
        small_sums[0],
        by_row[0],
        small_sums[1],
        by_col[0],
        small_sums[2],
        by_row[1],
        by_row[2],
        by_col[1],
    )


def solution(mesh):
    placed = (
        P("dp", "seq", "mp"),
        P("mp"),
        P(None, None, "mp"),
        P(None, "mp"),
        P("mp", None),
        P("mp"),
        P(None, "mp"),
        P(None, "mp"),
        P("mp", None),
        P("dp", "seq", "mp"),
    )
    sizes = mesh.shape
    fused = sizes["dp"] == 2 and sizes["seq"] == 4 and sizes["mp"] == 4
    return jax.shard_map(
        fused_device if fused else plain_device,
        mesh=mesh,
        in_specs=placed,
        out_specs=(
            P("dp", "seq", "mp"),
            P("dp", "seq", "mp"),
            P("mp"),
            P(("dp", "seq"), None, "mp"),
            P(None, "mp"),
            P("mp", ("dp", "seq")),
            P("mp"),
            P(("dp", "seq"), "mp"),
            P(("dp", "seq"), "mp"),
            P("mp", ("dp", "seq")),
        ),
        check_vma=False,
    )
```

```python
import functools

import jax
import jax.numpy as jnp
from jax import lax
from jax.experimental import pallas as pl
from jax.experimental.pallas import tpu as pltpu
from jax.sharding import PartitionSpec as P

EPS = 1e-05
MESH = pl.DeviceIdType.MESH
BF = jnp.bfloat16
F32 = jnp.float32
ROWS = 32
SECOND = 3
LAG = 3
WAIT = 3
PLACES = {
    "out_start": (2, (1, 4, 7, 8)),
    "out_share": (2, (2, 5, 8, 10)),
    "out_end": (1, (4, 7, 9, 12)),
    "a": (2, (3, 8, 10, 14)),
    "b": (2, (4, 9, 12, 15)),
    "c": (1, (8, 11, 14, 18)),
    "d": (2, (9, 13, 17, 19)),
    "e": (2, (12, 15, 18, 20)),
    "f": (2, (14, 16, 19, 21)),
    "g": (2, (15, 18, 20, 22)),
    "a1": (2, (15, 16, 17, 19)),
}
HIDDEN = (1, {2: 3, 3: 4, 4: 5, 5: 7, 6: 12})
ANY = pl.BlockSpec(memory_space=pl.ANY)
VMEM = pl.BlockSpec(memory_space=pltpu.VMEM)


def nn(left, right):
    return lax.dot_general(left, right, (((1,), (0,)), ((), ())), preferred_element_type=F32)


def nt(left, right):
    return lax.dot_general(left, right, (((1,), (1,)), ((), ())), preferred_element_type=F32)


def block_kernel(
    dims,
    x_in, cot_in, gain_mix_v, gain_ff_v, taps_v, wd_h, wg_h, wu_h, wo_h, wi_h,
    gdown_h, ggate_h, gup_h, gout_h, gin_h, gx_h, out_h, small_v,
    x_h, cot_h, h1_h, bcv_h,
    lt, r, w0, wg, wu, wo, cotc, xc, xo, bcv, bxp, dbuf, dcp, dhoc, dh1s, r1s, gv, own_v,
    xs, xr, s_buf, zs, zr, ob, vs, vr, vk,
    kf, cs, cr, ys, yr4, da2f, cs2, ys2, yr2,
    ins, inr, iys, iyr, gxb, halo_s, halo_r, before_s, before_r, small_r,
    xs_sem, xr_sem, zs_sem, zr_sem, ob_sem, c_sem, y_sem, f_sem, c2_sem, y2_sem,
    i_sem, iy_sem, halo_sem, before_sem, gather_sem, w_sem, l_sem, bcv_sem, h1_sem, gx_sem,
    small_sem, v_sem,
):
    tokens, chunk, width, ff, local, nseq = dims
    chunks = tokens // chunk
    block = width // (2 * nseq)
    per = block // ROWS
    beat = per + 1
    ticks = 4 * beat
    p = lax.axis_index("dp")
    z = lax.axis_index("seq")
    me = lax.axis_index("mp")
    y, c = me // 2, me % 2
    x_dev = {"dp": 1 - p}
    up_dev = {"seq": z + 1}
    dn_dev = {"seq": z - 1}
    y_dev = {"mp": (1 - y) * 2 + c}
    c_dev = {"mp": y * 2 + 1 - c}
    last = nseq - 1
    ck, ck2, qk2 = kf.at[pl.ds(0, 2)], kf.at[pl.ds(2, 2)], kf.at[4]
    third = ff // 3 // 128 * 128
    cuts = ((0, third), (third, third), (2 * third, ff - 2 * third))

    def remote(src, dst, sems, where, at=None):
        s_sem, r_sem = (sems.at[0], sems.at[1]) if at is None else (sems.at[0, at], sems.at[1, at])
        return pltpu.make_async_remote_copy(
            src_ref=src, dst_ref=dst, send_sem=s_sem, recv_sem=r_sem,
            device_id=where, device_id_type=MESH,
        )

    def load(src, dst, sem):
        return pltpu.make_async_copy(src, dst, sem)

    def wi_load(k):
        return load(wi_h.at[k], w0.at[pl.ds(0, width), pl.ds(k * local, local)], w_sem.at[k])

    wd_load = load(wd_h, w0, w_sem.at[3])
    wg_load = load(wg_h, wg, w_sem.at[4])
    wu_load = load(wu_h, wu, w_sem.at[5])
    wo_load = load(wo_h, wo, w_sem.at[6])
    for k in range(3):
        wi_load(k).start()
    wo_load.start()
    own_v[0:1, :] = gain_mix_v[...].astype(F32).reshape(1, local)
    own_v[1:2, :] = gain_ff_v[...].astype(F32).reshape(1, local)
    own_v[2:5, :] = taps_v[...].astype(F32)
    own_v[5:8, :] = jnp.zeros((3, local), F32)
    gv[me] = own_v[...]

    barrier = pltpu.get_barrier_semaphore()
    for dev in (x_dev, y_dev, c_dev):
        pl.semaphore_signal(barrier, inc=1, device_id=dev, device_id_type=MESH)

    @pl.when(z < last)
    def _():
        pl.semaphore_signal(barrier, inc=1, device_id=up_dev, device_id_type=MESH)

    @pl.when(z > 0)
    def _():
        pl.semaphore_signal(barrier, inc=1, device_id=dn_dev, device_id_type=MESH)

    peers = 3 + jnp.where(z < last, 1, 0) + jnp.where(z > 0, 1, 0)
    pl.semaphore_wait(barrier, peers)

    small_v[...] = jnp.zeros_like(small_v)

    def rows_at(i):
        return pl.ds(pl.multiple_of(i * chunk, chunk), chunk)

    def gather(which, i, leg):
        if which == 2:
            src = mine = own_v
            dst = gv
            at = (2, 0)
        else:
            src, dst = (x_in, x_h) if which == 0 else (cot_in, cot_h)
            mine = src.at[rows_at(i), :]
            at = (which, i)
        slot = (lambda q: dst.at[q]) if which == 2 else (lambda q: dst.at[q, rows_at(i), :])
        sems = [gather_sem.at[leg, way, at[0], at[1]] for way in (0, 1)]
        if leg == 0:
            pair, where = (mine, slot(me)), y_dev
        elif leg == 1:
            pair, where = (mine, slot(me)), c_dev
        else:
            from_y = (1 - y) * 2 + c
            pair, where = (slot(from_y), slot(from_y)), c_dev
        return pltpu.make_async_remote_copy(
            src_ref=pair[0], dst_ref=pair[1], send_sem=sems[0], recv_sem=sems[1],
            device_id=where, device_id_type=MESH,
        )

    def gather_start(which, i):
        gather(which, i, 0).start()
        gather(which, i, 1).start()

    def gather_pass(which, i):
        gather(which, i, 0).wait_recv()
        gather(which, i, 2).start()

    def gather_end(which, i):
        gather(which, i, 0).wait_send()
        gather(which, i, 1).wait()
        gather(which, i, 2).wait()

    for i in range(chunks):
        gather_start(0, i)
        if i == 0:
            gather_start(2, 0)
    wg_load.start()
    wu_load.start()

    def on_size(t, f):
        pl.when(t // beat < 3)(lambda: f(pl.ds(0, ff)))
        pl.when(t // beat == 3)(lambda: f(pl.ds(0, 4 * local)))

    def place(t):
        return lax.rem(t, beat)

    def is_first(t):
        return place(t) == 0

    def is_second(t):
        return place(t) == SECOND

    def is_plain(t):
        return jnp.logical_and(place(t) != 0, place(t) != SECOND)

    def row_block(t):
        plain = place(t) - jnp.where(place(t) > SECOND, 2, 1)
        return jnp.where(is_plain(t), plain, per - 1)

    def x_number(t):
        return t // beat * (per - 1) + row_block(t)

    def x_do(t, what):
        n = x_number(t)

        def f(cols):
            copy = pltpu.make_async_remote_copy(
                src_ref=xs.at[lax.rem(n, 3), :, cols], dst_ref=xr.at[lax.rem(n, 5), :, cols],
                send_sem=xs_sem.at[lax.rem(n, 3)], recv_sem=xr_sem.at[lax.rem(n, 5)],
                device_id=x_dev, device_id_type=MESH,
            )
            getattr(copy, what)()

        on_size(t, f)

    def v_do(t, what):
        def f(cols):
            copy = pltpu.make_async_remote_copy(
                src_ref=vs.at[:, cols], dst_ref=vr.at[:, cols], send_sem=v_sem.at[0], recv_sem=v_sem.at[1],
                device_id=x_dev, device_id_type=MESH,
            )
            getattr(copy, what)()

        on_size(t, f)

    def zs_at(t, step):
        return 2 * step + lax.rem(t, 2)

    def zr_at(t, step):
        count = 3 if 0 < step < last - 1 else 4
        return 3 * step + min(step, 1) + lax.rem(t, count)

    def z_do(t, way, step, what):
        def f(cols):
            copy = pltpu.make_async_remote_copy(
                src_ref=zs.at[way, zs_at(t, step), :, cols], dst_ref=zr.at[way, zr_at(t, step), :, cols],
                send_sem=zs_sem.at[way, zs_at(t, step)], recv_sem=zr_sem.at[way, zr_at(t, step)],
                device_id=dn_dev if way else up_dev, device_id_type=MESH,
            )
            getattr(copy, what)()

        on_size(t, f)

    def receives(way, step):
        if way:
            return jnp.logical_and(z < last, z >= last - 1 - step)
        return jnp.logical_and(z > 0, z <= step + 1)

    def can_send(way, step):
        if way:
            return jnp.logical_and(z > 0, z >= last - step)
        return jnp.logical_and(z < last, z <= step)

    def z_arrived(t, step):
        for way in (0, 1):
            @pl.when(receives(way, step))
            def _(way=way):
                z_do(t, way, step, "wait_recv")

            @pl.when(can_send(way, step))
            def _(way=way):
                z_do(t, way, step, "wait_send")

    def z_step(t, step):
        sl = lax.rem(t, LAG + 4)
        if step > 0:
            z_arrived(t, step - 1)
        for way in (0, 1):
            quarter = z - last + step if way else last - step + z
            fresh = can_send(way, step)
            if step > 0:
                @pl.when(jnp.logical_and(receives(way, step - 1), can_send(way, step)))
                def _(way=way, quarter=quarter):
                    value = s_buf[sl, pl.ds(quarter * ROWS, ROWS), :].astype(F32) + zr[
                        way, zr_at(t, step - 1)
                    ].astype(F32)
                    zs[way, zs_at(t, step)] = value.astype(BF)

                fresh = jnp.logical_and(fresh, jnp.logical_not(receives(way, step - 1)))

            @pl.when(fresh)
            def _(way=way, quarter=quarter):
                zs[way, zs_at(t, step)] = s_buf[sl, pl.ds(quarter * ROWS, ROWS), :]

        for way in (0, 1):
            @pl.when(can_send(way, step))
            def _(way=way):
                z_do(t, way, step, "start")

    def compute(t, kind):
        sl = lax.rem(t, LAG + 4)
        at = row_block(t) * ROWS
        m = ROWS * nseq

        def rows_of(index, half):
            rows = [pl.ds(pl.multiple_of((half * nseq + s) * block + at, ROWS), ROWS) for s in range(nseq)]
            if kind == 3 and index == 1:
                return [wg[some, pl.ds(0, tokens)] for some in rows]
            return [lt[index, some, :] for some in rows]

        if kind == 3:
            parts = [(0, 0, 0, local)] + [(1, 0, k * local, local) for k in (1, 2, 3)]
        elif kind == 0:
            parts = [(0, 0, lo, n) for lo, n in cuts]
        else:
            parts = [(1, t // beat, lo, n) for lo, n in cuts]

        @pl.when(is_plain(t))
        def _():
            slot = lax.rem(x_number(t), 3)
            left = [jnp.concatenate(rows_of(i, 1 - p) + rows_of(i, p), 0) for i in sorted({q[0] for q in parts})]
            for i, ri, lo, n in parts:
                cols = pl.ds(lo, n)
                out = nn(left[i if len(left) == 2 else 0], r[ri, :, cols])
                xs[slot, :, cols] = out[:m].astype(BF)
                s_buf[sl, :, cols] = out[m:].astype(BF)
            x_do(t, "start")

        @pl.when(jnp.logical_not(is_plain(t)))
        def _():
            half = jnp.where(is_first(t), p, 1 - p)
            left = [jnp.concatenate(rows_of(i, half), 0) for i in sorted({q[0] for q in parts})]
            for i, ri, lo, n in parts:
                cols = pl.ds(lo, n)
                s_buf[sl, :, cols] = nn(left[i if len(left) == 2 else 0], r[ri, :, cols]).astype(BF)

    def out_do(src, t, sems, what):
        rows = pl.ds(pl.multiple_of(row_block(t) * ROWS, ROWS), ROWS)
        for g, target in enumerate((gdown_h, ggate_h, gup_h)):
            @pl.when(t // beat == g)
            def _(target=target):
                getattr(load(src, target.at[rows, :], ob_sem.at[sems, 0]), what)()

        @pl.when(t // beat == 3)
        def _():
            getattr(load(src.at[:, pl.ds(0, local)], gout_h.at[rows, :], ob_sem.at[sems, 0]), what)()
            for k in range(3):
                part = src.at[:, pl.ds((k + 1) * local, local)]
                getattr(load(part, gin_h.at[k, rows, :], ob_sem.at[sems, 1 + k]), what)()

    def plain_out(t, what):
        slot = lax.rem(x_number(t), 2)
        out_do(ob.at[slot], t, slot, what)

    def finish(t):
        sl = lax.rem(t, LAG + 4)
        z_arrived(t, last - 1)

        def total(then):
            def end(ways):
                value = s_buf[sl, pl.ds(z * ROWS, ROWS), :].astype(F32)
                for way in ways:
                    value += zr[way, zr_at(t, last - 1)].astype(F32)
                then(value)

            pl.when(z == 0)(lambda: end((1,)))
            pl.when(z == last)(lambda: end((0,)))
            pl.when(jnp.logical_and(z > 0, z < last))(lambda: end((0, 1)))

        @pl.when(is_plain(t))
        def _():
            n = x_number(t)
            before = t - jnp.where(place(t) == per, 2, 3)

            @pl.when(n >= 2)
            def _():
                plain_out(before, "wait")

            def put(value):
                ob[lax.rem(n, 2)] = value.astype(BF)

            total(put)
            plain_out(t, "start")

        @pl.when(is_first(t))
        def _():
            def put(value):
                vk[...] = value

            total(put)

        @pl.when(is_second(t))
        def _():
            def put(value):
                vs[...] = value.astype(BF)

            total(put)
            v_do(t, "start")

    def v_end(t):
        @pl.when(is_second(t))
        def _():
            v_do(t, "wait")

            @pl.when(t >= beat)
            def _():
                out_do(ob.at[2], t - beat, 2, "wait")

            ob[2] = (vk[...] + vr[...].astype(F32)).astype(BF)
            out_do(ob.at[2], t, 2, "start")

    def within(t, f):
        @pl.when(jnp.logical_and(t >= 0, t < ticks))
        def _():
            f(t)

    def tick_a(t, full=False):
        within(t - LAG - 4 - WAIT, v_end)
        within(t - LAG - 4, finish)

        def x_in(u):
            @pl.when(is_plain(u))
            def _():
                x_do(u, "wait")
                sl = lax.rem(u, LAG + 4)
                arrived = xr[lax.rem(x_number(u), 5)].astype(F32)
                s_buf[sl] = (s_buf[sl].astype(F32) + arrived).astype(BF)

            z_step(u, 0)

        within(t - LAG, x_in)
        if full:
            pl.when(t // beat == 0)(lambda: compute(t, 0))
            pl.when(jnp.logical_and(t // beat > 0, t // beat < 3))(lambda: compute(t, 1))
            pl.when(t // beat == 3)(lambda: compute(t, 3))

    def tick_b(t):
        within(t - LAG - 1, lambda u: z_step(u, 1))

    def tick_c(t):
        within(t - LAG - 2, lambda u: z_step(u, 2))

    def in_slices(own, others, to, slot):
        copies = [load(own, to(me), l_sem.at[slot, 0])]
        for step in range(1, 4):
            q = lax.rem(me + step, 4)
            copies.append(load(others(q), to(q), l_sem.at[slot, step]))
        return copies

    def cot_load(i):
        return in_slices(
            cot_in.at[rows_at(i), :],
            lambda q: cot_h.at[q, rows_at(i), :],
            lambda q: cotc.at[:, pl.ds(pl.multiple_of(q * local, 128), local)],
            0,
        )

    def x_load(i):
        return in_slices(x_in.at[rows_at(i), :], lambda q: x_h.at[q, rows_at(i), :], lambda q: xc.at[q], 1)

    def start(copies):
        for one in copies:
            one.start()

    def wait(copies):
        for one in copies:
            one.wait()

    def h1_load(i):
        return load(h1_h.at[:, rows_at(i), :], xc, l_sem.at[2, 0])

    def bcv_load(i):
        return load(bcv_h.at[:, rows_at(i), :], bcv, l_sem.at[2, 1])

    def gain(row, q):
        return gv[q, row : row + 1, :]

    def by_sixteen(f):
        def body(b, _):
            f(pl.ds(pl.multiple_of(b * 16, 16), 16))
            return 0

        lax.fori_loop(0, chunk // 16, body, 0)

    def normed_to(src, row, after=None):
        def f(some):
            ssq = jnp.zeros((16, local), F32)
            for q in range(4):
                values = src(q, some).astype(F32)
                ssq += values * values
            scale = lax.rsqrt(jnp.sum(ssq, -1, keepdims=True) / width + EPS)
            for q in range(4):
                dhoc[some, pl.ds(q * local, local)] = (src(q, some).astype(F32) * scale * gain(row, q)).astype(BF)

        by_sixteen(f)

    def transposed_to(index, i):
        at = pl.multiple_of(i * chunk, chunk)
        for q in range(4):
            cols = pl.ds(q * local, local)
            lt[index, cols, pl.ds(at, chunk)] = dhoc[:, cols].T

    def before_copy(i):
        return remote(before_s.at[i], before_r.at[i], before_sem, up_dev, i)

    def bcv_store(i):
        return load(bcv, bcv_h.at[:, rows_at(i), :], bcv_sem)

    def h1_store(i, slot, pair, core):
        return load(da2f.at[slot, pair, core], h1_h.at[2 * pair + core, rows_at(i), :], h1_sem.at[pair, core])

    def project(i):
        gather_end(0, i)
        start(x_load(i))
        wait(x_load(i))
        normed_to(lambda q, some: xc[q, some, :], 0)
        value = nn(dhoc[...], w0[pl.ds(0, width), pl.ds(0, 3 * local)])

        @pl.when(i > 0)
        def _():
            bcv_store(i - 1).wait()

        for k in range(3):
            bcv[k] = value[:, k * local : (k + 1) * local].astype(BF)
        dcp[pl.ds(0, chunk), :] = value[:, local : 2 * local]
        bx = (value[:, :local] * value[:, 2 * local :]).astype(BF)
        bcv[3] = bx
        bxp[pl.ds(8, chunk), :] = bx.astype(F32)
        before_s[i] = bxp[pl.ds(chunk, 8), :]

        @pl.when(z < last)
        def _():
            before_copy(i).start()

        bcv_store(i).start()

    def conv_of():
        shifts = [bxp[pl.ds(6 + k, chunk), :] for k in range(3)]
        return sum(own_v[2 + k : 3 + k, :] * shifts[k] for k in range(3)), shifts

    def mix(i):
        slot = lax.rem(i, 2)

        @pl.when(z < last)
        def _():
            before_copy(i).wait_send()

        @pl.when(z > 0)
        def _():
            before_copy(i).wait_recv()

        @pl.when(z == 0)
        def _():
            before_r[i] = jnp.zeros((8, local), F32)

        bxp[pl.ds(0, 8), :] = before_r[i]
        mixed = (dcp[pl.ds(0, chunk), :] * conv_of()[0]).astype(BF)
        for pair in (0, 1):
            split_store(pair, nn(mixed, wo[:, pl.ds(pair * 2 * local, 2 * local)]), ck, cs)
        remote(cs, cr.at[slot], c_sem, c_dev, slot).start()

    def share(i):
        slot = lax.rem(i, 2)
        remote(cs, cr.at[slot], c_sem, c_dev, slot).wait()
        for pair in (0, 1):
            total = ck[pair] + cr[slot, pair].astype(F32)
            kf[2 + 2 * slot + pair] = total + xc[2 * pair + c].astype(F32)
            ys[slot, pair] = total.astype(BF)
        remote(ys.at[slot], yr4.at[i], y_sem, y_dev, i).start()

    def residual(i):
        slot = lax.rem(i, 2)
        remote(ys.at[slot], yr4.at[i], y_sem, y_dev, i).wait()

        @pl.when(i >= 1)
        def _():
            for pair in (0, 1):
                for core in (0, 1):
                    h1_store(i - 1, 1 - slot, pair, core).wait()

        for pair in (0, 1):
            h1 = kf[2 + 2 * slot + pair] + yr4[i, pair].astype(F32)
            da2f[slot, pair, c] = h1.astype(BF)

            @pl.when(y == pair)
            def _(h1=h1):
                dh1s[i] = h1
        remote(da2f.at[slot, :, c], da2f.at[slot, :, c], f_sem, c_dev, slot).start()

    def cot_turn(i):
        gather_end(1, i)
        start(cot_load(i))
        wait(cot_load(i))
        at = pl.multiple_of(i * chunk, chunk)
        for q in range(4):
            cols = pl.ds(q * local, local)
            lt[0, cols, pl.ds(at, chunk)] = cotc[:, cols].T

    def feed(i):
        slot = lax.rem(i, 2)
        remote(da2f.at[slot, :, c], da2f.at[slot, :, c], f_sem, c_dev, slot).wait()
        for pair in (0, 1):
            for core in (0, 1):
                h1_store(i, slot, pair, core).start()
        normed_to(lambda q, some: da2f[slot, q // 2, q % 2, some, :], 1)
        transposed_to(1, i)
        rows = rows_at(i)
        for lo, n in cuts:
            dbuf[:, pl.ds(0, n)] = nt(dhoc[...], wg[pl.ds(lo, n), :])
            r[2, rows, pl.ds(lo, n)] = nt(dhoc[...], wu[pl.ds(lo, n), :]).astype(BF)

            def by_rows(b, _, lo=lo, n=n):
                cols = pl.ds(lo, n)
                here = pl.ds(pl.multiple_of(b * 16, 16), 16)
                some = pl.ds(pl.multiple_of(i * chunk + b * 16, 16), 16)
                gate = dbuf[here, pl.ds(0, n)]
                up = r[2, some, cols].astype(F32)
                r[0, some, cols] = (gate * jax.nn.sigmoid(gate) * up).astype(BF)
                r[1, some, cols] = gate.astype(BF)
                return 0

            lax.fori_loop(0, chunk // 16, by_rows, 0)

    def hidden_back(piece):
        i = piece // 3

        @pl.when(lax.rem(piece, 3) == 0)
        def _():
            wait(cot_load(i))

        for k, cut in enumerate(cuts):
            pl.when(lax.rem(piece, 3) == k)(functools.partial(hidden_cut, i, *cut))

        @pl.when(jnp.logical_and(lax.rem(piece, 3) == 2, i + 1 < chunks))
        def _():
            start(cot_load(i + 1))

    def hidden_cut(i, lo, n):
        if True:
            cols = pl.ds(lo, n)
            dbuf[:, pl.ds(0, n)] = nt(cotc[...], w0[pl.ds(lo, n), :])

            def by_rows(b, _, cols=cols, n=n):
                some = pl.ds(pl.multiple_of(i * chunk + b * 16, 16), 16)
                dhid = dbuf[pl.ds(pl.multiple_of(b * 16, 16), 16), pl.ds(0, n)]
                gate = r[1, some, cols].astype(F32)
                up = r[2, some, cols].astype(F32)
                sig = jax.nn.sigmoid(gate)
                r[1, some, cols] = (dhid * up * sig * (1.0 + gate * (1.0 - sig))).astype(BF)
                r[2, some, cols] = (dhid * gate * sig).astype(BF)
                return 0

            lax.fori_loop(0, chunk // 16, by_rows, 0)

    def split_store(pair, value, keep, send):
        for side in (0, 1):
            part = value[:, side * local : (side + 1) * local]

            @pl.when(c == side)
            def _(part=part):
                keep[pair] = part

            @pl.when(c != side)
            def _(part=part):
                send[pair] = part.astype(BF)

    def stage_a(i):
        slot = lax.rem(i, 2)
        rows = rows_at(i)
        for pair in (0, 1):
            cols = pl.ds(pair * 2 * local, 2 * local)
            value = nn(r[1, rows, :], wg[:, cols]) + nn(r[2, rows, :], wu[:, cols])
            split_store(pair, value, ck, cs)
        remote(cs, cr.at[slot], c_sem, c_dev, slot).start()

        @pl.when(i == chunks - 1)
        def _():
            start(x_whole())

    def x_whole():
        copies = [load(x_in, wu.at[pl.ds(0, tokens), pl.ds(pl.multiple_of(me * local, 128), local)], l_sem.at[3, 0])]
        for step in range(1, 4):
            q = lax.rem(me + step, 4)
            cols = pl.ds(pl.multiple_of(q * local, 128), local)
            copies.append(load(x_h.at[q], wu.at[pl.ds(0, tokens), cols], l_sem.at[3, step]))
        return copies

    def stage_a1(i):
        @pl.when(i == 0)
        def _():
            wait(x_whole())

        at = pl.multiple_of(i * chunk, chunk)
        normed_to(lambda q, some: wu[pl.ds(at + some.start, 16), pl.ds(q * local, local)], 0)
        for q in range(4):
            cols = pl.ds(q * local, local)
            wg[cols, pl.ds(at, chunk)] = dhoc[:, cols].T

    def stage_loads(i):
        start(cot_load(i))
        h1_load(i).start()
        bcv_load(i).start()

    def stage_b(i):
        slot = lax.rem(i, 2)
        remote(cs, cr.at[slot], c_sem, c_dev, slot).wait()
        ys[slot] = (ck[...] + cr[slot].astype(F32)).astype(BF)
        remote(ys.at[slot], yr4.at[slot], y_sem, y_dev, slot).start()

    def stage_c(i):
        slot = lax.rem(i, 2)
        remote(ys.at[slot], yr4.at[slot], y_sem, y_dev, slot).wait()
        da2f[slot, :, c] = (ys[slot].astype(F32) + yr4[slot].astype(F32)).astype(BF)
        remote(da2f.at[slot, :, c], da2f.at[slot, :, c], f_sem, c_dev, slot).start()

    def stage_d(i):
        slot = lax.rem(i, 2)
        remote(da2f.at[slot, :, c], da2f.at[slot, :, c], f_sem, c_dev, slot).wait()
        wait(cot_load(i))
        h1_load(i).wait()
        bcv_load(i).wait()
        at = pl.multiple_of(i * chunk, chunk)
        own = pl.ds(pl.multiple_of(me * local, 128), local)

        def by_rows(b, _):
            some = pl.ds(pl.multiple_of(b * 16, 16), 16)
            ssq = jnp.zeros((16, local), F32)
            inner = jnp.zeros((16, local), F32)
            for q in range(4):
                cols = pl.ds(q * local, local)
                h1 = xc[q, some, :].astype(F32)
                ssq += h1 * h1
                inner += da2f[slot, q // 2, q % 2, some, :].astype(F32) * gain(1, q) * h1
            r2 = lax.rsqrt(jnp.sum(ssq, -1, keepdims=True) / width + EPS)
            scale = r2 * r2 * r2 * jnp.sum(inner, -1, keepdims=True) / width

            def grad(q, cols, da2):
                h1 = xc[q, some, :].astype(F32)
                return cotc[some, cols].astype(F32) + r2 * (da2 * gain(1, q)) - h1 * scale

            for q in range(4):
                cols = pl.ds(q * local, local)
                dhoc[some, cols] = grad(q, cols, da2f[slot, q // 2, q % 2, some, :].astype(F32)).astype(BF)
            da2 = da2f[slot, y, c, some, :].astype(F32)
            dh1s[i, some, :] = grad(me, own, da2)
            terms = da2 * xc[me, some, :].astype(F32) * r2
            small_v[pl.ds(8, 8), :] += terms[:8] + terms[8:]
            return 0

        lax.fori_loop(0, chunk // 16, by_rows, 0)
        start(x_load(i))
        transposed_to(0, i)
        dmixed = nt(dhoc[...], wo[...])
        c_gate = bcv[1]
        bxp[pl.ds(0, 8), :] = before_r[i]
        bxp[pl.ds(8, chunk), :] = bcv[3].astype(F32)
        conv, shifts = conv_of()
        r[0, pl.ds(at, chunk), pl.ds(0, local)] = (c_gate.astype(F32) * conv).astype(BF)
        r[0, pl.ds(at, chunk), pl.ds(2 * local, local)] = (dmixed * conv).astype(BF)
        dconv = (dmixed * c_gate.astype(F32)).astype(BF).astype(F32)
        dcp[pl.ds(0, chunk), :] = dconv
        halo_s[i] = dconv[:8]
        for k in range(3):
            small_v[1 + k : 2 + k, :] += jnp.sum(dconv * shifts[k], 0, keepdims=True)

        @pl.when(z > 0)
        def _():
            halo_copy(i).start()

    def halo_copy(i):
        return remote(halo_s.at[i], halo_r.at[i], halo_sem, dn_dev, i)

    def stage_e(i):
        slot = lax.rem(i, 2)

        @pl.when(i == 0)
        def _():
            for k in range(3):
                wi_load(k).wait()
            out_copy(chunks - 1).wait()

        wait(x_load(i))

        @pl.when(z > 0)
        def _():
            halo_copy(i).wait_send()

        @pl.when(z < last)
        def _():
            halo_copy(i).wait_recv()
            dcp[pl.ds(chunk, 8), :] = halo_r[i]

        @pl.when(z == last)
        def _():
            dcp[pl.ds(chunk, 8), :] = jnp.zeros((8, local), F32)

        dbx = sum(own_v[4 - k : 5 - k, :] * dcp[pl.ds(k, chunk), :] for k in range(3))
        rows = rows_at(i)
        r[0, rows, pl.ds(local, local)] = (dbx * bcv[2].astype(F32)).astype(BF)
        r[0, rows, pl.ds(3 * local, local)] = (dbx * bcv[0].astype(F32)).astype(BF)
        inner = jnp.zeros((chunk, 1), F32)
        ssq = jnp.zeros((chunk, 1), F32)
        for pair in (0, 1):
            cols = pl.ds(pair * 2 * local, 2 * local)
            value = nt(r[0, rows, pl.ds(local, 3 * local)], w0[cols, pl.ds(0, 3 * local)])
            for side in (0, 1):
                q = 2 * pair + side
                x = xc[q].astype(F32)
                part = value[:, side * local : (side + 1) * local]
                inner += jnp.sum(part * x * gain(0, q), -1, keepdims=True)
                ssq += jnp.sum(x * x, -1, keepdims=True)
            split_store(pair, value, ck2, cs2)
        xo[...] = xc[me]
        ins[...] = jnp.broadcast_to(inner, (chunk, 128)).T[:8]
        r1s[...] = jnp.broadcast_to(lax.rsqrt(ssq / width + EPS), r1s.shape)
        remote(cs2, yr4.at[2 + slot], c2_sem, c_dev, slot).start()
        remote(ins, inr.at[slot], i_sem, c_dev, slot).start()

        @pl.when(i + 1 < chunks)
        def _():
            stage_loads(i + 1)

    def stage_f(i):
        slot = lax.rem(i, 2)
        remote(cs2, yr4.at[2 + slot], c2_sem, c_dev, slot).wait()
        remote(ins, inr.at[slot], i_sem, c_dev, slot).wait()
        ys2[...] = (ck2[1 - y] + yr4[2 + slot, 1 - y].astype(F32)).astype(BF)
        qk2[...] = ck2[y] + yr4[2 + slot, y].astype(F32)
        iys[...] = ins[...] + inr[slot]
        remote(ys2, yr2.at[slot], y2_sem, y_dev, slot).start()
        remote(iys, iyr.at[slot], iy_sem, y_dev, slot).start()

    def gx_copy(i):
        return load(gxb, gx_h.at[rows_at(i), :], gx_sem)

    def stage_g(i):
        slot = lax.rem(i, 2)
        remote(ys2, yr2.at[slot], y2_sem, y_dev, slot).wait()
        remote(iys, iyr.at[slot], iy_sem, y_dev, slot).wait()
        da1 = qk2[...] + yr2[slot].astype(F32)
        inner = jnp.broadcast_to(iys[:1] + iyr[slot, :1], (128, chunk)).T[:, :1]
        r1 = r1s[:, :1]
        x = xo[...].astype(F32)
        scaled = gain(0, me)
        small_v[0:1, :] += jnp.sum(da1 * x * r1, 0, keepdims=True)

        @pl.when(i > 0)
        def _():
            gx_copy(i - 1).wait()

        gxb[...] = (dh1s[i] + r1 * scaled * da1 - x * (r1 * r1 * r1 * inner / width)).astype(BF)
        gx_copy(i).start()

    def out_start(i):
        rows = rows_at(i)
        for pair in (0, 1):
            cols = pl.ds(pair * 2 * local, 2 * local)
            split_store(pair, nn(r[0, rows, :], w0[:, cols]), ck2, cs2)
        remote(cs2, yr4.at[2 + lax.rem(i, 2)], c2_sem, c_dev, lax.rem(i, 2)).start()

        @pl.when(i == chunks - 1)
        def _():
            for k in range(3):
                wi_load(k).start()

    def out_share(i):
        slot = lax.rem(i, 2)
        remote(cs2, yr4.at[2 + slot], c2_sem, c_dev, slot).wait()
        ys2[...] = (ck2[1 - y] + yr4[2 + slot, 1 - y].astype(F32)).astype(BF)
        qk2[...] = ck2[y] + yr4[2 + slot, y].astype(F32)
        remote(ys2, yr2.at[slot], y2_sem, y_dev, slot).start()

    def out_copy(i):
        return load(gxb, out_h.at[rows_at(i), :], gx_sem)

    def out_end(i):
        slot = lax.rem(i, 2)
        remote(ys2, yr2.at[slot], y2_sem, y_dev, slot).wait()

        @pl.when(i > 0)
        def _():
            out_copy(i - 1).wait()

        gxb[...] = (dh1s[i] + (qk2[...] + yr2[slot].astype(F32))).astype(BF)
        out_copy(i).start()

    def valid(i, f):
        @pl.when(jnp.logical_and(i >= 0, i < chunks))
        def _():
            f(i)

    gather_pass(0, 0)
    gather_pass(2, 0)
    for k in range(3):
        wi_load(k).wait()
    wo_load.wait()
    gather_end(2, 0)

    def forward(j, _):
        @pl.when(j < chunks)
        def _():
            project(j)

            @pl.when(j + 1 < chunks)
            def _():
                gather_pass(0, j + 1)

            mix(j)

        @pl.when(j == chunks - 1)
        def _():
            wd_load.start()

        @pl.when(j >= 2)
        def _():
            residual(j - 2)

        @pl.when(j < chunks)
        def _():
            share(j)

        @pl.when(j < chunks - 2)
        def _():
            gather_start(1, j)

        @pl.when(j == chunks - 1)
        def _():
            gather_start(1, chunks - 2)
            gather_start(1, chunks - 1)

        @pl.when(j == 2)
        def _():
            wg_load.wait()
            wu_load.wait()

        @pl.when(j >= 2)
        def _():
            gather_pass(1, j - 2)
            feed(j - 2)

        @pl.when(j >= 3)
        def _():
            cot_turn(j - 3)

        return 0

    lax.fori_loop(0, chunks + 2, forward, 0)
    bcv_store(chunks - 1).wait()
    for pair in (0, 1):
        for core in (0, 1):
            h1_store(chunks - 1, (chunks - 1) % 2, pair, core).wait()

    cot_turn(chunks - 1)
    start(cot_load(0))

    def small_x():
        return pltpu.make_async_remote_copy(
            src_ref=small_v.at[pl.ds(0, 8)], dst_ref=small_r.at[0], send_sem=small_sem.at[0, 0],
            recv_sem=small_sem.at[0, 1], device_id=x_dev, device_id_type=MESH,
        )

    def small_z(way):
        return pltpu.make_async_remote_copy(
            src_ref=small_r.at[1 + way], dst_ref=small_r.at[3 + way], send_sem=small_sem.at[1 + way, 0],
            recv_sem=small_sem.at[1 + way, 1], device_id=dn_dev if way else up_dev, device_id_type=MESH,
        )

    def small_step(k):
        @pl.when(k == 0)
        def _():
            small_x().wait()
            total = small_v[pl.ds(0, 8), :] + small_r[0]
            small_v[pl.ds(0, 8), :] = total
            small_r[1] = total
            small_r[2] = total

        for way in (0, 1):
            turn = last - z if way else z

            @pl.when(jnp.logical_and(turn < last, k == turn))
            def _(way=way, turn=turn):
                @pl.when(turn > 0)
                def _():
                    small_z(way).wait_recv()
                    small_r[1 + way] = small_v[pl.ds(0, 8), :] + small_r[3 + way]

                small_z(way).start()

    def small_end():
        for way in (0, 1):
            turn = last - z if way else z

            @pl.when(turn < last)
            def _(way=way):
                small_z(way).wait_send()

            @pl.when(turn == last)
            def _(way=way):
                small_z(way).wait_recv()

            @pl.when(turn > 0)
            def _(way=way):
                small_v[pl.ds(0, 8), :] += small_r[3 + way]

    def stage_last(i):
        stage_g(i)

        @pl.when(i == chunks - 1)
        def _():
            small_v[4:5, :] = jnp.sum(small_v[8:16, :], 0, keepdims=True)
            small_x().start()

    order = (
        ("g", stage_last), ("out_end", out_end), ("out_share", out_share), ("b", stage_b), ("f", stage_f),
        ("c", stage_c), ("e", stage_e), ("d", stage_d), ("out_start", out_start), ("a", stage_a),
        ("hidden", None), ("a1", stage_a1),
    )

    def stages(t, third):
        for name, f in order:
            if name == "hidden":
                if HIDDEN[0] != third:
                    continue
                done = 0
                low = high = 0
                for at, upto in HIDDEN[1].items():
                    low = jnp.where(t == at, done, low)
                    high = jnp.where(t == at, upto, high)
                    done = upto

                def piece(k, _):
                    hidden_back(k)
                    return 0

                lax.fori_loop(low, high, piece, 0)
            elif PLACES[name][0] == third:
                where = PLACES[name][1]
                i = sum(jnp.where(t >= at, 1, 0) for at in where[1:])
                now = functools.reduce(jnp.logical_or, [t == at for at in where])
                pl.when(now)(functools.partial(f, i))

    def each_tick(t, _):
        tick_a(t, True)

        @pl.when(t == 0)
        def _():
            wd_load.wait()

        @pl.when(t == beat)
        def _():
            stage_loads(0)

        stages(t, 0)
        tick_b(t)
        stages(t, 1)
        tick_c(t)
        stages(t, 2)

        @pl.when(t > PLACES["g"][1][-1])
        def _():
            small_step(t - PLACES["g"][1][-1] - 1)

        return 0

    lax.fori_loop(0, ticks, each_tick, 0)
    gx_copy(chunks - 1).wait()

    def part_four(k, _):
        tick_a(ticks + k)
        tick_b(ticks + k)
        tick_c(ticks + k)
        return 0

    lax.fori_loop(0, LAG + 4, part_four, 0)
    small_end()
    plain_out(ticks - 2, "wait")
    plain_out(ticks - 1, "wait")
    out_do(ob.at[2], 3 * beat + SECOND, 2, "wait")


def block(dims, x_own, cot_own, gain_mix, gain_ff, taps, wd, wg, wu, wo, wi):
    tokens, chunk, width, ff, local, nseq = dims
    rows = width // (2 * nseq)
    chunks = tokens // chunk
    last = nseq - 1
    m = ROWS * nseq
    DMA = pltpu.SemaphoreType.DMA
    shape = jax.ShapeDtypeStruct
    third = ff // 3 // 128 * 128
    scratch = [
        pltpu.VMEM((2, width, tokens), BF),
        pltpu.VMEM((3, tokens, ff), BF),
        pltpu.VMEM((ff, width), BF),
        pltpu.VMEM((ff, width), BF),
        pltpu.VMEM((ff, width), BF),
        pltpu.VMEM((local, width), BF),
        pltpu.VMEM((chunk, width), BF),
        pltpu.VMEM((4, chunk, local), BF),
        pltpu.VMEM((chunk, local), BF),
        pltpu.VMEM((4, chunk, local), BF),
        pltpu.VMEM((8 + chunk, local), F32),
        pltpu.VMEM((chunk, ff - 2 * third), F32),
        pltpu.VMEM((8 + chunk, local), F32),
        pltpu.VMEM((chunk, width), BF),
        pltpu.VMEM((chunks, chunk, local), F32),
        pltpu.VMEM((chunk, 128), F32),
        pltpu.VMEM((4, 8, local), F32),
        pltpu.VMEM((8, local), F32),
        pltpu.VMEM((3, m, ff), BF),
        pltpu.VMEM((5, m, ff), BF),
        pltpu.VMEM((LAG + 4, m, ff), BF),
        pltpu.VMEM((2, 2 * last, ROWS, ff), BF),
        pltpu.VMEM((2, 3 * last + 2, ROWS, ff), BF),
        pltpu.VMEM((3, ROWS, ff), BF),
        pltpu.VMEM((ROWS, ff), BF),
        pltpu.VMEM((ROWS, ff), BF),
        pltpu.VMEM((ROWS, ff), F32),
        pltpu.VMEM((6, chunk, local), F32),
        pltpu.VMEM((2, chunk, local), BF),
        pltpu.VMEM((2, 2, chunk, local), BF),
        pltpu.VMEM((2, 2, chunk, local), BF),
        pltpu.VMEM((4, 2, chunk, local), BF),
        pltpu.VMEM((2, 2, 2, chunk, local), BF),
        pltpu.VMEM((2, chunk, local), BF),
        pltpu.VMEM((chunk, local), BF),
        pltpu.VMEM((2, chunk, local), BF),
        pltpu.VMEM((8, chunk), F32),
        pltpu.VMEM((2, 8, chunk), F32),
        pltpu.VMEM((8, chunk), F32),
        pltpu.VMEM((2, 8, chunk), F32),
        pltpu.VMEM((chunk, local), BF),
        pltpu.VMEM((chunks, 8, local), F32),
        pltpu.VMEM((chunks, 8, local), F32),
        pltpu.VMEM((chunks, 8, local), F32),
        pltpu.VMEM((chunks, 8, local), F32),
        pltpu.VMEM((5, 8, local), F32),
        DMA((3,)), DMA((5,)), DMA((2, 2 * last)), DMA((2, 3 * last + 2)), DMA((3, 4)),
        DMA((2, 2)), DMA((2, chunks)), DMA((2, 2)), DMA((2, 2)), DMA((2, 2)),
        DMA((2, 2)), DMA((2, 2)), DMA((2, chunks)), DMA((2, chunks)), DMA((3, 2, 3, chunks)),
        DMA((7,)), DMA((4, 4)), DMA(()), DMA((2, 2)), DMA(()), DMA((3, 2)), DMA((2,)),
    ]
    return pl.pallas_call(
        functools.partial(block_kernel, dims),
        out_shape=(
            shape((rows, ff), BF), shape((rows, ff), BF), shape((rows, ff), BF),
            shape((rows, local), BF), shape((3, rows, local), BF),
            shape((tokens, local), BF), shape((tokens, local), BF), shape((16, local), F32),
            shape((4, tokens, local), BF), shape((4, tokens, local), BF),
            shape((4, tokens, local), BF), shape((4, tokens, local), BF),
        ),
        in_specs=[ANY] * 2 + [VMEM] * 3 + [ANY] * 5,
        out_specs=(ANY,) * 7 + (VMEM,) + (ANY,) * 4,
        scratch_shapes=scratch,
        compiler_params=pltpu.CompilerParams(
            collective_id=0, has_side_effects=True, vmem_limit_bytes=63 * 2**20
        ),
    )(x_own, cot_own, gain_mix, gain_ff, taps, wd, wg, wu, wo, wi)


def shifted(array, axis, by):
    count = lax.axis_size(axis)
    pairs = [(i, i + by) for i in range(count) if 0 <= i + by < count]
    return lax.ppermute(array, axis, pairs)


def fused_device(inputs, gain_mix, w_in, kernel, w_out, gain_ff, w_gate, w_up, w_down, cotangent):
    groups, seq_rows, local = inputs.shape
    width = local * lax.axis_size("mp")
    ff = w_down.shape[0]
    tokens = groups * seq_rows
    dims = (tokens, seq_rows, width, ff, local, lax.axis_size("seq"))
    gdown, ggate, gup, gout, gin, gx, out, small = block(
        dims, inputs.reshape(tokens, local), cotangent.reshape(tokens, local), gain_mix, gain_ff, kernel,
        w_down, w_gate.T, w_up.T, w_out, w_in.transpose(1, 0, 2),
    )[:8]
    gdown, ggate, gup, gout, gin, gx, out, gmix, gtaps, gff = widen(
        gdown, ggate, gup, gout, gin, gx, out, small
    )
    whole = (groups, seq_rows, local)
    return (
        out.reshape(whole), gx.reshape(whole), gmix, gin.transpose(1, 0, 2), gtaps,
        gout.T, gff, ggate, gup, gdown.T,
    )


def widen_kernel(*refs):
    count = 7
    src, small, dst = refs[:count], refs[count], refs[count + 1 : 2 * count + 1]
    gmix, gtaps, gff = refs[2 * count + 1 : 2 * count + 4]
    narrow = refs[2 * count + 4 : 3 * count + 4]
    wide = refs[3 * count + 4 : 4 * count + 2]
    in_sem, out_sem = refs[4 * count + 2 :]
    loads = [pltpu.make_async_copy(src[k], narrow[k], in_sem.at[k]) for k in range(count)]
    stores = [
        pltpu.make_async_copy(wide[k] if k < count - 2 else narrow[k], dst[k], out_sem.at[k])
        for k in range(count)
    ]
    for one in loads:
        one.start()
    gmix[...] = small[0:1, :].reshape(gmix.shape)
    gtaps[...] = small[1:4, :]
    gff[...] = small[4:5, :].reshape(gff.shape)
    for k in range(count):
        loads[k].wait()
        if k < count - 2:
            wide[k][...] = narrow[k][...].astype(F32)
        stores[k].start()
    for one in stores:
        one.wait()


def widen(*arrays):
    big, small = arrays[:7], arrays[7]
    local = small.shape[1]
    shape = jax.ShapeDtypeStruct
    outs = [shape(a.shape, F32 if k < 5 else BF) for k, a in enumerate(big)]
    outs += [shape((local,), F32), shape((3, local), F32), shape((local,), F32)]
    return pl.pallas_call(
        widen_kernel,
        out_shape=outs,
        in_specs=[ANY] * 7 + [VMEM],
        out_specs=[ANY] * 7 + [VMEM] * 3,
        scratch_shapes=[pltpu.VMEM(a.shape, BF) for a in big]
        + [pltpu.VMEM(a.shape, F32) for a in big[:5]]
        + [pltpu.SemaphoreType.DMA((7,))] * 2,
        compiler_params=pltpu.CompilerParams(vmem_limit_bytes=63 * 2**20),
    )(*big, small)


def contract_rows(left, right):
    return lax.dot_general(
        left, right, (((0,), (0,)), ((), ())), preferred_element_type=jnp.float32
    )


def contract_cols(left, right):
    return lax.dot_general(
        left, right, (((1,), (1,)), ((), ())), preferred_element_type=jnp.float32
    )


def plain_device(inputs, gain_mix, w_in, kernel, w_out, gain_ff, w_gate, w_up, w_down, cotangent):
    groups, seq_rows, local_width = inputs.shape
    full_width = local_width * lax.axis_size("mp")
    tokens = groups * seq_rows
    x_float = inputs.reshape(tokens, local_width).astype(jnp.float32)
    gain_one = gain_mix.astype(jnp.float32)
    gain_two = gain_ff.astype(jnp.float32)
    taps = kernel.astype(jnp.float32)

    def row_total(values):
        return lax.psum(jnp.sum(values, axis=-1, keepdims=True), "mp")

    def all_features(values):
        return lax.all_gather(values, "mp", axis=1, tiled=True)

    def share_sums(values):
        return lax.psum_scatter(
            values.astype(jnp.bfloat16), "mp", scatter_dimension=1, tiled=True
        ).astype(jnp.float32)

    def scattered(values, dim):
        return lax.psum_scatter(
            values.astype(jnp.bfloat16), ("dp", "seq"), scatter_dimension=dim, tiled=True
        ).astype(jnp.float32)

    def norm_scale(values):
        return lax.rsqrt(row_total(values * values) / full_width + EPS)

    def norm_back(values, scale, gain_vec, upstream):
        inner = row_total(gain_vec * upstream * values)
        grad_values = scale * gain_vec * upstream - values * scale**3 * inner / full_width
        return (grad_values, jnp.sum(upstream * values * scale, axis=0))

    scale_one = norm_scale(x_float)
    normed_in = all_features((x_float * scale_one * gain_one).astype(jnp.bfloat16))
    proj = jnp.einsum("td,dkc->tkc", normed_in, w_in, preferred_element_type=jnp.float32)
    b_gate = proj[:, 0]
    c_gate = proj[:, 1]
    values_v = proj[:, 2]
    b_times_x = (b_gate * values_v).astype(jnp.bfloat16).reshape(groups, seq_rows, local_width)
    before = shifted(b_times_x[:, seq_rows - 2 :], "seq", 1)
    padded = jnp.concatenate([before, b_times_x], 1).astype(jnp.float32)
    conv = taps[0] * padded[:, :-2] + taps[1] * padded[:, 1:-1] + taps[2] * padded[:, 2:]
    conv = conv.reshape(tokens, local_width)
    mixed = (c_gate * conv).astype(jnp.bfloat16)
    hidden_one = x_float + share_sums(jnp.dot(mixed, w_out, preferred_element_type=jnp.float32))
    scale_two = norm_scale(hidden_one)
    normed_ff = all_features((hidden_one * scale_two * gain_two).astype(jnp.bfloat16))
    gate = jnp.dot(normed_ff, w_gate, preferred_element_type=jnp.float32)
    up_proj = jnp.dot(normed_ff, w_up, preferred_element_type=jnp.float32)
    sigma = jax.nn.sigmoid(gate)
    active = gate * sigma
    hidden = (active * up_proj).astype(jnp.bfloat16)
    ffn_out = share_sums(jnp.dot(hidden, w_down, preferred_element_type=jnp.float32))
    block_out = (hidden_one + ffn_out).astype(jnp.bfloat16).reshape(groups, seq_rows, local_width)
    grad_flat = cotangent.reshape(tokens, local_width)
    grad_full = all_features(grad_flat)
    grad_down = contract_rows(hidden, grad_full)
    grad_hidden = contract_cols(grad_full, w_down)
    grad_gate_act = (grad_hidden * up_proj * sigma * (1.0 + gate * (1.0 - sigma))).astype(
        jnp.bfloat16
    )
    grad_up_act = (grad_hidden * active).astype(jnp.bfloat16)
    grad_gate = contract_rows(normed_ff, grad_gate_act)
    grad_up = contract_rows(normed_ff, grad_up_act)
    grad_normed_ff = share_sums(
        contract_cols(grad_gate_act, w_gate) + contract_cols(grad_up_act, w_up)
    )
    grad_norm_two, grad_gain_two = norm_back(hidden_one, scale_two, gain_two, grad_normed_ff)
    grad_hidden_one = grad_flat.astype(jnp.float32) + grad_norm_two
    grad_out_full = all_features(grad_hidden_one.astype(jnp.bfloat16))
    grad_out = contract_rows(mixed, grad_out_full)
    grad_mixed = contract_cols(grad_out_full, w_out)
    grad_c = grad_mixed * conv
    grad_conv = (grad_mixed * c_gate).astype(jnp.bfloat16).reshape(groups, seq_rows, local_width)
    after = shifted(grad_conv[:, :2], "seq", -1)
    extended = jnp.concatenate([grad_conv, after], 1).astype(jnp.float32)
    grad_bx = taps[2] * extended[:, :-2] + taps[1] * extended[:, 1:-1] + taps[0] * extended[:, 2:]
    grad_bx = grad_bx.reshape(tokens, local_width)
    conv_grad_float = extended[:, :-2]
    grad_taps = jnp.stack(
        [
            jnp.sum(conv_grad_float * padded[:, :-2], axis=(0, 1)),
            jnp.sum(conv_grad_float * padded[:, 1:-1], axis=(0, 1)),
            jnp.sum(conv_grad_float * padded[:, 2:], axis=(0, 1)),
        ]
    )
    grad_proj = jnp.stack([grad_bx * values_v, grad_c, grad_bx * b_gate], 1).astype(jnp.bfloat16)
    grad_in = jnp.einsum("td,tkc->dkc", normed_in, grad_proj, preferred_element_type=jnp.float32)
    grad_normed_in = share_sums(
        jnp.einsum("tkc,dkc->td", grad_proj, w_in, preferred_element_type=jnp.float32)
    )
    grad_norm_one, grad_gain_one = norm_back(x_float, scale_one, gain_one, grad_normed_in)
    grad_input = (
        (grad_hidden_one + grad_norm_one)
        .astype(jnp.bfloat16)
        .reshape(groups, seq_rows, local_width)
    )
    small_sums = lax.psum((grad_gain_one, grad_taps, grad_gain_two), ("dp", "seq"))
    by_row = (
        scattered(grad_in, 0),
        scattered(grad_gate, 0),
        scattered(grad_up, 0),
    )
    by_col = (
        scattered(grad_out, 1),
        scattered(grad_down, 1),
    )
    return (
        block_out,
        grad_input,
        small_sums[0],
        by_row[0],
        small_sums[1],
        by_col[0],
        small_sums[2],
        by_row[1],
        by_row[2],
        by_col[1],
    )


def solution(mesh):
    placed = (
        P("dp", "seq", "mp"),
        P("mp"),
        P(None, None, "mp"),
        P(None, "mp"),
        P("mp", None),
        P("mp"),
        P(None, "mp"),
        P(None, "mp"),
        P("mp", None),
        P("dp", "seq", "mp"),
    )
    sizes = mesh.shape
    fused = sizes["dp"] == 2 and sizes["seq"] == 4 and sizes["mp"] == 4
    return jax.shard_map(
        fused_device if fused else plain_device,
        mesh=mesh,
        in_specs=placed,
        out_specs=(
            P("dp", "seq", "mp"),
            P("dp", "seq", "mp"),
            P("mp"),
            P(("dp", "seq"), None, "mp"),
            P(None, "mp"),
            P("mp", ("dp", "seq")),
            P("mp"),
            P(("dp", "seq"), "mp"),
            P(("dp", "seq"), "mp"),
            P("mp", ("dp", "seq")),
        ),
        check_vma=False,
    )
```

```python
import functools

import jax
import jax.numpy as jnp
from jax import lax
from jax.experimental import pallas as pl
from jax.experimental.pallas import tpu as pltpu
from jax.sharding import PartitionSpec as P

EPS = 1e-05
MESH = pl.DeviceIdType.MESH
BF = jnp.bfloat16
F32 = jnp.float32
ROWS = 32
SECOND = 3
LAG = 3
WAIT = 3
PLACES = {
    "out_start": (2, (1, 4, 7, 8)),
    "out_share": (2, (2, 5, 8, 10)),
    "out_end": (1, (4, 7, 9, 12)),
    "a": (2, (3, 8, 10, 14)),
    "b": (2, (4, 9, 12, 15)),
    "c": (1, (8, 11, 14, 18)),
    "d": (2, (9, 13, 17, 19)),
    "e": (2, (12, 15, 18, 20)),
    "f": (2, (14, 16, 19, 21)),
    "g": (2, (15, 18, 20, 22)),
    "a1": (2, (15, 16, 17, 19)),
}
HIDDEN = (1, {2: 3, 3: 4, 4: 5, 5: 7, 6: 12})
ANY = pl.BlockSpec(memory_space=pl.ANY)
VMEM = pl.BlockSpec(memory_space=pltpu.VMEM)


def nn(left, right):
    return lax.dot_general(left, right, (((1,), (0,)), ((), ())), preferred_element_type=F32)


def nt(left, right):
    return lax.dot_general(left, right, (((1,), (1,)), ((), ())), preferred_element_type=F32)


def block_kernel(
    dims,
    x_in, cot_in, gain_mix_v, gain_ff_v, taps_v, wd_h, wg_h, wu_h, wo_h, wi_h,
    gdown_h, ggate_h, gup_h, gout_h, gin_h, gx_h, out_h, small_v,
    x_h, cot_h, h1_h, bcv_h, woy_h,
    lt, r, w0, wg, wu, wof, cotc, xc, xo, bcv, bxp, dbuf, dcp, dhoc, dh1s, r1s, gv, own_v,
    xs, xr, s_buf, zs, zr, ob, vs, vr, vk,
    kf, cs, cr, ys, yr4, da2f, cs2, ys2, yr2,
    ins, inr, iys, iyr, gxb, halo_s, halo_r, before_s, before_r, small_r,
    xs_sem, xr_sem, zs_sem, zr_sem, ob_sem, c_sem, y_sem, f_sem, c2_sem, y2_sem,
    i_sem, iy_sem, halo_sem, before_sem, gather_sem, w_sem, l_sem, bcv_sem, h1_sem, gx_sem,
    small_sem, v_sem, wy_sem, wx_sem, wz_sem, wc_sem, wl_sem,
):
    tokens, chunk, width, ff, local, nseq = dims
    chunks = tokens // chunk
    block = width // (2 * nseq)
    per = block // ROWS
    beat = per + 1
    ticks = 4 * beat
    p = lax.axis_index("dp")
    z = lax.axis_index("seq")
    me = lax.axis_index("mp")
    y, c = me // 2, me % 2
    x_dev = {"dp": 1 - p}
    up_dev = {"seq": z + 1}
    dn_dev = {"seq": z - 1}
    y_dev = {"mp": (1 - y) * 2 + c}
    c_dev = {"mp": y * 2 + 1 - c}
    last = nseq - 1
    ck, ck2, qk2 = kf.at[pl.ds(0, 2)], kf.at[pl.ds(2, 2)], kf.at[4]
    third = ff // 3 // 128 * 128
    cuts = ((0, third), (third, third), (2 * third, ff - 2 * third))

    def remote(src, dst, sems, where, at=None):
        s_sem, r_sem = (sems.at[0], sems.at[1]) if at is None else (sems.at[0, at], sems.at[1, at])
        return pltpu.make_async_remote_copy(
            src_ref=src, dst_ref=dst, send_sem=s_sem, recv_sem=r_sem,
            device_id=where, device_id_type=MESH,
        )

    def load(src, dst, sem):
        return pltpu.make_async_copy(src, dst, sem)

    def wi_load(k):
        return load(wi_h.at[k], w0.at[pl.ds(0, width), pl.ds(k * local, local)], w_sem.at[k])

    wd_load = load(wd_h, w0, w_sem.at[3])
    wg_load = load(wg_h, wg, w_sem.at[4])
    wu_load = load(wu_h, wu, w_sem.at[5])
    def wo_load(q):
        return load(wo_h.at[:, pl.ds(q * local, local)], wof.at[0, pl.ds(q * local, local), :], wl_sem.at[q])

    for k in range(3):
        wi_load(k).start()
    own_v[0:1, :] = gain_mix_v[...].astype(F32).reshape(1, local)
    own_v[1:2, :] = gain_ff_v[...].astype(F32).reshape(1, local)
    own_v[2:5, :] = taps_v[...].astype(F32)
    own_v[5:8, :] = jnp.zeros((3, local), F32)
    gv[me] = own_v[...]

    barrier = pltpu.get_barrier_semaphore()
    for dev in (x_dev, y_dev, c_dev):
        pl.semaphore_signal(barrier, inc=1, device_id=dev, device_id_type=MESH)

    @pl.when(z < last)
    def _():
        pl.semaphore_signal(barrier, inc=1, device_id=up_dev, device_id_type=MESH)

    @pl.when(z > 0)
    def _():
        pl.semaphore_signal(barrier, inc=1, device_id=dn_dev, device_id_type=MESH)

    peers = 3 + jnp.where(z < last, 1, 0) + jnp.where(z > 0, 1, 0)
    pl.semaphore_wait(barrier, peers)

    small_v[...] = jnp.zeros_like(small_v)

    def rows_at(i):
        return pl.ds(pl.multiple_of(i * chunk, chunk), chunk)

    def mixed_at(q, i):
        return r.at[0, rows_at(i), pl.ds(pl.multiple_of(q * local, 128), local)]

    share = local // (2 * nseq)

    def piece(zz):
        return woy_h.at[pl.ds(pl.multiple_of((p * nseq + zz) * share, 16), share), :]

    def wy():
        mine = wo_h.at[pl.ds(pl.multiple_of((p * nseq + z) * share, 16), share), :]
        return pltpu.make_async_remote_copy(
            src_ref=mine, dst_ref=piece(z), send_sem=wy_sem.at[0], recv_sem=wy_sem.at[1],
            device_id=y_dev, device_id_type=MESH,
        )

    def wx(zz):
        return remote(piece(zz), piece(zz), wx_sem, x_dev, zz)

    def wz(way, step):
        part = piece(z + step if way else z - step)
        return pltpu.make_async_remote_copy(
            src_ref=part, dst_ref=part, send_sem=wz_sem.at[0, way, step], recv_sem=wz_sem.at[1, way, step],
            device_id=dn_dev if way else up_dev, device_id_type=MESH,
        )

    def wz_sends(way, step):
        return jnp.logical_and(z > 0, z + step <= last) if way else jnp.logical_and(z < last, z >= step)

    def wz_receives(way, step):
        return z + 1 + step <= last if way else z >= step + 1

    def wo_step(step):
        if step == 0:
            wy().wait_recv()
            wx(z).start()
        for way in (0, 1):
            if step > 0:
                @pl.when(wz_receives(way, step - 1))
                def _(way=way):
                    wz(way, step - 1).wait_recv()
                    wx(z + step if way else z - step).start()
            if step < last:
                @pl.when(wz_sends(way, step))
                def _(way=way):
                    wz(way, step).start()

    def wo_columns(src, q, kind):
        rows = pl.ds(pl.multiple_of(q * local, 128), local)
        for pair in (0, 1):
            cols = pl.ds(pl.multiple_of((2 * pair + c) * local, 128), local)
            yield load(src.at[:, cols], wof.at[pair, rows, :], wl_sem.at[2 * kind + pair])
            cols = pl.ds(pl.multiple_of((2 * pair + 1 - c) * local, 128), local)
            yield remote(src.at[:, cols], wof.at[pair, rows, :], wc_sem, c_dev, 2 * kind + pair)

    def wo_end():
        wy().wait_send()
        for zz in range(nseq):
            wx(zz).wait()
        for way in (0, 1):
            for step in range(last):
                @pl.when(wz_sends(way, step))
                def _(way=way, step=step):
                    wz(way, step).wait_send()
        for one in wo_columns(woy_h, (1 - y) * 2 + c, 1):
            one.start()

    def gather(which, i, leg):
        if which == 2:
            src = mine = own_v
            dst = gv
            at = (2, 0)
        elif which == 3:
            mine = mixed_at(me, i)
            at = (3, i)
        else:
            src, dst = (x_in, x_h) if which == 0 else (cot_in, cot_h)
            mine = src.at[rows_at(i), :]
            at = (which, i)
        if which == 3:
            slot = lambda q: mixed_at(q, i)
        else:
            slot = (lambda q: dst.at[q]) if which == 2 else (lambda q: dst.at[q, rows_at(i), :])
        sems = [gather_sem.at[leg, way, at[0], at[1]] for way in (0, 1)]
        if leg == 0:
            pair, where = (mine, slot(me)), y_dev
        elif leg == 1:
            pair, where = (mine, slot(me)), c_dev
        else:
            from_y = (1 - y) * 2 + c
            pair, where = (slot(from_y), slot(from_y)), c_dev
        return pltpu.make_async_remote_copy(
            src_ref=pair[0], dst_ref=pair[1], send_sem=sems[0], recv_sem=sems[1],
            device_id=where, device_id_type=MESH,
        )

    def gather_start(which, i):
        gather(which, i, 0).start()
        gather(which, i, 1).start()

    def gather_pass(which, i):
        gather(which, i, 0).wait_recv()
        gather(which, i, 2).start()

    def gather_end(which, i):
        gather(which, i, 0).wait_send()
        gather(which, i, 1).wait()
        gather(which, i, 2).wait()

    gather(0, 0, 0).start()
    gather_start(2, 0)
    for i in range(chunks):
        gather(0, i, 1).start()
    for one in wo_columns(wo_h, me, 0):
        one.start()
    wg_load.start()
    wu_load.start()

    def on_size(t, f):
        pl.when(t // beat < 3)(lambda: f(pl.ds(0, ff)))
        pl.when(t // beat == 3)(lambda: f(pl.ds(0, 4 * local)))

    def place(t):
        return lax.rem(t, beat)

    def is_first(t):
        return place(t) == 0

    def is_second(t):
        return place(t) == SECOND

    def is_plain(t):
        return jnp.logical_and(place(t) != 0, place(t) != SECOND)

    def row_block(t):
        plain = place(t) - jnp.where(place(t) > SECOND, 2, 1)
        return jnp.where(is_plain(t), plain, per - 1)

    def x_number(t):
        return t // beat * (per - 1) + row_block(t)

    def x_do(t, what):
        n = x_number(t)

        def f(cols):
            copy = pltpu.make_async_remote_copy(
                src_ref=xs.at[lax.rem(n, 3), :, cols], dst_ref=xr.at[lax.rem(n, 5), :, cols],
                send_sem=xs_sem.at[lax.rem(n, 3)], recv_sem=xr_sem.at[lax.rem(n, 5)],
                device_id=x_dev, device_id_type=MESH,
            )
            getattr(copy, what)()

        on_size(t, f)

    def v_do(t, what):
        def f(cols):
            copy = pltpu.make_async_remote_copy(
                src_ref=vs.at[:, cols], dst_ref=vr.at[:, cols], send_sem=v_sem.at[0], recv_sem=v_sem.at[1],
                device_id=x_dev, device_id_type=MESH,
            )
            getattr(copy, what)()

        on_size(t, f)

    def zs_at(t, step):
        return 2 * step + lax.rem(t, 2)

    def zr_at(t, step):
        count = 3 if 0 < step < last - 1 else 4
        return 3 * step + min(step, 1) + lax.rem(t, count)

    def z_do(t, way, step, what):
        def f(cols):
            copy = pltpu.make_async_remote_copy(
                src_ref=zs.at[way, zs_at(t, step), :, cols], dst_ref=zr.at[way, zr_at(t, step), :, cols],
                send_sem=zs_sem.at[way, zs_at(t, step)], recv_sem=zr_sem.at[way, zr_at(t, step)],
                device_id=dn_dev if way else up_dev, device_id_type=MESH,
            )
            getattr(copy, what)()

        on_size(t, f)

    def receives(way, step):
        if way:
            return jnp.logical_and(z < last, z >= last - 1 - step)
        return jnp.logical_and(z > 0, z <= step + 1)

    def can_send(way, step):
        if way:
            return jnp.logical_and(z > 0, z >= last - step)
        return jnp.logical_and(z < last, z <= step)

    def z_arrived(t, step):
        for way in (0, 1):
            @pl.when(receives(way, step))
            def _(way=way):
                z_do(t, way, step, "wait_recv")

            @pl.when(can_send(way, step))
            def _(way=way):
                z_do(t, way, step, "wait_send")

    def z_step(t, step):
        sl = lax.rem(t, LAG + 4)
        if step > 0:
            z_arrived(t, step - 1)
        for way in (0, 1):
            quarter = z - last + step if way else last - step + z
            fresh = can_send(way, step)
            if step > 0:
                @pl.when(jnp.logical_and(receives(way, step - 1), can_send(way, step)))
                def _(way=way, quarter=quarter):
                    value = s_buf[sl, pl.ds(quarter * ROWS, ROWS), :].astype(F32) + zr[
                        way, zr_at(t, step - 1)
                    ].astype(F32)
                    zs[way, zs_at(t, step)] = value.astype(BF)

                fresh = jnp.logical_and(fresh, jnp.logical_not(receives(way, step - 1)))

            @pl.when(fresh)
            def _(way=way, quarter=quarter):
                zs[way, zs_at(t, step)] = s_buf[sl, pl.ds(quarter * ROWS, ROWS), :]

        for way in (0, 1):
            @pl.when(can_send(way, step))
            def _(way=way):
                z_do(t, way, step, "start")

    def compute(t, kind):
        sl = lax.rem(t, LAG + 4)
        at = row_block(t) * ROWS
        m = ROWS * nseq

        def rows_of(index, half):
            rows = [pl.ds(pl.multiple_of((half * nseq + s) * block + at, ROWS), ROWS) for s in range(nseq)]
            if kind == 3 and index == 1:
                return [wg[some, pl.ds(0, tokens)] for some in rows]
            return [lt[index, some, :] for some in rows]

        if kind == 3:
            parts = [(0, 0, 0, local)] + [(1, 0, k * local, local) for k in (1, 2, 3)]
        elif kind == 0:
            parts = [(0, 0, lo, n) for lo, n in cuts]
        else:
            parts = [(1, t // beat, lo, n) for lo, n in cuts]

        @pl.when(is_plain(t))
        def _():
            slot = lax.rem(x_number(t), 3)
            left = [jnp.concatenate(rows_of(i, 1 - p) + rows_of(i, p), 0) for i in sorted({q[0] for q in parts})]
            for i, ri, lo, n in parts:
                cols = pl.ds(lo, n)
                out = nn(left[i if len(left) == 2 else 0], r[ri, :, cols])
                xs[slot, :, cols] = out[:m].astype(BF)
                s_buf[sl, :, cols] = out[m:].astype(BF)
            x_do(t, "start")

        @pl.when(jnp.logical_not(is_plain(t)))
        def _():
            half = jnp.where(is_first(t), p, 1 - p)
            left = [jnp.concatenate(rows_of(i, half), 0) for i in sorted({q[0] for q in parts})]
            for i, ri, lo, n in parts:
                cols = pl.ds(lo, n)
                s_buf[sl, :, cols] = nn(left[i if len(left) == 2 else 0], r[ri, :, cols]).astype(BF)

    def out_do(src, t, sems, what):
        rows = pl.ds(pl.multiple_of(row_block(t) * ROWS, ROWS), ROWS)
        for g, target in enumerate((gdown_h, ggate_h, gup_h)):
            @pl.when(t // beat == g)
            def _(target=target):
                getattr(load(src, target.at[rows, :], ob_sem.at[sems, 0]), what)()

        @pl.when(t // beat == 3)
        def _():
            getattr(load(src.at[:, pl.ds(0, local)], gout_h.at[rows, :], ob_sem.at[sems, 0]), what)()
            for k in range(3):
                part = src.at[:, pl.ds((k + 1) * local, local)]
                getattr(load(part, gin_h.at[k, rows, :], ob_sem.at[sems, 1 + k]), what)()

    def plain_out(t, what):
        slot = lax.rem(x_number(t), 2)
        out_do(ob.at[slot], t, slot, what)

    def finish(t):
        sl = lax.rem(t, LAG + 4)
        z_arrived(t, last - 1)

        def total(then):
            def end(ways):
                value = s_buf[sl, pl.ds(z * ROWS, ROWS), :].astype(F32)
                for way in ways:
                    value += zr[way, zr_at(t, last - 1)].astype(F32)
                then(value)

            pl.when(z == 0)(lambda: end((1,)))
            pl.when(z == last)(lambda: end((0,)))
            pl.when(jnp.logical_and(z > 0, z < last))(lambda: end((0, 1)))

        @pl.when(is_plain(t))
        def _():
            n = x_number(t)
            before = t - jnp.where(place(t) == per, 2, 3)

            @pl.when(n >= 2)
            def _():
                plain_out(before, "wait")

            def put(value):
                ob[lax.rem(n, 2)] = value.astype(BF)

            total(put)
            plain_out(t, "start")

        @pl.when(is_first(t))
        def _():
            def put(value):
                vk[...] = value

            total(put)

        @pl.when(is_second(t))
        def _():
            def put(value):
                vs[...] = value.astype(BF)

            total(put)
            v_do(t, "start")

    def v_end(t):
        @pl.when(is_second(t))
        def _():
            v_do(t, "wait")

            @pl.when(t >= beat)
            def _():
                out_do(ob.at[2], t - beat, 2, "wait")

            ob[2] = (vk[...] + vr[...].astype(F32)).astype(BF)
            out_do(ob.at[2], t, 2, "start")

    def within(t, f):
        @pl.when(jnp.logical_and(t >= 0, t < ticks))
        def _():
            f(t)

    def tick_a(t, full=False):
        within(t - LAG - 4 - WAIT, v_end)
        within(t - LAG - 4, finish)

        def x_in(u):
            @pl.when(is_plain(u))
            def _():
                x_do(u, "wait")
                sl = lax.rem(u, LAG + 4)
                arrived = xr[lax.rem(x_number(u), 5)].astype(F32)
                s_buf[sl] = (s_buf[sl].astype(F32) + arrived).astype(BF)

            z_step(u, 0)

        within(t - LAG, x_in)
        if full:
            pl.when(t // beat == 0)(lambda: compute(t, 0))
            pl.when(jnp.logical_and(t // beat > 0, t // beat < 3))(lambda: compute(t, 1))
            pl.when(t // beat == 3)(lambda: compute(t, 3))

    def tick_b(t):
        within(t - LAG - 1, lambda u: z_step(u, 1))

    def tick_c(t):
        within(t - LAG - 2, lambda u: z_step(u, 2))

    def in_slices(own, others, to, slot):
        copies = [load(own, to(me), l_sem.at[slot, 0])]
        for step in range(1, 4):
            q = lax.rem(me + step, 4)
            copies.append(load(others(q), to(q), l_sem.at[slot, step]))
        return copies

    def cot_load(i):
        return in_slices(
            cot_in.at[rows_at(i), :],
            lambda q: cot_h.at[q, rows_at(i), :],
            lambda q: cotc.at[:, pl.ds(pl.multiple_of(q * local, 128), local)],
            0,
        )

    def x_load(i):
        return in_slices(x_in.at[rows_at(i), :], lambda q: x_h.at[q, rows_at(i), :], lambda q: xc.at[q], 1)

    def start(copies):
        for one in copies:
            one.start()

    def wait(copies):
        for one in copies:
            one.wait()

    def h1_load(i):
        return load(h1_h.at[:, rows_at(i), :], xc, l_sem.at[2, 0])

    def bcv_load(i):
        return load(bcv_h.at[:, rows_at(i), :], bcv, l_sem.at[2, 1])

    def gain(row, q):
        return gv[q, row : row + 1, :]

    def by_rows_of(count, f):
        def body(b, _):
            f(pl.ds(pl.multiple_of(b * count, count), count))
            return 0

        lax.fori_loop(0, chunk // count, body, 0)

    def normed_to(src, row, after=None):
        def f(some):
            ssq = jnp.zeros((64, local), F32)
            for q in range(4):
                values = src(q, some).astype(F32)
                ssq += values * values
            scale = lax.rsqrt(jnp.sum(ssq, -1, keepdims=True) / width + EPS)
            for q in range(4):
                dhoc[some, pl.ds(q * local, local)] = (src(q, some).astype(F32) * scale * gain(row, q)).astype(BF)

        by_rows_of(64, f)

    def transposed_to(index, i):
        at = pl.multiple_of(i * chunk, chunk)
        for q in range(4):
            cols = pl.ds(q * local, local)
            lt[index, cols, pl.ds(at, chunk)] = dhoc[:, cols].T

    def before_copy(i):
        return remote(before_s.at[i], before_r.at[i], before_sem, up_dev, i)

    def bcv_store(i):
        return load(bcv, bcv_h.at[:, rows_at(i), :], bcv_sem)

    def h1_store(i, slot, pair, core):
        return load(da2f.at[slot, pair, core], h1_h.at[2 * pair + core, rows_at(i), :], h1_sem.at[pair, core])

    def project(i):
        wait(x_load(i))
        normed_to(lambda q, some: xc[q, some, :], 0)
        value = nn(dhoc[...], w0[pl.ds(0, width), pl.ds(0, 3 * local)])

        @pl.when(i > 0)
        def _():
            bcv_store(i - 1).wait()

        for k in range(3):
            bcv[k] = value[:, k * local : (k + 1) * local].astype(BF)
        dcp[pl.ds(0, chunk), :] = value[:, local : 2 * local]
        bx = (value[:, :local] * value[:, 2 * local :]).astype(BF)
        bcv[3] = bx
        bxp[pl.ds(8, chunk), :] = bx.astype(F32)
        before_s[i] = bxp[pl.ds(chunk, 8), :]

        @pl.when(z < last)
        def _():
            before_copy(i).start()

        bcv_store(i).start()

    def conv_of():
        shifts = [bxp[pl.ds(6 + k, chunk), :] for k in range(3)]
        return sum(own_v[2 + k : 3 + k, :] * shifts[k] for k in range(3)), shifts

    def mix(i):
        @pl.when(z < last)
        def _():
            before_copy(i).wait_send()

        @pl.when(z > 0)
        def _():
            before_copy(i).wait_recv()

        @pl.when(z == 0)
        def _():
            before_r[i] = jnp.zeros((8, local), F32)

        bxp[pl.ds(0, 8), :] = before_r[i]
        mixed = (dcp[pl.ds(0, chunk), :] * conv_of()[0]).astype(BF)
        r[0, rows_at(i), pl.ds(pl.multiple_of(me * local, 128), local)] = mixed
        gather_start(3, i)

    def x_two(i):
        return [
            load(x_in.at[rows_at(i), :], cs2.at[y], l_sem.at[2, 2]),
            load(x_h.at[(1 - y) * 2 + c, rows_at(i), :], cs2.at[1 - y], l_sem.at[2, 3]),
        ]

    def residual(i):
        slot = lax.rem(i, 2)
        gather_end(3, i)
        wait(x_two(i))

        @pl.when(i >= 1)
        def _():
            for pair in (0, 1):
                for core in (0, 1):
                    h1_store(i - 1, 1 - slot, pair, core).wait()

        for pair in (0, 1):
            h1 = nn(r[0, rows_at(i), pl.ds(0, width)], wof[pair]) + cs2[pair].astype(F32)
            da2f[slot, pair, c] = h1.astype(BF)

            @pl.when(y == pair)
            def _(h1=h1):
                dh1s[i] = h1
        remote(da2f.at[slot, :, c], da2f.at[slot, :, c], f_sem, c_dev, slot).start()

        @pl.when(i + 1 < chunks)
        def _():
            start(x_two(i + 1))

    def cot_turn(i):
        gather_end(1, i)
        start(cot_load(i))
        wait(cot_load(i))
        at = pl.multiple_of(i * chunk, chunk)
        for q in range(4):
            cols = pl.ds(q * local, local)
            lt[0, cols, pl.ds(at, chunk)] = cotc[:, cols].T

    def feed(i):
        slot = lax.rem(i, 2)
        remote(da2f.at[slot, :, c], da2f.at[slot, :, c], f_sem, c_dev, slot).wait()
        for pair in (0, 1):
            for core in (0, 1):
                h1_store(i, slot, pair, core).start()
        normed_to(lambda q, some: da2f[slot, q // 2, q % 2, some, :], 1)
        transposed_to(1, i)
        rows = rows_at(i)
        for lo, n in cuts:
            dbuf[:, pl.ds(0, n)] = nt(dhoc[...], wg[pl.ds(lo, n), :])
            r[2, rows, pl.ds(lo, n)] = nt(dhoc[...], wu[pl.ds(lo, n), :]).astype(BF)

            def by_rows(b, _, lo=lo, n=n):
                cols = pl.ds(lo, n)
                here = pl.ds(pl.multiple_of(b * 64, 64), 64)
                some = pl.ds(pl.multiple_of(i * chunk + b * 64, 64), 64)
                gate = dbuf[here, pl.ds(0, n)]
                up = r[2, some, cols].astype(F32)
                r[0, some, cols] = (gate * jax.nn.sigmoid(gate) * up).astype(BF)
                r[1, some, cols] = gate.astype(BF)
                return 0

            lax.fori_loop(0, chunk // 64, by_rows, 0)

    def hidden_back(piece):
        i = piece // 3

        @pl.when(lax.rem(piece, 3) == 0)
        def _():
            wait(cot_load(i))

        for k, cut in enumerate(cuts):
            pl.when(lax.rem(piece, 3) == k)(functools.partial(hidden_cut, i, *cut))

        @pl.when(jnp.logical_and(lax.rem(piece, 3) == 2, i + 1 < chunks))
        def _():
            start(cot_load(i + 1))

    def hidden_cut(i, lo, n):
        if True:
            cols = pl.ds(lo, n)
            dbuf[:, pl.ds(0, n)] = nt(cotc[...], w0[pl.ds(lo, n), :])

            def by_rows(b, _, cols=cols, n=n):
                some = pl.ds(pl.multiple_of(i * chunk + b * 32, 32), 32)
                dhid = dbuf[pl.ds(pl.multiple_of(b * 32, 32), 32), pl.ds(0, n)]
                gate = r[1, some, cols].astype(F32)
                up = r[2, some, cols].astype(F32)
                sig = jax.nn.sigmoid(gate)
                r[1, some, cols] = (dhid * up * sig * (1.0 + gate * (1.0 - sig))).astype(BF)
                r[2, some, cols] = (dhid * gate * sig).astype(BF)
                return 0

            lax.fori_loop(0, chunk // 32, by_rows, 0)

    def split_store(pair, value, keep, send):
        for side in (0, 1):
            part = value[:, side * local : (side + 1) * local]

            @pl.when(c == side)
            def _(part=part):
                keep[pair] = part

            @pl.when(c != side)
            def _(part=part):
                send[pair] = part.astype(BF)

    def stage_a(i):
        slot = lax.rem(i, 2)
        rows = rows_at(i)
        for pair in (0, 1):
            cols = pl.ds(pair * 2 * local, 2 * local)
            value = nn(r[1, rows, :], wg[:, cols]) + nn(r[2, rows, :], wu[:, cols])
            split_store(pair, value, ck, cs)
        remote(cs, cr.at[slot], c_sem, c_dev, slot).start()

        @pl.when(i == chunks - 1)
        def _():
            start(x_whole())

    def x_whole():
        copies = [load(x_in, wu.at[pl.ds(0, tokens), pl.ds(pl.multiple_of(me * local, 128), local)], l_sem.at[3, 0])]
        for step in range(1, 4):
            q = lax.rem(me + step, 4)
            cols = pl.ds(pl.multiple_of(q * local, 128), local)
            copies.append(load(x_h.at[q], wu.at[pl.ds(0, tokens), cols], l_sem.at[3, step]))
        return copies

    def stage_a1(i):
        @pl.when(i == 0)
        def _():
            wait(x_whole())

        at = pl.multiple_of(i * chunk, chunk)
        normed_to(lambda q, some: wu[pl.ds(at + some.start, some.size), pl.ds(q * local, local)], 0)
        for q in range(4):
            cols = pl.ds(q * local, local)
            wg[cols, pl.ds(at, chunk)] = dhoc[:, cols].T

    def stage_loads(i):
        start(cot_load(i))
        h1_load(i).start()
        bcv_load(i).start()

    def stage_b(i):
        slot = lax.rem(i, 2)
        remote(cs, cr.at[slot], c_sem, c_dev, slot).wait()
        ys[...] = (ck[...] + cr[slot].astype(F32)).astype(BF)
        remote(ys, yr4.at[slot], y_sem, y_dev, slot).start()

    def stage_c(i):
        slot = lax.rem(i, 2)
        remote(ys, yr4.at[slot], y_sem, y_dev, slot).wait()
        da2f[slot, :, c] = (ys[...].astype(F32) + yr4[slot].astype(F32)).astype(BF)
        remote(da2f.at[slot, :, c], da2f.at[slot, :, c], f_sem, c_dev, slot).start()

    def stage_d(i):
        slot = lax.rem(i, 2)
        remote(da2f.at[slot, :, c], da2f.at[slot, :, c], f_sem, c_dev, slot).wait()
        wait(cot_load(i))
        h1_load(i).wait()
        bcv_load(i).wait()
        at = pl.multiple_of(i * chunk, chunk)
        own = pl.ds(pl.multiple_of(me * local, 128), local)

        def by_rows(b, _):
            some = pl.ds(pl.multiple_of(b * 64, 64), 64)
            ssq = jnp.zeros((64, local), F32)
            inner = jnp.zeros((64, local), F32)
            for q in range(4):
                cols = pl.ds(q * local, local)
                h1 = xc[q, some, :].astype(F32)
                ssq += h1 * h1
                inner += da2f[slot, q // 2, q % 2, some, :].astype(F32) * gain(1, q) * h1
            r2 = lax.rsqrt(jnp.sum(ssq, -1, keepdims=True) / width + EPS)
            scale = r2 * r2 * r2 * jnp.sum(inner, -1, keepdims=True) / width

            def grad(q, cols, da2):
                h1 = xc[q, some, :].astype(F32)
                return cotc[some, cols].astype(F32) + r2 * (da2 * gain(1, q)) - h1 * scale

            for q in range(4):
                cols = pl.ds(q * local, local)
                dhoc[some, cols] = grad(q, cols, da2f[slot, q // 2, q % 2, some, :].astype(F32)).astype(BF)
            da2 = da2f[slot, y, c, some, :].astype(F32)
            dh1s[i, some, :] = grad(me, own, da2)
            terms = da2 * xc[me, some, :].astype(F32) * r2
            small_v[pl.ds(8, 8), :] += sum(terms[8 * k : 8 * k + 8] for k in range(8))
            return 0

        lax.fori_loop(0, chunk // 64, by_rows, 0)
        start(x_load(i))
        transposed_to(0, i)
        @pl.when(i == 0)
        def _():
            for q in range(4):
                wo_load(q).wait()

        dmixed = jnp.zeros((chunk, local), F32)
        for q in range(4):
            cols = pl.ds(q * local, local)
            dmixed += nt(dhoc[:, cols], wof[0, cols, :])
        c_gate = bcv[1]
        bxp[pl.ds(0, 8), :] = before_r[i]
        bxp[pl.ds(8, chunk), :] = bcv[3].astype(F32)
        conv, shifts = conv_of()
        r[0, pl.ds(at, chunk), pl.ds(0, local)] = (c_gate.astype(F32) * conv).astype(BF)
        r[0, pl.ds(at, chunk), pl.ds(2 * local, local)] = (dmixed * conv).astype(BF)
        dconv = (dmixed * c_gate.astype(F32)).astype(BF).astype(F32)
        dcp[pl.ds(0, chunk), :] = dconv
        halo_s[i] = dconv[:8]
        for k in range(3):
            small_v[1 + k : 2 + k, :] += jnp.sum(dconv * shifts[k], 0, keepdims=True)

        @pl.when(z > 0)
        def _():
            halo_copy(i).start()

    def halo_copy(i):
        return remote(halo_s.at[i], halo_r.at[i], halo_sem, dn_dev, i)

    def stage_e(i):
        slot = lax.rem(i, 2)

        @pl.when(i == 0)
        def _():
            for k in range(3):
                wi_load(k).wait()
            out_copy(chunks - 1).wait()

        wait(x_load(i))

        @pl.when(z > 0)
        def _():
            halo_copy(i).wait_send()

        @pl.when(z < last)
        def _():
            halo_copy(i).wait_recv()
            dcp[pl.ds(chunk, 8), :] = halo_r[i]

        @pl.when(z == last)
        def _():
            dcp[pl.ds(chunk, 8), :] = jnp.zeros((8, local), F32)

        dbx = sum(own_v[4 - k : 5 - k, :] * dcp[pl.ds(k, chunk), :] for k in range(3))
        rows = rows_at(i)
        r[0, rows, pl.ds(local, local)] = (dbx * bcv[2].astype(F32)).astype(BF)
        r[0, rows, pl.ds(3 * local, local)] = (dbx * bcv[0].astype(F32)).astype(BF)
        inner = jnp.zeros((chunk, 1), F32)
        ssq = jnp.zeros((chunk, 1), F32)
        for pair in (0, 1):
            cols = pl.ds(pair * 2 * local, 2 * local)
            value = nt(r[0, rows, pl.ds(local, 3 * local)], w0[cols, pl.ds(0, 3 * local)])
            for side in (0, 1):
                q = 2 * pair + side
                x = xc[q].astype(F32)
                part = value[:, side * local : (side + 1) * local]
                inner += jnp.sum(part * x * gain(0, q), -1, keepdims=True)
                ssq += jnp.sum(x * x, -1, keepdims=True)
            split_store(pair, value, ck2, cs2)
        xo[...] = xc[me]
        ins[...] = jnp.broadcast_to(inner, (chunk, 128)).T[:8]
        r1s[...] = jnp.broadcast_to(lax.rsqrt(ssq / width + EPS), r1s.shape)
        remote(cs2, yr4.at[2 + slot], c2_sem, c_dev, slot).start()
        remote(ins, inr.at[slot], i_sem, c_dev, slot).start()

        @pl.when(i + 1 < chunks)
        def _():
            stage_loads(i + 1)

    def stage_f(i):
        slot = lax.rem(i, 2)
        remote(cs2, yr4.at[2 + slot], c2_sem, c_dev, slot).wait()
        remote(ins, inr.at[slot], i_sem, c_dev, slot).wait()
        ys2[...] = (ck2[1 - y] + yr4[2 + slot, 1 - y].astype(F32)).astype(BF)
        qk2[...] = ck2[y] + yr4[2 + slot, y].astype(F32)
        iys[...] = ins[...] + inr[slot]
        remote(ys2, yr2.at[slot], y2_sem, y_dev, slot).start()
        remote(iys, iyr.at[slot], iy_sem, y_dev, slot).start()

    def gx_copy(i):
        return load(gxb, gx_h.at[rows_at(i), :], gx_sem)

    def stage_g(i):
        slot = lax.rem(i, 2)
        remote(ys2, yr2.at[slot], y2_sem, y_dev, slot).wait()
        remote(iys, iyr.at[slot], iy_sem, y_dev, slot).wait()
        da1 = qk2[...] + yr2[slot].astype(F32)
        inner = jnp.broadcast_to(iys[:1] + iyr[slot, :1], (128, chunk)).T[:, :1]
        r1 = r1s[:, :1]
        x = xo[...].astype(F32)
        scaled = gain(0, me)
        small_v[0:1, :] += jnp.sum(da1 * x * r1, 0, keepdims=True)

        @pl.when(i > 0)
        def _():
            gx_copy(i - 1).wait()

        gxb[...] = (dh1s[i] + r1 * scaled * da1 - x * (r1 * r1 * r1 * inner / width)).astype(BF)
        gx_copy(i).start()

    def out_start(i):
        rows = rows_at(i)
        for pair in (0, 1):
            cols = pl.ds(pair * 2 * local, 2 * local)
            split_store(pair, nn(r[0, rows, :], w0[:, cols]), ck2, cs2)
        remote(cs2, yr4.at[2 + lax.rem(i, 2)], c2_sem, c_dev, lax.rem(i, 2)).start()

        @pl.when(i == chunks - 1)
        def _():
            for k in range(3):
                wi_load(k).start()

    def out_share(i):
        slot = lax.rem(i, 2)
        remote(cs2, yr4.at[2 + slot], c2_sem, c_dev, slot).wait()
        ys2[...] = (ck2[1 - y] + yr4[2 + slot, 1 - y].astype(F32)).astype(BF)
        qk2[...] = ck2[y] + yr4[2 + slot, y].astype(F32)
        remote(ys2, yr2.at[slot], y2_sem, y_dev, slot).start()

    def out_copy(i):
        return load(gxb, out_h.at[rows_at(i), :], gx_sem)

    def out_end(i):
        slot = lax.rem(i, 2)
        remote(ys2, yr2.at[slot], y2_sem, y_dev, slot).wait()

        @pl.when(i > 0)
        def _():
            out_copy(i - 1).wait()

        gxb[...] = (dh1s[i] + (qk2[...] + yr2[slot].astype(F32))).astype(BF)
        out_copy(i).start()

    def valid(i, f):
        @pl.when(jnp.logical_and(i >= 0, i < chunks))
        def _():
            f(i)

    gather_pass(0, 0)
    gather(0, 1, 0).start()
    wy().start()
    gather_pass(2, 0)
    for k in range(3):
        wi_load(k).wait()
    gather_end(2, 0)

    gather_end(0, 0)
    start(x_load(0))

    def forward(j, _):
        @pl.when(j < chunks)
        def _():
            project(j)

        @pl.when(j + 1 < chunks)
        def _():
            gather_pass(0, j + 1)

        @pl.when(j + 2 < chunks)
        def _():
            gather(0, j + 2, 0).start()

        pl.when(j == 0)(lambda: wo_step(0))
        pl.when(j == 1)(lambda: wo_step(2))

        @pl.when(j == chunks)
        def _():
            cot_turn(0)

        @pl.when(j == chunks + 1)
        def _():
            cot_turn(1)

        @pl.when(j == chunks + 2)
        def _():
            cot_turn(2)

        @pl.when(j == 3)
        def _():
            wg_load.wait()
            wu_load.wait()

        @pl.when(j >= 3)
        def _():
            feed(j - 3)

        @pl.when(j < chunks)
        def _():
            mix(j)

        @pl.when(j + 1 < chunks)
        def _():
            gather_end(0, j + 1)
            start(x_load(j + 1))

        pl.when(j == 0)(lambda: wo_step(1))
        pl.when(j == 1)(lambda: wo_step(3))

        @pl.when(jnp.logical_and(j > 0, j < chunks))
        def _():
            gather_pass(3, j - 1)

        @pl.when(j == 2)
        def _():
            wo_end()
            start(x_two(0))
            for i in range(chunks):
                gather(1, i, 1).start()
            for i in range(2):
                gather(1, i, 0).start()
            for kind, src in ((0, wo_h), (1, woy_h)):
                for one in wo_columns(src, me if kind == 0 else (1 - y) * 2 + c, kind):
                    one.wait()

        @pl.when(j == chunks - 1)
        def _():
            wd_load.start()

        @pl.when(jnp.logical_and(j >= 2, j < chunks + 2))
        def _():
            residual(j - 2)

        @pl.when(j == 3)
        def _():
            for k in range(2):
                gather_pass(1, k)
            for k in range(2, chunks):
                gather(1, k, 0).start()

        @pl.when(j == chunks)
        def _():
            gather_pass(3, chunks - 1)
            for k in range(2, chunks):
                gather_pass(1, k)

        return 0

    lax.fori_loop(0, chunks + 3, forward, 0)
    for q in range(4):
        wo_load(q).start()
    bcv_store(chunks - 1).wait()
    for pair in (0, 1):
        for core in (0, 1):
            h1_store(chunks - 1, (chunks - 1) % 2, pair, core).wait()

    cot_turn(chunks - 1)
    start(cot_load(0))

    def small_x():
        return pltpu.make_async_remote_copy(
            src_ref=small_v.at[pl.ds(0, 8)], dst_ref=small_r.at[0], send_sem=small_sem.at[0, 0],
            recv_sem=small_sem.at[0, 1], device_id=x_dev, device_id_type=MESH,
        )

    def small_z(way):
        return pltpu.make_async_remote_copy(
            src_ref=small_r.at[1 + way], dst_ref=small_r.at[3 + way], send_sem=small_sem.at[1 + way, 0],
            recv_sem=small_sem.at[1 + way, 1], device_id=dn_dev if way else up_dev, device_id_type=MESH,
        )

    def small_step(k):
        @pl.when(k == 0)
        def _():
            small_x().wait()
            total = small_v[pl.ds(0, 8), :] + small_r[0]
            small_v[pl.ds(0, 8), :] = total
            small_r[1] = total
            small_r[2] = total

        for way in (0, 1):
            turn = last - z if way else z

            @pl.when(jnp.logical_and(turn < last, k == turn))
            def _(way=way, turn=turn):
                @pl.when(turn > 0)
                def _():
                    small_z(way).wait_recv()
                    small_r[1 + way] = small_v[pl.ds(0, 8), :] + small_r[3 + way]

                small_z(way).start()

    def small_end():
        for way in (0, 1):
            turn = last - z if way else z

            @pl.when(turn < last)
            def _(way=way):
                small_z(way).wait_send()

            @pl.when(turn == last)
            def _(way=way):
                small_z(way).wait_recv()

            @pl.when(turn > 0)
            def _(way=way):
                small_v[pl.ds(0, 8), :] += small_r[3 + way]

    def stage_last(i):
        stage_g(i)

        @pl.when(i == chunks - 1)
        def _():
            small_v[4:5, :] = jnp.sum(small_v[8:16, :], 0, keepdims=True)
            small_x().start()

    order = (
        ("g", stage_last), ("out_end", out_end), ("out_share", out_share), ("b", stage_b), ("f", stage_f),
        ("c", stage_c), ("e", stage_e), ("d", stage_d), ("out_start", out_start), ("a", stage_a),
        ("hidden", None), ("a1", stage_a1),
    )

    def stages(t, third):
        for name, f in order:
            if name == "hidden":
                if HIDDEN[0] != third:
                    continue
                done = 0
                low = high = 0
                for at, upto in HIDDEN[1].items():
                    low = jnp.where(t == at, done, low)
                    high = jnp.where(t == at, upto, high)
                    done = upto

                def piece(k, _):
                    hidden_back(k)
                    return 0

                lax.fori_loop(low, high, piece, 0)
            elif PLACES[name][0] == third:
                where = PLACES[name][1]
                i = sum(jnp.where(t >= at, 1, 0) for at in where[1:])
                now = functools.reduce(jnp.logical_or, [t == at for at in where])
                pl.when(now)(functools.partial(f, i))

    def each_tick(t, _):
        tick_a(t, True)

        @pl.when(t == 0)
        def _():
            wd_load.wait()

        @pl.when(t == beat)
        def _():
            stage_loads(0)

        stages(t, 0)
        tick_b(t)
        stages(t, 1)
        tick_c(t)
        stages(t, 2)

        @pl.when(t > PLACES["g"][1][-1])
        def _():
            small_step(t - PLACES["g"][1][-1] - 1)

        return 0

    lax.fori_loop(0, ticks, each_tick, 0)
    gx_copy(chunks - 1).wait()

    def part_four(k, _):
        tick_a(ticks + k)
        tick_b(ticks + k)
        tick_c(ticks + k)
        return 0

    lax.fori_loop(0, LAG + 4, part_four, 0)
    small_end()
    plain_out(ticks - 2, "wait")
    plain_out(ticks - 1, "wait")
    out_do(ob.at[2], 3 * beat + SECOND, 2, "wait")


def block(dims, x_own, cot_own, gain_mix, gain_ff, taps, wd, wg, wu, wo, wi):
    tokens, chunk, width, ff, local, nseq = dims
    rows = width // (2 * nseq)
    chunks = tokens // chunk
    last = nseq - 1
    m = ROWS * nseq
    DMA = pltpu.SemaphoreType.DMA
    shape = jax.ShapeDtypeStruct
    third = ff // 3 // 128 * 128
    scratch = [
        pltpu.VMEM((2, width, tokens), BF),
        pltpu.VMEM((3, tokens, ff), BF),
        pltpu.VMEM((ff, width), BF),
        pltpu.VMEM((ff, width), BF),
        pltpu.VMEM((ff, width), BF),
        pltpu.VMEM((2, width, local), BF),
        pltpu.VMEM((chunk, width), BF),
        pltpu.VMEM((4, chunk, local), BF),
        pltpu.VMEM((chunk, local), BF),
        pltpu.VMEM((4, chunk, local), BF),
        pltpu.VMEM((8 + chunk, local), F32),
        pltpu.VMEM((chunk, ff - 2 * third), F32),
        pltpu.VMEM((8 + chunk, local), F32),
        pltpu.VMEM((chunk, width), BF),
        pltpu.VMEM((chunks, chunk, local), F32),
        pltpu.VMEM((chunk, 128), F32),
        pltpu.VMEM((4, 8, local), F32),
        pltpu.VMEM((8, local), F32),
        pltpu.VMEM((3, m, ff), BF),
        pltpu.VMEM((5, m, ff), BF),
        pltpu.VMEM((LAG + 4, m, ff), BF),
        pltpu.VMEM((2, 2 * last, ROWS, ff), BF),
        pltpu.VMEM((2, 3 * last + 2, ROWS, ff), BF),
        pltpu.VMEM((3, ROWS, ff), BF),
        pltpu.VMEM((ROWS, ff), BF),
        pltpu.VMEM((ROWS, ff), BF),
        pltpu.VMEM((ROWS, ff), F32),
        pltpu.VMEM((5, chunk, local), F32),
        pltpu.VMEM((2, chunk, local), BF),
        pltpu.VMEM((2, 2, chunk, local), BF),
        pltpu.VMEM((2, chunk, local), BF),
        pltpu.VMEM((4, 2, chunk, local), BF),
        pltpu.VMEM((2, 2, 2, chunk, local), BF),
        pltpu.VMEM((2, chunk, local), BF),
        pltpu.VMEM((chunk, local), BF),
        pltpu.VMEM((2, chunk, local), BF),
        pltpu.VMEM((8, chunk), F32),
        pltpu.VMEM((2, 8, chunk), F32),
        pltpu.VMEM((8, chunk), F32),
        pltpu.VMEM((2, 8, chunk), F32),
        pltpu.VMEM((chunk, local), BF),
        pltpu.VMEM((chunks, 8, local), F32),
        pltpu.VMEM((chunks, 8, local), F32),
        pltpu.VMEM((chunks, 8, local), F32),
        pltpu.VMEM((chunks, 8, local), F32),
        pltpu.VMEM((5, 8, local), F32),
        DMA((3,)), DMA((5,)), DMA((2, 2 * last)), DMA((2, 3 * last + 2)), DMA((3, 4)),
        DMA((2, 2)), DMA((2, chunks)), DMA((2, 2)), DMA((2, 2)), DMA((2, 2)),
        DMA((2, 2)), DMA((2, 2)), DMA((2, chunks)), DMA((2, chunks)), DMA((3, 2, 4, chunks)),
        DMA((7,)), DMA((4, 4)), DMA(()), DMA((2, 2)), DMA(()), DMA((3, 2)), DMA((2,)), DMA((2,)), DMA((2, nseq)), DMA((2, 2, last)), DMA((2, 4)), DMA((4,)),
    ]
    return pl.pallas_call(
        functools.partial(block_kernel, dims),
        out_shape=(
            shape((rows, ff), BF), shape((rows, ff), BF), shape((rows, ff), BF),
            shape((rows, local), BF), shape((3, rows, local), BF),
            shape((tokens, local), BF), shape((tokens, local), BF), shape((16, local), F32),
            shape((4, tokens, local), BF), shape((4, tokens, local), BF),
            shape((4, tokens, local), BF), shape((4, tokens, local), BF), shape((local, width), BF),
        ),
        in_specs=[ANY] * 2 + [VMEM] * 3 + [ANY] * 5,
        out_specs=(ANY,) * 7 + (VMEM,) + (ANY,) * 5,
        scratch_shapes=scratch,
        compiler_params=pltpu.CompilerParams(
            collective_id=0, has_side_effects=True, vmem_limit_bytes=63 * 2**20
        ),
    )(x_own, cot_own, gain_mix, gain_ff, taps, wd, wg, wu, wo, wi)


def shifted(array, axis, by):
    count = lax.axis_size(axis)
    pairs = [(i, i + by) for i in range(count) if 0 <= i + by < count]
    return lax.ppermute(array, axis, pairs)


def fused_device(inputs, gain_mix, w_in, kernel, w_out, gain_ff, w_gate, w_up, w_down, cotangent):
    groups, seq_rows, local = inputs.shape
    width = local * lax.axis_size("mp")
    ff = w_down.shape[0]
    tokens = groups * seq_rows
    dims = (tokens, seq_rows, width, ff, local, lax.axis_size("seq"))
    gdown, ggate, gup, gout, gin, gx, out, small = block(
        dims, inputs.reshape(tokens, local), cotangent.reshape(tokens, local), gain_mix, gain_ff, kernel,
        w_down, w_gate.T, w_up.T, w_out, w_in.transpose(1, 0, 2),
    )[:8]
    gdown, ggate, gup, gout, gin, gx, out, gmix, gtaps, gff = widen(
        gdown, ggate, gup, gout, gin, gx, out, small
    )
    whole = (groups, seq_rows, local)
    return (
        out.reshape(whole), gx.reshape(whole), gmix, gin.transpose(1, 0, 2), gtaps,
        gout.T, gff, ggate, gup, gdown.T,
    )


def widen_kernel(*refs):
    count = 7
    src, small, dst = refs[:count], refs[count], refs[count + 1 : 2 * count + 1]
    gmix, gtaps, gff = refs[2 * count + 1 : 2 * count + 4]
    narrow = refs[2 * count + 4 : 3 * count + 4]
    wide = refs[3 * count + 4 : 4 * count + 2]
    in_sem, out_sem = refs[4 * count + 2 :]
    loads = [pltpu.make_async_copy(src[k], narrow[k], in_sem.at[k]) for k in range(count)]
    stores = [
        pltpu.make_async_copy(wide[k] if k < count - 2 else narrow[k], dst[k], out_sem.at[k])
        for k in range(count)
    ]
    for one in loads:
        one.start()
    gmix[...] = small[0:1, :].reshape(gmix.shape)
    gtaps[...] = small[1:4, :]
    gff[...] = small[4:5, :].reshape(gff.shape)
    for k in range(count):
        loads[k].wait()
        if k < count - 2:
            wide[k][...] = narrow[k][...].astype(F32)
        stores[k].start()
    for one in stores:
        one.wait()


def widen(*arrays):
    big, small = arrays[:7], arrays[7]
    local = small.shape[1]
    shape = jax.ShapeDtypeStruct
    outs = [shape(a.shape, F32 if k < 5 else BF) for k, a in enumerate(big)]
    outs += [shape((local,), F32), shape((3, local), F32), shape((local,), F32)]
    return pl.pallas_call(
        widen_kernel,
        out_shape=outs,
        in_specs=[ANY] * 7 + [VMEM],
        out_specs=[ANY] * 7 + [VMEM] * 3,
        scratch_shapes=[pltpu.VMEM(a.shape, BF) for a in big]
        + [pltpu.VMEM(a.shape, F32) for a in big[:5]]
        + [pltpu.SemaphoreType.DMA((7,))] * 2,
        compiler_params=pltpu.CompilerParams(vmem_limit_bytes=63 * 2**20),
    )(*big, small)


def contract_rows(left, right):
    return lax.dot_general(
        left, right, (((0,), (0,)), ((), ())), preferred_element_type=jnp.float32
    )


def contract_cols(left, right):
    return lax.dot_general(
        left, right, (((1,), (1,)), ((), ())), preferred_element_type=jnp.float32
    )


def plain_device(inputs, gain_mix, w_in, kernel, w_out, gain_ff, w_gate, w_up, w_down, cotangent):
    groups, seq_rows, local_width = inputs.shape
    full_width = local_width * lax.axis_size("mp")
    tokens = groups * seq_rows
    x_float = inputs.reshape(tokens, local_width).astype(jnp.float32)
    gain_one = gain_mix.astype(jnp.float32)
    gain_two = gain_ff.astype(jnp.float32)
    taps = kernel.astype(jnp.float32)

    def row_total(values):
        return lax.psum(jnp.sum(values, axis=-1, keepdims=True), "mp")

    def all_features(values):
        return lax.all_gather(values, "mp", axis=1, tiled=True)

    def share_sums(values):
        return lax.psum_scatter(
            values.astype(jnp.bfloat16), "mp", scatter_dimension=1, tiled=True
        ).astype(jnp.float32)

    def scattered(values, dim):
        return lax.psum_scatter(
            values.astype(jnp.bfloat16), ("dp", "seq"), scatter_dimension=dim, tiled=True
        ).astype(jnp.float32)

    def norm_scale(values):
        return lax.rsqrt(row_total(values * values) / full_width + EPS)

    def norm_back(values, scale, gain_vec, upstream):
        inner = row_total(gain_vec * upstream * values)
        grad_values = scale * gain_vec * upstream - values * scale**3 * inner / full_width
        return (grad_values, jnp.sum(upstream * values * scale, axis=0))

    scale_one = norm_scale(x_float)
    normed_in = all_features((x_float * scale_one * gain_one).astype(jnp.bfloat16))
    proj = jnp.einsum("td,dkc->tkc", normed_in, w_in, preferred_element_type=jnp.float32)
    b_gate = proj[:, 0]
    c_gate = proj[:, 1]
    values_v = proj[:, 2]
    b_times_x = (b_gate * values_v).astype(jnp.bfloat16).reshape(groups, seq_rows, local_width)
    before = shifted(b_times_x[:, seq_rows - 2 :], "seq", 1)
    padded = jnp.concatenate([before, b_times_x], 1).astype(jnp.float32)
    conv = taps[0] * padded[:, :-2] + taps[1] * padded[:, 1:-1] + taps[2] * padded[:, 2:]
    conv = conv.reshape(tokens, local_width)
    mixed = (c_gate * conv).astype(jnp.bfloat16)
    hidden_one = x_float + share_sums(jnp.dot(mixed, w_out, preferred_element_type=jnp.float32))
    scale_two = norm_scale(hidden_one)
    normed_ff = all_features((hidden_one * scale_two * gain_two).astype(jnp.bfloat16))
    gate = jnp.dot(normed_ff, w_gate, preferred_element_type=jnp.float32)
    up_proj = jnp.dot(normed_ff, w_up, preferred_element_type=jnp.float32)
    sigma = jax.nn.sigmoid(gate)
    active = gate * sigma
    hidden = (active * up_proj).astype(jnp.bfloat16)
    ffn_out = share_sums(jnp.dot(hidden, w_down, preferred_element_type=jnp.float32))
    block_out = (hidden_one + ffn_out).astype(jnp.bfloat16).reshape(groups, seq_rows, local_width)
    grad_flat = cotangent.reshape(tokens, local_width)
    grad_full = all_features(grad_flat)
    grad_down = contract_rows(hidden, grad_full)
    grad_hidden = contract_cols(grad_full, w_down)
    grad_gate_act = (grad_hidden * up_proj * sigma * (1.0 + gate * (1.0 - sigma))).astype(
        jnp.bfloat16
    )
    grad_up_act = (grad_hidden * active).astype(jnp.bfloat16)
    grad_gate = contract_rows(normed_ff, grad_gate_act)
    grad_up = contract_rows(normed_ff, grad_up_act)
    grad_normed_ff = share_sums(
        contract_cols(grad_gate_act, w_gate) + contract_cols(grad_up_act, w_up)
    )
    grad_norm_two, grad_gain_two = norm_back(hidden_one, scale_two, gain_two, grad_normed_ff)
    grad_hidden_one = grad_flat.astype(jnp.float32) + grad_norm_two
    grad_out_full = all_features(grad_hidden_one.astype(jnp.bfloat16))
    grad_out = contract_rows(mixed, grad_out_full)
    grad_mixed = contract_cols(grad_out_full, w_out)
    grad_c = grad_mixed * conv
    grad_conv = (grad_mixed * c_gate).astype(jnp.bfloat16).reshape(groups, seq_rows, local_width)
    after = shifted(grad_conv[:, :2], "seq", -1)
    extended = jnp.concatenate([grad_conv, after], 1).astype(jnp.float32)
    grad_bx = taps[2] * extended[:, :-2] + taps[1] * extended[:, 1:-1] + taps[0] * extended[:, 2:]
    grad_bx = grad_bx.reshape(tokens, local_width)
    conv_grad_float = extended[:, :-2]
    grad_taps = jnp.stack(
        [
            jnp.sum(conv_grad_float * padded[:, :-2], axis=(0, 1)),
            jnp.sum(conv_grad_float * padded[:, 1:-1], axis=(0, 1)),
            jnp.sum(conv_grad_float * padded[:, 2:], axis=(0, 1)),
        ]
    )
    grad_proj = jnp.stack([grad_bx * values_v, grad_c, grad_bx * b_gate], 1).astype(jnp.bfloat16)
    grad_in = jnp.einsum("td,tkc->dkc", normed_in, grad_proj, preferred_element_type=jnp.float32)
    grad_normed_in = share_sums(
        jnp.einsum("tkc,dkc->td", grad_proj, w_in, preferred_element_type=jnp.float32)
    )
    grad_norm_one, grad_gain_one = norm_back(x_float, scale_one, gain_one, grad_normed_in)
    grad_input = (
        (grad_hidden_one + grad_norm_one)
        .astype(jnp.bfloat16)
        .reshape(groups, seq_rows, local_width)
    )
    small_sums = lax.psum((grad_gain_one, grad_taps, grad_gain_two), ("dp", "seq"))
    by_row = (
        scattered(grad_in, 0),
        scattered(grad_gate, 0),
        scattered(grad_up, 0),
    )
    by_col = (
        scattered(grad_out, 1),
        scattered(grad_down, 1),
    )
    return (
        block_out,
        grad_input,
        small_sums[0],
        by_row[0],
        small_sums[1],
        by_col[0],
        small_sums[2],
        by_row[1],
        by_row[2],
        by_col[1],
    )


def solution(mesh):
    placed = (
        P("dp", "seq", "mp"),
        P("mp"),
        P(None, None, "mp"),
        P(None, "mp"),
        P("mp", None),
        P("mp"),
        P(None, "mp"),
        P(None, "mp"),
        P("mp", None),
        P("dp", "seq", "mp"),
    )
    sizes = mesh.shape
    fused = sizes["dp"] == 2 and sizes["seq"] == 4 and sizes["mp"] == 4
    return jax.shard_map(
        fused_device if fused else plain_device,
        mesh=mesh,
        in_specs=placed,
        out_specs=(
            P("dp", "seq", "mp"),
            P("dp", "seq", "mp"),
            P("mp"),
            P(("dp", "seq"), None, "mp"),
            P(None, "mp"),
            P("mp", ("dp", "seq")),
            P("mp"),
            P(("dp", "seq"), "mp"),
            P(("dp", "seq"), "mp"),
            P("mp", ("dp", "seq")),
        ),
        check_vma=False,
    )
```

```python
import functools

import jax
import jax.numpy as jnp
from jax import lax
from jax.experimental import pallas as pl
from jax.experimental.pallas import tpu as pltpu
from jax.sharding import PartitionSpec as P

EPS = 1e-05
MESH = pl.DeviceIdType.MESH
BF = jnp.bfloat16
F32 = jnp.float32
ROWS = 32
SECOND = 3
LAG = 3
WAIT = 3
PLACES = {
    "out_start": (2, (1, 4, 7, 8)),
    "out_share": (2, (2, 5, 8, 10)),
    "out_end": (1, (4, 7, 9, 12)),
    "a": (2, (3, 8, 10, 14)),
    "b": (2, (4, 9, 12, 15)),
    "c": (1, (8, 11, 14, 18)),
    "d": (2, (9, 13, 17, 19)),
    "e": (2, (12, 15, 18, 20)),
    "f": (2, (14, 16, 19, 21)),
    "g": (2, (15, 18, 20, 22)),
    "a1": (2, (15, 16, 17, 19)),
}
HIDDEN = (1, {2: 3, 3: 4, 4: 5, 5: 7, 6: 12})
ANY = pl.BlockSpec(memory_space=pl.ANY)
VMEM = pl.BlockSpec(memory_space=pltpu.VMEM)


def nn(left, right):
    return lax.dot_general(left, right, (((1,), (0,)), ((), ())), preferred_element_type=F32)


def nt(left, right):
    return lax.dot_general(left, right, (((1,), (1,)), ((), ())), preferred_element_type=F32)


def block_kernel(
    dims,
    x_in, cot_in, gain_mix_v, gain_ff_v, taps_v, wd_h, wg_h, wu_h, wo_h, wi_h,
    gdown_h, ggate_h, gup_h, gout_h, gin_h, gx_h, out_h, small_v,
    x_h, cot_h, h1_h, bcv_h, woy_h,
    lt, r, w0, wg, wu, wof, cotc, xc, xo, bcv, bxp, dbuf, dcp, dhoc, dh1s, r1s, gv, own_v,
    xs, xr, s_buf, zs, zr, ob, vs, vr, vk,
    kf, cs, cr, ys, yr4, da2f, cs2, ys2, yr2,
    ins, inr, iys, iyr, gxb, halo_s, halo_r, before_s, before_r, small_r,
    xs_sem, xr_sem, zs_sem, zr_sem, ob_sem, c_sem, y_sem, f_sem, c2_sem, y2_sem,
    i_sem, iy_sem, halo_sem, before_sem, gather_sem, w_sem, l_sem, bcv_sem, h1_sem, gx_sem,
    small_sem, v_sem, wy_sem, wx_sem, wz_sem, wc_sem, wl_sem,
):
    tokens, chunk, width, ff, local, nseq = dims
    chunks = tokens // chunk
    block = width // (2 * nseq)
    per = block // ROWS
    beat = per + 1
    ticks = 4 * beat
    p = lax.axis_index("dp")
    z = lax.axis_index("seq")
    me = lax.axis_index("mp")
    y, c = me // 2, me % 2
    x_dev = {"dp": 1 - p}
    up_dev = {"seq": z + 1}
    dn_dev = {"seq": z - 1}
    y_dev = {"mp": (1 - y) * 2 + c}
    c_dev = {"mp": y * 2 + 1 - c}
    last = nseq - 1
    ck, ck2, qk2 = kf.at[pl.ds(0, 2)], kf.at[pl.ds(2, 2)], kf.at[4]
    third = ff // 3 // 128 * 128
    cuts = ((0, third), (third, third), (2 * third, ff - 2 * third))

    def remote(src, dst, sems, where, at=None):
        s_sem, r_sem = (sems.at[0], sems.at[1]) if at is None else (sems.at[0, at], sems.at[1, at])
        return pltpu.make_async_remote_copy(
            src_ref=src, dst_ref=dst, send_sem=s_sem, recv_sem=r_sem,
            device_id=where, device_id_type=MESH,
        )

    def load(src, dst, sem):
        return pltpu.make_async_copy(src, dst, sem)

    def wi_load(k):
        return load(wi_h.at[k], w0.at[pl.ds(0, width), pl.ds(k * local, local)], w_sem.at[k])

    wd_load = load(wd_h, w0, w_sem.at[3])
    wg_load = load(wg_h, wg, w_sem.at[4])
    wu_load = load(wu_h, wu, w_sem.at[5])
    def wo_load(q):
        return load(wo_h.at[:, pl.ds(q * local, local)], wof.at[0, pl.ds(q * local, local), :], wl_sem.at[q])

    for k in range(3):
        wi_load(k).start()
    own_v[0:1, :] = gain_mix_v[...].astype(F32).reshape(1, local)
    own_v[1:2, :] = gain_ff_v[...].astype(F32).reshape(1, local)
    own_v[2:5, :] = taps_v[...].astype(F32)
    own_v[5:8, :] = jnp.zeros((3, local), F32)
    gv[me] = own_v[...]

    barrier = pltpu.get_barrier_semaphore()
    for dev in (x_dev, y_dev, c_dev):
        pl.semaphore_signal(barrier, inc=1, device_id=dev, device_id_type=MESH)

    @pl.when(z < last)
    def _():
        pl.semaphore_signal(barrier, inc=1, device_id=up_dev, device_id_type=MESH)

    @pl.when(z > 0)
    def _():
        pl.semaphore_signal(barrier, inc=1, device_id=dn_dev, device_id_type=MESH)

    peers = 3 + jnp.where(z < last, 1, 0) + jnp.where(z > 0, 1, 0)
    pl.semaphore_wait(barrier, peers)

    small_v[...] = jnp.zeros_like(small_v)

    def rows_at(i):
        return pl.ds(pl.multiple_of(i * chunk, chunk), chunk)

    def mixed_at(q, i):
        return r.at[0, rows_at(i), pl.ds(pl.multiple_of(q * local, 128), local)]

    share = local // (2 * nseq)

    def piece(zz):
        return woy_h.at[pl.ds(pl.multiple_of((p * nseq + zz) * share, 16), share), :]

    def wy():
        mine = wo_h.at[pl.ds(pl.multiple_of((p * nseq + z) * share, 16), share), :]
        return pltpu.make_async_remote_copy(
            src_ref=mine, dst_ref=piece(z), send_sem=wy_sem.at[0], recv_sem=wy_sem.at[1],
            device_id=y_dev, device_id_type=MESH,
        )

    def wx(zz):
        return remote(piece(zz), piece(zz), wx_sem, x_dev, zz)

    def wz(way, step):
        part = piece(z + step if way else z - step)
        return pltpu.make_async_remote_copy(
            src_ref=part, dst_ref=part, send_sem=wz_sem.at[0, way, step], recv_sem=wz_sem.at[1, way, step],
            device_id=dn_dev if way else up_dev, device_id_type=MESH,
        )

    def wz_sends(way, step):
        return jnp.logical_and(z > 0, z + step <= last) if way else jnp.logical_and(z < last, z >= step)

    def wz_receives(way, step):
        return z + 1 + step <= last if way else z >= step + 1

    def wo_step(step):
        if step == 0:
            wy().wait_recv()
            wx(z).start()
        for way in (0, 1):
            if step > 0:
                @pl.when(wz_receives(way, step - 1))
                def _(way=way):
                    wz(way, step - 1).wait_recv()
                    wx(z + step if way else z - step).start()
            if step < last:
                @pl.when(wz_sends(way, step))
                def _(way=way):
                    wz(way, step).start()

    def wo_columns(src, q, kind):
        rows = pl.ds(pl.multiple_of(q * local, 128), local)
        for pair in (0, 1):
            cols = pl.ds(pl.multiple_of((2 * pair + c) * local, 128), local)
            yield load(src.at[:, cols], wof.at[pair, rows, :], wl_sem.at[2 * kind + pair])
            cols = pl.ds(pl.multiple_of((2 * pair + 1 - c) * local, 128), local)
            yield remote(src.at[:, cols], wof.at[pair, rows, :], wc_sem, c_dev, 2 * kind + pair)

    def wo_end():
        wy().wait_send()
        for zz in range(nseq):
            wx(zz).wait()
        for way in (0, 1):
            for step in range(last):
                @pl.when(wz_sends(way, step))
                def _(way=way, step=step):
                    wz(way, step).wait_send()
        for one in wo_columns(woy_h, (1 - y) * 2 + c, 1):
            one.start()

    def gather(which, i, leg):
        if which == 2:
            src = mine = own_v
            dst = gv
            at = (2, 0)
        elif which == 3:
            mine = mixed_at(me, i)
            at = (3, i)
        else:
            src, dst = (x_in, x_h) if which == 0 else (cot_in, cot_h)
            mine = src.at[rows_at(i), :]
            at = (which, i)
        if which == 3:
            slot = lambda q: mixed_at(q, i)
        else:
            slot = (lambda q: dst.at[q]) if which == 2 else (lambda q: dst.at[q, rows_at(i), :])
        sems = [gather_sem.at[leg, way, at[0], at[1]] for way in (0, 1)]
        if leg == 0:
            pair, where = (mine, slot(me)), y_dev
        elif leg == 1:
            pair, where = (mine, slot(me)), c_dev
        else:
            from_y = (1 - y) * 2 + c
            pair, where = (slot(from_y), slot(from_y)), c_dev
        return pltpu.make_async_remote_copy(
            src_ref=pair[0], dst_ref=pair[1], send_sem=sems[0], recv_sem=sems[1],
            device_id=where, device_id_type=MESH,
        )

    def gather_start(which, i):
        gather(which, i, 0).start()
        gather(which, i, 1).start()

    def gather_pass(which, i):
        gather(which, i, 0).wait_recv()
        gather(which, i, 2).start()

    def gather_end(which, i):
        gather(which, i, 0).wait_send()
        gather(which, i, 1).wait()
        gather(which, i, 2).wait()

    gather(0, 0, 0).start()
    gather_start(2, 0)
    for i in range(chunks):
        gather(0, i, 1).start()
    for one in wo_columns(wo_h, me, 0):
        one.start()
    wg_load.start()
    wu_load.start()

    def on_size(t, f):
        pl.when(t // beat < 3)(lambda: f(pl.ds(0, ff)))
        pl.when(t // beat == 3)(lambda: f(pl.ds(0, 4 * local)))

    def place(t):
        return lax.rem(t, beat)

    def is_first(t):
        return place(t) == 0

    def is_second(t):
        return place(t) == SECOND

    def is_plain(t):
        return jnp.logical_and(place(t) != 0, place(t) != SECOND)

    def row_block(t):
        plain = place(t) - jnp.where(place(t) > SECOND, 2, 1)
        return jnp.where(is_plain(t), plain, per - 1)

    def x_number(t):
        return t // beat * (per - 1) + row_block(t)

    def x_do(t, what):
        n = x_number(t)

        def f(cols):
            copy = pltpu.make_async_remote_copy(
                src_ref=xs.at[lax.rem(n, 3), :, cols], dst_ref=xr.at[lax.rem(n, 5), :, cols],
                send_sem=xs_sem.at[lax.rem(n, 3)], recv_sem=xr_sem.at[lax.rem(n, 5)],
                device_id=x_dev, device_id_type=MESH,
            )
            getattr(copy, what)()

        on_size(t, f)

    def v_do(t, what):
        def f(cols):
            copy = pltpu.make_async_remote_copy(
                src_ref=vs.at[:, cols], dst_ref=vr.at[:, cols], send_sem=v_sem.at[0], recv_sem=v_sem.at[1],
                device_id=x_dev, device_id_type=MESH,
            )
            getattr(copy, what)()

        on_size(t, f)

    def zs_at(t, step):
        return 2 * step + lax.rem(t, 2)

    def zr_at(t, step):
        count = 3 if 0 < step < last - 1 else 4
        return 3 * step + min(step, 1) + lax.rem(t, count)

    def z_do(t, way, step, what):
        def f(cols):
            copy = pltpu.make_async_remote_copy(
                src_ref=zs.at[way, zs_at(t, step), :, cols], dst_ref=zr.at[way, zr_at(t, step), :, cols],
                send_sem=zs_sem.at[way, zs_at(t, step)], recv_sem=zr_sem.at[way, zr_at(t, step)],
                device_id=dn_dev if way else up_dev, device_id_type=MESH,
            )
            getattr(copy, what)()

        on_size(t, f)

    def receives(way, step):
        if way:
            return jnp.logical_and(z < last, z >= last - 1 - step)
        return jnp.logical_and(z > 0, z <= step + 1)

    def can_send(way, step):
        if way:
            return jnp.logical_and(z > 0, z >= last - step)
        return jnp.logical_and(z < last, z <= step)

    def z_arrived(t, step):
        for way in (0, 1):
            @pl.when(receives(way, step))
            def _(way=way):
                z_do(t, way, step, "wait_recv")

            @pl.when(can_send(way, step))
            def _(way=way):
                z_do(t, way, step, "wait_send")

    def z_step(t, step):
        sl = lax.rem(t, LAG + 4)
        if step > 0:
            z_arrived(t, step - 1)
        for way in (0, 1):
            quarter = z - last + step if way else last - step + z
            fresh = can_send(way, step)
            if step > 0:
                @pl.when(jnp.logical_and(receives(way, step - 1), can_send(way, step)))
                def _(way=way, quarter=quarter):
                    value = s_buf[sl, pl.ds(quarter * ROWS, ROWS), :].astype(F32) + zr[
                        way, zr_at(t, step - 1)
                    ].astype(F32)
                    zs[way, zs_at(t, step)] = value.astype(BF)

                fresh = jnp.logical_and(fresh, jnp.logical_not(receives(way, step - 1)))

            @pl.when(fresh)
            def _(way=way, quarter=quarter):
                zs[way, zs_at(t, step)] = s_buf[sl, pl.ds(quarter * ROWS, ROWS), :]

        for way in (0, 1):
            @pl.when(can_send(way, step))
            def _(way=way):
                z_do(t, way, step, "start")

    def compute(t, kind):
        sl = lax.rem(t, LAG + 4)
        at = row_block(t) * ROWS
        m = ROWS * nseq

        def rows_of(index, half):
            rows = [pl.ds(pl.multiple_of((half * nseq + s) * block + at, ROWS), ROWS) for s in range(nseq)]
            if kind == 3 and index == 1:
                return [wg[some, pl.ds(0, tokens)] for some in rows]
            return [lt[index, some, :] for some in rows]

        if kind == 3:
            parts = [(0, 0, 0, local)] + [(1, 0, k * local, local) for k in (1, 2, 3)]
        elif kind == 0:
            parts = [(0, 0, lo, n) for lo, n in cuts]
        else:
            parts = [(1, t // beat, lo, n) for lo, n in cuts]

        @pl.when(is_plain(t))
        def _():
            slot = lax.rem(x_number(t), 3)
            left = [jnp.concatenate(rows_of(i, 1 - p) + rows_of(i, p), 0) for i in sorted({q[0] for q in parts})]
            for i, ri, lo, n in parts:
                cols = pl.ds(lo, n)
                out = nn(left[i if len(left) == 2 else 0], r[ri, :, cols])
                xs[slot, :, cols] = out[:m].astype(BF)
                s_buf[sl, :, cols] = out[m:].astype(BF)
            x_do(t, "start")

        @pl.when(jnp.logical_not(is_plain(t)))
        def _():
            half = jnp.where(is_first(t), p, 1 - p)
            left = [jnp.concatenate(rows_of(i, half), 0) for i in sorted({q[0] for q in parts})]
            for i, ri, lo, n in parts:
                cols = pl.ds(lo, n)
                s_buf[sl, :, cols] = nn(left[i if len(left) == 2 else 0], r[ri, :, cols]).astype(BF)

    def out_do(src, t, sems, what):
        rows = pl.ds(pl.multiple_of(row_block(t) * ROWS, ROWS), ROWS)
        for g, target in enumerate((gdown_h, ggate_h, gup_h)):
            @pl.when(t // beat == g)
            def _(target=target):
                getattr(load(src, target.at[rows, :], ob_sem.at[sems, 0]), what)()

        @pl.when(t // beat == 3)
        def _():
            getattr(load(src.at[:, pl.ds(0, local)], gout_h.at[rows, :], ob_sem.at[sems, 0]), what)()
            for k in range(3):
                part = src.at[:, pl.ds((k + 1) * local, local)]
                getattr(load(part, gin_h.at[k, rows, :], ob_sem.at[sems, 1 + k]), what)()

    def plain_out(t, what):
        slot = lax.rem(x_number(t), 2)
        out_do(ob.at[slot], t, slot, what)

    def finish(t):
        sl = lax.rem(t, LAG + 4)
        z_arrived(t, last - 1)

        def total(then):
            def end(ways):
                value = s_buf[sl, pl.ds(z * ROWS, ROWS), :].astype(F32)
                for way in ways:
                    value += zr[way, zr_at(t, last - 1)].astype(F32)
                then(value)

            pl.when(z == 0)(lambda: end((1,)))
            pl.when(z == last)(lambda: end((0,)))
            pl.when(jnp.logical_and(z > 0, z < last))(lambda: end((0, 1)))

        @pl.when(is_plain(t))
        def _():
            n = x_number(t)
            before = t - jnp.where(place(t) == per, 2, 3)

            @pl.when(n >= 2)
            def _():
                plain_out(before, "wait")

            def put(value):
                ob[lax.rem(n, 2)] = value.astype(BF)

            total(put)
            plain_out(t, "start")

        @pl.when(is_first(t))
        def _():
            def put(value):
                vk[...] = value

            total(put)

        @pl.when(is_second(t))
        def _():
            def put(value):
                vs[...] = value.astype(BF)

            total(put)
            v_do(t, "start")

    def v_end(t):
        @pl.when(is_second(t))
        def _():
            v_do(t, "wait")

            @pl.when(t >= beat)
            def _():
                out_do(ob.at[2], t - beat, 2, "wait")

            ob[2] = (vk[...] + vr[...].astype(F32)).astype(BF)
            out_do(ob.at[2], t, 2, "start")

    def within(t, f):
        @pl.when(jnp.logical_and(t >= 0, t < ticks))
        def _():
            f(t)

    def tick_a(t, full=False):
        within(t - LAG - 4 - WAIT, v_end)
        within(t - LAG - 4, finish)

        def x_in(u):
            @pl.when(is_plain(u))
            def _():
                x_do(u, "wait")
                sl = lax.rem(u, LAG + 4)
                arrived = xr[lax.rem(x_number(u), 5)].astype(F32)
                s_buf[sl] = (s_buf[sl].astype(F32) + arrived).astype(BF)

            z_step(u, 0)

        within(t - LAG, x_in)
        if full:
            pl.when(t // beat == 0)(lambda: compute(t, 0))
            pl.when(jnp.logical_and(t // beat > 0, t // beat < 3))(lambda: compute(t, 1))
            pl.when(t // beat == 3)(lambda: compute(t, 3))

    def tick_b(t):
        within(t - LAG - 1, lambda u: z_step(u, 1))

    def tick_c(t):
        within(t - LAG - 2, lambda u: z_step(u, 2))

    def in_slices(own, others, to, slot):
        copies = [load(own, to(me), l_sem.at[slot, 0])]
        for step in range(1, 4):
            q = lax.rem(me + step, 4)
            copies.append(load(others(q), to(q), l_sem.at[slot, step]))
        return copies

    def cot_load(i):
        return in_slices(
            cot_in.at[rows_at(i), :],
            lambda q: cot_h.at[q, rows_at(i), :],
            lambda q: cotc.at[:, pl.ds(pl.multiple_of(q * local, 128), local)],
            0,
        )

    def x_load(i):
        return in_slices(x_in.at[rows_at(i), :], lambda q: x_h.at[q, rows_at(i), :], lambda q: xc.at[q], 1)

    def start(copies):
        for one in copies:
            one.start()

    def wait(copies):
        for one in copies:
            one.wait()

    def h1_load(i):
        return load(h1_h.at[:, rows_at(i), :], xc, l_sem.at[2, 0])

    def bcv_load(i):
        return load(bcv_h.at[:, rows_at(i), :], bcv, l_sem.at[2, 1])

    def gain(row, q):
        return gv[q, row : row + 1, :]

    def by_rows_of(count, f):
        def body(b, _):
            f(pl.ds(pl.multiple_of(b * count, count), count))
            return 0

        lax.fori_loop(0, chunk // count, body, 0)

    def normed_to(src, row, after=None):
        def f(some):
            ssq = jnp.zeros((64, local), F32)
            for q in range(4):
                values = src(q, some).astype(F32)
                ssq += values * values
            scale = lax.rsqrt(jnp.sum(ssq, -1, keepdims=True) / width + EPS)
            for q in range(4):
                dhoc[some, pl.ds(q * local, local)] = (src(q, some).astype(F32) * scale * gain(row, q)).astype(BF)

        by_rows_of(64, f)

    def transposed_to(index, i):
        at = pl.multiple_of(i * chunk, chunk)
        for q in range(4):
            cols = pl.ds(q * local, local)
            lt[index, cols, pl.ds(at, chunk)] = dhoc[:, cols].T

    def before_copy(i):
        return remote(before_s.at[i], before_r.at[i], before_sem, up_dev, i)

    def bcv_store(i):
        return load(bcv, bcv_h.at[:, rows_at(i), :], bcv_sem)

    def h1_store(i, slot, pair, core):
        return load(da2f.at[slot, pair, core], h1_h.at[2 * pair + core, rows_at(i), :], h1_sem.at[pair, core])

    def project(i):
        wait(x_load(i))
        normed_to(lambda q, some: xc[q, some, :], 0)
        value = nn(dhoc[...], w0[pl.ds(0, width), pl.ds(0, 3 * local)])

        @pl.when(i > 0)
        def _():
            bcv_store(i - 1).wait()

        for k in range(3):
            bcv[k] = value[:, k * local : (k + 1) * local].astype(BF)
        dcp[pl.ds(0, chunk), :] = value[:, local : 2 * local]
        bx = (value[:, :local] * value[:, 2 * local :]).astype(BF)
        bcv[3] = bx
        bxp[pl.ds(8, chunk), :] = bx.astype(F32)
        before_s[i] = bxp[pl.ds(chunk, 8), :]

        @pl.when(z < last)
        def _():
            before_copy(i).start()

        bcv_store(i).start()

    def conv_of():
        shifts = [bxp[pl.ds(6 + k, chunk), :] for k in range(3)]
        return sum(own_v[2 + k : 3 + k, :] * shifts[k] for k in range(3)), shifts

    def mix(i):
        @pl.when(z < last)
        def _():
            before_copy(i).wait_send()

        @pl.when(z > 0)
        def _():
            before_copy(i).wait_recv()

        @pl.when(z == 0)
        def _():
            before_r[i] = jnp.zeros((8, local), F32)

        bxp[pl.ds(0, 8), :] = before_r[i]
        mixed = (dcp[pl.ds(0, chunk), :] * conv_of()[0]).astype(BF)
        r[0, rows_at(i), pl.ds(pl.multiple_of(me * local, 128), local)] = mixed
        gather_start(3, i)

    def x_two(i):
        return [
            load(x_in.at[rows_at(i), :], cs2.at[y], l_sem.at[2, 2]),
            load(x_h.at[(1 - y) * 2 + c, rows_at(i), :], cs2.at[1 - y], l_sem.at[2, 3]),
        ]

    def residual(i):
        slot = lax.rem(i, 2)
        gather_end(3, i)
        wait(x_two(i))

        @pl.when(i >= 1)
        def _():
            for pair in (0, 1):
                for core in (0, 1):
                    h1_store(i - 1, 1 - slot, pair, core).wait()

        for pair in (0, 1):
            h1 = nn(r[0, rows_at(i), pl.ds(0, width)], wof[pair]) + cs2[pair].astype(F32)
            da2f[slot, pair, c] = h1.astype(BF)

            @pl.when(y == pair)
            def _(h1=h1):
                dh1s[i] = h1
        remote(da2f.at[slot, :, c], da2f.at[slot, :, c], f_sem, c_dev, slot).start()

        @pl.when(i + 1 < chunks)
        def _():
            start(x_two(i + 1))

    def cot_fetch(i):
        gather_end(1, i)
        start(cot_load(i))

    def cot_turn(i):
        wait(cot_load(i))
        at = pl.multiple_of(i * chunk, chunk)
        for q in range(4):
            cols = pl.ds(q * local, local)
            lt[0, cols, pl.ds(at, chunk)] = cotc[:, cols].T

    def feed(i):
        slot = lax.rem(i, 2)
        remote(da2f.at[slot, :, c], da2f.at[slot, :, c], f_sem, c_dev, slot).wait()
        for pair in (0, 1):
            for core in (0, 1):
                h1_store(i, slot, pair, core).start()
        normed_to(lambda q, some: da2f[slot, q // 2, q % 2, some, :], 1)
        transposed_to(1, i)
        rows = rows_at(i)
        for lo, n in cuts:
            dbuf[:, pl.ds(0, n)] = nt(dhoc[...], wg[pl.ds(lo, n), :])
            r[2, rows, pl.ds(lo, n)] = nt(dhoc[...], wu[pl.ds(lo, n), :]).astype(BF)

            def by_rows(b, _, lo=lo, n=n):
                cols = pl.ds(lo, n)
                here = pl.ds(pl.multiple_of(b * 64, 64), 64)
                some = pl.ds(pl.multiple_of(i * chunk + b * 64, 64), 64)
                gate = dbuf[here, pl.ds(0, n)]
                up = r[2, some, cols].astype(F32)
                r[0, some, cols] = (gate * jax.nn.sigmoid(gate) * up).astype(BF)
                r[1, some, cols] = gate.astype(BF)
                return 0

            lax.fori_loop(0, chunk // 64, by_rows, 0)

    def hidden_back(piece):
        i = piece // 3

        @pl.when(lax.rem(piece, 3) == 0)
        def _():
            wait(cot_load(i))

        for k, cut in enumerate(cuts):
            pl.when(lax.rem(piece, 3) == k)(functools.partial(hidden_cut, i, *cut))

        @pl.when(jnp.logical_and(lax.rem(piece, 3) == 2, i + 1 < chunks))
        def _():
            start(cot_load(i + 1))

    def hidden_cut(i, lo, n):
        if True:
            cols = pl.ds(lo, n)
            dbuf[:, pl.ds(0, n)] = nt(cotc[...], w0[pl.ds(lo, n), :])

            def by_rows(b, _, cols=cols, n=n):
                some = pl.ds(pl.multiple_of(i * chunk + b * 32, 32), 32)
                dhid = dbuf[pl.ds(pl.multiple_of(b * 32, 32), 32), pl.ds(0, n)]
                gate = r[1, some, cols].astype(F32)
                up = r[2, some, cols].astype(F32)
                sig = jax.nn.sigmoid(gate)
                r[1, some, cols] = (dhid * up * sig * (1.0 + gate * (1.0 - sig))).astype(BF)
                r[2, some, cols] = (dhid * gate * sig).astype(BF)
                return 0

            lax.fori_loop(0, chunk // 32, by_rows, 0)

    def split_store(pair, value, keep, send):
        for side in (0, 1):
            part = value[:, side * local : (side + 1) * local]

            @pl.when(c == side)
            def _(part=part):
                keep[pair] = part

            @pl.when(c != side)
            def _(part=part):
                send[pair] = part.astype(BF)

    def stage_a(i):
        slot = lax.rem(i, 2)
        rows = rows_at(i)
        for pair in (0, 1):
            cols = pl.ds(pair * 2 * local, 2 * local)
            value = nn(r[1, rows, :], wg[:, cols]) + nn(r[2, rows, :], wu[:, cols])
            split_store(pair, value, ck, cs)
        remote(cs, cr.at[slot], c_sem, c_dev, slot).start()

        @pl.when(i == chunks - 1)
        def _():
            start(x_whole())

    def x_whole():
        copies = [load(x_in, wu.at[pl.ds(0, tokens), pl.ds(pl.multiple_of(me * local, 128), local)], l_sem.at[3, 0])]
        for step in range(1, 4):
            q = lax.rem(me + step, 4)
            cols = pl.ds(pl.multiple_of(q * local, 128), local)
            copies.append(load(x_h.at[q], wu.at[pl.ds(0, tokens), cols], l_sem.at[3, step]))
        return copies

    def stage_a1(i):
        @pl.when(i == 0)
        def _():
            wait(x_whole())

        at = pl.multiple_of(i * chunk, chunk)
        normed_to(lambda q, some: wu[pl.ds(at + some.start, some.size), pl.ds(q * local, local)], 0)
        for q in range(4):
            cols = pl.ds(q * local, local)
            wg[cols, pl.ds(at, chunk)] = dhoc[:, cols].T

    def stage_loads(i):
        start(cot_load(i))
        h1_load(i).start()
        bcv_load(i).start()

    def stage_b(i):
        slot = lax.rem(i, 2)
        remote(cs, cr.at[slot], c_sem, c_dev, slot).wait()
        ys[...] = (ck[...] + cr[slot].astype(F32)).astype(BF)
        remote(ys, yr4.at[slot], y_sem, y_dev, slot).start()

    def stage_c(i):
        slot = lax.rem(i, 2)
        remote(ys, yr4.at[slot], y_sem, y_dev, slot).wait()
        da2f[slot, :, c] = (ys[...].astype(F32) + yr4[slot].astype(F32)).astype(BF)
        remote(da2f.at[slot, :, c], da2f.at[slot, :, c], f_sem, c_dev, slot).start()

    def stage_d(i):
        slot = lax.rem(i, 2)
        remote(da2f.at[slot, :, c], da2f.at[slot, :, c], f_sem, c_dev, slot).wait()
        wait(cot_load(i))
        h1_load(i).wait()
        bcv_load(i).wait()
        at = pl.multiple_of(i * chunk, chunk)
        own = pl.ds(pl.multiple_of(me * local, 128), local)

        def by_rows(b, _):
            some = pl.ds(pl.multiple_of(b * 64, 64), 64)
            ssq = jnp.zeros((64, local), F32)
            inner = jnp.zeros((64, local), F32)
            for q in range(4):
                cols = pl.ds(q * local, local)
                h1 = xc[q, some, :].astype(F32)
                ssq += h1 * h1
                inner += da2f[slot, q // 2, q % 2, some, :].astype(F32) * gain(1, q) * h1
            r2 = lax.rsqrt(jnp.sum(ssq, -1, keepdims=True) / width + EPS)
            scale = r2 * r2 * r2 * jnp.sum(inner, -1, keepdims=True) / width

            def grad(q, cols, da2):
                h1 = xc[q, some, :].astype(F32)
                return cotc[some, cols].astype(F32) + r2 * (da2 * gain(1, q)) - h1 * scale

            for q in range(4):
                cols = pl.ds(q * local, local)
                dhoc[some, cols] = grad(q, cols, da2f[slot, q // 2, q % 2, some, :].astype(F32)).astype(BF)
            da2 = da2f[slot, y, c, some, :].astype(F32)
            dh1s[i, some, :] = grad(me, own, da2)
            terms = da2 * xc[me, some, :].astype(F32) * r2
            small_v[pl.ds(8, 8), :] += sum(terms[8 * k : 8 * k + 8] for k in range(8))
            return 0

        lax.fori_loop(0, chunk // 64, by_rows, 0)
        start(x_load(i))
        transposed_to(0, i)
        @pl.when(i == 0)
        def _():
            for q in range(4):
                wo_load(q).wait()

        dmixed = jnp.zeros((chunk, local), F32)
        for q in range(4):
            cols = pl.ds(q * local, local)
            dmixed += nt(dhoc[:, cols], wof[0, cols, :])
        c_gate = bcv[1]
        bxp[pl.ds(0, 8), :] = before_r[i]
        bxp[pl.ds(8, chunk), :] = bcv[3].astype(F32)
        conv, shifts = conv_of()
        r[0, pl.ds(at, chunk), pl.ds(0, local)] = (c_gate.astype(F32) * conv).astype(BF)
        r[0, pl.ds(at, chunk), pl.ds(2 * local, local)] = (dmixed * conv).astype(BF)
        dconv = (dmixed * c_gate.astype(F32)).astype(BF).astype(F32)
        dcp[pl.ds(0, chunk), :] = dconv
        halo_s[i] = dconv[:8]
        for k in range(3):
            small_v[1 + k : 2 + k, :] += jnp.sum(dconv * shifts[k], 0, keepdims=True)

        @pl.when(z > 0)
        def _():
            halo_copy(i).start()

    def halo_copy(i):
        return remote(halo_s.at[i], halo_r.at[i], halo_sem, dn_dev, i)

    def stage_e(i):
        slot = lax.rem(i, 2)

        @pl.when(i == 0)
        def _():
            for k in range(3):
                wi_load(k).wait()
            out_copy(chunks - 1).wait()

        wait(x_load(i))

        @pl.when(z > 0)
        def _():
            halo_copy(i).wait_send()

        @pl.when(z < last)
        def _():
            halo_copy(i).wait_recv()
            dcp[pl.ds(chunk, 8), :] = halo_r[i]

        @pl.when(z == last)
        def _():
            dcp[pl.ds(chunk, 8), :] = jnp.zeros((8, local), F32)

        dbx = sum(own_v[4 - k : 5 - k, :] * dcp[pl.ds(k, chunk), :] for k in range(3))
        rows = rows_at(i)
        r[0, rows, pl.ds(local, local)] = (dbx * bcv[2].astype(F32)).astype(BF)
        r[0, rows, pl.ds(3 * local, local)] = (dbx * bcv[0].astype(F32)).astype(BF)
        inner = jnp.zeros((chunk, 1), F32)
        ssq = jnp.zeros((chunk, 1), F32)
        for pair in (0, 1):
            cols = pl.ds(pair * 2 * local, 2 * local)
            value = nt(r[0, rows, pl.ds(local, 3 * local)], w0[cols, pl.ds(0, 3 * local)])
            for side in (0, 1):
                q = 2 * pair + side
                x = xc[q].astype(F32)
                part = value[:, side * local : (side + 1) * local]
                inner += jnp.sum(part * x * gain(0, q), -1, keepdims=True)
                ssq += jnp.sum(x * x, -1, keepdims=True)
            split_store(pair, value, ck2, cs2)
        xo[...] = xc[me]
        ins[...] = jnp.broadcast_to(inner, (chunk, 128)).T[:8]
        r1s[...] = jnp.broadcast_to(lax.rsqrt(ssq / width + EPS), r1s.shape)
        remote(cs2, yr4.at[2 + slot], c2_sem, c_dev, slot).start()
        remote(ins, inr.at[slot], i_sem, c_dev, slot).start()

        @pl.when(i + 1 < chunks)
        def _():
            stage_loads(i + 1)

    def stage_f(i):
        slot = lax.rem(i, 2)
        remote(cs2, yr4.at[2 + slot], c2_sem, c_dev, slot).wait()
        remote(ins, inr.at[slot], i_sem, c_dev, slot).wait()
        ys2[...] = (ck2[1 - y] + yr4[2 + slot, 1 - y].astype(F32)).astype(BF)
        qk2[...] = ck2[y] + yr4[2 + slot, y].astype(F32)
        iys[...] = ins[...] + inr[slot]
        remote(ys2, yr2.at[slot], y2_sem, y_dev, slot).start()
        remote(iys, iyr.at[slot], iy_sem, y_dev, slot).start()

    def gx_copy(i):
        return load(gxb, gx_h.at[rows_at(i), :], gx_sem)

    def stage_g(i):
        slot = lax.rem(i, 2)
        remote(ys2, yr2.at[slot], y2_sem, y_dev, slot).wait()
        remote(iys, iyr.at[slot], iy_sem, y_dev, slot).wait()
        da1 = qk2[...] + yr2[slot].astype(F32)
        inner = jnp.broadcast_to(iys[:1] + iyr[slot, :1], (128, chunk)).T[:, :1]
        r1 = r1s[:, :1]
        x = xo[...].astype(F32)
        scaled = gain(0, me)
        small_v[0:1, :] += jnp.sum(da1 * x * r1, 0, keepdims=True)

        @pl.when(i > 0)
        def _():
            gx_copy(i - 1).wait()

        gxb[...] = (dh1s[i] + r1 * scaled * da1 - x * (r1 * r1 * r1 * inner / width)).astype(BF)
        gx_copy(i).start()

    def out_start(i):
        rows = rows_at(i)
        for pair in (0, 1):
            cols = pl.ds(pair * 2 * local, 2 * local)
            split_store(pair, nn(r[0, rows, :], w0[:, cols]), ck2, cs2)
        remote(cs2, yr4.at[2 + lax.rem(i, 2)], c2_sem, c_dev, lax.rem(i, 2)).start()

        @pl.when(i == chunks - 1)
        def _():
            for k in range(3):
                wi_load(k).start()

    def out_share(i):
        slot = lax.rem(i, 2)
        remote(cs2, yr4.at[2 + slot], c2_sem, c_dev, slot).wait()
        ys2[...] = (ck2[1 - y] + yr4[2 + slot, 1 - y].astype(F32)).astype(BF)
        qk2[...] = ck2[y] + yr4[2 + slot, y].astype(F32)
        remote(ys2, yr2.at[slot], y2_sem, y_dev, slot).start()

    def out_copy(i):
        return load(gxb, out_h.at[rows_at(i), :], gx_sem)

    def out_end(i):
        slot = lax.rem(i, 2)
        remote(ys2, yr2.at[slot], y2_sem, y_dev, slot).wait()

        @pl.when(i > 0)
        def _():
            out_copy(i - 1).wait()

        gxb[...] = (dh1s[i] + (qk2[...] + yr2[slot].astype(F32))).astype(BF)
        out_copy(i).start()

    def valid(i, f):
        @pl.when(jnp.logical_and(i >= 0, i < chunks))
        def _():
            f(i)

    gather_pass(0, 0)
    gather(0, 1, 0).start()
    wy().start()
    gather_pass(2, 0)
    for k in range(3):
        wi_load(k).wait()
    gather_end(2, 0)

    gather_end(0, 0)
    start(x_load(0))

    def when(now, *calls):
        @pl.when(now)
        def _():
            for f in calls:
                f()

    def weights_there():
        wg_load.wait()
        wu_load.wait()

    def wo_there():
        wo_end()
        for kind, src in ((0, wo_h), (1, woy_h)):
            for one in wo_columns(src, me if kind == 0 else (1 - y) * 2 + c, kind):
                one.wait()

    def forward(j, _):
        when(j < chunks, lambda: project(j))
        when(j + 1 < chunks, lambda: gather_pass(0, j + 1))
        when(j + 2 < chunks, lambda: gather(0, j + 2, 0).start())
        when(j == 0, lambda: wo_step(0))
        when(j == 1, lambda: wo_step(1))
        when(j == 2, lambda: wo_step(3))
        when(j == 3, wo_there, weights_there)
        when(j >= 3, lambda: residual(j - 3))
        when(j < chunks, lambda: mix(j))
        when(j + 1 < chunks, lambda: gather_end(0, j + 1), lambda: start(x_load(j + 1)))
        when(j == 1, lambda: wo_step(2))
        when(j == 2, lambda: start(x_two(0)), lambda: gather(1, 0, 0).start(), lambda: gather(1, 1, 0).start())
        when(jnp.logical_and(j > 0, j < chunks), lambda: gather_pass(3, j - 1))
        when(j > 3, lambda: cot_turn(j - 4))
        when(j == 5, *[functools.partial(gather_pass, 1, k) for k in range(2, chunks)])
        when(j > 3, lambda: cot_fetch(j - 3))
        when(j >= 3, lambda: feed(j - 3))
        when(
            j == 3, wd_load.start, *[functools.partial(gather_pass, 1, k) for k in range(2)],
            *[gather(1, k, 0).start for k in range(2, chunks)], lambda: cot_fetch(0),
        )
        when(j == 4, lambda: gather_pass(3, chunks - 1))
        return 0

    for i in range(chunks):
        gather(1, i, 1).start()
    lax.fori_loop(0, chunks + 3, forward, 0)
    for q in range(4):
        wo_load(q).start()
    bcv_store(chunks - 1).wait()
    for pair in (0, 1):
        for core in (0, 1):
            h1_store(chunks - 1, (chunks - 1) % 2, pair, core).wait()

    cot_turn(chunks - 1)
    start(cot_load(0))

    def small_x():
        return pltpu.make_async_remote_copy(
            src_ref=small_v.at[pl.ds(0, 8)], dst_ref=small_r.at[0], send_sem=small_sem.at[0, 0],
            recv_sem=small_sem.at[0, 1], device_id=x_dev, device_id_type=MESH,
        )

    def small_z(way):
        return pltpu.make_async_remote_copy(
            src_ref=small_r.at[1 + way], dst_ref=small_r.at[3 + way], send_sem=small_sem.at[1 + way, 0],
            recv_sem=small_sem.at[1 + way, 1], device_id=dn_dev if way else up_dev, device_id_type=MESH,
        )

    def small_step(k):
        @pl.when(k == 0)
        def _():
            small_x().wait()
            total = small_v[pl.ds(0, 8), :] + small_r[0]
            small_v[pl.ds(0, 8), :] = total
            small_r[1] = total
            small_r[2] = total

        for way in (0, 1):
            turn = last - z if way else z

            @pl.when(jnp.logical_and(turn < last, k == turn))
            def _(way=way, turn=turn):
                @pl.when(turn > 0)
                def _():
                    small_z(way).wait_recv()
                    small_r[1 + way] = small_v[pl.ds(0, 8), :] + small_r[3 + way]

                small_z(way).start()

    def small_end():
        for way in (0, 1):
            turn = last - z if way else z

            @pl.when(turn < last)
            def _(way=way):
                small_z(way).wait_send()

            @pl.when(turn == last)
            def _(way=way):
                small_z(way).wait_recv()

            @pl.when(turn > 0)
            def _(way=way):
                small_v[pl.ds(0, 8), :] += small_r[3 + way]

    def stage_last(i):
        stage_g(i)

        @pl.when(i == chunks - 1)
        def _():
            small_v[4:5, :] = jnp.sum(small_v[8:16, :], 0, keepdims=True)
            small_x().start()

    order = (
        ("g", stage_last), ("out_end", out_end), ("out_share", out_share), ("b", stage_b), ("f", stage_f),
        ("c", stage_c), ("e", stage_e), ("d", stage_d), ("out_start", out_start), ("a", stage_a),
        ("hidden", None), ("a1", stage_a1),
    )

    def stages(t, third):
        for name, f in order:
            if name == "hidden":
                if HIDDEN[0] != third:
                    continue
                done = 0
                low = high = 0
                for at, upto in HIDDEN[1].items():
                    low = jnp.where(t == at, done, low)
                    high = jnp.where(t == at, upto, high)
                    done = upto

                def piece(k, _):
                    hidden_back(k)
                    return 0

                lax.fori_loop(low, high, piece, 0)
            elif PLACES[name][0] == third:
                where = PLACES[name][1]
                i = sum(jnp.where(t >= at, 1, 0) for at in where[1:])
                now = functools.reduce(jnp.logical_or, [t == at for at in where])
                pl.when(now)(functools.partial(f, i))

    def each_tick(t, _):
        tick_a(t, True)

        @pl.when(t == 0)
        def _():
            wd_load.wait()

        @pl.when(t == beat)
        def _():
            stage_loads(0)

        stages(t, 0)
        tick_b(t)
        stages(t, 1)
        tick_c(t)
        stages(t, 2)

        @pl.when(t > PLACES["g"][1][-1])
        def _():
            small_step(t - PLACES["g"][1][-1] - 1)

        return 0

    lax.fori_loop(0, ticks, each_tick, 0)
    gx_copy(chunks - 1).wait()

    def part_four(k, _):
        tick_a(ticks + k)
        tick_b(ticks + k)
        tick_c(ticks + k)
        return 0

    lax.fori_loop(0, LAG + 4, part_four, 0)
    small_end()
    plain_out(ticks - 2, "wait")
    plain_out(ticks - 1, "wait")
    out_do(ob.at[2], 3 * beat + SECOND, 2, "wait")


def block(dims, x_own, cot_own, gain_mix, gain_ff, taps, wd, wg, wu, wo, wi):
    tokens, chunk, width, ff, local, nseq = dims
    rows = width // (2 * nseq)
    chunks = tokens // chunk
    last = nseq - 1
    m = ROWS * nseq
    DMA = pltpu.SemaphoreType.DMA
    shape = jax.ShapeDtypeStruct
    third = ff // 3 // 128 * 128
    scratch = [
        pltpu.VMEM((2, width, tokens), BF),
        pltpu.VMEM((3, tokens, ff), BF),
        pltpu.VMEM((ff, width), BF),
        pltpu.VMEM((ff, width), BF),
        pltpu.VMEM((ff, width), BF),
        pltpu.VMEM((2, width, local), BF),
        pltpu.VMEM((chunk, width), BF),
        pltpu.VMEM((4, chunk, local), BF),
        pltpu.VMEM((chunk, local), BF),
        pltpu.VMEM((4, chunk, local), BF),
        pltpu.VMEM((8 + chunk, local), F32),
        pltpu.VMEM((chunk, ff - 2 * third), F32),
        pltpu.VMEM((8 + chunk, local), F32),
        pltpu.VMEM((chunk, width), BF),
        pltpu.VMEM((chunks, chunk, local), F32),
        pltpu.VMEM((chunk, 128), F32),
        pltpu.VMEM((4, 8, local), F32),
        pltpu.VMEM((8, local), F32),
        pltpu.VMEM((3, m, ff), BF),
        pltpu.VMEM((5, m, ff), BF),
        pltpu.VMEM((LAG + 4, m, ff), BF),
        pltpu.VMEM((2, 2 * last, ROWS, ff), BF),
        pltpu.VMEM((2, 3 * last + 2, ROWS, ff), BF),
        pltpu.VMEM((3, ROWS, ff), BF),
        pltpu.VMEM((ROWS, ff), BF),
        pltpu.VMEM((ROWS, ff), BF),
        pltpu.VMEM((ROWS, ff), F32),
        pltpu.VMEM((5, chunk, local), F32),
        pltpu.VMEM((2, chunk, local), BF),
        pltpu.VMEM((2, 2, chunk, local), BF),
        pltpu.VMEM((2, chunk, local), BF),
        pltpu.VMEM((4, 2, chunk, local), BF),
        pltpu.VMEM((2, 2, 2, chunk, local), BF),
        pltpu.VMEM((2, chunk, local), BF),
        pltpu.VMEM((chunk, local), BF),
        pltpu.VMEM((2, chunk, local), BF),
        pltpu.VMEM((8, chunk), F32),
        pltpu.VMEM((2, 8, chunk), F32),
        pltpu.VMEM((8, chunk), F32),
        pltpu.VMEM((2, 8, chunk), F32),
        pltpu.VMEM((chunk, local), BF),
        pltpu.VMEM((chunks, 8, local), F32),
        pltpu.VMEM((chunks, 8, local), F32),
        pltpu.VMEM((chunks, 8, local), F32),
        pltpu.VMEM((chunks, 8, local), F32),
        pltpu.VMEM((5, 8, local), F32),
        DMA((3,)), DMA((5,)), DMA((2, 2 * last)), DMA((2, 3 * last + 2)), DMA((3, 4)),
        DMA((2, 2)), DMA((2, chunks)), DMA((2, 2)), DMA((2, 2)), DMA((2, 2)),
        DMA((2, 2)), DMA((2, 2)), DMA((2, chunks)), DMA((2, chunks)), DMA((3, 2, 4, chunks)),
        DMA((7,)), DMA((4, 4)), DMA(()), DMA((2, 2)), DMA(()), DMA((3, 2)), DMA((2,)), DMA((2,)), DMA((2, nseq)), DMA((2, 2, last)), DMA((2, 4)), DMA((4,)),
    ]
    return pl.pallas_call(
        functools.partial(block_kernel, dims),
        out_shape=(
            shape((rows, ff), BF), shape((rows, ff), BF), shape((rows, ff), BF),
            shape((rows, local), BF), shape((3, rows, local), BF),
            shape((tokens, local), BF), shape((tokens, local), BF), shape((16, local), F32),
            shape((4, tokens, local), BF), shape((4, tokens, local), BF),
            shape((4, tokens, local), BF), shape((4, tokens, local), BF), shape((local, width), BF),
        ),
        in_specs=[ANY] * 2 + [VMEM] * 3 + [ANY] * 5,
        out_specs=(ANY,) * 7 + (VMEM,) + (ANY,) * 5,
        scratch_shapes=scratch,
        compiler_params=pltpu.CompilerParams(
            collective_id=0, has_side_effects=True, vmem_limit_bytes=63 * 2**20
        ),
    )(x_own, cot_own, gain_mix, gain_ff, taps, wd, wg, wu, wo, wi)


def shifted(array, axis, by):
    count = lax.axis_size(axis)
    pairs = [(i, i + by) for i in range(count) if 0 <= i + by < count]
    return lax.ppermute(array, axis, pairs)


def fused_device(inputs, gain_mix, w_in, kernel, w_out, gain_ff, w_gate, w_up, w_down, cotangent):
    groups, seq_rows, local = inputs.shape
    width = local * lax.axis_size("mp")
    ff = w_down.shape[0]
    tokens = groups * seq_rows
    dims = (tokens, seq_rows, width, ff, local, lax.axis_size("seq"))
    gdown, ggate, gup, gout, gin, gx, out, small = block(
        dims, inputs.reshape(tokens, local), cotangent.reshape(tokens, local), gain_mix, gain_ff, kernel,
        w_down, w_gate.T, w_up.T, w_out, w_in.transpose(1, 0, 2),
    )[:8]
    gdown, ggate, gup, gout, gin, gx, out, gmix, gtaps, gff = widen(
        gdown, ggate, gup, gout, gin, gx, out, small
    )
    whole = (groups, seq_rows, local)
    return (
        out.reshape(whole), gx.reshape(whole), gmix, gin.transpose(1, 0, 2), gtaps,
        gout.T, gff, ggate, gup, gdown.T,
    )


def widen_kernel(*refs):
    count = 7
    src, small, dst = refs[:count], refs[count], refs[count + 1 : 2 * count + 1]
    gmix, gtaps, gff = refs[2 * count + 1 : 2 * count + 4]
    narrow = refs[2 * count + 4 : 3 * count + 4]
    wide = refs[3 * count + 4 : 4 * count + 2]
    in_sem, out_sem = refs[4 * count + 2 :]
    loads = [pltpu.make_async_copy(src[k], narrow[k], in_sem.at[k]) for k in range(count)]
    stores = [
        pltpu.make_async_copy(wide[k] if k < count - 2 else narrow[k], dst[k], out_sem.at[k])
        for k in range(count)
    ]
    for one in loads:
        one.start()
    gmix[...] = small[0:1, :].reshape(gmix.shape)
    gtaps[...] = small[1:4, :]
    gff[...] = small[4:5, :].reshape(gff.shape)
    for k in range(count):
        loads[k].wait()
        if k < count - 2:
            wide[k][...] = narrow[k][...].astype(F32)
        stores[k].start()
    for one in stores:
        one.wait()


def widen(*arrays):
    big, small = arrays[:7], arrays[7]
    local = small.shape[1]
    shape = jax.ShapeDtypeStruct
    outs = [shape(a.shape, F32 if k < 5 else BF) for k, a in enumerate(big)]
    outs += [shape((local,), F32), shape((3, local), F32), shape((local,), F32)]
    return pl.pallas_call(
        widen_kernel,
        out_shape=outs,
        in_specs=[ANY] * 7 + [VMEM],
        out_specs=[ANY] * 7 + [VMEM] * 3,
        scratch_shapes=[pltpu.VMEM(a.shape, BF) for a in big]
        + [pltpu.VMEM(a.shape, F32) for a in big[:5]]
        + [pltpu.SemaphoreType.DMA((7,))] * 2,
        compiler_params=pltpu.CompilerParams(vmem_limit_bytes=63 * 2**20),
    )(*big, small)


def contract_rows(left, right):
    return lax.dot_general(
        left, right, (((0,), (0,)), ((), ())), preferred_element_type=jnp.float32
    )


def contract_cols(left, right):
    return lax.dot_general(
        left, right, (((1,), (1,)), ((), ())), preferred_element_type=jnp.float32
    )


def plain_device(inputs, gain_mix, w_in, kernel, w_out, gain_ff, w_gate, w_up, w_down, cotangent):
    groups, seq_rows, local_width = inputs.shape
    full_width = local_width * lax.axis_size("mp")
    tokens = groups * seq_rows
    x_float = inputs.reshape(tokens, local_width).astype(jnp.float32)
    gain_one = gain_mix.astype(jnp.float32)
    gain_two = gain_ff.astype(jnp.float32)
    taps = kernel.astype(jnp.float32)

    def row_total(values):
        return lax.psum(jnp.sum(values, axis=-1, keepdims=True), "mp")

    def all_features(values):
        return lax.all_gather(values, "mp", axis=1, tiled=True)

    def share_sums(values):
        return lax.psum_scatter(
            values.astype(jnp.bfloat16), "mp", scatter_dimension=1, tiled=True
        ).astype(jnp.float32)

    def scattered(values, dim):
        return lax.psum_scatter(
            values.astype(jnp.bfloat16), ("dp", "seq"), scatter_dimension=dim, tiled=True
        ).astype(jnp.float32)

    def norm_scale(values):
        return lax.rsqrt(row_total(values * values) / full_width + EPS)

    def norm_back(values, scale, gain_vec, upstream):
        inner = row_total(gain_vec * upstream * values)
        grad_values = scale * gain_vec * upstream - values * scale**3 * inner / full_width
        return (grad_values, jnp.sum(upstream * values * scale, axis=0))

    scale_one = norm_scale(x_float)
    normed_in = all_features((x_float * scale_one * gain_one).astype(jnp.bfloat16))
    proj = jnp.einsum("td,dkc->tkc", normed_in, w_in, preferred_element_type=jnp.float32)
    b_gate = proj[:, 0]
    c_gate = proj[:, 1]
    values_v = proj[:, 2]
    b_times_x = (b_gate * values_v).astype(jnp.bfloat16).reshape(groups, seq_rows, local_width)
    before = shifted(b_times_x[:, seq_rows - 2 :], "seq", 1)
    padded = jnp.concatenate([before, b_times_x], 1).astype(jnp.float32)
    conv = taps[0] * padded[:, :-2] + taps[1] * padded[:, 1:-1] + taps[2] * padded[:, 2:]
    conv = conv.reshape(tokens, local_width)
    mixed = (c_gate * conv).astype(jnp.bfloat16)
    hidden_one = x_float + share_sums(jnp.dot(mixed, w_out, preferred_element_type=jnp.float32))
    scale_two = norm_scale(hidden_one)
    normed_ff = all_features((hidden_one * scale_two * gain_two).astype(jnp.bfloat16))
    gate = jnp.dot(normed_ff, w_gate, preferred_element_type=jnp.float32)
    up_proj = jnp.dot(normed_ff, w_up, preferred_element_type=jnp.float32)
    sigma = jax.nn.sigmoid(gate)
    active = gate * sigma
    hidden = (active * up_proj).astype(jnp.bfloat16)
    ffn_out = share_sums(jnp.dot(hidden, w_down, preferred_element_type=jnp.float32))
    block_out = (hidden_one + ffn_out).astype(jnp.bfloat16).reshape(groups, seq_rows, local_width)
    grad_flat = cotangent.reshape(tokens, local_width)
    grad_full = all_features(grad_flat)
    grad_down = contract_rows(hidden, grad_full)
    grad_hidden = contract_cols(grad_full, w_down)
    grad_gate_act = (grad_hidden * up_proj * sigma * (1.0 + gate * (1.0 - sigma))).astype(
        jnp.bfloat16
    )
    grad_up_act = (grad_hidden * active).astype(jnp.bfloat16)
    grad_gate = contract_rows(normed_ff, grad_gate_act)
    grad_up = contract_rows(normed_ff, grad_up_act)
    grad_normed_ff = share_sums(
        contract_cols(grad_gate_act, w_gate) + contract_cols(grad_up_act, w_up)
    )
    grad_norm_two, grad_gain_two = norm_back(hidden_one, scale_two, gain_two, grad_normed_ff)
    grad_hidden_one = grad_flat.astype(jnp.float32) + grad_norm_two
    grad_out_full = all_features(grad_hidden_one.astype(jnp.bfloat16))
    grad_out = contract_rows(mixed, grad_out_full)
    grad_mixed = contract_cols(grad_out_full, w_out)
    grad_c = grad_mixed * conv
    grad_conv = (grad_mixed * c_gate).astype(jnp.bfloat16).reshape(groups, seq_rows, local_width)
    after = shifted(grad_conv[:, :2], "seq", -1)
    extended = jnp.concatenate([grad_conv, after], 1).astype(jnp.float32)
    grad_bx = taps[2] * extended[:, :-2] + taps[1] * extended[:, 1:-1] + taps[0] * extended[:, 2:]
    grad_bx = grad_bx.reshape(tokens, local_width)
    conv_grad_float = extended[:, :-2]
    grad_taps = jnp.stack(
        [
            jnp.sum(conv_grad_float * padded[:, :-2], axis=(0, 1)),
            jnp.sum(conv_grad_float * padded[:, 1:-1], axis=(0, 1)),
            jnp.sum(conv_grad_float * padded[:, 2:], axis=(0, 1)),
        ]
    )
    grad_proj = jnp.stack([grad_bx * values_v, grad_c, grad_bx * b_gate], 1).astype(jnp.bfloat16)
    grad_in = jnp.einsum("td,tkc->dkc", normed_in, grad_proj, preferred_element_type=jnp.float32)
    grad_normed_in = share_sums(
        jnp.einsum("tkc,dkc->td", grad_proj, w_in, preferred_element_type=jnp.float32)
    )
    grad_norm_one, grad_gain_one = norm_back(x_float, scale_one, gain_one, grad_normed_in)
    grad_input = (
        (grad_hidden_one + grad_norm_one)
        .astype(jnp.bfloat16)
        .reshape(groups, seq_rows, local_width)
    )
    small_sums = lax.psum((grad_gain_one, grad_taps, grad_gain_two), ("dp", "seq"))
    by_row = (
        scattered(grad_in, 0),
        scattered(grad_gate, 0),
        scattered(grad_up, 0),
    )
    by_col = (
        scattered(grad_out, 1),
        scattered(grad_down, 1),
    )
    return (
        block_out,
        grad_input,
        small_sums[0],
        by_row[0],
        small_sums[1],
        by_col[0],
        small_sums[2],
        by_row[1],
        by_row[2],
        by_col[1],
    )


def solution(mesh):
    placed = (
        P("dp", "seq", "mp"),
        P("mp"),
        P(None, None, "mp"),
        P(None, "mp"),
        P("mp", None),
        P("mp"),
        P(None, "mp"),
        P(None, "mp"),
        P("mp", None),
        P("dp", "seq", "mp"),
    )
    sizes = mesh.shape
    fused = sizes["dp"] == 2 and sizes["seq"] == 4 and sizes["mp"] == 4
    return jax.shard_map(
        fused_device if fused else plain_device,
        mesh=mesh,
        in_specs=placed,
        out_specs=(
            P("dp", "seq", "mp"),
            P("dp", "seq", "mp"),
            P("mp"),
            P(("dp", "seq"), None, "mp"),
            P(None, "mp"),
            P("mp", ("dp", "seq")),
            P("mp"),
            P(("dp", "seq"), "mp"),
            P(("dp", "seq"), "mp"),
            P("mp", ("dp", "seq")),
        ),
        check_vma=False,
    )
```

```python
import functools

import jax
import jax.numpy as jnp
from jax import lax
from jax.experimental import pallas as pl
from jax.experimental.pallas import tpu as pltpu
from jax.sharding import PartitionSpec as P

EPS = 1e-05
MESH = pl.DeviceIdType.MESH
BF = jnp.bfloat16
F32 = jnp.float32
ROWS = 32
SECOND = 3
LAG = 3
WAIT = 3
PLACES = {
    "out_start": (2, (1, 4, 7, 8)),
    "out_share": (2, (2, 5, 8, 10)),
    "out_end": (1, (4, 7, 9, 12)),
    "a": (2, (3, 8, 10, 14)),
    "b": (2, (4, 9, 12, 15)),
    "c": (1, (8, 11, 14, 18)),
    "d": (2, (9, 13, 17, 19)),
    "e": (2, (12, 15, 18, 20)),
    "f": (2, (14, 16, 19, 21)),
    "g": (2, (15, 18, 20, 22)),
    "a1": (2, (15, 16, 17, 19)),
}
HIDDEN = (1, {2: 3, 3: 4, 4: 5, 5: 7, 6: 12})
ANY = pl.BlockSpec(memory_space=pl.ANY)
VMEM = pl.BlockSpec(memory_space=pltpu.VMEM)


def nn(left, right):
    return lax.dot_general(left, right, (((1,), (0,)), ((), ())), preferred_element_type=F32)


def nt(left, right):
    return lax.dot_general(left, right, (((1,), (1,)), ((), ())), preferred_element_type=F32)


def block_kernel(
    dims,
    x_in, cot_in, gain_mix_v, gain_ff_v, taps_v, wd_h, wg_h, wu_h, wo_h, wi_h,
    gdown_h, ggate_h, gup_h, gout_h, gin_h, gx_h, out_h, small_v,
    x_h, cot_h, h1_h, bcv_h, woy_h,
    lt, r, w0, wg, wu, wof, cotc, xc, xo, bcv, bxp, dbuf, dcp, dhoc, dh1s, r1s, gv, own_v,
    xs, xr, s_buf, zs, zr, ob, vs, vr, vk,
    kf, cs, cr, ys, yr4, da2f, cs2, ys2, yr2,
    ins, inr, iys, iyr, gxb, halo_s, halo_r, before_s, before_r, small_r,
    xs_sem, xr_sem, zs_sem, zr_sem, ob_sem, c_sem, y_sem, f_sem, c2_sem, y2_sem,
    i_sem, iy_sem, halo_sem, before_sem, gather_sem, w_sem, l_sem, bcv_sem, h1_sem, gx_sem,
    small_sem, v_sem, wy_sem, wx_sem, wz_sem, wc_sem, wl_sem,
):
    tokens, chunk, width, ff, local, nseq = dims
    chunks = tokens // chunk
    block = width // (2 * nseq)
    per = block // ROWS
    beat = per + 1
    ticks = 4 * beat
    p = lax.axis_index("dp")
    z = lax.axis_index("seq")
    me = lax.axis_index("mp")
    y, c = me // 2, me % 2
    x_dev = {"dp": 1 - p}
    up_dev = {"seq": z + 1}
    dn_dev = {"seq": z - 1}
    y_dev = {"mp": (1 - y) * 2 + c}
    c_dev = {"mp": y * 2 + 1 - c}
    last = nseq - 1
    ck, ck2, qk2 = kf.at[pl.ds(0, 2)], kf.at[pl.ds(2, 2)], kf.at[4]
    third = ff // 3 // 128 * 128
    cuts = ((0, third), (third, third), (2 * third, ff - 2 * third))

    def remote(src, dst, sems, where, at=None):
        s_sem, r_sem = (sems.at[0], sems.at[1]) if at is None else (sems.at[0, at], sems.at[1, at])
        return pltpu.make_async_remote_copy(
            src_ref=src, dst_ref=dst, send_sem=s_sem, recv_sem=r_sem,
            device_id=where, device_id_type=MESH,
        )

    def load(src, dst, sem):
        return pltpu.make_async_copy(src, dst, sem)

    def wi_load(k):
        return load(wi_h.at[k], w0.at[pl.ds(0, width), pl.ds(k * local, local)], w_sem.at[k])

    wd_load = load(wd_h, w0, w_sem.at[3])
    wg_load = load(wg_h, wg, w_sem.at[4])
    wu_load = load(wu_h, wu, w_sem.at[5])
    def wo_load(q):
        return load(wo_h.at[:, pl.ds(q * local, local)], wof.at[0, pl.ds(q * local, local), :], wl_sem.at[q])

    for k in range(3):
        wi_load(k).start()
    own_v[0:1, :] = gain_mix_v[...].astype(F32).reshape(1, local)
    own_v[1:2, :] = gain_ff_v[...].astype(F32).reshape(1, local)
    own_v[2:5, :] = taps_v[...].astype(F32)
    own_v[5:8, :] = jnp.zeros((3, local), F32)
    gv[me] = own_v[...]

    barrier = pltpu.get_barrier_semaphore()
    for dev in (x_dev, y_dev, c_dev):
        pl.semaphore_signal(barrier, inc=1, device_id=dev, device_id_type=MESH)

    @pl.when(z < last)
    def _():
        pl.semaphore_signal(barrier, inc=1, device_id=up_dev, device_id_type=MESH)

    @pl.when(z > 0)
    def _():
        pl.semaphore_signal(barrier, inc=1, device_id=dn_dev, device_id_type=MESH)

    peers = 3 + jnp.where(z < last, 1, 0) + jnp.where(z > 0, 1, 0)
    pl.semaphore_wait(barrier, peers)

    small_v[...] = jnp.zeros_like(small_v)

    def rows_at(i):
        return pl.ds(pl.multiple_of(i * chunk, chunk), chunk)

    def mixed_at(q, i):
        return r.at[0, rows_at(i), pl.ds(pl.multiple_of(q * local, 128), local)]

    share = local // (2 * nseq)

    def piece(zz):
        return woy_h.at[pl.ds(pl.multiple_of((p * nseq + zz) * share, 16), share), :]

    def wy():
        mine = wo_h.at[pl.ds(pl.multiple_of((p * nseq + z) * share, 16), share), :]
        return pltpu.make_async_remote_copy(
            src_ref=mine, dst_ref=piece(z), send_sem=wy_sem.at[0], recv_sem=wy_sem.at[1],
            device_id=y_dev, device_id_type=MESH,
        )

    def wx(zz):
        return remote(piece(zz), piece(zz), wx_sem, x_dev, zz)

    def wz(way, step):
        part = piece(z + step if way else z - step)
        return pltpu.make_async_remote_copy(
            src_ref=part, dst_ref=part, send_sem=wz_sem.at[0, way, step], recv_sem=wz_sem.at[1, way, step],
            device_id=dn_dev if way else up_dev, device_id_type=MESH,
        )

    def wz_sends(way, step):
        return jnp.logical_and(z > 0, z + step <= last) if way else jnp.logical_and(z < last, z >= step)

    def wz_receives(way, step):
        return z + 1 + step <= last if way else z >= step + 1

    def wo_step(step):
        if step == 0:
            wy().wait_recv()
            wx(z).start()
        for way in (0, 1):
            if step > 0:
                @pl.when(wz_receives(way, step - 1))
                def _(way=way):
                    wz(way, step - 1).wait_recv()
                    wx(z + step if way else z - step).start()
            if step < last:
                @pl.when(wz_sends(way, step))
                def _(way=way):
                    wz(way, step).start()

    def wo_columns(src, q, kind):
        rows = pl.ds(pl.multiple_of(q * local, 128), local)
        for pair in (0, 1):
            cols = pl.ds(pl.multiple_of((2 * pair + c) * local, 128), local)
            yield load(src.at[:, cols], wof.at[pair, rows, :], wl_sem.at[2 * kind + pair])
            cols = pl.ds(pl.multiple_of((2 * pair + 1 - c) * local, 128), local)
            yield remote(src.at[:, cols], wof.at[pair, rows, :], wc_sem, c_dev, 2 * kind + pair)

    def wo_end():
        wy().wait_send()
        for zz in range(nseq):
            wx(zz).wait()
        for way in (0, 1):
            for step in range(last):
                @pl.when(wz_sends(way, step))
                def _(way=way, step=step):
                    wz(way, step).wait_send()
        for one in wo_columns(woy_h, (1 - y) * 2 + c, 1):
            one.start()

    def gather(which, i, leg):
        if which == 2:
            src = mine = own_v
            dst = gv
            at = (2, 0)
        elif which == 3:
            mine = mixed_at(me, i)
            at = (3, i)
        else:
            src, dst = (x_in, x_h) if which == 0 else (cot_in, cot_h)
            mine = src.at[rows_at(i), :]
            at = (which, i)
        if which == 3:
            slot = lambda q: mixed_at(q, i)
        else:
            slot = (lambda q: dst.at[q]) if which == 2 else (lambda q: dst.at[q, rows_at(i), :])
        sems = [gather_sem.at[leg, way, at[0], at[1]] for way in (0, 1)]
        if leg == 0:
            pair, where = (mine, slot(me)), y_dev
        elif leg == 1:
            pair, where = (mine, slot(me)), c_dev
        else:
            from_y = (1 - y) * 2 + c
            pair, where = (slot(from_y), slot(from_y)), c_dev
        return pltpu.make_async_remote_copy(
            src_ref=pair[0], dst_ref=pair[1], send_sem=sems[0], recv_sem=sems[1],
            device_id=where, device_id_type=MESH,
        )

    def gather_start(which, i):
        gather(which, i, 0).start()
        gather(which, i, 1).start()

    def gather_pass(which, i):
        gather(which, i, 0).wait_recv()
        gather(which, i, 2).start()

    def gather_end(which, i):
        gather(which, i, 0).wait_send()
        gather(which, i, 1).wait()
        gather(which, i, 2).wait()

    gather(0, 0, 0).start()
    gather_start(2, 0)
    for i in range(chunks):
        gather(0, i, 1).start()
    for one in wo_columns(wo_h, me, 0):
        one.start()
    wg_load.start()
    wu_load.start()

    def on_size(t, f):
        pl.when(t // beat < 3)(lambda: f(pl.ds(0, ff)))
        pl.when(t // beat == 3)(lambda: f(pl.ds(0, 4 * local)))

    def place(t):
        return lax.rem(t, beat)

    def is_first(t):
        return place(t) == 0

    def is_second(t):
        return place(t) == SECOND

    def is_plain(t):
        return jnp.logical_and(place(t) != 0, place(t) != SECOND)

    def row_block(t):
        plain = place(t) - jnp.where(place(t) > SECOND, 2, 1)
        return jnp.where(is_plain(t), plain, per - 1)

    def x_number(t):
        return t // beat * (per - 1) + row_block(t)

    def x_do(t, what):
        n = x_number(t)

        def f(cols):
            copy = pltpu.make_async_remote_copy(
                src_ref=xs.at[lax.rem(n, 3), :, cols], dst_ref=xr.at[lax.rem(n, 5), :, cols],
                send_sem=xs_sem.at[lax.rem(n, 3)], recv_sem=xr_sem.at[lax.rem(n, 5)],
                device_id=x_dev, device_id_type=MESH,
            )
            getattr(copy, what)()

        on_size(t, f)

    def v_do(t, what):
        def f(cols):
            copy = pltpu.make_async_remote_copy(
                src_ref=vs.at[:, cols], dst_ref=vr.at[:, cols], send_sem=v_sem.at[0], recv_sem=v_sem.at[1],
                device_id=x_dev, device_id_type=MESH,
            )
            getattr(copy, what)()

        on_size(t, f)

    def zs_at(t, step):
        return sum(k + 2 for k in range(step)) + lax.rem(t, step + 2)

    def zr_at(t, step):
        return 4 * step + lax.rem(t, 6 if step == last - 1 else 4)

    def z_do(t, way, step, what):
        def f(cols):
            copy = pltpu.make_async_remote_copy(
                src_ref=zs.at[way, zs_at(t, step), :, cols], dst_ref=zr.at[way, zr_at(t, step), :, cols],
                send_sem=zs_sem.at[way, zs_at(t, step)], recv_sem=zr_sem.at[way, zr_at(t, step)],
                device_id=dn_dev if way else up_dev, device_id_type=MESH,
            )
            getattr(copy, what)()

        on_size(t, f)

    def receives(way, step):
        if way:
            return jnp.logical_and(z < last, z >= last - 1 - step)
        return jnp.logical_and(z > 0, z <= step + 1)

    def can_send(way, step):
        if way:
            return jnp.logical_and(z > 0, z >= last - step)
        return jnp.logical_and(z < last, z <= step)

    def z_arrived(t, step):
        for way in (0, 1):
            @pl.when(receives(way, step))
            def _(way=way):
                z_do(t, way, step, "wait_recv")

            @pl.when(can_send(way, step))
            def _(way=way):
                z_do(t, way, step, "wait_send")

    def z_step(t, step):
        sl = lax.rem(t, LAG + 4)

        def quarter(way, k):
            at = z - last + k if way else last - k + z
            return s_buf[sl, pl.ds(at * ROWS, ROWS), :]

        if step == 0:
            for way, end in ((0, 0), (1, last)):
                @pl.when(z == end)
                def _(way=way):
                    for k in range(last):
                        zs[way, zs_at(t, k)] = quarter(way, k)
                        z_do(t, way, k, "start")

            return
        z_arrived(t, step - 1)
        onward = [jnp.logical_and(receives(way, step - 1), can_send(way, step)) for way in (0, 1)]
        for way in (0, 1):
            @pl.when(onward[way])
            def _(way=way):
                value = quarter(way, step).astype(F32) + zr[way, zr_at(t, step - 1)].astype(F32)
                zs[way, zs_at(t, step)] = value.astype(BF)

        for way in (0, 1):
            @pl.when(onward[way])
            def _(way=way):
                z_do(t, way, step, "start")

    def compute(t, kind):
        sl = lax.rem(t, LAG + 4)
        at = row_block(t) * ROWS
        m = ROWS * nseq

        def rows_of(index, half):
            rows = [pl.ds(pl.multiple_of((half * nseq + s) * block + at, ROWS), ROWS) for s in range(nseq)]
            if kind == 3 and index == 1:
                return [wg[some, pl.ds(0, tokens)] for some in rows]
            return [lt[index, some, :] for some in rows]

        if kind == 3:
            parts = [(0, 0, 0, local)] + [(1, 0, k * local, local) for k in (1, 2, 3)]
        elif kind == 0:
            parts = [(0, 0, lo, n) for lo, n in cuts]
        else:
            parts = [(1, t // beat, lo, n) for lo, n in cuts]

        @pl.when(is_plain(t))
        def _():
            slot = lax.rem(x_number(t), 3)
            left = [jnp.concatenate(rows_of(i, 1 - p) + rows_of(i, p), 0) for i in sorted({q[0] for q in parts})]
            for i, ri, lo, n in parts:
                cols = pl.ds(lo, n)
                out = nn(left[i if len(left) == 2 else 0], r[ri, :, cols])
                xs[slot, :, cols] = out[:m].astype(BF)
                s_buf[sl, :, cols] = out[m:].astype(BF)
            x_do(t, "start")

        @pl.when(jnp.logical_not(is_plain(t)))
        def _():
            half = jnp.where(is_first(t), p, 1 - p)
            left = [jnp.concatenate(rows_of(i, half), 0) for i in sorted({q[0] for q in parts})]
            for i, ri, lo, n in parts:
                cols = pl.ds(lo, n)
                s_buf[sl, :, cols] = nn(left[i if len(left) == 2 else 0], r[ri, :, cols]).astype(BF)

    def out_do(src, t, sems, what):
        rows = pl.ds(pl.multiple_of(row_block(t) * ROWS, ROWS), ROWS)
        for g, target in enumerate((gdown_h, ggate_h, gup_h)):
            @pl.when(t // beat == g)
            def _(target=target):
                getattr(load(src, target.at[rows, :], ob_sem.at[sems, 0]), what)()

        @pl.when(t // beat == 3)
        def _():
            getattr(load(src.at[:, pl.ds(0, local)], gout_h.at[rows, :], ob_sem.at[sems, 0]), what)()
            for k in range(3):
                part = src.at[:, pl.ds((k + 1) * local, local)]
                getattr(load(part, gin_h.at[k, rows, :], ob_sem.at[sems, 1 + k]), what)()

    def plain_out(t, what):
        slot = lax.rem(x_number(t), 2)
        out_do(ob.at[slot], t, slot, what)

    def finish(t):
        sl = lax.rem(t, LAG + 4)
        z_arrived(t, last - 1)

        def total(then):
            def end(ways):
                value = s_buf[sl, pl.ds(z * ROWS, ROWS), :].astype(F32)
                for way in ways:
                    value += zr[way, zr_at(t, last - 1)].astype(F32)
                then(value)

            pl.when(z == 0)(lambda: end((1,)))
            pl.when(z == last)(lambda: end((0,)))
            pl.when(jnp.logical_and(z > 0, z < last))(lambda: end((0, 1)))

        @pl.when(is_plain(t))
        def _():
            n = x_number(t)
            before = t - jnp.where(place(t) == per, 2, 3)

            @pl.when(n >= 2)
            def _():
                plain_out(before, "wait")

            def put(value):
                ob[lax.rem(n, 2)] = value.astype(BF)

            total(put)
            plain_out(t, "start")

        @pl.when(is_first(t))
        def _():
            def put(value):
                vk[...] = value

            total(put)

        @pl.when(is_second(t))
        def _():
            def put(value):
                vs[...] = value.astype(BF)

            total(put)
            v_do(t, "start")

    def v_end(t):
        @pl.when(is_second(t))
        def _():
            v_do(t, "wait")

            @pl.when(t >= beat)
            def _():
                out_do(ob.at[2], t - beat, 2, "wait")

            ob[2] = (vk[...] + vr[...].astype(F32)).astype(BF)
            out_do(ob.at[2], t, 2, "start")

    def within(t, f):
        @pl.when(jnp.logical_and(t >= 0, t < ticks))
        def _():
            f(t)

    def tick_a(t, full=False):
        within(t - LAG - 4 - WAIT, v_end)
        within(t - LAG - 4, finish)

        def x_in(u):
            @pl.when(is_plain(u))
            def _():
                x_do(u, "wait")
                sl = lax.rem(u, LAG + 4)
                arrived = xr[lax.rem(x_number(u), 5)].astype(F32)
                s_buf[sl] = (s_buf[sl].astype(F32) + arrived).astype(BF)

            z_step(u, 0)

        within(t - LAG, x_in)
        if full:
            pl.when(t // beat == 0)(lambda: compute(t, 0))
            pl.when(jnp.logical_and(t // beat > 0, t // beat < 3))(lambda: compute(t, 1))
            pl.when(t // beat == 3)(lambda: compute(t, 3))

    def tick_b(t):
        within(t - LAG - 1, lambda u: z_step(u, 1))

    def tick_c(t):
        within(t - LAG - 2, lambda u: z_step(u, 2))

    def in_slices(own, others, to, slot):
        copies = [load(own, to(me), l_sem.at[slot, 0])]
        for step in range(1, 4):
            q = lax.rem(me + step, 4)
            copies.append(load(others(q), to(q), l_sem.at[slot, step]))
        return copies

    def cot_load(i):
        return in_slices(
            cot_in.at[rows_at(i), :],
            lambda q: cot_h.at[q, rows_at(i), :],
            lambda q: cotc.at[:, pl.ds(pl.multiple_of(q * local, 128), local)],
            0,
        )

    def x_load(i):
        return in_slices(x_in.at[rows_at(i), :], lambda q: x_h.at[q, rows_at(i), :], lambda q: xc.at[q], 1)

    def start(copies):
        for one in copies:
            one.start()

    def wait(copies):
        for one in copies:
            one.wait()

    def h1_load(i):
        return load(h1_h.at[:, rows_at(i), :], xc, l_sem.at[2, 0])

    def bcv_load(i):
        return load(bcv_h.at[:, rows_at(i), :], bcv, l_sem.at[2, 1])

    def gain(row, q):
        return gv[q, row : row + 1, :]

    def by_rows_of(count, f):
        def body(b, _):
            f(pl.ds(pl.multiple_of(b * count, count), count))
            return 0

        lax.fori_loop(0, chunk // count, body, 0)

    def normed_to(src, row, after=None):
        def f(some):
            ssq = jnp.zeros((64, local), F32)
            for q in range(4):
                values = src(q, some).astype(F32)
                ssq += values * values
            scale = lax.rsqrt(jnp.sum(ssq, -1, keepdims=True) / width + EPS)
            for q in range(4):
                dhoc[some, pl.ds(q * local, local)] = (src(q, some).astype(F32) * scale * gain(row, q)).astype(BF)

        by_rows_of(64, f)

    def transposed_to(index, i):
        at = pl.multiple_of(i * chunk, chunk)
        for q in range(4):
            cols = pl.ds(q * local, local)
            lt[index, cols, pl.ds(at, chunk)] = dhoc[:, cols].T

    def before_copy(i):
        return remote(before_s.at[i], before_r.at[i], before_sem, up_dev, i)

    def bcv_store(i):
        return load(bcv, bcv_h.at[:, rows_at(i), :], bcv_sem)

    def h1_store(i, slot, pair, core):
        return load(da2f.at[slot, pair, core], h1_h.at[2 * pair + core, rows_at(i), :], h1_sem.at[pair, core])

    def project(i):
        wait(x_load(i))
        normed_to(lambda q, some: xc[q, some, :], 0)
        value = nn(dhoc[...], w0[pl.ds(0, width), pl.ds(0, 3 * local)])

        @pl.when(i > 0)
        def _():
            bcv_store(i - 1).wait()

        for k in range(3):
            bcv[k] = value[:, k * local : (k + 1) * local].astype(BF)
        dcp[pl.ds(0, chunk), :] = value[:, local : 2 * local]
        bx = (value[:, :local] * value[:, 2 * local :]).astype(BF)
        bcv[3] = bx
        bxp[pl.ds(8, chunk), :] = bx.astype(F32)
        before_s[i] = bxp[pl.ds(chunk, 8), :]

        @pl.when(z < last)
        def _():
            before_copy(i).start()

        bcv_store(i).start()

    def conv_of():
        shifts = [bxp[pl.ds(6 + k, chunk), :] for k in range(3)]
        return sum(own_v[2 + k : 3 + k, :] * shifts[k] for k in range(3)), shifts

    def mix(i):
        @pl.when(z < last)
        def _():
            before_copy(i).wait_send()

        @pl.when(z > 0)
        def _():
            before_copy(i).wait_recv()

        @pl.when(z == 0)
        def _():
            before_r[i] = jnp.zeros((8, local), F32)

        bxp[pl.ds(0, 8), :] = before_r[i]
        mixed = (dcp[pl.ds(0, chunk), :] * conv_of()[0]).astype(BF)
        r[0, rows_at(i), pl.ds(pl.multiple_of(me * local, 128), local)] = mixed
        gather_start(3, i)

    def x_two(i):
        return [
            load(x_in.at[rows_at(i), :], cs2.at[y], l_sem.at[2, 2]),
            load(x_h.at[(1 - y) * 2 + c, rows_at(i), :], cs2.at[1 - y], l_sem.at[2, 3]),
        ]

    def residual(i):
        slot = lax.rem(i, 2)
        gather_end(3, i)
        wait(x_two(i))

        @pl.when(i >= 1)
        def _():
            for pair in (0, 1):
                for core in (0, 1):
                    h1_store(i - 1, 1 - slot, pair, core).wait()

        for pair in (0, 1):
            h1 = nn(r[0, rows_at(i), pl.ds(0, width)], wof[pair]) + cs2[pair].astype(F32)
            da2f[slot, pair, c] = h1.astype(BF)

            @pl.when(y == pair)
            def _(h1=h1):
                dh1s[i] = h1
        remote(da2f.at[slot, :, c], da2f.at[slot, :, c], f_sem, c_dev, slot).start()

        @pl.when(i + 1 < chunks)
        def _():
            start(x_two(i + 1))

    def cot_fetch(i):
        gather_end(1, i)
        start(cot_load(i))

    def cot_turn(i):
        wait(cot_load(i))
        at = pl.multiple_of(i * chunk, chunk)
        for q in range(4):
            cols = pl.ds(q * local, local)
            lt[0, cols, pl.ds(at, chunk)] = cotc[:, cols].T

    def feed(i):
        slot = lax.rem(i, 2)
        remote(da2f.at[slot, :, c], da2f.at[slot, :, c], f_sem, c_dev, slot).wait()
        for pair in (0, 1):
            for core in (0, 1):
                h1_store(i, slot, pair, core).start()
        normed_to(lambda q, some: da2f[slot, q // 2, q % 2, some, :], 1)
        transposed_to(1, i)
        rows = rows_at(i)
        for lo, n in cuts:
            dbuf[:, pl.ds(0, n)] = nt(dhoc[...], wg[pl.ds(lo, n), :])
            r[2, rows, pl.ds(lo, n)] = nt(dhoc[...], wu[pl.ds(lo, n), :]).astype(BF)

            def by_rows(b, _, lo=lo, n=n):
                cols = pl.ds(lo, n)
                here = pl.ds(pl.multiple_of(b * 64, 64), 64)
                some = pl.ds(pl.multiple_of(i * chunk + b * 64, 64), 64)
                gate = dbuf[here, pl.ds(0, n)]
                up = r[2, some, cols].astype(F32)
                r[0, some, cols] = (gate * jax.nn.sigmoid(gate) * up).astype(BF)
                r[1, some, cols] = gate.astype(BF)
                return 0

            lax.fori_loop(0, chunk // 64, by_rows, 0)

    def hidden_back(piece):
        i = piece // 3

        @pl.when(lax.rem(piece, 3) == 0)
        def _():
            wait(cot_load(i))

        for k, cut in enumerate(cuts):
            pl.when(lax.rem(piece, 3) == k)(functools.partial(hidden_cut, i, *cut))

        @pl.when(jnp.logical_and(lax.rem(piece, 3) == 2, i + 1 < chunks))
        def _():
            start(cot_load(i + 1))

    def hidden_cut(i, lo, n):
        if True:
            cols = pl.ds(lo, n)
            dbuf[:, pl.ds(0, n)] = nt(cotc[...], w0[pl.ds(lo, n), :])

            def by_rows(b, _, cols=cols, n=n):
                some = pl.ds(pl.multiple_of(i * chunk + b * 32, 32), 32)
                dhid = dbuf[pl.ds(pl.multiple_of(b * 32, 32), 32), pl.ds(0, n)]
                gate = r[1, some, cols].astype(F32)
                up = r[2, some, cols].astype(F32)
                sig = jax.nn.sigmoid(gate)
                r[1, some, cols] = (dhid * up * sig * (1.0 + gate * (1.0 - sig))).astype(BF)
                r[2, some, cols] = (dhid * gate * sig).astype(BF)
                return 0

            lax.fori_loop(0, chunk // 32, by_rows, 0)

    def split_store(pair, value, keep, send):
        for side in (0, 1):
            part = value[:, side * local : (side + 1) * local]

            @pl.when(c == side)
            def _(part=part):
                keep[pair] = part

            @pl.when(c != side)
            def _(part=part):
                send[pair] = part.astype(BF)

    def stage_a(i):
        slot = lax.rem(i, 2)
        rows = rows_at(i)
        for pair in (0, 1):
            cols = pl.ds(pair * 2 * local, 2 * local)
            value = nn(r[1, rows, :], wg[:, cols]) + nn(r[2, rows, :], wu[:, cols])
            split_store(pair, value, ck, cs)
        remote(cs, cr.at[slot], c_sem, c_dev, slot).start()

        @pl.when(i == chunks - 1)
        def _():
            start(x_whole())

    def x_whole():
        copies = [load(x_in, wu.at[pl.ds(0, tokens), pl.ds(pl.multiple_of(me * local, 128), local)], l_sem.at[3, 0])]
        for step in range(1, 4):
            q = lax.rem(me + step, 4)
            cols = pl.ds(pl.multiple_of(q * local, 128), local)
            copies.append(load(x_h.at[q], wu.at[pl.ds(0, tokens), cols], l_sem.at[3, step]))
        return copies

    def stage_a1(i):
        @pl.when(i == 0)
        def _():
            wait(x_whole())

        at = pl.multiple_of(i * chunk, chunk)
        normed_to(lambda q, some: wu[pl.ds(at + some.start, some.size), pl.ds(q * local, local)], 0)
        for q in range(4):
            cols = pl.ds(q * local, local)
            wg[cols, pl.ds(at, chunk)] = dhoc[:, cols].T

    def stage_loads(i):
        start(cot_load(i))
        h1_load(i).start()
        bcv_load(i).start()

    def stage_b(i):
        slot = lax.rem(i, 2)
        remote(cs, cr.at[slot], c_sem, c_dev, slot).wait()
        ys[...] = (ck[...] + cr[slot].astype(F32)).astype(BF)
        remote(ys, yr4.at[slot], y_sem, y_dev, slot).start()

    def stage_c(i):
        slot = lax.rem(i, 2)
        remote(ys, yr4.at[slot], y_sem, y_dev, slot).wait()
        da2f[slot, :, c] = (ys[...].astype(F32) + yr4[slot].astype(F32)).astype(BF)
        remote(da2f.at[slot, :, c], da2f.at[slot, :, c], f_sem, c_dev, slot).start()

    def stage_d(i):
        slot = lax.rem(i, 2)
        remote(da2f.at[slot, :, c], da2f.at[slot, :, c], f_sem, c_dev, slot).wait()
        wait(cot_load(i))
        h1_load(i).wait()
        bcv_load(i).wait()
        at = pl.multiple_of(i * chunk, chunk)
        own = pl.ds(pl.multiple_of(me * local, 128), local)

        def by_rows(b, _):
            some = pl.ds(pl.multiple_of(b * 64, 64), 64)
            ssq = jnp.zeros((64, local), F32)
            inner = jnp.zeros((64, local), F32)
            for q in range(4):
                cols = pl.ds(q * local, local)
                h1 = xc[q, some, :].astype(F32)
                ssq += h1 * h1
                inner += da2f[slot, q // 2, q % 2, some, :].astype(F32) * gain(1, q) * h1
            r2 = lax.rsqrt(jnp.sum(ssq, -1, keepdims=True) / width + EPS)
            scale = r2 * r2 * r2 * jnp.sum(inner, -1, keepdims=True) / width

            def grad(q, cols, da2):
                h1 = xc[q, some, :].astype(F32)
                return cotc[some, cols].astype(F32) + r2 * (da2 * gain(1, q)) - h1 * scale

            for q in range(4):
                cols = pl.ds(q * local, local)
                dhoc[some, cols] = grad(q, cols, da2f[slot, q // 2, q % 2, some, :].astype(F32)).astype(BF)
            da2 = da2f[slot, y, c, some, :].astype(F32)
            dh1s[i, some, :] = grad(me, own, da2)
            terms = da2 * xc[me, some, :].astype(F32) * r2
            small_v[pl.ds(8, 8), :] += sum(terms[8 * k : 8 * k + 8] for k in range(8))
            return 0

        lax.fori_loop(0, chunk // 64, by_rows, 0)
        start(x_load(i))
        transposed_to(0, i)
        @pl.when(i == 0)
        def _():
            for q in range(4):
                wo_load(q).wait()

        dmixed = jnp.zeros((chunk, local), F32)
        for q in range(4):
            cols = pl.ds(q * local, local)
            dmixed += nt(dhoc[:, cols], wof[0, cols, :])
        c_gate = bcv[1]
        bxp[pl.ds(0, 8), :] = before_r[i]
        bxp[pl.ds(8, chunk), :] = bcv[3].astype(F32)
        conv, shifts = conv_of()
        r[0, pl.ds(at, chunk), pl.ds(0, local)] = (c_gate.astype(F32) * conv).astype(BF)
        r[0, pl.ds(at, chunk), pl.ds(2 * local, local)] = (dmixed * conv).astype(BF)
        dconv = (dmixed * c_gate.astype(F32)).astype(BF).astype(F32)
        dcp[pl.ds(0, chunk), :] = dconv
        halo_s[i] = dconv[:8]
        for k in range(3):
            small_v[1 + k : 2 + k, :] += jnp.sum(dconv * shifts[k], 0, keepdims=True)

        @pl.when(z > 0)
        def _():
            halo_copy(i).start()

    def halo_copy(i):
        return remote(halo_s.at[i], halo_r.at[i], halo_sem, dn_dev, i)

    def stage_e(i):
        slot = lax.rem(i, 2)

        @pl.when(i == 0)
        def _():
            for k in range(3):
                wi_load(k).wait()
            out_copy(chunks - 1).wait()

        wait(x_load(i))

        @pl.when(z > 0)
        def _():
            halo_copy(i).wait_send()

        @pl.when(z < last)
        def _():
            halo_copy(i).wait_recv()
            dcp[pl.ds(chunk, 8), :] = halo_r[i]

        @pl.when(z == last)
        def _():
            dcp[pl.ds(chunk, 8), :] = jnp.zeros((8, local), F32)

        dbx = sum(own_v[4 - k : 5 - k, :] * dcp[pl.ds(k, chunk), :] for k in range(3))
        rows = rows_at(i)
        r[0, rows, pl.ds(local, local)] = (dbx * bcv[2].astype(F32)).astype(BF)
        r[0, rows, pl.ds(3 * local, local)] = (dbx * bcv[0].astype(F32)).astype(BF)
        inner = jnp.zeros((chunk, 1), F32)
        ssq = jnp.zeros((chunk, 1), F32)
        for pair in (0, 1):
            cols = pl.ds(pair * 2 * local, 2 * local)
            value = nt(r[0, rows, pl.ds(local, 3 * local)], w0[cols, pl.ds(0, 3 * local)])
            for side in (0, 1):
                q = 2 * pair + side
                x = xc[q].astype(F32)
                part = value[:, side * local : (side + 1) * local]
                inner += jnp.sum(part * x * gain(0, q), -1, keepdims=True)
                ssq += jnp.sum(x * x, -1, keepdims=True)
            split_store(pair, value, ck2, cs2)
        xo[...] = xc[me]
        ins[...] = jnp.broadcast_to(inner, (chunk, 128)).T[:8]
        r1s[...] = jnp.broadcast_to(lax.rsqrt(ssq / width + EPS), r1s.shape)
        remote(cs2, yr4.at[2 + slot], c2_sem, c_dev, slot).start()
        remote(ins, inr.at[slot], i_sem, c_dev, slot).start()

        @pl.when(i + 1 < chunks)
        def _():
            stage_loads(i + 1)

    def stage_f(i):
        slot = lax.rem(i, 2)
        remote(cs2, yr4.at[2 + slot], c2_sem, c_dev, slot).wait()
        remote(ins, inr.at[slot], i_sem, c_dev, slot).wait()
        ys2[...] = (ck2[1 - y] + yr4[2 + slot, 1 - y].astype(F32)).astype(BF)
        qk2[...] = ck2[y] + yr4[2 + slot, y].astype(F32)
        iys[...] = ins[...] + inr[slot]
        remote(ys2, yr2.at[slot], y2_sem, y_dev, slot).start()
        remote(iys, iyr.at[slot], iy_sem, y_dev, slot).start()

    def gx_copy(i):
        return load(gxb, gx_h.at[rows_at(i), :], gx_sem)

    def stage_g(i):
        slot = lax.rem(i, 2)
        remote(ys2, yr2.at[slot], y2_sem, y_dev, slot).wait()
        remote(iys, iyr.at[slot], iy_sem, y_dev, slot).wait()
        da1 = qk2[...] + yr2[slot].astype(F32)
        inner = jnp.broadcast_to(iys[:1] + iyr[slot, :1], (128, chunk)).T[:, :1]
        r1 = r1s[:, :1]
        x = xo[...].astype(F32)
        scaled = gain(0, me)
        small_v[0:1, :] += jnp.sum(da1 * x * r1, 0, keepdims=True)

        @pl.when(i > 0)
        def _():
            gx_copy(i - 1).wait()

        gxb[...] = (dh1s[i] + r1 * scaled * da1 - x * (r1 * r1 * r1 * inner / width)).astype(BF)
        gx_copy(i).start()

    def out_start(i):
        rows = rows_at(i)
        for pair in (0, 1):
            cols = pl.ds(pair * 2 * local, 2 * local)
            split_store(pair, nn(r[0, rows, :], w0[:, cols]), ck2, cs2)
        remote(cs2, yr4.at[2 + lax.rem(i, 2)], c2_sem, c_dev, lax.rem(i, 2)).start()

        @pl.when(i == chunks - 1)
        def _():
            for k in range(3):
                wi_load(k).start()

    def out_share(i):
        slot = lax.rem(i, 2)
        remote(cs2, yr4.at[2 + slot], c2_sem, c_dev, slot).wait()
        ys2[...] = (ck2[1 - y] + yr4[2 + slot, 1 - y].astype(F32)).astype(BF)
        qk2[...] = ck2[y] + yr4[2 + slot, y].astype(F32)
        remote(ys2, yr2.at[slot], y2_sem, y_dev, slot).start()

    def out_copy(i):
        return load(gxb, out_h.at[rows_at(i), :], gx_sem)

    def out_end(i):
        slot = lax.rem(i, 2)
        remote(ys2, yr2.at[slot], y2_sem, y_dev, slot).wait()

        @pl.when(i > 0)
        def _():
            out_copy(i - 1).wait()

        gxb[...] = (dh1s[i] + (qk2[...] + yr2[slot].astype(F32))).astype(BF)
        out_copy(i).start()

    def valid(i, f):
        @pl.when(jnp.logical_and(i >= 0, i < chunks))
        def _():
            f(i)

    gather_pass(0, 0)
    gather(0, 1, 0).start()
    wy().start()
    gather_pass(2, 0)
    for k in range(3):
        wi_load(k).wait()
    gather_end(2, 0)

    gather_end(0, 0)
    start(x_load(0))

    def when(now, *calls):
        @pl.when(now)
        def _():
            for f in calls:
                f()

    def weights_there():
        wg_load.wait()
        wu_load.wait()

    def wo_there():
        wo_end()
        for kind, src in ((0, wo_h), (1, woy_h)):
            for one in wo_columns(src, me if kind == 0 else (1 - y) * 2 + c, kind):
                one.wait()

    def forward(j, _):
        when(j < chunks, lambda: project(j))
        when(j + 1 < chunks, lambda: gather_pass(0, j + 1))
        when(j + 2 < chunks, lambda: gather(0, j + 2, 0).start())
        when(j == 0, lambda: wo_step(0))
        when(j == 1, lambda: wo_step(1))
        when(j == 2, lambda: wo_step(3))
        when(j == 3, wo_there, weights_there)
        when(j >= 3, lambda: residual(j - 3))
        when(j < chunks, lambda: mix(j))
        when(j + 1 < chunks, lambda: gather_end(0, j + 1), lambda: start(x_load(j + 1)))
        when(j == 1, lambda: wo_step(2))
        when(j == 2, lambda: start(x_two(0)), lambda: gather(1, 0, 0).start(), lambda: gather(1, 1, 0).start())
        when(jnp.logical_and(j > 0, j < chunks), lambda: gather_pass(3, j - 1))
        when(j > 3, lambda: cot_turn(j - 4))
        when(j == 5, *[functools.partial(gather_pass, 1, k) for k in range(2, chunks)])
        when(j > 3, lambda: cot_fetch(j - 3))
        when(j >= 3, lambda: feed(j - 3))
        when(
            j == 3, wd_load.start, *[functools.partial(gather_pass, 1, k) for k in range(2)],
            *[gather(1, k, 0).start for k in range(2, chunks)], lambda: cot_fetch(0),
        )
        when(j == 4, lambda: gather_pass(3, chunks - 1))
        return 0

    for i in range(chunks):
        gather(1, i, 1).start()
    lax.fori_loop(0, chunks + 3, forward, 0)
    for q in range(4):
        wo_load(q).start()
    bcv_store(chunks - 1).wait()
    for pair in (0, 1):
        for core in (0, 1):
            h1_store(chunks - 1, (chunks - 1) % 2, pair, core).wait()

    cot_turn(chunks - 1)
    start(cot_load(0))

    def small_x():
        return pltpu.make_async_remote_copy(
            src_ref=small_v.at[pl.ds(0, 8)], dst_ref=small_r.at[0], send_sem=small_sem.at[0, 0],
            recv_sem=small_sem.at[0, 1], device_id=x_dev, device_id_type=MESH,
        )

    def small_z(way):
        return pltpu.make_async_remote_copy(
            src_ref=small_r.at[1 + way], dst_ref=small_r.at[3 + way], send_sem=small_sem.at[1 + way, 0],
            recv_sem=small_sem.at[1 + way, 1], device_id=dn_dev if way else up_dev, device_id_type=MESH,
        )

    def small_step(k):
        @pl.when(k == 0)
        def _():
            small_x().wait()
            total = small_v[pl.ds(0, 8), :] + small_r[0]
            small_v[pl.ds(0, 8), :] = total
            small_r[1] = total
            small_r[2] = total

        for way in (0, 1):
            turn = last - z if way else z

            @pl.when(jnp.logical_and(turn < last, k == turn))
            def _(way=way, turn=turn):
                @pl.when(turn > 0)
                def _():
                    small_z(way).wait_recv()
                    small_r[1 + way] = small_v[pl.ds(0, 8), :] + small_r[3 + way]

                small_z(way).start()

    def small_end():
        for way in (0, 1):
            turn = last - z if way else z

            @pl.when(turn < last)
            def _(way=way):
                small_z(way).wait_send()

            @pl.when(turn == last)
            def _(way=way):
                small_z(way).wait_recv()

            @pl.when(turn > 0)
            def _(way=way):
                small_v[pl.ds(0, 8), :] += small_r[3 + way]

    def stage_last(i):
        stage_g(i)

        @pl.when(i == chunks - 1)
        def _():
            small_v[4:5, :] = jnp.sum(small_v[8:16, :], 0, keepdims=True)
            small_x().start()

    order = (
        ("g", stage_last), ("out_end", out_end), ("out_share", out_share), ("b", stage_b), ("f", stage_f),
        ("c", stage_c), ("e", stage_e), ("d", stage_d), ("out_start", out_start), ("a", stage_a),
        ("hidden", None), ("a1", stage_a1),
    )

    def stages(t, third):
        for name, f in order:
            if name == "hidden":
                if HIDDEN[0] != third:
                    continue
                done = 0
                low = high = 0
                for at, upto in HIDDEN[1].items():
                    low = jnp.where(t == at, done, low)
                    high = jnp.where(t == at, upto, high)
                    done = upto

                def piece(k, _):
                    hidden_back(k)
                    return 0

                lax.fori_loop(low, high, piece, 0)
            elif PLACES[name][0] == third:
                where = PLACES[name][1]
                i = sum(jnp.where(t >= at, 1, 0) for at in where[1:])
                now = functools.reduce(jnp.logical_or, [t == at for at in where])
                pl.when(now)(functools.partial(f, i))

    def each_tick(t, _):
        tick_a(t, True)

        @pl.when(t == 0)
        def _():
            wd_load.wait()

        @pl.when(t == beat)
        def _():
            stage_loads(0)

        stages(t, 0)
        tick_b(t)
        stages(t, 1)
        tick_c(t)
        stages(t, 2)

        @pl.when(t > PLACES["g"][1][-1])
        def _():
            small_step(t - PLACES["g"][1][-1] - 1)

        return 0

    lax.fori_loop(0, ticks, each_tick, 0)
    gx_copy(chunks - 1).wait()

    def part_four(k, _):
        tick_a(ticks + k)
        tick_b(ticks + k)
        tick_c(ticks + k)
        return 0

    lax.fori_loop(0, LAG + 4, part_four, 0)
    small_end()
    plain_out(ticks - 2, "wait")
    plain_out(ticks - 1, "wait")
    out_do(ob.at[2], 3 * beat + SECOND, 2, "wait")


def block(dims, x_own, cot_own, gain_mix, gain_ff, taps, wd, wg, wu, wo, wi):
    tokens, chunk, width, ff, local, nseq = dims
    rows = width // (2 * nseq)
    chunks = tokens // chunk
    last = nseq - 1
    m = ROWS * nseq
    DMA = pltpu.SemaphoreType.DMA
    shape = jax.ShapeDtypeStruct
    third = ff // 3 // 128 * 128
    scratch = [
        pltpu.VMEM((2, width, tokens), BF),
        pltpu.VMEM((3, tokens, ff), BF),
        pltpu.VMEM((ff, width), BF),
        pltpu.VMEM((ff, width), BF),
        pltpu.VMEM((ff, width), BF),
        pltpu.VMEM((2, width, local), BF),
        pltpu.VMEM((chunk, width), BF),
        pltpu.VMEM((4, chunk, local), BF),
        pltpu.VMEM((chunk, local), BF),
        pltpu.VMEM((4, chunk, local), BF),
        pltpu.VMEM((8 + chunk, local), F32),
        pltpu.VMEM((chunk, ff - 2 * third), F32),
        pltpu.VMEM((8 + chunk, local), F32),
        pltpu.VMEM((chunk, width), BF),
        pltpu.VMEM((chunks, chunk, local), F32),
        pltpu.VMEM((chunk, 128), F32),
        pltpu.VMEM((4, 8, local), F32),
        pltpu.VMEM((8, local), F32),
        pltpu.VMEM((3, m, ff), BF),
        pltpu.VMEM((5, m, ff), BF),
        pltpu.VMEM((LAG + 4, m, ff), BF),
        pltpu.VMEM((2, last * (last + 3) // 2, ROWS, ff), BF),
        pltpu.VMEM((2, 4 * last + 2, ROWS, ff), BF),
        pltpu.VMEM((3, ROWS, ff), BF),
        pltpu.VMEM((ROWS, ff), BF),
        pltpu.VMEM((ROWS, ff), BF),
        pltpu.VMEM((ROWS, ff), F32),
        pltpu.VMEM((5, chunk, local), F32),
        pltpu.VMEM((2, chunk, local), BF),
        pltpu.VMEM((2, 2, chunk, local), BF),
        pltpu.VMEM((2, chunk, local), BF),
        pltpu.VMEM((4, 2, chunk, local), BF),
        pltpu.VMEM((2, 2, 2, chunk, local), BF),
        pltpu.VMEM((2, chunk, local), BF),
        pltpu.VMEM((chunk, local), BF),
        pltpu.VMEM((2, chunk, local), BF),
        pltpu.VMEM((8, chunk), F32),
        pltpu.VMEM((2, 8, chunk), F32),
        pltpu.VMEM((8, chunk), F32),
        pltpu.VMEM((2, 8, chunk), F32),
        pltpu.VMEM((chunk, local), BF),
        pltpu.VMEM((chunks, 8, local), F32),
        pltpu.VMEM((chunks, 8, local), F32),
        pltpu.VMEM((chunks, 8, local), F32),
        pltpu.VMEM((chunks, 8, local), F32),
        pltpu.VMEM((5, 8, local), F32),
        DMA((3,)), DMA((5,)), DMA((2, last * (last + 3) // 2)), DMA((2, 4 * last + 2)), DMA((3, 4)),
        DMA((2, 2)), DMA((2, chunks)), DMA((2, 2)), DMA((2, 2)), DMA((2, 2)),
        DMA((2, 2)), DMA((2, 2)), DMA((2, chunks)), DMA((2, chunks)), DMA((3, 2, 4, chunks)),
        DMA((7,)), DMA((4, 4)), DMA(()), DMA((2, 2)), DMA(()), DMA((3, 2)), DMA((2,)), DMA((2,)), DMA((2, nseq)), DMA((2, 2, last)), DMA((2, 4)), DMA((4,)),
    ]
    return pl.pallas_call(
        functools.partial(block_kernel, dims),
        out_shape=(
            shape((rows, ff), BF), shape((rows, ff), BF), shape((rows, ff), BF),
            shape((rows, local), BF), shape((3, rows, local), BF),
            shape((tokens, local), BF), shape((tokens, local), BF), shape((16, local), F32),
            shape((4, tokens, local), BF), shape((4, tokens, local), BF),
            shape((4, tokens, local), BF), shape((4, tokens, local), BF), shape((local, width), BF),
        ),
        in_specs=[ANY] * 2 + [VMEM] * 3 + [ANY] * 5,
        out_specs=(ANY,) * 7 + (VMEM,) + (ANY,) * 5,
        scratch_shapes=scratch,
        compiler_params=pltpu.CompilerParams(
            collective_id=0, has_side_effects=True, vmem_limit_bytes=63 * 2**20
        ),
    )(x_own, cot_own, gain_mix, gain_ff, taps, wd, wg, wu, wo, wi)


def shifted(array, axis, by):
    count = lax.axis_size(axis)
    pairs = [(i, i + by) for i in range(count) if 0 <= i + by < count]
    return lax.ppermute(array, axis, pairs)


def fused_device(inputs, gain_mix, w_in, kernel, w_out, gain_ff, w_gate, w_up, w_down, cotangent):
    groups, seq_rows, local = inputs.shape
    width = local * lax.axis_size("mp")
    ff = w_down.shape[0]
    tokens = groups * seq_rows
    dims = (tokens, seq_rows, width, ff, local, lax.axis_size("seq"))
    gdown, ggate, gup, gout, gin, gx, out, small = block(
        dims, inputs.reshape(tokens, local), cotangent.reshape(tokens, local), gain_mix, gain_ff, kernel,
        w_down, w_gate.T, w_up.T, w_out, w_in.transpose(1, 0, 2),
    )[:8]
    gdown, ggate, gup, gout, gin, gx, out, gmix, gtaps, gff = widen(
        gdown, ggate, gup, gout, gin, gx, out, small
    )
    whole = (groups, seq_rows, local)
    return (
        out.reshape(whole), gx.reshape(whole), gmix, gin.transpose(1, 0, 2), gtaps,
        gout.T, gff, ggate, gup, gdown.T,
    )


def widen_kernel(*refs):
    count = 7
    src, small, dst = refs[:count], refs[count], refs[count + 1 : 2 * count + 1]
    gmix, gtaps, gff = refs[2 * count + 1 : 2 * count + 4]
    narrow = refs[2 * count + 4 : 3 * count + 4]
    wide = refs[3 * count + 4 : 4 * count + 2]
    in_sem, out_sem = refs[4 * count + 2 :]
    loads = [pltpu.make_async_copy(src[k], narrow[k], in_sem.at[k]) for k in range(count)]
    stores = [
        pltpu.make_async_copy(wide[k] if k < count - 2 else narrow[k], dst[k], out_sem.at[k])
        for k in range(count)
    ]
    order = (*range(count - 2, count), *range(count - 2))
    for k in order:
        loads[k].start()
    gmix[...] = small[0:1, :].reshape(gmix.shape)
    gtaps[...] = small[1:4, :]
    gff[...] = small[4:5, :].reshape(gff.shape)
    for k in order:
        loads[k].wait()
        if k < count - 2:
            wide[k][...] = narrow[k][...].astype(F32)
        stores[k].start()
    for one in stores:
        one.wait()


def widen(*arrays):
    big, small = arrays[:7], arrays[7]
    local = small.shape[1]
    shape = jax.ShapeDtypeStruct
    outs = [shape(a.shape, F32 if k < 5 else BF) for k, a in enumerate(big)]
    outs += [shape((local,), F32), shape((3, local), F32), shape((local,), F32)]
    return pl.pallas_call(
        widen_kernel,
        out_shape=outs,
        in_specs=[ANY] * 7 + [VMEM],
        out_specs=[ANY] * 7 + [VMEM] * 3,
        scratch_shapes=[pltpu.VMEM(a.shape, BF) for a in big]
        + [pltpu.VMEM(a.shape, F32) for a in big[:5]]
        + [pltpu.SemaphoreType.DMA((7,))] * 2,
        compiler_params=pltpu.CompilerParams(vmem_limit_bytes=63 * 2**20),
    )(*big, small)


def contract_rows(left, right):
    return lax.dot_general(
        left, right, (((0,), (0,)), ((), ())), preferred_element_type=jnp.float32
    )


def contract_cols(left, right):
    return lax.dot_general(
        left, right, (((1,), (1,)), ((), ())), preferred_element_type=jnp.float32
    )


def plain_device(inputs, gain_mix, w_in, kernel, w_out, gain_ff, w_gate, w_up, w_down, cotangent):
    groups, seq_rows, local_width = inputs.shape
    full_width = local_width * lax.axis_size("mp")
    tokens = groups * seq_rows
    x_float = inputs.reshape(tokens, local_width).astype(jnp.float32)
    gain_one = gain_mix.astype(jnp.float32)
    gain_two = gain_ff.astype(jnp.float32)
    taps = kernel.astype(jnp.float32)

    def row_total(values):
        return lax.psum(jnp.sum(values, axis=-1, keepdims=True), "mp")

    def all_features(values):
        return lax.all_gather(values, "mp", axis=1, tiled=True)

    def share_sums(values):
        return lax.psum_scatter(
            values.astype(jnp.bfloat16), "mp", scatter_dimension=1, tiled=True
        ).astype(jnp.float32)

    def scattered(values, dim):
        return lax.psum_scatter(
            values.astype(jnp.bfloat16), ("dp", "seq"), scatter_dimension=dim, tiled=True
        ).astype(jnp.float32)

    def norm_scale(values):
        return lax.rsqrt(row_total(values * values) / full_width + EPS)

    def norm_back(values, scale, gain_vec, upstream):
        inner = row_total(gain_vec * upstream * values)
        grad_values = scale * gain_vec * upstream - values * scale**3 * inner / full_width
        return (grad_values, jnp.sum(upstream * values * scale, axis=0))

    scale_one = norm_scale(x_float)
    normed_in = all_features((x_float * scale_one * gain_one).astype(jnp.bfloat16))
    proj = jnp.einsum("td,dkc->tkc", normed_in, w_in, preferred_element_type=jnp.float32)
    b_gate = proj[:, 0]
    c_gate = proj[:, 1]
    values_v = proj[:, 2]
    b_times_x = (b_gate * values_v).astype(jnp.bfloat16).reshape(groups, seq_rows, local_width)
    before = shifted(b_times_x[:, seq_rows - 2 :], "seq", 1)
    padded = jnp.concatenate([before, b_times_x], 1).astype(jnp.float32)
    conv = taps[0] * padded[:, :-2] + taps[1] * padded[:, 1:-1] + taps[2] * padded[:, 2:]
    conv = conv.reshape(tokens, local_width)
    mixed = (c_gate * conv).astype(jnp.bfloat16)
    hidden_one = x_float + share_sums(jnp.dot(mixed, w_out, preferred_element_type=jnp.float32))
    scale_two = norm_scale(hidden_one)
    normed_ff = all_features((hidden_one * scale_two * gain_two).astype(jnp.bfloat16))
    gate = jnp.dot(normed_ff, w_gate, preferred_element_type=jnp.float32)
    up_proj = jnp.dot(normed_ff, w_up, preferred_element_type=jnp.float32)
    sigma = jax.nn.sigmoid(gate)
    active = gate * sigma
    hidden = (active * up_proj).astype(jnp.bfloat16)
    ffn_out = share_sums(jnp.dot(hidden, w_down, preferred_element_type=jnp.float32))
    block_out = (hidden_one + ffn_out).astype(jnp.bfloat16).reshape(groups, seq_rows, local_width)
    grad_flat = cotangent.reshape(tokens, local_width)
    grad_full = all_features(grad_flat)
    grad_down = contract_rows(hidden, grad_full)
    grad_hidden = contract_cols(grad_full, w_down)
    grad_gate_act = (grad_hidden * up_proj * sigma * (1.0 + gate * (1.0 - sigma))).astype(
        jnp.bfloat16
    )
    grad_up_act = (grad_hidden * active).astype(jnp.bfloat16)
    grad_gate = contract_rows(normed_ff, grad_gate_act)
    grad_up = contract_rows(normed_ff, grad_up_act)
    grad_normed_ff = share_sums(
        contract_cols(grad_gate_act, w_gate) + contract_cols(grad_up_act, w_up)
    )
    grad_norm_two, grad_gain_two = norm_back(hidden_one, scale_two, gain_two, grad_normed_ff)
    grad_hidden_one = grad_flat.astype(jnp.float32) + grad_norm_two
    grad_out_full = all_features(grad_hidden_one.astype(jnp.bfloat16))
    grad_out = contract_rows(mixed, grad_out_full)
    grad_mixed = contract_cols(grad_out_full, w_out)
    grad_c = grad_mixed * conv
    grad_conv = (grad_mixed * c_gate).astype(jnp.bfloat16).reshape(groups, seq_rows, local_width)
    after = shifted(grad_conv[:, :2], "seq", -1)
    extended = jnp.concatenate([grad_conv, after], 1).astype(jnp.float32)
    grad_bx = taps[2] * extended[:, :-2] + taps[1] * extended[:, 1:-1] + taps[0] * extended[:, 2:]
    grad_bx = grad_bx.reshape(tokens, local_width)
    conv_grad_float = extended[:, :-2]
    grad_taps = jnp.stack(
        [
            jnp.sum(conv_grad_float * padded[:, :-2], axis=(0, 1)),
            jnp.sum(conv_grad_float * padded[:, 1:-1], axis=(0, 1)),
            jnp.sum(conv_grad_float * padded[:, 2:], axis=(0, 1)),
        ]
    )
    grad_proj = jnp.stack([grad_bx * values_v, grad_c, grad_bx * b_gate], 1).astype(jnp.bfloat16)
    grad_in = jnp.einsum("td,tkc->dkc", normed_in, grad_proj, preferred_element_type=jnp.float32)
    grad_normed_in = share_sums(
        jnp.einsum("tkc,dkc->td", grad_proj, w_in, preferred_element_type=jnp.float32)
    )
    grad_norm_one, grad_gain_one = norm_back(x_float, scale_one, gain_one, grad_normed_in)
    grad_input = (
        (grad_hidden_one + grad_norm_one)
        .astype(jnp.bfloat16)
        .reshape(groups, seq_rows, local_width)
    )
    small_sums = lax.psum((grad_gain_one, grad_taps, grad_gain_two), ("dp", "seq"))
    by_row = (
        scattered(grad_in, 0),
        scattered(grad_gate, 0),
        scattered(grad_up, 0),
    )
    by_col = (
        scattered(grad_out, 1),
        scattered(grad_down, 1),
    )
    return (
        block_out,
        grad_input,
        small_sums[0],
        by_row[0],
        small_sums[1],
        by_col[0],
        small_sums[2],
        by_row[1],
        by_row[2],
        by_col[1],
    )


def solution(mesh):
    placed = (
        P("dp", "seq", "mp"),
        P("mp"),
        P(None, None, "mp"),
        P(None, "mp"),
        P("mp", None),
        P("mp"),
        P(None, "mp"),
        P(None, "mp"),
        P("mp", None),
        P("dp", "seq", "mp"),
    )
    sizes = mesh.shape
    fused = sizes["dp"] == 2 and sizes["seq"] == 4 and sizes["mp"] == 4
    return jax.shard_map(
        fused_device if fused else plain_device,
        mesh=mesh,
        in_specs=placed,
        out_specs=(
            P("dp", "seq", "mp"),
            P("dp", "seq", "mp"),
            P("mp"),
            P(("dp", "seq"), None, "mp"),
            P(None, "mp"),
            P("mp", ("dp", "seq")),
            P("mp"),
            P(("dp", "seq"), "mp"),
            P(("dp", "seq"), "mp"),
            P("mp", ("dp", "seq")),
        ),
        check_vma=False,
    )
```

```python
import functools

import jax
import jax.numpy as jnp
from jax import lax
from jax.experimental import pallas as pl
from jax.experimental.pallas import tpu as pltpu
from jax.sharding import PartitionSpec as P

EPS = 1e-05
MESH = pl.DeviceIdType.MESH
BF = jnp.bfloat16
F32 = jnp.float32
ROWS = 32
SECOND = 3
LAG = 3
WAIT = 3
PLACES = {
    "out_start": (2, (1, 4, 7, 8)),
    "out_share": (2, (2, 5, 8, 10)),
    "out_end": (1, (4, 7, 9, 12)),
    "a": (2, (3, 8, 10, 14)),
    "b": (2, (4, 9, 12, 15)),
    "c": (1, (8, 11, 14, 18)),
    "d": (2, (9, 13, 17, 19)),
    "e": (2, (12, 15, 18, 20)),
    "f": (2, (14, 16, 19, 21)),
    "g": (2, (15, 18, 20, 22)),
    "a1": (2, (15, 16, 17, 19)),
}
HIDDEN = (1, {2: 3, 3: 4, 4: 5, 5: 7, 6: 12})
ANY = pl.BlockSpec(memory_space=pl.ANY)
VMEM = pl.BlockSpec(memory_space=pltpu.VMEM)


def nn(left, right):
    return lax.dot_general(left, right, (((1,), (0,)), ((), ())), preferred_element_type=F32)


def nt(left, right):
    return lax.dot_general(left, right, (((1,), (1,)), ((), ())), preferred_element_type=F32)


def block_kernel(
    dims,
    x_in, cot_in, gain_mix_v, gain_ff_v, taps_v, wd_h, wg_h, wu_h, wo_h, wi_h,
    gdown_h, ggate_h, gup_h, gout_h, gin_h, gx_h, out_h, small_v,
    x_h, cot_h, h1_h, bcv_h, woy_h,
    lt, r, w0, wg, wu, wof, cotc, xc, xo, bcv, bxp, dbuf, dcp, dhoc, dh1s, r1s, gv, own_v,
    xs, xr, s_buf, zs, zr, ob, vs, vr, vk,
    kf, cs, cr, ys, yr4, da2f, cs2, ys2, yr2,
    ins, inr, iys, iyr, gxb, halo_s, halo_r, before_s, before_r, small_r,
    xs_sem, xr_sem, zs_sem, zr_sem, ob_sem, c_sem, y_sem, f_sem, c2_sem, y2_sem,
    i_sem, iy_sem, halo_sem, before_sem, gather_sem, w_sem, l_sem, bcv_sem, h1_sem, gx_sem,
    small_sem, v_sem, wy_sem, wx_sem, wz_sem, wc_sem, wl_sem,
):
    tokens, chunk, width, ff, local, nseq = dims
    chunks = tokens // chunk
    block = width // (2 * nseq)
    per = block // ROWS
    beat = per + 1
    ticks = 4 * beat
    p = lax.axis_index("dp")
    z = lax.axis_index("seq")
    me = lax.axis_index("mp")
    y, c = me // 2, me % 2
    x_dev = {"dp": 1 - p}
    up_dev = {"seq": z + 1}
    dn_dev = {"seq": z - 1}
    y_dev = {"mp": (1 - y) * 2 + c}
    c_dev = {"mp": y * 2 + 1 - c}
    last = nseq - 1
    ck, ck2, qk2 = kf.at[pl.ds(0, 2)], kf.at[pl.ds(2, 2)], kf.at[4]
    third = ff // 3 // 128 * 128
    cuts = ((0, third), (third, third), (2 * third, ff - 2 * third))

    def remote(src, dst, sems, where, at=None):
        s_sem, r_sem = (sems.at[0], sems.at[1]) if at is None else (sems.at[0, at], sems.at[1, at])
        return pltpu.make_async_remote_copy(
            src_ref=src, dst_ref=dst, send_sem=s_sem, recv_sem=r_sem,
            device_id=where, device_id_type=MESH,
        )

    def load(src, dst, sem):
        return pltpu.make_async_copy(src, dst, sem)

    def wi_load(k):
        return load(wi_h.at[k], w0.at[pl.ds(0, width), pl.ds(k * local, local)], w_sem.at[k])

    wd_load = load(wd_h, w0, w_sem.at[3])
    wg_load = load(wg_h, wg, w_sem.at[4])
    wu_load = load(wu_h, wu, w_sem.at[5])
    def wo_load(q):
        return load(wo_h.at[:, pl.ds(q * local, local)], wof.at[pl.ds(q * local, local), pl.ds(0, local)], wl_sem.at[q])

    for k in range(3):
        wi_load(k).start()
    own_v[0:1, :] = gain_mix_v[...].astype(F32).reshape(1, local)
    own_v[1:2, :] = gain_ff_v[...].astype(F32).reshape(1, local)
    own_v[2:5, :] = taps_v[...].astype(F32)
    own_v[5:8, :] = jnp.zeros((3, local), F32)
    gv[me] = own_v[...]

    barrier = pltpu.get_barrier_semaphore()
    for dev in (x_dev, y_dev, c_dev):
        pl.semaphore_signal(barrier, inc=1, device_id=dev, device_id_type=MESH)

    @pl.when(z < last)
    def _():
        pl.semaphore_signal(barrier, inc=1, device_id=up_dev, device_id_type=MESH)

    @pl.when(z > 0)
    def _():
        pl.semaphore_signal(barrier, inc=1, device_id=dn_dev, device_id_type=MESH)

    peers = 3 + jnp.where(z < last, 1, 0) + jnp.where(z > 0, 1, 0)
    pl.semaphore_wait(barrier, peers)

    small_v[...] = jnp.zeros_like(small_v)

    def rows_at(i):
        return pl.ds(pl.multiple_of(i * chunk, chunk), chunk)

    def mixed_at(q, i):
        return r.at[0, rows_at(i), pl.ds(pl.multiple_of(q * local, 128), local)]

    share = local // (2 * nseq)

    def piece(zz):
        return woy_h.at[pl.ds(pl.multiple_of((p * nseq + zz) * share, 16), share), :]

    def wy():
        mine = wo_h.at[pl.ds(pl.multiple_of((p * nseq + z) * share, 16), share), :]
        return pltpu.make_async_remote_copy(
            src_ref=mine, dst_ref=piece(z), send_sem=wy_sem.at[0], recv_sem=wy_sem.at[1],
            device_id=y_dev, device_id_type=MESH,
        )

    def wx(zz):
        return remote(piece(zz), piece(zz), wx_sem, x_dev, zz)

    def wz(way, step):
        part = piece(z + step if way else z - step)
        return pltpu.make_async_remote_copy(
            src_ref=part, dst_ref=part, send_sem=wz_sem.at[0, way, step], recv_sem=wz_sem.at[1, way, step],
            device_id=dn_dev if way else up_dev, device_id_type=MESH,
        )

    def wz_sends(way, step):
        return jnp.logical_and(z > 0, z + step <= last) if way else jnp.logical_and(z < last, z >= step)

    def wz_receives(way, step):
        return z + 1 + step <= last if way else z >= step + 1

    def wo_step(step):
        if step == 0:
            wy().wait_recv()
            wx(z).start()
        for way in (0, 1):
            if step > 0:
                @pl.when(wz_receives(way, step - 1))
                def _(way=way):
                    wz(way, step - 1).wait_recv()
                    wx(z + step if way else z - step).start()
            if step < last:
                @pl.when(wz_sends(way, step))
                def _(way=way):
                    wz(way, step).start()

    def wo_columns(src, q, kind):
        rows = pl.ds(pl.multiple_of(q * local, 128), local)
        for pair in (0, 1):
            cols = pl.ds(pl.multiple_of((2 * pair + c) * local, 128), local)
            yield load(src.at[:, cols], wof.at[rows, pl.ds(pair * local, local)], wl_sem.at[2 * kind + pair])
            cols = pl.ds(pl.multiple_of((2 * pair + 1 - c) * local, 128), local)
            yield remote(src.at[:, cols], wof.at[rows, pl.ds(pair * local, local)], wc_sem, c_dev, 2 * kind + pair)

    def wo_end():
        wy().wait_send()
        for zz in range(nseq):
            wx(zz).wait()
        for way in (0, 1):
            for step in range(last):
                @pl.when(wz_sends(way, step))
                def _(way=way, step=step):
                    wz(way, step).wait_send()
        for one in wo_columns(woy_h, (1 - y) * 2 + c, 1):
            one.start()

    def gather(which, i, leg):
        if which == 2:
            src = mine = own_v
            dst = gv
            at = (2, 0)
        elif which == 3:
            mine = mixed_at(me, i)
            at = (3, i)
        else:
            src, dst = (x_in, x_h) if which == 0 else (cot_in, cot_h)
            mine = src.at[rows_at(i), :]
            at = (which, i)
        if which == 3:
            slot = lambda q: mixed_at(q, i)
        else:
            slot = (lambda q: dst.at[q]) if which == 2 else (lambda q: dst.at[q, rows_at(i), :])
        sems = [gather_sem.at[leg, way, at[0], at[1]] for way in (0, 1)]
        if leg == 0:
            pair, where = (mine, slot(me)), y_dev
        elif leg == 1:
            pair, where = (mine, slot(me)), c_dev
        else:
            from_y = (1 - y) * 2 + c
            pair, where = (slot(from_y), slot(from_y)), c_dev
        return pltpu.make_async_remote_copy(
            src_ref=pair[0], dst_ref=pair[1], send_sem=sems[0], recv_sem=sems[1],
            device_id=where, device_id_type=MESH,
        )

    def gather_start(which, i):
        gather(which, i, 0).start()
        gather(which, i, 1).start()

    def gather_pass(which, i):
        gather(which, i, 0).wait_recv()
        gather(which, i, 2).start()

    def gather_end(which, i):
        gather(which, i, 0).wait_send()
        gather(which, i, 1).wait()
        gather(which, i, 2).wait()

    gather(0, 0, 0).start()
    gather_start(2, 0)
    for i in range(chunks):
        gather(0, i, 1).start()

    def on_size(t, f):
        pl.when(t // beat < 3)(lambda: f(pl.ds(0, ff)))
        pl.when(t // beat == 3)(lambda: f(pl.ds(0, 4 * local)))

    def place(t):
        return lax.rem(t, beat)

    def is_first(t):
        return place(t) == 0

    def is_second(t):
        return place(t) == SECOND

    def is_plain(t):
        return jnp.logical_and(place(t) != 0, place(t) != SECOND)

    def row_block(t):
        plain = place(t) - jnp.where(place(t) > SECOND, 2, 1)
        return jnp.where(is_plain(t), plain, per - 1)

    def x_number(t):
        return t // beat * (per - 1) + row_block(t)

    def x_do(t, what):
        n = x_number(t)

        def f(cols):
            copy = pltpu.make_async_remote_copy(
                src_ref=xs.at[lax.rem(n, 3), :, cols], dst_ref=xr.at[lax.rem(n, 5), :, cols],
                send_sem=xs_sem.at[lax.rem(n, 3)], recv_sem=xr_sem.at[lax.rem(n, 5)],
                device_id=x_dev, device_id_type=MESH,
            )
            getattr(copy, what)()

        on_size(t, f)

    def v_do(t, what):
        def f(cols):
            copy = pltpu.make_async_remote_copy(
                src_ref=vs.at[:, cols], dst_ref=vr.at[:, cols], send_sem=v_sem.at[0], recv_sem=v_sem.at[1],
                device_id=x_dev, device_id_type=MESH,
            )
            getattr(copy, what)()

        on_size(t, f)

    def zs_at(t, step):
        return sum(k + 2 for k in range(step)) + lax.rem(t, step + 2)

    def zr_at(t, step):
        return 4 * step + lax.rem(t, 6 if step == last - 1 else 4)

    def z_do(t, way, step, what):
        def f(cols):
            copy = pltpu.make_async_remote_copy(
                src_ref=zs.at[way, zs_at(t, step), :, cols], dst_ref=zr.at[way, zr_at(t, step), :, cols],
                send_sem=zs_sem.at[way, zs_at(t, step)], recv_sem=zr_sem.at[way, zr_at(t, step)],
                device_id=dn_dev if way else up_dev, device_id_type=MESH,
            )
            getattr(copy, what)()

        on_size(t, f)

    def receives(way, step):
        if way:
            return jnp.logical_and(z < last, z >= last - 1 - step)
        return jnp.logical_and(z > 0, z <= step + 1)

    def can_send(way, step):
        if way:
            return jnp.logical_and(z > 0, z >= last - step)
        return jnp.logical_and(z < last, z <= step)

    def z_arrived(t, step):
        for way in (0, 1):
            @pl.when(receives(way, step))
            def _(way=way):
                z_do(t, way, step, "wait_recv")

            @pl.when(can_send(way, step))
            def _(way=way):
                z_do(t, way, step, "wait_send")

    def z_step(t, step):
        sl = lax.rem(t, LAG + 4)

        def quarter(way, k):
            at = z - last + k if way else last - k + z
            return s_buf[sl, pl.ds(at * ROWS, ROWS), :]

        if step == 0:
            for way, end in ((0, 0), (1, last)):
                @pl.when(z == end)
                def _(way=way):
                    for k in range(last):
                        zs[way, zs_at(t, k)] = quarter(way, k)
                        z_do(t, way, k, "start")

            return
        z_arrived(t, step - 1)
        onward = [jnp.logical_and(receives(way, step - 1), can_send(way, step)) for way in (0, 1)]
        for way in (0, 1):
            @pl.when(onward[way])
            def _(way=way):
                value = quarter(way, step).astype(F32) + zr[way, zr_at(t, step - 1)].astype(F32)
                zs[way, zs_at(t, step)] = value.astype(BF)

        for way in (0, 1):
            @pl.when(onward[way])
            def _(way=way):
                z_do(t, way, step, "start")

    def compute(t, kind):
        sl = lax.rem(t, LAG + 4)
        at = row_block(t) * ROWS
        m = ROWS * nseq

        def rows_of(index, half):
            rows = [pl.ds(pl.multiple_of((half * nseq + s) * block + at, ROWS), ROWS) for s in range(nseq)]
            if kind == 3 and index == 1:
                return [wg[some, pl.ds(0, tokens)] for some in rows]
            return [lt[index, some, :] for some in rows]

        if kind == 3:
            parts = [(0, 0, 0, local)] + [(1, 0, k * local, local) for k in (1, 2, 3)]
        elif kind == 0:
            parts = [(0, 0, lo, n) for lo, n in cuts]
        else:
            parts = [(1, t // beat, lo, n) for lo, n in cuts]

        @pl.when(is_plain(t))
        def _():
            slot = lax.rem(x_number(t), 3)
            left = [jnp.concatenate(rows_of(i, 1 - p) + rows_of(i, p), 0) for i in sorted({q[0] for q in parts})]
            for i, ri, lo, n in parts:
                cols = pl.ds(lo, n)
                out = nn(left[i if len(left) == 2 else 0], r[ri, :, cols])
                xs[slot, :, cols] = out[:m].astype(BF)
                s_buf[sl, :, cols] = out[m:].astype(BF)
            x_do(t, "start")

        @pl.when(jnp.logical_not(is_plain(t)))
        def _():
            half = jnp.where(is_first(t), p, 1 - p)
            left = [jnp.concatenate(rows_of(i, half), 0) for i in sorted({q[0] for q in parts})]
            for i, ri, lo, n in parts:
                cols = pl.ds(lo, n)
                s_buf[sl, :, cols] = nn(left[i if len(left) == 2 else 0], r[ri, :, cols]).astype(BF)

    def out_do(src, t, sems, what):
        rows = pl.ds(pl.multiple_of(row_block(t) * ROWS, ROWS), ROWS)
        for g, target in enumerate((gdown_h, ggate_h, gup_h)):
            @pl.when(t // beat == g)
            def _(target=target):
                getattr(load(src, target.at[rows, :], ob_sem.at[sems, 0]), what)()

        @pl.when(t // beat == 3)
        def _():
            getattr(load(src.at[:, pl.ds(0, local)], gout_h.at[rows, :], ob_sem.at[sems, 0]), what)()
            for k in range(3):
                part = src.at[:, pl.ds((k + 1) * local, local)]
                getattr(load(part, gin_h.at[k, rows, :], ob_sem.at[sems, 1 + k]), what)()

    def plain_out(t, what):
        slot = lax.rem(x_number(t), 2)
        out_do(ob.at[slot], t, slot, what)

    def finish(t):
        sl = lax.rem(t, LAG + 4)
        z_arrived(t, last - 1)

        def total(then):
            def end(ways):
                value = s_buf[sl, pl.ds(z * ROWS, ROWS), :].astype(F32)
                for way in ways:
                    value += zr[way, zr_at(t, last - 1)].astype(F32)
                then(value)

            pl.when(z == 0)(lambda: end((1,)))
            pl.when(z == last)(lambda: end((0,)))
            pl.when(jnp.logical_and(z > 0, z < last))(lambda: end((0, 1)))

        @pl.when(is_plain(t))
        def _():
            n = x_number(t)
            before = t - jnp.where(place(t) == per, 2, 3)

            @pl.when(n >= 2)
            def _():
                plain_out(before, "wait")

            def put(value):
                ob[lax.rem(n, 2)] = value.astype(BF)

            total(put)
            plain_out(t, "start")

        @pl.when(is_first(t))
        def _():
            def put(value):
                vk[...] = value

            total(put)

        @pl.when(is_second(t))
        def _():
            def put(value):
                vs[...] = value.astype(BF)

            total(put)
            v_do(t, "start")

    def v_end(t):
        @pl.when(is_second(t))
        def _():
            v_do(t, "wait")

            @pl.when(t >= beat)
            def _():
                out_do(ob.at[2], t - beat, 2, "wait")

            ob[2] = (vk[...] + vr[...].astype(F32)).astype(BF)
            out_do(ob.at[2], t, 2, "start")

    def within(t, f):
        @pl.when(jnp.logical_and(t >= 0, t < ticks))
        def _():
            f(t)

    def tick_a(t, full=False):
        within(t - LAG - 4 - WAIT, v_end)
        within(t - LAG - 4, finish)

        def x_in(u):
            @pl.when(is_plain(u))
            def _():
                x_do(u, "wait")
                sl = lax.rem(u, LAG + 4)
                arrived = xr[lax.rem(x_number(u), 5)].astype(F32)
                s_buf[sl] = (s_buf[sl].astype(F32) + arrived).astype(BF)

            z_step(u, 0)

        within(t - LAG, x_in)
        if full:
            pl.when(t // beat == 0)(lambda: compute(t, 0))
            pl.when(jnp.logical_and(t // beat > 0, t // beat < 3))(lambda: compute(t, 1))
            pl.when(t // beat == 3)(lambda: compute(t, 3))

    def tick_b(t):
        within(t - LAG - 1, lambda u: z_step(u, 1))

    def tick_c(t):
        within(t - LAG - 2, lambda u: z_step(u, 2))

    def in_slices(own, others, to, slot):
        copies = [load(own, to(me), l_sem.at[slot, 0])]
        for step in range(1, 4):
            q = lax.rem(me + step, 4)
            copies.append(load(others(q), to(q), l_sem.at[slot, step]))
        return copies

    def cot_load(i):
        return in_slices(
            cot_in.at[rows_at(i), :],
            lambda q: cot_h.at[q, rows_at(i), :],
            lambda q: cotc.at[:, pl.ds(pl.multiple_of(q * local, 128), local)],
            0,
        )

    def x_load(i):
        return in_slices(x_in.at[rows_at(i), :], lambda q: x_h.at[q, rows_at(i), :], lambda q: xc.at[q], 1)

    def start(copies):
        for one in copies:
            one.start()

    def wait(copies):
        for one in copies:
            one.wait()

    def h1_load(i):
        return load(h1_h.at[:, rows_at(i), :], xc, l_sem.at[2, 0])

    def bcv_load(i):
        return load(bcv_h.at[:, rows_at(i), :], bcv, l_sem.at[2, 1])

    def gain(row, q):
        return gv[q, row : row + 1, :]

    def by_rows_of(count, f):
        def body(b, _):
            f(pl.ds(pl.multiple_of(b * count, count), count))
            return 0

        lax.fori_loop(0, chunk // count, body, 0)

    def normed_to(src, row, after=None):
        def f(some):
            ssq = jnp.zeros((64, local), F32)
            for q in range(4):
                values = src(q, some).astype(F32)
                ssq += values * values
            scale = lax.rsqrt(jnp.sum(ssq, -1, keepdims=True) / width + EPS)
            for q in range(4):
                dhoc[some, pl.ds(q * local, local)] = (src(q, some).astype(F32) * scale * gain(row, q)).astype(BF)

        by_rows_of(64, f)

    def transposed_to(index, i):
        at = pl.multiple_of(i * chunk, chunk)
        for q in range(4):
            cols = pl.ds(q * local, local)
            lt[index, cols, pl.ds(at, chunk)] = dhoc[:, cols].T

    def before_copy(i):
        return remote(before_s.at[i], before_r.at[i], before_sem, up_dev, i)

    def bcv_store(i):
        return load(bcv, bcv_h.at[:, rows_at(i), :], bcv_sem)

    def h1_store(i, slot, pair, core):
        return load(da2f.at[slot, pair, core], h1_h.at[2 * pair + core, rows_at(i), :], h1_sem.at[pair, core])

    def project(i):
        wait(x_load(i))
        normed_to(lambda q, some: xc[q, some, :], 0)
        value = nn(dhoc[...], w0[pl.ds(0, width), pl.ds(0, 3 * local)])

        @pl.when(i > 0)
        def _():
            bcv_store(i - 1).wait()

        for k in range(3):
            bcv[k] = value[:, k * local : (k + 1) * local].astype(BF)
        dcp[pl.ds(0, chunk), :] = value[:, local : 2 * local]
        bx = (value[:, :local] * value[:, 2 * local :]).astype(BF)
        bcv[3] = bx
        bxp[pl.ds(8, chunk), :] = bx.astype(F32)
        before_s[i] = bxp[pl.ds(chunk, 8), :]

        @pl.when(z < last)
        def _():
            before_copy(i).start()

        bcv_store(i).start()

    def conv_of():
        shifts = [bxp[pl.ds(6 + k, chunk), :] for k in range(3)]
        return sum(own_v[2 + k : 3 + k, :] * shifts[k] for k in range(3)), shifts

    def mix(i):
        @pl.when(z < last)
        def _():
            before_copy(i).wait_send()

        @pl.when(z > 0)
        def _():
            before_copy(i).wait_recv()

        @pl.when(z == 0)
        def _():
            before_r[i] = jnp.zeros((8, local), F32)

        bxp[pl.ds(0, 8), :] = before_r[i]
        mixed = (dcp[pl.ds(0, chunk), :] * conv_of()[0]).astype(BF)
        r[0, rows_at(i), pl.ds(pl.multiple_of(me * local, 128), local)] = mixed
        gather_start(3, i)

    def x_two(i):
        return [
            load(x_in.at[rows_at(i), :], cs2.at[y], l_sem.at[2, 2]),
            load(x_h.at[(1 - y) * 2 + c, rows_at(i), :], cs2.at[1 - y], l_sem.at[2, 3]),
        ]

    def residual(i):
        slot = lax.rem(i, 2)
        gather_end(3, i)
        wait(x_two(i))

        @pl.when(i >= 1)
        def _():
            for pair in (0, 1):
                for core in (0, 1):
                    h1_store(i - 1, 1 - slot, pair, core).wait()

        product = nn(r[0, rows_at(i), pl.ds(0, width)], wof[...])
        for pair in (0, 1):
            h1 = product[:, pair * local : (pair + 1) * local] + cs2[pair].astype(F32)
            da2f[slot, pair, c] = h1.astype(BF)

            @pl.when(y == pair)
            def _(h1=h1):
                dh1s[i] = h1
        remote(da2f.at[slot, :, c], da2f.at[slot, :, c], f_sem, c_dev, slot).start()

        @pl.when(i + 1 < chunks)
        def _():
            start(x_two(i + 1))

    def cot_fetch(i):
        gather_end(1, i)
        start(cot_load(i))

    def cot_turn(i):
        wait(cot_load(i))
        at = pl.multiple_of(i * chunk, chunk)
        for q in range(4):
            cols = pl.ds(q * local, local)
            lt[0, cols, pl.ds(at, chunk)] = cotc[:, cols].T

    def feed(i):
        slot = lax.rem(i, 2)
        remote(da2f.at[slot, :, c], da2f.at[slot, :, c], f_sem, c_dev, slot).wait()
        for pair in (0, 1):
            for core in (0, 1):
                h1_store(i, slot, pair, core).start()
        normed_to(lambda q, some: da2f[slot, q // 2, q % 2, some, :], 1)
        transposed_to(1, i)
        rows = rows_at(i)
        for lo, n in cuts:
            dbuf[:, pl.ds(0, n)] = nt(dhoc[...], wg[pl.ds(lo, n), :])
            r[2, rows, pl.ds(lo, n)] = nt(dhoc[...], wu[pl.ds(lo, n), :]).astype(BF)

            def by_rows(b, _, lo=lo, n=n):
                cols = pl.ds(lo, n)
                here = pl.ds(pl.multiple_of(b * 64, 64), 64)
                some = pl.ds(pl.multiple_of(i * chunk + b * 64, 64), 64)
                gate = dbuf[here, pl.ds(0, n)]
                up = r[2, some, cols].astype(F32)
                r[0, some, cols] = (gate * jax.nn.sigmoid(gate) * up).astype(BF)
                r[1, some, cols] = gate.astype(BF)
                return 0

            lax.fori_loop(0, chunk // 64, by_rows, 0)

    def hidden_back(piece):
        i = piece // 3

        @pl.when(lax.rem(piece, 3) == 0)
        def _():
            wait(cot_load(i))

        for k, cut in enumerate(cuts):
            pl.when(lax.rem(piece, 3) == k)(functools.partial(hidden_cut, i, *cut))

        @pl.when(jnp.logical_and(lax.rem(piece, 3) == 2, i + 1 < chunks))
        def _():
            start(cot_load(i + 1))

    def hidden_cut(i, lo, n):
        if True:
            cols = pl.ds(lo, n)
            dbuf[:, pl.ds(0, n)] = nt(cotc[...], w0[pl.ds(lo, n), :])

            def by_rows(b, _, cols=cols, n=n):
                some = pl.ds(pl.multiple_of(i * chunk + b * 32, 32), 32)
                dhid = dbuf[pl.ds(pl.multiple_of(b * 32, 32), 32), pl.ds(0, n)]
                gate = r[1, some, cols].astype(F32)
                up = r[2, some, cols].astype(F32)
                sig = jax.nn.sigmoid(gate)
                r[1, some, cols] = (dhid * up * sig * (1.0 + gate * (1.0 - sig))).astype(BF)
                r[2, some, cols] = (dhid * gate * sig).astype(BF)
                return 0

            lax.fori_loop(0, chunk // 32, by_rows, 0)

    def split_store(pair, value, keep, send):
        for side in (0, 1):
            part = value[:, side * local : (side + 1) * local]

            @pl.when(c == side)
            def _(part=part):
                keep[pair] = part

            @pl.when(c != side)
            def _(part=part):
                send[pair] = part.astype(BF)

    def stage_a(i):
        slot = lax.rem(i, 2)
        rows = rows_at(i)
        for pair in (0, 1):
            cols = pl.ds(pair * 2 * local, 2 * local)
            value = nn(r[1, rows, :], wg[:, cols]) + nn(r[2, rows, :], wu[:, cols])
            split_store(pair, value, ck, cs)
        remote(cs, cr.at[slot], c_sem, c_dev, slot).start()

        @pl.when(i == chunks - 1)
        def _():
            start(x_whole())

    def x_whole():
        copies = [load(x_in, wu.at[pl.ds(0, tokens), pl.ds(pl.multiple_of(me * local, 128), local)], l_sem.at[3, 0])]
        for step in range(1, 4):
            q = lax.rem(me + step, 4)
            cols = pl.ds(pl.multiple_of(q * local, 128), local)
            copies.append(load(x_h.at[q], wu.at[pl.ds(0, tokens), cols], l_sem.at[3, step]))
        return copies

    def stage_a1(i):
        @pl.when(i == 0)
        def _():
            wait(x_whole())

        at = pl.multiple_of(i * chunk, chunk)
        normed_to(lambda q, some: wu[pl.ds(at + some.start, some.size), pl.ds(q * local, local)], 0)
        for q in range(4):
            cols = pl.ds(q * local, local)
            wg[cols, pl.ds(at, chunk)] = dhoc[:, cols].T

    def stage_loads(i):
        start(cot_load(i))
        h1_load(i).start()
        bcv_load(i).start()

    def stage_b(i):
        slot = lax.rem(i, 2)
        remote(cs, cr.at[slot], c_sem, c_dev, slot).wait()
        ys[...] = (ck[...] + cr[slot].astype(F32)).astype(BF)
        remote(ys, yr4.at[slot], y_sem, y_dev, slot).start()

    def stage_c(i):
        slot = lax.rem(i, 2)
        remote(ys, yr4.at[slot], y_sem, y_dev, slot).wait()
        da2f[slot, :, c] = (ys[...].astype(F32) + yr4[slot].astype(F32)).astype(BF)
        remote(da2f.at[slot, :, c], da2f.at[slot, :, c], f_sem, c_dev, slot).start()

    def stage_d(i):
        slot = lax.rem(i, 2)
        remote(da2f.at[slot, :, c], da2f.at[slot, :, c], f_sem, c_dev, slot).wait()
        wait(cot_load(i))
        h1_load(i).wait()
        bcv_load(i).wait()
        at = pl.multiple_of(i * chunk, chunk)
        own = pl.ds(pl.multiple_of(me * local, 128), local)

        def by_rows(b, _):
            some = pl.ds(pl.multiple_of(b * 64, 64), 64)
            ssq = jnp.zeros((64, local), F32)
            inner = jnp.zeros((64, local), F32)
            for q in range(4):
                cols = pl.ds(q * local, local)
                h1 = xc[q, some, :].astype(F32)
                ssq += h1 * h1
                inner += da2f[slot, q // 2, q % 2, some, :].astype(F32) * gain(1, q) * h1
            r2 = lax.rsqrt(jnp.sum(ssq, -1, keepdims=True) / width + EPS)
            scale = r2 * r2 * r2 * jnp.sum(inner, -1, keepdims=True) / width

            def grad(q, cols, da2):
                h1 = xc[q, some, :].astype(F32)
                return cotc[some, cols].astype(F32) + r2 * (da2 * gain(1, q)) - h1 * scale

            for q in range(4):
                cols = pl.ds(q * local, local)
                dhoc[some, cols] = grad(q, cols, da2f[slot, q // 2, q % 2, some, :].astype(F32)).astype(BF)
            da2 = da2f[slot, y, c, some, :].astype(F32)
            dh1s[i, some, :] = grad(me, own, da2)
            terms = da2 * xc[me, some, :].astype(F32) * r2
            small_v[pl.ds(8, 8), :] += sum(terms[8 * k : 8 * k + 8] for k in range(8))
            return 0

        lax.fori_loop(0, chunk // 64, by_rows, 0)
        start(x_load(i))
        transposed_to(0, i)
        @pl.when(i == 0)
        def _():
            for q in range(4):
                wo_load(q).wait()

        dmixed = jnp.zeros((chunk, local), F32)
        for q in range(4):
            cols = pl.ds(q * local, local)
            dmixed += nt(dhoc[:, cols], wof[cols, pl.ds(0, local)])
        c_gate = bcv[1]
        bxp[pl.ds(0, 8), :] = before_r[i]
        bxp[pl.ds(8, chunk), :] = bcv[3].astype(F32)
        conv, shifts = conv_of()
        r[0, pl.ds(at, chunk), pl.ds(0, local)] = (c_gate.astype(F32) * conv).astype(BF)
        r[0, pl.ds(at, chunk), pl.ds(2 * local, local)] = (dmixed * conv).astype(BF)
        dconv = (dmixed * c_gate.astype(F32)).astype(BF).astype(F32)
        dcp[pl.ds(0, chunk), :] = dconv
        halo_s[i] = dconv[:8]
        for k in range(3):
            small_v[1 + k : 2 + k, :] += jnp.sum(dconv * shifts[k], 0, keepdims=True)

        @pl.when(z > 0)
        def _():
            halo_copy(i).start()

    def halo_copy(i):
        return remote(halo_s.at[i], halo_r.at[i], halo_sem, dn_dev, i)

    def stage_e(i):
        slot = lax.rem(i, 2)

        @pl.when(i == 0)
        def _():
            for k in range(3):
                wi_load(k).wait()
            out_copy(chunks - 1).wait()

        wait(x_load(i))

        @pl.when(z > 0)
        def _():
            halo_copy(i).wait_send()

        @pl.when(z < last)
        def _():
            halo_copy(i).wait_recv()
            dcp[pl.ds(chunk, 8), :] = halo_r[i]

        @pl.when(z == last)
        def _():
            dcp[pl.ds(chunk, 8), :] = jnp.zeros((8, local), F32)

        dbx = sum(own_v[4 - k : 5 - k, :] * dcp[pl.ds(k, chunk), :] for k in range(3))
        rows = rows_at(i)
        r[0, rows, pl.ds(local, local)] = (dbx * bcv[2].astype(F32)).astype(BF)
        r[0, rows, pl.ds(3 * local, local)] = (dbx * bcv[0].astype(F32)).astype(BF)
        inner = jnp.zeros((chunk, 1), F32)
        ssq = jnp.zeros((chunk, 1), F32)
        for pair in (0, 1):
            cols = pl.ds(pair * 2 * local, 2 * local)
            value = nt(r[0, rows, pl.ds(local, 3 * local)], w0[cols, pl.ds(0, 3 * local)])
            for side in (0, 1):
                q = 2 * pair + side
                x = xc[q].astype(F32)
                part = value[:, side * local : (side + 1) * local]
                inner += jnp.sum(part * x * gain(0, q), -1, keepdims=True)
                ssq += jnp.sum(x * x, -1, keepdims=True)
            split_store(pair, value, ck2, cs2)
        xo[...] = xc[me]
        ins[...] = jnp.broadcast_to(inner, (chunk, 128)).T[:8]
        r1s[...] = jnp.broadcast_to(lax.rsqrt(ssq / width + EPS), r1s.shape)
        remote(cs2, yr4.at[2 + slot], c2_sem, c_dev, slot).start()
        remote(ins, inr.at[slot], i_sem, c_dev, slot).start()

        @pl.when(i + 1 < chunks)
        def _():
            stage_loads(i + 1)

    def stage_f(i):
        slot = lax.rem(i, 2)
        remote(cs2, yr4.at[2 + slot], c2_sem, c_dev, slot).wait()
        remote(ins, inr.at[slot], i_sem, c_dev, slot).wait()
        ys2[...] = (ck2[1 - y] + yr4[2 + slot, 1 - y].astype(F32)).astype(BF)
        qk2[...] = ck2[y] + yr4[2 + slot, y].astype(F32)
        iys[...] = ins[...] + inr[slot]
        remote(ys2, yr2.at[slot], y2_sem, y_dev, slot).start()
        remote(iys, iyr.at[slot], iy_sem, y_dev, slot).start()

    def gx_copy(i):
        return load(gxb, gx_h.at[rows_at(i), :], gx_sem)

    def stage_g(i):
        slot = lax.rem(i, 2)
        remote(ys2, yr2.at[slot], y2_sem, y_dev, slot).wait()
        remote(iys, iyr.at[slot], iy_sem, y_dev, slot).wait()
        da1 = qk2[...] + yr2[slot].astype(F32)
        inner = jnp.broadcast_to(iys[:1] + iyr[slot, :1], (128, chunk)).T[:, :1]
        r1 = r1s[:, :1]
        x = xo[...].astype(F32)
        scaled = gain(0, me)
        small_v[0:1, :] += jnp.sum(da1 * x * r1, 0, keepdims=True)

        @pl.when(i > 0)
        def _():
            gx_copy(i - 1).wait()

        gxb[...] = (dh1s[i] + r1 * scaled * da1 - x * (r1 * r1 * r1 * inner / width)).astype(BF)
        gx_copy(i).start()

    def out_start(i):
        rows = rows_at(i)
        for pair in (0, 1):
            cols = pl.ds(pair * 2 * local, 2 * local)
            split_store(pair, nn(r[0, rows, :], w0[:, cols]), ck2, cs2)
        remote(cs2, yr4.at[2 + lax.rem(i, 2)], c2_sem, c_dev, lax.rem(i, 2)).start()

        @pl.when(i == chunks - 1)
        def _():
            for k in range(3):
                wi_load(k).start()

    def out_share(i):
        slot = lax.rem(i, 2)
        remote(cs2, yr4.at[2 + slot], c2_sem, c_dev, slot).wait()
        ys2[...] = (ck2[1 - y] + yr4[2 + slot, 1 - y].astype(F32)).astype(BF)
        qk2[...] = ck2[y] + yr4[2 + slot, y].astype(F32)
        remote(ys2, yr2.at[slot], y2_sem, y_dev, slot).start()

    def out_copy(i):
        return load(gxb, out_h.at[rows_at(i), :], gx_sem)

    def out_end(i):
        slot = lax.rem(i, 2)
        remote(ys2, yr2.at[slot], y2_sem, y_dev, slot).wait()

        @pl.when(i > 0)
        def _():
            out_copy(i - 1).wait()

        gxb[...] = (dh1s[i] + (qk2[...] + yr2[slot].astype(F32))).astype(BF)
        out_copy(i).start()

    def valid(i, f):
        @pl.when(jnp.logical_and(i >= 0, i < chunks))
        def _():
            f(i)

    gather_pass(0, 0)
    gather(0, 1, 0).start()
    wy().start()
    gather_pass(2, 0)
    for k in range(3):
        wi_load(k).wait()
    gather_end(2, 0)

    gather_end(0, 0)
    start(x_load(0))

    def when(now, *calls):
        @pl.when(now)
        def _():
            for f in calls:
                f()

    def weights_there():
        wg_load.wait()
        wu_load.wait()

    def wo_there():
        wo_end()
        for kind, src in ((0, wo_h), (1, woy_h)):
            for one in wo_columns(src, me if kind == 0 else (1 - y) * 2 + c, kind):
                one.wait()

    def forward(j, _):
        when(j < chunks, lambda: project(j))
        when(j + 1 < chunks, lambda: gather_pass(0, j + 1))
        when(j + 2 < chunks, lambda: gather(0, j + 2, 0).start())
        when(j == 0, lambda: wo_step(0), wg_load.start, wu_load.start, *[one.start for one in wo_columns(wo_h, me, 0)])
        when(j == 1, lambda: wo_step(1))
        when(j == 2, lambda: wo_step(3))
        when(j == 3, wo_there, weights_there)
        when(j >= 3, lambda: residual(j - 3))
        when(j < chunks, lambda: mix(j))
        when(j + 1 < chunks, lambda: gather_end(0, j + 1), lambda: start(x_load(j + 1)))
        when(j == 1, lambda: wo_step(2))
        when(j == 2, lambda: start(x_two(0)), lambda: gather(1, 0, 0).start(), lambda: gather(1, 1, 0).start())
        when(jnp.logical_and(j > 0, j < chunks), lambda: gather_pass(3, j - 1))
        when(j > 3, lambda: cot_turn(j - 4))
        when(j == 5, *[functools.partial(gather_pass, 1, k) for k in range(2, chunks)])
        when(j > 3, lambda: cot_fetch(j - 3))
        when(j >= 3, lambda: feed(j - 3))
        when(
            j == 3, wd_load.start, *[functools.partial(gather_pass, 1, k) for k in range(2)],
            *[gather(1, k, 0).start for k in range(2, chunks)], lambda: cot_fetch(0),
        )
        when(j == 4, lambda: gather_pass(3, chunks - 1))
        return 0

    for i in range(chunks):
        gather(1, i, 1).start()
    lax.fori_loop(0, chunks + 3, forward, 0)
    for q in range(4):
        wo_load(q).start()
    bcv_store(chunks - 1).wait()
    for pair in (0, 1):
        for core in (0, 1):
            h1_store(chunks - 1, (chunks - 1) % 2, pair, core).wait()

    cot_turn(chunks - 1)
    start(cot_load(0))

    def small_x():
        return pltpu.make_async_remote_copy(
            src_ref=small_v.at[pl.ds(0, 8)], dst_ref=small_r.at[0], send_sem=small_sem.at[0, 0],
            recv_sem=small_sem.at[0, 1], device_id=x_dev, device_id_type=MESH,
        )

    def small_z(way):
        return pltpu.make_async_remote_copy(
            src_ref=small_r.at[1 + way], dst_ref=small_r.at[3 + way], send_sem=small_sem.at[1 + way, 0],
            recv_sem=small_sem.at[1 + way, 1], device_id=dn_dev if way else up_dev, device_id_type=MESH,
        )

    def small_step(k):
        @pl.when(k == 0)
        def _():
            small_x().wait()
            total = small_v[pl.ds(0, 8), :] + small_r[0]
            small_v[pl.ds(0, 8), :] = total
            small_r[1] = total
            small_r[2] = total

        for way in (0, 1):
            turn = last - z if way else z

            @pl.when(jnp.logical_and(turn < last, k == turn))
            def _(way=way, turn=turn):
                @pl.when(turn > 0)
                def _():
                    small_z(way).wait_recv()
                    small_r[1 + way] = small_v[pl.ds(0, 8), :] + small_r[3 + way]

                small_z(way).start()

    def small_end():
        for way in (0, 1):
            turn = last - z if way else z

            @pl.when(turn < last)
            def _(way=way):
                small_z(way).wait_send()

            @pl.when(turn == last)
            def _(way=way):
                small_z(way).wait_recv()

            @pl.when(turn > 0)
            def _(way=way):
                small_v[pl.ds(0, 8), :] += small_r[3 + way]

    def stage_last(i):
        stage_g(i)

        @pl.when(i == chunks - 1)
        def _():
            small_v[4:5, :] = jnp.sum(small_v[8:16, :], 0, keepdims=True)
            small_x().start()

    order = (
        ("g", stage_last), ("out_end", out_end), ("out_share", out_share), ("b", stage_b), ("f", stage_f),
        ("c", stage_c), ("e", stage_e), ("d", stage_d), ("out_start", out_start), ("a", stage_a),
        ("hidden", None), ("a1", stage_a1),
    )

    def stages(t, third):
        for name, f in order:
            if name == "hidden":
                if HIDDEN[0] != third:
                    continue
                done = 0
                low = high = 0
                for at, upto in HIDDEN[1].items():
                    low = jnp.where(t == at, done, low)
                    high = jnp.where(t == at, upto, high)
                    done = upto

                def piece(k, _):
                    hidden_back(k)
                    return 0

                lax.fori_loop(low, high, piece, 0)
            elif PLACES[name][0] == third:
                where = PLACES[name][1]
                i = sum(jnp.where(t >= at, 1, 0) for at in where[1:])
                now = functools.reduce(jnp.logical_or, [t == at for at in where])
                pl.when(now)(functools.partial(f, i))

    def each_tick(t, _):
        tick_a(t, True)

        @pl.when(t == 0)
        def _():
            wd_load.wait()

        @pl.when(t == beat)
        def _():
            stage_loads(0)

        stages(t, 0)
        tick_b(t)
        stages(t, 1)
        tick_c(t)
        stages(t, 2)

        @pl.when(t > PLACES["g"][1][-1])
        def _():
            small_step(t - PLACES["g"][1][-1] - 1)

        return 0

    lax.fori_loop(0, ticks, each_tick, 0)
    gx_copy(chunks - 1).wait()

    def part_four(k, _):
        tick_a(ticks + k)
        tick_b(ticks + k)
        tick_c(ticks + k)
        return 0

    lax.fori_loop(0, LAG + 4, part_four, 0)
    small_end()
    plain_out(ticks - 2, "wait")
    plain_out(ticks - 1, "wait")
    out_do(ob.at[2], 3 * beat + SECOND, 2, "wait")


def block(dims, x_own, cot_own, gain_mix, gain_ff, taps, wd, wg, wu, wo, wi):
    tokens, chunk, width, ff, local, nseq = dims
    rows = width // (2 * nseq)
    chunks = tokens // chunk
    last = nseq - 1
    m = ROWS * nseq
    DMA = pltpu.SemaphoreType.DMA
    shape = jax.ShapeDtypeStruct
    third = ff // 3 // 128 * 128
    scratch = [
        pltpu.VMEM((2, width, tokens), BF),
        pltpu.VMEM((3, tokens, ff), BF),
        pltpu.VMEM((ff, width), BF),
        pltpu.VMEM((ff, width), BF),
        pltpu.VMEM((ff, width), BF),
        pltpu.VMEM((width, 2 * local), BF),
        pltpu.VMEM((chunk, width), BF),
        pltpu.VMEM((4, chunk, local), BF),
        pltpu.VMEM((chunk, local), BF),
        pltpu.VMEM((4, chunk, local), BF),
        pltpu.VMEM((8 + chunk, local), F32),
        pltpu.VMEM((chunk, ff - 2 * third), F32),
        pltpu.VMEM((8 + chunk, local), F32),
        pltpu.VMEM((chunk, width), BF),
        pltpu.VMEM((chunks, chunk, local), F32),
        pltpu.VMEM((chunk, 128), F32),
        pltpu.VMEM((4, 8, local), F32),
        pltpu.VMEM((8, local), F32),
        pltpu.VMEM((3, m, ff), BF),
        pltpu.VMEM((5, m, ff), BF),
        pltpu.VMEM((LAG + 4, m, ff), BF),
        pltpu.VMEM((2, last * (last + 3) // 2, ROWS, ff), BF),
        pltpu.VMEM((2, 4 * last + 2, ROWS, ff), BF),
        pltpu.VMEM((3, ROWS, ff), BF),
        pltpu.VMEM((ROWS, ff), BF),
        pltpu.VMEM((ROWS, ff), BF),
        pltpu.VMEM((ROWS, ff), F32),
        pltpu.VMEM((5, chunk, local), F32),
        pltpu.VMEM((2, chunk, local), BF),
        pltpu.VMEM((2, 2, chunk, local), BF),
        pltpu.VMEM((2, chunk, local), BF),
        pltpu.VMEM((4, 2, chunk, local), BF),
        pltpu.VMEM((2, 2, 2, chunk, local), BF),
        pltpu.VMEM((2, chunk, local), BF),
        pltpu.VMEM((chunk, local), BF),
        pltpu.VMEM((2, chunk, local), BF),
        pltpu.VMEM((8, chunk), F32),
        pltpu.VMEM((2, 8, chunk), F32),
        pltpu.VMEM((8, chunk), F32),
        pltpu.VMEM((2, 8, chunk), F32),
        pltpu.VMEM((chunk, local), BF),
        pltpu.VMEM((chunks, 8, local), F32),
        pltpu.VMEM((chunks, 8, local), F32),
        pltpu.VMEM((chunks, 8, local), F32),
        pltpu.VMEM((chunks, 8, local), F32),
        pltpu.VMEM((5, 8, local), F32),
        DMA((3,)), DMA((5,)), DMA((2, last * (last + 3) // 2)), DMA((2, 4 * last + 2)), DMA((3, 4)),
        DMA((2, 2)), DMA((2, chunks)), DMA((2, 2)), DMA((2, 2)), DMA((2, 2)),
        DMA((2, 2)), DMA((2, 2)), DMA((2, chunks)), DMA((2, chunks)), DMA((3, 2, 4, chunks)),
        DMA((7,)), DMA((4, 4)), DMA(()), DMA((2, 2)), DMA(()), DMA((3, 2)), DMA((2,)), DMA((2,)), DMA((2, nseq)), DMA((2, 2, last)), DMA((2, 4)), DMA((4,)),
    ]
    return pl.pallas_call(
        functools.partial(block_kernel, dims),
        out_shape=(
            shape((rows, ff), BF), shape((rows, ff), BF), shape((rows, ff), BF),
            shape((rows, local), BF), shape((3, rows, local), BF),
            shape((tokens, local), BF), shape((tokens, local), BF), shape((16, local), F32),
            shape((4, tokens, local), BF), shape((4, tokens, local), BF),
            shape((4, tokens, local), BF), shape((4, tokens, local), BF), shape((local, width), BF),
        ),
        in_specs=[ANY] * 2 + [VMEM] * 3 + [ANY] * 5,
        out_specs=(ANY,) * 7 + (VMEM,) + (ANY,) * 5,
        scratch_shapes=scratch,
        compiler_params=pltpu.CompilerParams(
            collective_id=0, has_side_effects=True, vmem_limit_bytes=63 * 2**20
        ),
    )(x_own, cot_own, gain_mix, gain_ff, taps, wd, wg, wu, wo, wi)


def shifted(array, axis, by):
    count = lax.axis_size(axis)
    pairs = [(i, i + by) for i in range(count) if 0 <= i + by < count]
    return lax.ppermute(array, axis, pairs)


def fused_device(inputs, gain_mix, w_in, kernel, w_out, gain_ff, w_gate, w_up, w_down, cotangent):
    groups, seq_rows, local = inputs.shape
    width = local * lax.axis_size("mp")
    ff = w_down.shape[0]
    tokens = groups * seq_rows
    dims = (tokens, seq_rows, width, ff, local, lax.axis_size("seq"))
    gdown, ggate, gup, gout, gin, gx, out, small = block(
        dims, inputs.reshape(tokens, local), cotangent.reshape(tokens, local), gain_mix, gain_ff, kernel,
        w_down, w_gate.T, w_up.T, w_out, w_in.transpose(1, 0, 2),
    )[:8]
    gdown, ggate, gup, gout, gin, gx, out, gmix, gtaps, gff = widen(
        gdown, ggate, gup, gout, gin, gx, out, small
    )
    whole = (groups, seq_rows, local)
    return (
        out.reshape(whole), gx.reshape(whole), gmix, gin.transpose(1, 0, 2), gtaps,
        gout.T, gff, ggate, gup, gdown.T,
    )


def widen_kernel(*refs):
    count = 7
    src, small, dst = refs[:count], refs[count], refs[count + 1 : 2 * count + 1]
    gmix, gtaps, gff = refs[2 * count + 1 : 2 * count + 4]
    narrow = refs[2 * count + 4 : 3 * count + 4]
    wide = refs[3 * count + 4 : 4 * count + 2]
    in_sem, out_sem = refs[4 * count + 2 :]
    loads = [pltpu.make_async_copy(src[k], narrow[k], in_sem.at[k]) for k in range(count)]
    stores = [
        pltpu.make_async_copy(wide[k] if k < count - 2 else narrow[k], dst[k], out_sem.at[k])
        for k in range(count)
    ]
    order = (*range(count - 2, count), *range(count - 2))
    for k in order:
        loads[k].start()
    gmix[...] = small[0:1, :].reshape(gmix.shape)
    gtaps[...] = small[1:4, :]
    gff[...] = small[4:5, :].reshape(gff.shape)
    for k in order:
        loads[k].wait()
        if k < count - 2:
            wide[k][...] = narrow[k][...].astype(F32)
        stores[k].start()
    for one in stores:
        one.wait()


def widen(*arrays):
    big, small = arrays[:7], arrays[7]
    local = small.shape[1]
    shape = jax.ShapeDtypeStruct
    outs = [shape(a.shape, F32 if k < 5 else BF) for k, a in enumerate(big)]
    outs += [shape((local,), F32), shape((3, local), F32), shape((local,), F32)]
    return pl.pallas_call(
        widen_kernel,
        out_shape=outs,
        in_specs=[ANY] * 7 + [VMEM],
        out_specs=[ANY] * 7 + [VMEM] * 3,
        scratch_shapes=[pltpu.VMEM(a.shape, BF) for a in big]
        + [pltpu.VMEM(a.shape, F32) for a in big[:5]]
        + [pltpu.SemaphoreType.DMA((7,))] * 2,
        compiler_params=pltpu.CompilerParams(vmem_limit_bytes=63 * 2**20),
    )(*big, small)


def contract_rows(left, right):
    return lax.dot_general(
        left, right, (((0,), (0,)), ((), ())), preferred_element_type=jnp.float32
    )


def contract_cols(left, right):
    return lax.dot_general(
        left, right, (((1,), (1,)), ((), ())), preferred_element_type=jnp.float32
    )


def plain_device(inputs, gain_mix, w_in, kernel, w_out, gain_ff, w_gate, w_up, w_down, cotangent):
    groups, seq_rows, local_width = inputs.shape
    full_width = local_width * lax.axis_size("mp")
    tokens = groups * seq_rows
    x_float = inputs.reshape(tokens, local_width).astype(jnp.float32)
    gain_one = gain_mix.astype(jnp.float32)
    gain_two = gain_ff.astype(jnp.float32)
    taps = kernel.astype(jnp.float32)

    def row_total(values):
        return lax.psum(jnp.sum(values, axis=-1, keepdims=True), "mp")

    def all_features(values):
        return lax.all_gather(values, "mp", axis=1, tiled=True)

    def share_sums(values):
        return lax.psum_scatter(
            values.astype(jnp.bfloat16), "mp", scatter_dimension=1, tiled=True
        ).astype(jnp.float32)

    def scattered(values, dim):
        return lax.psum_scatter(
            values.astype(jnp.bfloat16), ("dp", "seq"), scatter_dimension=dim, tiled=True
        ).astype(jnp.float32)

    def norm_scale(values):
        return lax.rsqrt(row_total(values * values) / full_width + EPS)

    def norm_back(values, scale, gain_vec, upstream):
        inner = row_total(gain_vec * upstream * values)
        grad_values = scale * gain_vec * upstream - values * scale**3 * inner / full_width
        return (grad_values, jnp.sum(upstream * values * scale, axis=0))

    scale_one = norm_scale(x_float)
    normed_in = all_features((x_float * scale_one * gain_one).astype(jnp.bfloat16))
    proj = jnp.einsum("td,dkc->tkc", normed_in, w_in, preferred_element_type=jnp.float32)
    b_gate = proj[:, 0]
    c_gate = proj[:, 1]
    values_v = proj[:, 2]
    b_times_x = (b_gate * values_v).astype(jnp.bfloat16).reshape(groups, seq_rows, local_width)
    before = shifted(b_times_x[:, seq_rows - 2 :], "seq", 1)
    padded = jnp.concatenate([before, b_times_x], 1).astype(jnp.float32)
    conv = taps[0] * padded[:, :-2] + taps[1] * padded[:, 1:-1] + taps[2] * padded[:, 2:]
    conv = conv.reshape(tokens, local_width)
    mixed = (c_gate * conv).astype(jnp.bfloat16)
    hidden_one = x_float + share_sums(jnp.dot(mixed, w_out, preferred_element_type=jnp.float32))
    scale_two = norm_scale(hidden_one)
    normed_ff = all_features((hidden_one * scale_two * gain_two).astype(jnp.bfloat16))
    gate = jnp.dot(normed_ff, w_gate, preferred_element_type=jnp.float32)
    up_proj = jnp.dot(normed_ff, w_up, preferred_element_type=jnp.float32)
    sigma = jax.nn.sigmoid(gate)
    active = gate * sigma
    hidden = (active * up_proj).astype(jnp.bfloat16)
    ffn_out = share_sums(jnp.dot(hidden, w_down, preferred_element_type=jnp.float32))
    block_out = (hidden_one + ffn_out).astype(jnp.bfloat16).reshape(groups, seq_rows, local_width)
    grad_flat = cotangent.reshape(tokens, local_width)
    grad_full = all_features(grad_flat)
    grad_down = contract_rows(hidden, grad_full)
    grad_hidden = contract_cols(grad_full, w_down)
    grad_gate_act = (grad_hidden * up_proj * sigma * (1.0 + gate * (1.0 - sigma))).astype(
        jnp.bfloat16
    )
    grad_up_act = (grad_hidden * active).astype(jnp.bfloat16)
    grad_gate = contract_rows(normed_ff, grad_gate_act)
    grad_up = contract_rows(normed_ff, grad_up_act)
    grad_normed_ff = share_sums(
        contract_cols(grad_gate_act, w_gate) + contract_cols(grad_up_act, w_up)
    )
    grad_norm_two, grad_gain_two = norm_back(hidden_one, scale_two, gain_two, grad_normed_ff)
    grad_hidden_one = grad_flat.astype(jnp.float32) + grad_norm_two
    grad_out_full = all_features(grad_hidden_one.astype(jnp.bfloat16))
    grad_out = contract_rows(mixed, grad_out_full)
    grad_mixed = contract_cols(grad_out_full, w_out)
    grad_c = grad_mixed * conv
    grad_conv = (grad_mixed * c_gate).astype(jnp.bfloat16).reshape(groups, seq_rows, local_width)
    after = shifted(grad_conv[:, :2], "seq", -1)
    extended = jnp.concatenate([grad_conv, after], 1).astype(jnp.float32)
    grad_bx = taps[2] * extended[:, :-2] + taps[1] * extended[:, 1:-1] + taps[0] * extended[:, 2:]
    grad_bx = grad_bx.reshape(tokens, local_width)
    conv_grad_float = extended[:, :-2]
    grad_taps = jnp.stack(
        [
            jnp.sum(conv_grad_float * padded[:, :-2], axis=(0, 1)),
            jnp.sum(conv_grad_float * padded[:, 1:-1], axis=(0, 1)),
            jnp.sum(conv_grad_float * padded[:, 2:], axis=(0, 1)),
        ]
    )
    grad_proj = jnp.stack([grad_bx * values_v, grad_c, grad_bx * b_gate], 1).astype(jnp.bfloat16)
    grad_in = jnp.einsum("td,tkc->dkc", normed_in, grad_proj, preferred_element_type=jnp.float32)
    grad_normed_in = share_sums(
        jnp.einsum("tkc,dkc->td", grad_proj, w_in, preferred_element_type=jnp.float32)
    )
    grad_norm_one, grad_gain_one = norm_back(x_float, scale_one, gain_one, grad_normed_in)
    grad_input = (
        (grad_hidden_one + grad_norm_one)
        .astype(jnp.bfloat16)
        .reshape(groups, seq_rows, local_width)
    )
    small_sums = lax.psum((grad_gain_one, grad_taps, grad_gain_two), ("dp", "seq"))
    by_row = (
        scattered(grad_in, 0),
        scattered(grad_gate, 0),
        scattered(grad_up, 0),
    )
    by_col = (
        scattered(grad_out, 1),
        scattered(grad_down, 1),
    )
    return (
        block_out,
        grad_input,
        small_sums[0],
        by_row[0],
        small_sums[1],
        by_col[0],
        small_sums[2],
        by_row[1],
        by_row[2],
        by_col[1],
    )


def solution(mesh):
    placed = (
        P("dp", "seq", "mp"),
        P("mp"),
        P(None, None, "mp"),
        P(None, "mp"),
        P("mp", None),
        P("mp"),
        P(None, "mp"),
        P(None, "mp"),
        P("mp", None),
        P("dp", "seq", "mp"),
    )
    sizes = mesh.shape
    fused = sizes["dp"] == 2 and sizes["seq"] == 4 and sizes["mp"] == 4
    return jax.shard_map(
        fused_device if fused else plain_device,
        mesh=mesh,
        in_specs=placed,
        out_specs=(
            P("dp", "seq", "mp"),
            P("dp", "seq", "mp"),
            P("mp"),
            P(("dp", "seq"), None, "mp"),
            P(None, "mp"),
            P("mp", ("dp", "seq")),
            P("mp"),
            P(("dp", "seq"), "mp"),
            P(("dp", "seq"), "mp"),
            P("mp", ("dp", "seq")),
        ),
        check_vma=False,
    )
```
